32 devices in a mesh: grp: 4 (over y, x), seq: 8 (over z, core).
Axes of the slice: x: 2, y: 2, z: 4, core: 2. Of those that a mesh axis runs over, the one named last changes fastest.
Arguments:
- query_input: bfloat16 [4096, 4096], P(('grp', 'seq')), may hold values from -8 to 8
- key_input: bfloat16 [4096, 512], P(('grp', 'seq')), may hold values from -8 to 8
- value_input: bfloat16 [4096, 512], P(('grp', 'seq')), may hold values from -6 to 6
- out_grad: bfloat16 [4096, 4096], P(('grp', 'seq')), may hold values from -6 to 6
- key_blocks: int32 [32, 12], replicated, may hold values from 0 to 31, as said below
- key_counts: int32 [32], replicated, may hold values from 1 to 12, as said below
- block_position: int32 [32], replicated, may hold values from 0 to 31, each once
Outputs:
- attn_out: bfloat16 [4096, 4096], P(('grp', 'seq'))
- query_grad: bfloat16 [4096, 4096], P(('grp', 'seq'))
- key_grad: bfloat16 [4096, 512], P(('grp', 'seq'))
- value_grad: bfloat16 [4096, 512], P(('grp', 'seq'))
The draws below stay inside these ranges and needn't reach their ends.
Inputs may be any that keep to these rules, and one draw needn't show every extreme that they name: `key_blocks`: in row b the first key_counts[b] entries are distinct, the first is b itself and the others are earlier blocks of the same group of 8 blocks or of the group before; the remaining entries equal b. `key_counts`: the last block's count is 12.
All inputs are finite; a program needn't handle non-finite values.
Results may differ from the reference program's by a relative error of at most 0.015.
Values may be sent and summed in bfloat16 or wider, within the bound.
No kernel may reach another device: no remote copies, remote signals or barrier semaphores. Data moves between devices by JAX's collectives and lax.ppermute only.
A program may use at most 128 MiB of HBM per device.

```python
import math
import jax
import jax.numpy as jnp
from jax import lax

HEADS = 32
KV_HEADS = 4
HEAD_DIM = 128
BLK = 128
KB = 12
GB = 8
NB = 32
TOKENS = 4096


def mask_tables(key):
    block_ids = jnp.arange(NB, dtype=jnp.int32)
    group_ids = block_ids // GB
    lowest = jnp.maximum(group_ids - 1, 0) * GB
    reachable = block_ids - lowest + 1
    drawn_counts = jax.random.randint(jax.random.fold_in(key, 11), (NB,), 1, KB + 1, dtype=jnp.int32)
    counts = jnp.minimum(drawn_counts, reachable)
    counts = jnp.where(block_ids == NB - 1, KB, counts).astype(jnp.int32)
    window_size = 2 * GB - 1
    offsets = jnp.arange(1, window_size + 1, dtype=jnp.int32)
    random_part = jax.random.randint(jax.random.fold_in(key, 12), (NB, window_size), 0, 2 ** 20, dtype=jnp.int32)
    candidates = block_ids[:, None] - offsets[None, :]
    scores = jnp.where(candidates >= lowest[:, None], random_part * window_size + offsets[None, :], -offsets[None, :])
    top_scores, picked = lax.top_k(scores, KB - 1)
    chosen = block_ids[:, None] - (picked.astype(jnp.int32) + 1)
    listed = jnp.concatenate([block_ids[:, None], chosen], axis=1)
    slot_ids = jnp.arange(KB, dtype=jnp.int32)
    listed = jnp.where(slot_ids[None, :] < counts[:, None], listed, block_ids[:, None])
    return (listed.astype(jnp.int32), counts)


def draw_key_blocks(key, part):
    return mask_tables(key)[0]


def draw_key_counts(key, part):
    return mask_tables(key)[1]


def drawn_fields(key):
    head_ratio = HEADS // KV_HEADS
    base_query = jnp.clip(jax.random.normal(jax.random.fold_in(key, 21), (TOKENS, KV_HEADS, head_ratio, HEAD_DIM), jnp.float32), -6.0, 6.0)
    base_key = jnp.clip(jax.random.normal(jax.random.fold_in(key, 22), (TOKENS, KV_HEADS, HEAD_DIM), jnp.float32), -6.0, 6.0)
    return (base_query.reshape(TOKENS, HEADS * HEAD_DIM), base_key.reshape(TOKENS, KV_HEADS * HEAD_DIM))


def draw_query_input(key, part):
    return drawn_fields(key)[0].astype(jnp.bfloat16)


def draw_key_input(key, part):
    return drawn_fields(key)[1].astype(jnp.bfloat16)


def block_scale(key, extent, shards, smallest, largest):
    gain = 1.0
    for dim, blocks in shards:
        steps = jax.random.uniform(jax.random.fold_in(jax.random.fold_in(key, 6), dim), (blocks,), jnp.float32, smallest / len(shards), largest / len(shards))
        gain = gain * jnp.repeat(jnp.exp(steps), extent[dim] // blocks).reshape((-1,) + (1,) * (len(extent) - 1 - dim))
    return gain


def bell_draw(key, extent, deviation, bound, cuts=(), kind=jnp.bfloat16):
    entries = deviation * jax.random.normal(key, extent, jnp.float32)
    if cuts:
        entries = entries * block_scale(key, extent, cuts, -0.22, 0.18)
    return jnp.clip(entries, -bound, bound).astype(kind)


def setup_inputs(seed: int = 0) -> dict:
    seeds = jax.random.split(jax.random.key(seed), 8)
    return {
        "query_input": draw_query_input(jax.random.fold_in(seeds[7], 71), 0),
        "key_input": draw_key_input(jax.random.fold_in(seeds[7], 71), 0),
        "value_input": bell_draw(seeds[2], (TOKENS, KV_HEADS * HEAD_DIM), 1.0, 6.0, ((0, 32),)),
        "out_grad": bell_draw(seeds[3], (TOKENS, HEADS * HEAD_DIM), 1.0, 6.0, ((0, 32),)),
        "key_blocks": draw_key_blocks(jax.random.fold_in(seeds[7], 71), 0),
        "key_counts": draw_key_counts(jax.random.fold_in(seeds[7], 71), 0),
        "block_position": jax.random.permutation(seeds[6], NB).astype(jnp.int32),
    }


def rope_tables(places):
    offsets = jnp.arange(BLK, dtype=jnp.int32)
    positions = (places[:, None] * BLK + offsets[None, :]).astype(jnp.float32)
    exponents = jnp.arange(HEAD_DIM // 2, dtype=jnp.float32) * (2.0 / HEAD_DIM)
    frequency = jnp.power(jnp.float32(500000.0), -exponents)
    angles = positions[:, :, None] * frequency
    return (jnp.cos(angles), jnp.sin(angles))

def rotate(values, cosine, sine_part):
    half_dim = HEAD_DIM // 2
    first_half = values[..., :half_dim]
    second_half = values[..., half_dim:]
    return jnp.concatenate([first_half * cosine - second_half * sine_part, second_half * cosine + first_half * sine_part], axis=-1)

def unrotate(values, cosine, sine_part):
    half_dim = HEAD_DIM // 2
    first_half = values[..., :half_dim]
    second_half = values[..., half_dim:]
    return jnp.concatenate([first_half * cosine + second_half * sine_part, second_half * cosine - first_half * sine_part], axis=-1)

def reference(query_input, key_input, value_input, out_grad, key_blocks, key_counts, block_position):
    head_ratio = HEADS // KV_HEADS
    score_scale = 1.0 / math.sqrt(HEAD_DIM)
    cosine, sine_part = rope_tables(block_position)
    query_cos = cosine[:, :, None, None, :]
    query_sin = sine_part[:, :, None, None, :]
    key_cos = cosine[:, :, None, :]
    key_sin = sine_part[:, :, None, :]
    q_rot = rotate(query_input.astype(jnp.float32).reshape(NB, BLK, KV_HEADS, head_ratio, HEAD_DIM), query_cos, query_sin).astype(jnp.bfloat16)
    k_rot = rotate(key_input.astype(jnp.float32).reshape(NB, BLK, KV_HEADS, HEAD_DIM), key_cos, key_sin).astype(jnp.bfloat16)
    value_blocks = value_input.reshape(NB, BLK, KV_HEADS, HEAD_DIM)
    grad_blocks = out_grad.reshape(NB, BLK, KV_HEADS, head_ratio, HEAD_DIM)
    offsets = jnp.arange(BLK, dtype=jnp.int32)
    causal_lower = offsets[None, :] <= offsets[:, None]
    slot_ids = jnp.arange(KB, dtype=jnp.int32)

    def advance(running, block_id):
        key_acc, value_acc = running
        listed = key_blocks[block_id]
        usable = slot_ids < key_counts[block_id]
        diagonal_hit = listed == block_id
        allowed = usable[None, :, None] & (jnp.logical_not(diagonal_hit)[None, :, None] | causal_lower[:, None, :])
        query_here = q_rot[block_id].astype(jnp.float32)
        key_here = k_rot[listed].astype(jnp.float32)
        value_here = value_blocks[listed].astype(jnp.float32)
        grad_here = grad_blocks[block_id].astype(jnp.float32)
        scores = jnp.einsum('tgrd,jugd->grtju', query_here, key_here) * score_scale
        scores = jnp.where(allowed[None, None], scores, -jnp.inf)
        row_max = lax.optimization_barrier(jnp.max(scores, axis=(3, 4), keepdims=True))
        weights = jnp.exp(scores - row_max)
        probs_full = weights / lax.optimization_barrier(jnp.sum(weights, axis=(3, 4), keepdims=True))
        probs_low = lax.optimization_barrier(probs_full.astype(jnp.bfloat16)).astype(jnp.float32)
        attended = lax.optimization_barrier(jnp.einsum('grtju,jugd->tgrd', probs_low, value_here).astype(jnp.bfloat16))
        row_delta = lax.optimization_barrier(jnp.sum(grad_here * attended.astype(jnp.float32), axis=-1))
        dprobs = jnp.einsum('tgrd,jugd->grtju', grad_here, value_here)
        dscores = probs_full * (dprobs - jnp.transpose(row_delta, (1, 2, 0))[:, :, :, None, None])
        dscores_low = lax.optimization_barrier(dscores.astype(jnp.bfloat16)).astype(jnp.float32)
        query_part = (jnp.einsum('grtju,jugd->tgrd', dscores_low, key_here) * score_scale).astype(jnp.bfloat16)
        key_part = jnp.einsum('grtju,tgrd->jugd', dscores_low, query_here) * score_scale
        value_part = jnp.einsum('grtju,tgrd->jugd', probs_low, grad_here)
        key_acc = key_acc.at[listed].add(key_part)
        value_acc = value_acc.at[listed].add(value_part)
        return ((key_acc, value_acc), (attended, query_part))
    zero_grads = jnp.zeros((NB, BLK, KV_HEADS, HEAD_DIM), jnp.float32)
    (key_acc, value_acc), (out_blocks, dq_blocks) = lax.scan(advance, (zero_grads, zero_grads), jnp.arange(NB, dtype=jnp.int32))
    attn_out = out_blocks.reshape(TOKENS, HEADS * HEAD_DIM)
    query_grad = unrotate(dq_blocks.astype(jnp.float32), query_cos, query_sin).astype(jnp.bfloat16).reshape(TOKENS, HEADS * HEAD_DIM)
    key_grad = unrotate(key_acc, key_cos, key_sin).astype(jnp.bfloat16).reshape(TOKENS, KV_HEADS * HEAD_DIM)
    value_grad = value_acc.astype(jnp.bfloat16).reshape(TOKENS, KV_HEADS * HEAD_DIM)
    return (attn_out, query_grad, key_grad, value_grad)
```

```python
import functools
import math

import jax
import jax.numpy as jnp
import numpy as np
from jax import lax
from jax.experimental import pallas as pl
from jax.experimental.pallas import tpu as pltpu
from jax.sharding import PartitionSpec as P

HEADS = 32
KV_HEADS = 4
HEAD_DIM = 128
BLK = 128
CORES = 2
RATIO = HEADS // KV_HEADS
HALF_KV = KV_HEADS // CORES
ROWS = RATIO * BLK
SCALE = 1.0 / math.sqrt(HEAD_DIM)
TO_LOG2 = SCALE * math.log2(math.e)
F32 = jnp.float32
BF16 = jnp.bfloat16
CHUNK = 256

VMEM_SPEC = pl.BlockSpec(memory_space=pltpu.VMEM)
SMEM_SPEC = pl.BlockSpec(memory_space=pltpu.SMEM)


def trig_tables(n_blocks):
    half = HEAD_DIM // 2
    frequency = np.power(500000.0, -np.arange(half) * (2.0 / HEAD_DIM))
    tables = []
    for places in (np.arange(n_blocks) * BLK, np.arange(BLK)):
        angles = places[:, None] * frequency
        for part in (np.cos(angles), np.sin(angles)):
            tables.append(np.concatenate([part, part], axis=1).astype(np.float32))
    return tables


def block_tables(place, block_cos, block_sin, token_cos, token_sin):
    cos_b = block_cos[pl.ds(place, 1), :]
    sin_b = block_sin[pl.ds(place, 1), :]
    cosine = cos_b * token_cos[...] - sin_b * token_sin[...]
    sine = sin_b * token_cos[...] + cos_b * token_sin[...]
    lanes = lax.broadcasted_iota(jnp.int32, sine.shape, 1)
    return cosine, jnp.where(lanes < HEAD_DIM // 2, -sine, sine)


def turn(values, cosine, signed_sine):
    return values * cosine + pltpu.roll(values, HEAD_DIM // 2, 1) * signed_sine


def dot_nt(a, b):
    return lax.dot_general(a, b, (((1,), (1,)), ((), ())), preferred_element_type=F32)


def dot_nn(a, b):
    return lax.dot_general(a, b, (((1,), (0,)), ((), ())), preferred_element_type=F32)


def here(n_seq):
    member = lax.axis_index("seq")
    group = lax.axis_index("grp")
    return group, member, lax.rem(member, CORES)


def call(kernel, out_shape, n_smem, n_vmem, scratch=(), flops=0, moved=0, name=None):
    return pl.pallas_call(
        kernel,
        out_shape=out_shape,
        in_specs=[SMEM_SPEC] * n_smem + [VMEM_SPEC] * n_vmem,
        out_specs=jax.tree.map(lambda _: VMEM_SPEC, out_shape),
        scratch_shapes=list(scratch),
        compiler_params=pltpu.CompilerParams(vmem_limit_bytes=56 * 2**20),
        cost_estimate=pl.CostEstimate(flops=flops, bytes_accessed=moved, transcendentals=0),
        name=name,
    )


def prepare_kv(n_seq, place_ref, key, value, bc, bs, tc, ts, keep, send):
    group, member, core = here(n_seq)
    cosine, sine = block_tables(place_ref[group * n_seq + member], bc, bs, tc, ts)
    for out, half in ((keep, core), (send, 1 - core)):
        for h in range(HALF_KV):
            columns = pl.ds(pl.multiple_of((half * HALF_KV + h) * HEAD_DIM, HEAD_DIM), HEAD_DIM)
            out[0, h] = turn(key[:, columns].astype(F32), cosine, sine).astype(BF16)
            out[1, h] = value[:, columns]


def prepare_queries(n_seq, place_ref, query, grad, bc, bs, tc, ts, keep, send):
    group, member, core = here(n_seq)
    cosine, sine = block_tables(place_ref[group * n_seq + member], bc, bs, tc, ts)
    for out, half in ((keep, core), (send, 1 - core)):
        for h in range(HALF_KV):
            for r in range(RATIO):
                head = (half * HALF_KV + h) * RATIO + r
                columns = pl.ds(pl.multiple_of(head * HEAD_DIM, HEAD_DIM), HEAD_DIM)
                out[0, h, r] = turn(query[:, columns].astype(F32), cosine, sine).astype(BF16)
                out[1, h, r] = grad[:, columns]


def list_blocks(n_seq, current, block, group, core, key_blocks, key_counts, found):
    base = group * n_seq
    n_listed = key_blocks.shape[1]

    def look(j, n):
        entry = key_blocks[block, j]
        if current:
            hit = jnp.logical_and(j < key_counts[block], entry >= base)
            offset = entry - base
        else:
            hit = jnp.logical_and(j < key_counts[block], entry < base)
            offset = entry - base + n_seq
        offset = jnp.where(hit, offset, 0)

        @pl.when(hit)
        def _():
            found[n] = lax.bitwise_xor(offset, core)

        return n + hit.astype(jnp.int32)

    return lax.fori_loop(1, n_listed, look, jnp.int32(0))


def causal():
    keys = lax.broadcasted_iota(jnp.int32, (BLK, CHUNK), 0)
    tokens = lax.rem(lax.broadcasted_iota(jnp.int32, (BLK, CHUNK), 1), BLK)
    return keys <= tokens


def pair_of(store, e, h, rows_q, rows_g, at, diagonal):
    scores = dot_nt(store[e, 0, h], rows_q[at])
    if diagonal:
        scores = jnp.where(causal(), scores, -1e30)
    return scores, dot_nt(store[e, 1, h], rows_g[at])


def chunks():
    per = CHUNK // BLK
    return [(slice(c * per, (c + 1) * per), slice(c * CHUNK, (c + 1) * CHUNK)) for c in range(ROWS // CHUNK)]


def heads_of(block, what, h, rows):
    return block[what, h, rows].reshape(CHUNK, HEAD_DIM)


def gather_stats(store, e, block, stats, i, diagonal, first, keep=None):
    for h in range(HALF_KV):
        for rows, columns in chunks():
            scores = dot_nt(store[e, 0, h], heads_of(block, 0, h, rows))
            if diagonal:
                scores = jnp.where(causal(), scores, -1e30)
            dprobs = dot_nt(store[e, 1, h], heads_of(block, 1, h, rows))
            if keep is not None:
                n, kept_scores, kept_dprobs = keep
                kept_scores[n, h, :, columns] = scores
                kept_dprobs[n, h, :, columns] = dprobs
            top = jnp.max(scores, axis=0, keepdims=True)
            if not first:
                old_top = stats[i, h, 0:1, columns]
                top = jnp.maximum(top, old_top)
            weights = jnp.exp2((scores - top) * TO_LOG2)
            total = jnp.sum(weights, axis=0, keepdims=True)
            mixed = jnp.sum(weights * dprobs, axis=0, keepdims=True)
            if not first:
                shrink = jnp.exp2((old_top - top) * TO_LOG2)
                total += stats[i, h, 1:2, columns] * shrink
                mixed += stats[i, h, 2:3, columns] * shrink
            stats[i, h, 0:1, columns] = top
            stats[i, h, 1:2, columns] = total
            stats[i, h, 2:3, columns] = mixed


def current_stats(n_seq, key_blocks, key_counts, store, own, other, stats, found):
    group, member, core = here(n_seq)
    for i, block in enumerate((own, other)):
        offset = member if i == 0 else lax.bitwise_xor(member, 1)
        gather_stats(store, lax.bitwise_xor(offset, core), block, stats, i, True, True)
        count = list_blocks(
            n_seq, True, group * n_seq + offset, group, core, key_blocks, key_counts, found
        )

        def step(n, _):
            gather_stats(store, found[n], block, stats, i, False, False)
            return 0

        lax.fori_loop(0, count, step, 0)


def previous_grads(
    n_seq, key_blocks, key_counts, keys, values, own, other, stats_in,
    dk_out, dv_out, stats, found, kept_scores, kept_dprobs, dk_acc, dv_acc,
):
    group, member, core = here(n_seq)
    dk_acc[...] = jnp.zeros_like(dk_acc)
    dv_acc[...] = jnp.zeros_like(dv_acc)
    stats[...] = stats_in[...]
    for i, block in enumerate((own, other)):
        offset = member if i == 0 else lax.bitwise_xor(member, 1)
        count = list_blocks(
            n_seq, False, group * n_seq + offset, group, core, key_blocks, key_counts, found
        )

        def look(n, _):
            e = found[n]
            for h in range(HALF_KV):
                for rows, columns in chunks():
                    scores = dot_nt(keys[e, h], heads_of(block, 0, h, rows))
                    dprobs = dot_nt(values[e, h], heads_of(block, 1, h, rows))
                    kept_scores[n, h, :, columns] = scores
                    kept_dprobs[n, h, :, columns] = dprobs
                    old_top = stats[i, h, 0:1, columns]
                    top = jnp.maximum(jnp.max(scores, axis=0, keepdims=True), old_top)
                    weights = jnp.exp2((scores - top) * TO_LOG2)
                    shrink = jnp.exp2((old_top - top) * TO_LOG2)
                    stats[i, h, 0:1, columns] = top
                    stats[i, h, 1:2, columns] = stats[i, h, 1:2, columns] * shrink + jnp.sum(
                        weights, axis=0, keepdims=True
                    )
                    stats[i, h, 2:3, columns] = stats[i, h, 2:3, columns] * shrink + jnp.sum(
                        weights * dprobs, axis=0, keepdims=True
                    )
            return 0

        lax.fori_loop(0, count, look, 0)
        for h in range(HALF_KV):
            total = stats[i, h, 1:2, :]
            stats[i, h, 0:1, :] = stats[i, h, 0:1, :] * TO_LOG2 + jnp.log2(total)
            stats[i, h, 2:3, :] = stats[i, h, 2:3, :] / total

        def add(n, _):
            e = found[n]
            for h in range(HALF_KV):
                dk = dk_acc[e, h]
                dv = dv_acc[e, h]
                for rows, columns in chunks():
                    probs = jnp.exp2(
                        kept_scores[n, h, :, columns] * TO_LOG2 - stats[i, h, 0:1, columns]
                    )
                    dscores = probs * (kept_dprobs[n, h, :, columns] - stats[i, h, 2:3, columns])
                    dv += dot_nn(probs.astype(BF16), heads_of(block, 1, h, rows))
                    dk += dot_nn(dscores.astype(BF16), heads_of(block, 0, h, rows))
                dk_acc[e, h] = dk
                dv_acc[e, h] = dv
            return 0

        lax.fori_loop(0, count, add, 0)
    dk_out[...] = (dk_acc[...] * SCALE).astype(BF16)
    dv_out[...] = dv_acc[...].astype(BF16)


def from_block(keys, values, e, block, stats, i, diagonal, out_acc, dq_acc, grads):
    for h in range(HALF_KV):
        key = keys[e]
        value = values[e]
        key, value = key[h], value[h]
        key_t, value_t = key.T, value.T
        if grads is not None:
            dk, dv = grads[0][e, h], grads[1][e, h]
        for rows, columns in chunks():
            query = heads_of(block, 0, h, rows)
            grad = heads_of(block, 1, h, rows)
            scores = dot_nt(key, query)
            if diagonal:
                scores = jnp.where(causal(), scores, -1e30)
            dprobs = dot_nt(value, grad)
            probs = jnp.exp2(scores * TO_LOG2 - stats[i, h, 0:1, columns])
            dscores = (probs * (dprobs - stats[i, h, 2:3, columns])).astype(BF16)
            probs = probs.astype(BF16)
            if grads is not None:
                dv += dot_nn(probs, grad)
                dk += dot_nn(dscores, query)
            attended = dot_nn(value_t, probs)
            query_part = dot_nn(key_t, dscores)
            if diagonal:
                out_acc[i, h, :, columns] = attended
                dq_acc[i, h, :, columns] = query_part
            else:
                out_acc[i, h, :, columns] += attended
                dq_acc[i, h, :, columns] += query_part
        if grads is not None:
            grads[0][e, h] = dk
            grads[1][e, h] = dv


def current_grads(
    n_seq, key_blocks, key_counts, store, own, other, stats,
    dk_out, dv_out, out_acc, dq_acc, found, dk_acc, dv_acc,
):
    group, member, core = here(n_seq)
    dk_acc[...] = jnp.zeros_like(dk_acc)
    dv_acc[...] = jnp.zeros_like(dv_acc)
    keys = KeysOf(store, 0)
    values = KeysOf(store, 1)
    for i, block in enumerate((own, other)):
        offset = member if i == 0 else lax.bitwise_xor(member, 1)
        count = list_blocks(
            n_seq, True, group * n_seq + offset, group, core, key_blocks, key_counts, found
        )
        from_block(
            keys, values, lax.bitwise_xor(offset, core), block, stats, i, True,
            out_acc, dq_acc, (dk_acc, dv_acc),
        )

        def step(n, _):
            from_block(
                keys, values, found[n], block, stats, i, False, out_acc, dq_acc, (dk_acc, dv_acc)
            )
            return 0

        lax.fori_loop(0, count, step, 0)
    dk_out[...] = dk_acc[...] * SCALE
    dv_out[...] = dv_acc[...]


class KeysOf:
    def __init__(self, store, which):
        self.store, self.which = store, which

    def __getitem__(self, e):
        return self.store[e, self.which]


def query_results(
    n_seq, key_blocks, key_counts, place_ref, keys, values, own, other, stats, out_in, dq_in,
    bc, bs, tc, ts, own_out, other_out, found, out_acc, dq_acc,
):
    group, member, core = here(n_seq)
    out_acc[...] = out_in[...]
    dq_acc[...] = dq_in[...]
    for i, block in enumerate((own, other)):
        offset = member if i == 0 else lax.bitwise_xor(member, 1)
        count = list_blocks(
            n_seq, False, group * n_seq + offset, group, core, key_blocks, key_counts, found
        )

        def step(n, _):
            from_block(
                keys, values, found[n], block, stats, i, False, out_acc, dq_acc, None
            )
            return 0

        lax.fori_loop(0, count, step, 0)
        cosine, sine = block_tables(place_ref[group * n_seq + offset], bc, bs, tc, ts)
        result = own_out if i == 0 else other_out
        for h in range(HALF_KV):
            for r in range(RATIO):
                rows = slice(r * BLK, (r + 1) * BLK)
                columns = slice((h * RATIO + r) * HEAD_DIM, (h * RATIO + r + 1) * HEAD_DIM)
                result[0, :, columns] = out_acc[i, h, :, rows].T.astype(BF16)
                dq = dq_acc[i, h, :, rows].T * SCALE
                result[1, :, columns] = turn(dq, cosine, -sine).astype(BF16)


def finish_kv(n_seq, place_ref, summed, extra, bc, bs, tc, ts, keep, send):
    group, member, core = here(n_seq)
    for i, result in enumerate((keep, send)):
        offset = member if i == 0 else lax.bitwise_xor(member, 1)
        cosine, sine = block_tables(place_ref[group * n_seq + offset], bc, bs, tc, ts)
        for h in range(HALF_KV):
            columns = slice(h * HEAD_DIM, (h + 1) * HEAD_DIM)
            dk = summed[i, 0, h].astype(F32) + extra[i, h].astype(F32)
            result[0, :, columns] = turn(dk, cosine, -sine).astype(BF16)
            result[1, :, columns] = summed[i, 1, h]


def local(query_input, key_input, value_input, out_grad, key_blocks, key_counts, block_position):
    n_seq = lax.axis_size("seq")
    n_grp = lax.axis_size("grp")
    core = lax.rem(lax.axis_index("seq"), CORES)
    lines = [[m for m in range(n_seq) if m % CORES == c] for c in range(CORES)]
    swap = [(m, m ^ 1) for m in range(n_seq)]
    onward = [(g, g + 1) for g in range(n_grp - 1)]
    back = [(g + 1, g) for g in range(n_grp - 1)]
    tables = trig_tables(block_position.shape[0])
    n_tab = len(tables)
    n_far = min(n_seq, key_blocks.shape[1] - 1)
    piece = (2, HALF_KV, BLK, HEAD_DIM)
    q_shape = jax.ShapeDtypeStruct((2, HALF_KV, RATIO, BLK, HEAD_DIM), BF16)
    kv_shape = jax.ShapeDtypeStruct(piece, BF16)
    stats_shape = jax.ShapeDtypeStruct((2, HALF_KV, 8, ROWS), F32)
    acc_shape = (2, HALF_KV, HEAD_DIM, ROWS)
    grad_shape = (n_seq, HALF_KV, BLK, HEAD_DIM)
    list_scratch = pltpu.SMEM((key_blocks.shape[1],), jnp.int32)
    unit = 2 * HALF_KV * RATIO * 128**3 * key_blocks.shape[1]

    kv_keep, kv_send = call(
        functools.partial(prepare_kv, n_seq), (kv_shape, kv_shape), 1, 2 + n_tab,
        moved=2**20, name="rotate_keys",
    )(block_position, key_input, value_input, *tables)
    kv_got = lax.ppermute(kv_send, "seq", swap)
    kv_chip = jnp.stack([kv_keep, kv_got])
    q_keep, q_send = call(
        functools.partial(prepare_queries, n_seq), (q_shape, q_shape), 1, 2 + n_tab,
        moved=2**23, name="rotate_queries",
    )(block_position, query_input, out_grad, *tables)
    q_got = lax.ppermute(q_send, "seq", swap)

    def gather(array):
        return lax.all_gather(array, "seq", axis=0, tiled=True, axis_index_groups=lines)

    def scatter(array):
        return lax.psum_scatter(
            array, "seq", scatter_dimension=0, tiled=True, axis_index_groups=lines
        )

    store = gather(kv_chip)
    keys_before = lax.ppermute(kv_chip[:, 0], "grp", onward)
    far_values = lax.ppermute(store[:, 1], "grp", onward)
    far_keys = gather(keys_before)

    stats_1 = call(
        functools.partial(current_stats, n_seq), stats_shape, 2, 3, [list_scratch],
        flops=2 * unit, moved=2**20, name="current_statistics",
    )(key_blocks, key_counts, store, q_keep, q_got)

    far_grad = jax.ShapeDtypeStruct(grad_shape, BF16)
    kept = pltpu.VMEM((n_far, HALF_KV, BLK, ROWS), F32)
    dk_far, dv_far, stats = call(
        functools.partial(previous_grads, n_seq), (far_grad, far_grad, stats_shape), 2, 5,
        [list_scratch, kept, kept, pltpu.VMEM(grad_shape, F32), pltpu.VMEM(grad_shape, F32)],
        flops=4 * unit, moved=2**20, name="previous_gradients",
    )(key_blocks, key_counts, far_keys, far_values, q_keep, q_got, stats_1)

    dv_back = lax.ppermute(dv_far, "grp", back)
    dk_back = lax.ppermute(scatter(dk_far), "grp", back)

    near_grad = jax.ShapeDtypeStruct(grad_shape, F32)
    acc = jax.ShapeDtypeStruct(acc_shape, F32)
    dk_near, dv_near, out_1, dq_1 = call(
        functools.partial(current_grads, n_seq), (near_grad, near_grad, acc, acc), 2, 4,
        [list_scratch, pltpu.VMEM(grad_shape, F32), pltpu.VMEM(grad_shape, F32)],
        flops=6 * unit, moved=2**20, name="current_gradients",
    )(key_blocks, key_counts, store, q_keep, q_got, stats)
    near = jnp.stack([dk_near, dv_near + dv_back.astype(F32)], axis=1).astype(BF16)
    summed = scatter(near)

    half_out = jax.ShapeDtypeStruct((2, BLK, HEADS // CORES * HEAD_DIM), BF16)
    own_half, other_half = call(
        functools.partial(query_results, n_seq), (half_out, half_out), 3, 7 + n_tab,
        [list_scratch, pltpu.VMEM(acc_shape, F32), pltpu.VMEM(acc_shape, F32)],
        flops=4 * unit, moved=2**23, name="query_results",
    )(
        key_blocks, key_counts, block_position, far_keys, far_values, q_keep, q_got, stats,
        out_1, dq_1, *tables,
    )
    got_half = lax.ppermute(other_half, "seq", swap)

    def join(mine, received):
        first = jnp.where(core == 0, mine, received)
        second = jnp.where(core == 0, received, mine)
        return jnp.concatenate([first, second], axis=1)

    out_rows = join(own_half[0], got_half[0])
    query_grad = join(own_half[1], got_half[1])

    kv_half = jax.ShapeDtypeStruct((2, BLK, HALF_KV * HEAD_DIM), BF16)
    own_kv, other_kv = call(
        functools.partial(finish_kv, n_seq), (kv_half, kv_half), 1, 2 + n_tab,
        moved=2**20, name="key_gradients",
    )(block_position, summed, dk_back, *tables)
    got_kv = lax.ppermute(other_kv, "seq", swap)
    key_grad = join(own_kv[0], got_kv[0])
    value_grad = join(own_kv[1], got_kv[1])
    return (out_rows, query_grad, key_grad, value_grad)


def solution(mesh):
    split = P(("grp", "seq"), None)
    return jax.shard_map(
        local,
        mesh=mesh,
        in_specs=(split, split, split, split, P(), P(), P()),
        out_specs=(split, split, split, split),
        check_vma=False,
    )
```

```python
import functools
import math

import jax
import jax.numpy as jnp
import numpy as np
from jax import lax
from jax.experimental import pallas as pl
from jax.experimental.pallas import tpu as pltpu
from jax.sharding import PartitionSpec as P

HEADS = 32
KV_HEADS = 4
HEAD_DIM = 128
BLK = 128
CORES = 2
RATIO = HEADS // KV_HEADS
HALF_KV = KV_HEADS // CORES
ROWS = RATIO * BLK
SCALE = 1.0 / math.sqrt(HEAD_DIM)
TO_LOG2 = SCALE * math.log2(math.e)
F32 = jnp.float32
BF16 = jnp.bfloat16
CHUNK = 256

VMEM_SPEC = pl.BlockSpec(memory_space=pltpu.VMEM)
SMEM_SPEC = pl.BlockSpec(memory_space=pltpu.SMEM)


def trig_tables(n_blocks):
    half = HEAD_DIM // 2
    frequency = np.power(500000.0, -np.arange(half) * (2.0 / HEAD_DIM))
    tables = []
    for places in (np.arange(n_blocks) * BLK, np.arange(BLK)):
        angles = places[:, None] * frequency
        for part in (np.cos(angles), np.sin(angles)):
            tables.append(np.concatenate([part, part], axis=1).astype(np.float32))
    return tables


def block_tables(place, block_cos, block_sin, token_cos, token_sin):
    cos_b = block_cos[pl.ds(place, 1), :]
    sin_b = block_sin[pl.ds(place, 1), :]
    cosine = cos_b * token_cos[...] - sin_b * token_sin[...]
    sine = sin_b * token_cos[...] + cos_b * token_sin[...]
    lanes = lax.broadcasted_iota(jnp.int32, sine.shape, 1)
    return cosine, jnp.where(lanes < HEAD_DIM // 2, -sine, sine)


def turn(values, cosine, signed_sine):
    return values * cosine + pltpu.roll(values, HEAD_DIM // 2, 1) * signed_sine


def dot_nt(a, b):
    return lax.dot_general(a, b, (((1,), (1,)), ((), ())), preferred_element_type=F32)


def dot_nn(a, b):
    return lax.dot_general(a, b, (((1,), (0,)), ((), ())), preferred_element_type=F32)


def here(n_seq):
    member = lax.axis_index("seq")
    group = lax.axis_index("grp")
    return group, member, lax.rem(member, CORES)


def size_of(array):
    return math.prod(array.shape) * jnp.dtype(array.dtype).itemsize


def call(kernel, out_shape, n_smem, scratch=(), us=1, name=None):
    def run(*arrays):
        held = sum(size_of(a) for a in arrays[n_smem:])
        held += sum(size_of(a) for a in jax.tree.leaves(out_shape))
        held += sum(size_of(a) for a in scratch)
        return pl.pallas_call(
            kernel,
            out_shape=out_shape,
            in_specs=[SMEM_SPEC] * n_smem + [VMEM_SPEC] * (len(arrays) - n_smem),
            out_specs=jax.tree.map(lambda _: VMEM_SPEC, out_shape),
            scratch_shapes=list(scratch),
            compiler_params=pltpu.CompilerParams(vmem_limit_bytes=held + 6 * 2**20),
            cost_estimate=pl.CostEstimate(
                flops=us * 10**9, bytes_accessed=2**20, transcendentals=0
            ),
            name=name,
        )(*arrays)

    return run


def prepare_kv(n_seq, place_ref, key, value, bc, bs, tc, ts, keep, send):
    group, member, core = here(n_seq)
    cosine, sine = block_tables(place_ref[group * n_seq + member], bc, bs, tc, ts)
    for out, half in ((keep, core), (send, 1 - core)):
        for h in range(HALF_KV):
            columns = pl.ds(pl.multiple_of((half * HALF_KV + h) * HEAD_DIM, HEAD_DIM), HEAD_DIM)
            out[0, h] = turn(key[:, columns].astype(F32), cosine, sine).astype(BF16)
            out[1, h] = value[:, columns]


def prepare_queries(n_seq, place_ref, query, grad, bc, bs, tc, ts, keep, send):
    group, member, core = here(n_seq)
    cosine, sine = block_tables(place_ref[group * n_seq + member], bc, bs, tc, ts)
    for out, half in ((keep, core), (send, 1 - core)):
        for h in range(HALF_KV):
            for r in range(RATIO):
                head = (half * HALF_KV + h) * RATIO + r
                columns = pl.ds(pl.multiple_of(head * HEAD_DIM, HEAD_DIM), HEAD_DIM)
                out[0, h, r] = turn(query[:, columns].astype(F32), cosine, sine).astype(BF16)
                out[1, h, r] = grad[:, columns]


def list_blocks(n_seq, side, block, group, member, key_blocks, key_counts, found):
    base = (group - 1 + side) * n_seq

    def look(j, n):
        offset = key_blocks[block, j] - base
        hit = jnp.logical_and(offset >= 0, offset < n_seq)

        @pl.when(hit)
        def _():
            found[n] = lax.bitwise_xor(offset, member)

        return n + hit.astype(jnp.int32)

    return lax.fori_loop(1, key_counts[block], look, jnp.int32(0))


def list_all(n_seq, block, group, member, key_blocks, key_counts, found):
    base = (group - 1) * n_seq

    def look(j, n):
        offset = key_blocks[block, j] - base
        found[n] = lax.bitwise_xor(offset, member)
        return n + 1

    return lax.fori_loop(1, key_counts[block], look, jnp.int32(0))


def causal():
    keys = lax.broadcasted_iota(jnp.int32, (BLK, CHUNK), 0)
    tokens = lax.rem(lax.broadcasted_iota(jnp.int32, (BLK, CHUNK), 1), BLK)
    return keys <= tokens


def chunks():
    per = CHUNK // BLK
    return [
        (slice(c * per, (c + 1) * per), slice(c * CHUNK, (c + 1) * CHUNK))
        for c in range(ROWS // CHUNK)
    ]


def heads_of(block, what, h, rows):
    return block[what, h, rows].reshape(CHUNK, HEAD_DIM)


def fill(store, pieces, first=0):
    for k, piece in enumerate(pieces):
        store[first + CORES * k : first + CORES * (k + 1)] = piece[...]


def pair_scores(store, e, h, block, rows, diagonal):
    scores = dot_nt(store[e, 0, h], heads_of(block, 0, h, rows))
    if diagonal:
        scores = jnp.where(causal(), scores, -1e30)
    return scores, dot_nt(store[e, 1, h], heads_of(block, 1, h, rows))


def gather_stats(store, e, block, stats, i, diagonal, kept=None):
    for h in range(HALF_KV):
        for rows, columns in chunks():
            scores, dprobs = pair_scores(store, e, h, block, rows, diagonal)
            if kept is not None:
                n, kept_scores, kept_dprobs = kept
                kept_scores[n, h, :, columns] = scores
                kept_dprobs[n, h, :, columns] = dprobs
            top = jnp.max(scores, axis=0, keepdims=True)
            if not diagonal:
                old_top = stats[i, h, 0:1, columns]
                top = jnp.maximum(top, old_top)
            weights = jnp.exp2((scores - top) * TO_LOG2)
            total = jnp.sum(weights, axis=0, keepdims=True)
            mixed = jnp.sum(weights * dprobs, axis=0, keepdims=True)
            if not diagonal:
                shrink = jnp.exp2((old_top - top) * TO_LOG2)
                total += stats[i, h, 1:2, columns] * shrink
                mixed += stats[i, h, 2:3, columns] * shrink
            stats[i, h, 0:1, columns] = top
            stats[i, h, 1:2, columns] = total
            stats[i, h, 2:3, columns] = mixed


def add_grads(scores, dprobs, stats, i, h, block, rows, columns, dk, dv):
    probs = jnp.exp2(scores * TO_LOG2 - stats[i, h, 0:1, columns])
    dscores = probs * (dprobs - stats[i, h, 2:3, columns])
    dv += dot_nn(probs.astype(BF16), heads_of(block, 1, h, rows))
    dk += dot_nn(dscores.astype(BF16), heads_of(block, 0, h, rows))
    return dk, dv


def write_grads(acc, outs):
    for k, out in enumerate(outs):
        part = slice(CORES * k, CORES * (k + 1))
        out[:, 0] = (acc[part, 0] * SCALE).astype(out.dtype)
        out[:, 1] = acc[part, 1].astype(out.dtype)


def current_stats(n_seq, key_blocks, key_counts, own, other, *rest):
    n_pieces = n_seq // CORES
    pieces, (stats, store, found) = rest[:n_pieces], rest[n_pieces:]
    group, member, _ = here(n_seq)
    fill(store, pieces)
    for i, block in enumerate((own, other)):
        gather_stats(store, i, block, stats, i, True)
        count = list_blocks(
            n_seq, 1, group * n_seq + lax.bitwise_xor(member, i), group, member,
            key_blocks, key_counts, found,
        )

        def step(n, _):
            gather_stats(store, found[n], block, stats, i, False)
            return 0

        lax.fori_loop(0, count, step, 0)


def previous_grads(n_seq, key_blocks, key_counts, own, other, stats_in, *rest):
    n_pieces = n_seq // CORES
    pieces, outs = rest[:n_pieces], rest[n_pieces : 2 * n_pieces]
    stats, store, found, kept_scores, kept_dprobs, acc = rest[2 * n_pieces :]
    group, member, _ = here(n_seq)
    fill(store, pieces)
    acc[...] = jnp.zeros_like(acc)
    stats[...] = stats_in[...]
    for i, block in enumerate((own, other)):
        count = list_blocks(
            n_seq, 0, group * n_seq + lax.bitwise_xor(member, i), group, member,
            key_blocks, key_counts, found,
        )

        def look(n, _):
            gather_stats(store, found[n], block, stats, i, False, (n, kept_scores, kept_dprobs))
            return 0

        lax.fori_loop(0, count, look, 0)
        for h in range(HALF_KV):
            total = stats[i, h, 1:2, :]
            stats[i, h, 0:1, :] = stats[i, h, 0:1, :] * TO_LOG2 + jnp.log2(total)
            stats[i, h, 2:3, :] = stats[i, h, 2:3, :] / total

        def add(n, _):
            e = found[n]
            for h in range(HALF_KV):
                dk, dv = acc[e, 0, h], acc[e, 1, h]
                for rows, columns in chunks():
                    dk, dv = add_grads(
                        kept_scores[n, h, :, columns], kept_dprobs[n, h, :, columns],
                        stats, i, h, block, rows, columns, dk, dv,
                    )
                acc[e, 0, h] = dk
                acc[e, 1, h] = dv
            return 0

        lax.fori_loop(0, count, add, 0)
    write_grads(acc, outs)


def current_grads(n_seq, key_blocks, key_counts, own, other, stats, *rest):
    n_pieces = n_seq // CORES
    pieces, outs = rest[:n_pieces], rest[n_pieces : 2 * n_pieces]
    store, found, acc = rest[2 * n_pieces :]
    group, member, _ = here(n_seq)
    fill(store, pieces)
    acc[...] = jnp.zeros_like(acc)
    for i, block in enumerate((own, other)):
        count = list_blocks(
            n_seq, 1, group * n_seq + lax.bitwise_xor(member, i), group, member,
            key_blocks, key_counts, found,
        )

        def add(e, diagonal):
            for h in range(HALF_KV):
                dk, dv = acc[e, 0, h], acc[e, 1, h]
                for rows, columns in chunks():
                    scores, dprobs = pair_scores(store, e, h, block, rows, diagonal)
                    dk, dv = add_grads(
                        scores, dprobs, stats, i, h, block, rows, columns, dk, dv
                    )
                acc[e, 0, h] = dk
                acc[e, 1, h] = dv
            return 0

        add(i, True)
        lax.fori_loop(0, count, lambda n, _: add(found[n], False), 0)
    write_grads(acc, outs)


def query_results(n_seq, i, key_blocks, key_counts, place_ref, block, stats, *rest):
    n_pieces = n_seq // CORES
    far, near = rest[:n_pieces], rest[n_pieces : 2 * n_pieces]
    bc, bs, tc, ts, result, store, found, shift, delta, out_acc, dq_acc = rest[2 * n_pieces :]
    group, member, _ = here(n_seq)
    fill(store, far)
    fill(store, near, n_seq)
    keys_at = lax.broadcasted_iota(jnp.int32, (BLK, BLK), 1)
    tokens_at = lax.broadcasted_iota(jnp.int32, (BLK, BLK), 0)
    offset = lax.bitwise_xor(member, i)
    count = list_all(n_seq, group * n_seq + offset, group, member, key_blocks, key_counts, found)
    for h in range(HALF_KV):
        for r in range(RATIO):
            rows = slice(r * BLK, (r + 1) * BLK)
            wide = (BLK, BLK)
            shift[h, rows] = jnp.broadcast_to(stats[i, h, 0:1, rows], wide).T
            delta[h, rows] = jnp.broadcast_to(stats[i, h, 2:3, rows], wide).T

    def step(entries, first):
        for h in range(HALF_KV):
            keys = jnp.concatenate([store[e, 0, h] for e in entries], axis=0)
            values = jnp.concatenate([store[e, 1, h] for e in entries], axis=0)
            for rows, span in chunks():
                scores = dot_nt(heads_of(block, 0, h, rows), keys)
                dprobs = dot_nt(heads_of(block, 1, h, rows), values)
                parts = [[], []]
                for n in range(len(entries)):
                    lanes = slice(n * BLK, (n + 1) * BLK)
                    probs = jnp.exp2(scores[:, lanes] * TO_LOG2 - shift[h, span])
                    if first and n == 0:
                        allowed = jnp.tile(keys_at <= tokens_at, (CHUNK // BLK, 1))
                        probs = jnp.where(allowed, probs, 0.0)
                    parts[0].append(probs.astype(BF16))
                    dscores = probs * (dprobs[:, lanes] - delta[h, span])
                    parts[1].append(dscores.astype(BF16))
                probs, dscores = (jnp.concatenate(part, axis=1) for part in parts)
                attended = dot_nn(probs, values)
                query_part = dot_nn(dscores, keys)
                if first:
                    out_acc[h, span] = attended
                    dq_acc[h, span] = query_part
                else:
                    out_acc[h, span] += attended
                    dq_acc[h, span] += query_part

    odd = lax.rem(count, 2)

    @pl.when(odd == 1)
    def _():
        step([n_seq + i, found[count - 1]], True)

    @pl.when(odd == 0)
    def _():
        step([n_seq + i], True)

    def pair(n, _):
        step([found[2 * n], found[2 * n + 1]], False)
        return 0

    lax.fori_loop(0, lax.div(count, 2), pair, 0)
    cosine, sine = block_tables(place_ref[group * n_seq + offset], bc, bs, tc, ts)
    for h in range(HALF_KV):
        for r in range(RATIO):
            rows = slice(r * BLK, (r + 1) * BLK)
            columns = slice((h * RATIO + r) * HEAD_DIM, (h * RATIO + r + 1) * HEAD_DIM)
            result[0, :, columns] = out_acc[h, rows].astype(BF16)
            dq = dq_acc[h, rows] * SCALE
            result[1, :, columns] = turn(dq, cosine, -sine).astype(BF16)


def finish_kv(n_seq, place_ref, *rest):
    *terms, bc, bs, tc, ts, keep, send = rest
    group, member, _ = here(n_seq)
    for i, result in enumerate((keep, send)):
        offset = lax.bitwise_xor(member, i)
        cosine, sine = block_tables(place_ref[group * n_seq + offset], bc, bs, tc, ts)
        for h in range(HALF_KV):
            columns = slice(h * HEAD_DIM, (h + 1) * HEAD_DIM)
            dk, dv = (sum(term[i, w, h].astype(F32) for term in terms) for w in range(2))
            result[0, :, columns] = turn(dk, cosine, -sine).astype(BF16)
            result[1, :, columns] = dv.astype(BF16)


def local(query_input, key_input, value_input, out_grad, key_blocks, key_counts, block_position):
    n_seq = lax.axis_size("seq")
    n_grp = lax.axis_size("grp")
    n_pieces = n_seq // CORES
    core = lax.rem(lax.axis_index("seq"), CORES)
    n_listed = key_blocks.shape[1]

    def cross(array, by):
        return lax.ppermute(array, "seq", [(m, m ^ by) for m in range(n_seq)])

    def along(array, by):
        return cross(array, CORES * by)

    def onward(array):
        return lax.ppermute(array, "grp", [(g, g + 1) for g in range(n_grp - 1)])

    def back(array):
        return lax.ppermute(array, "grp", [(g + 1, g) for g in range(n_grp - 1)])

    tables = trig_tables(block_position.shape[0])
    n_far = min(n_seq, n_listed - 1)
    piece = (2, HALF_KV, BLK, HEAD_DIM)
    chip = (CORES, *piece)
    q_shape = jax.ShapeDtypeStruct((2, HALF_KV, RATIO, BLK, HEAD_DIM), BF16)
    kv_shape = jax.ShapeDtypeStruct(piece, BF16)
    stats_shape = jax.ShapeDtypeStruct((2, HALF_KV, 8, ROWS), F32)
    found = pltpu.SMEM((n_listed,), jnp.int32)
    store = pltpu.VMEM((n_seq, *piece), BF16)
    acc = pltpu.VMEM((n_seq, *piece), F32)
    low = jax.ShapeDtypeStruct(chip, BF16)
    high = jax.ShapeDtypeStruct(chip, F32)

    kv_keep, kv_send = call(
        functools.partial(prepare_kv, n_seq), (kv_shape, kv_shape), 1, us=2, name="rotate_keys"
    )(block_position, key_input, value_input, *tables)
    near = [jnp.stack([kv_keep, cross(kv_send, 1)])]
    near += [along(near[0], 1)]
    far = [onward(near[0]), None]
    for k in range(2, n_pieces, 2):
        near += [along(near[0], k), None]
        ready, far[0] = lax.optimization_barrier((near[k], far[0]))
        far += [onward(ready), None]
    far[1] = onward(near[1])
    for k in range(3, n_pieces, 2):
        near[k] = along(near[k - 1], 1)
        far[k] = along(far[k - 1], 1)

    query_late, _ = lax.optimization_barrier((query_input, far[0]))
    q_keep, q_send = call(
        functools.partial(prepare_queries, n_seq), (q_shape, q_shape), 1, us=4,
        name="rotate_queries",
    )(block_position, query_late, out_grad, *tables)
    q_got = cross(q_send, 1)

    stats = call(
        functools.partial(current_stats, n_seq), stats_shape, 2, [store, found],
        us=6, name="current_statistics",
    )(key_blocks, key_counts, q_keep, q_got, *near)

    kept = pltpu.VMEM((n_far, HALF_KV, BLK, ROWS), F32)
    *far_grads, stats = call(
        functools.partial(previous_grads, n_seq), (low,) * n_pieces + (stats_shape,), 2,
        [store, found, kept, kept, acc],
        us=14, name="previous_gradients",
    )(key_blocks, key_counts, q_keep, q_got, stats, *far)

    near_grads = call(
        functools.partial(current_grads, n_seq),
        tuple(low if k % 2 and k > 1 else high for k in range(n_pieces)), 2,
        [store, found, acc], us=10, name="current_gradients",
    )(key_blocks, key_counts, q_keep, q_got, stats, *near)

    half_out = jax.ShapeDtypeStruct((2, BLK, HEADS // CORES * HEAD_DIM), BF16)
    wide = pltpu.VMEM((HALF_KV, ROWS, HEAD_DIM), F32)

    def results(i, block, after):
        stats_late, _ = lax.optimization_barrier((stats, after))
        return call(
            functools.partial(query_results, n_seq, i), half_out, 3,
            [pltpu.VMEM((2 * n_seq, *piece), BF16), found, wide, wide, wide, wide],
            us=10, name="query_results",
        )(key_blocks, key_counts, block_position, block, stats_late, *far, *near, *tables)

    def total(*terms):
        return sum(term.astype(F32) for term in terms).astype(BF16)

    arrived = [back(far_grads[1])]
    for k in range(2, n_pieces, 2):
        arrived.append(back(total(far_grads[k], along(far_grads[k + 1], 1))))
    merged = [total(near_grads[1], arrived[0])]
    other_half = results(1, q_got, merged[0])
    got_half = cross(other_half, 1)
    for n, k in enumerate(range(2, n_pieces, 2)):
        ready, _ = lax.optimization_barrier((near_grads[k], other_half))
        merged.append(total(ready, arrived[1 + n], along(near_grads[k + 1], 1)))
    own_half = results(0, q_keep, merged[1:])
    final = [near_grads[0], back(far_grads[0]), along(merged[0], 1)]
    final += [along(merged[1 + n], k) for n, k in enumerate(range(2, n_pieces, 2))]
    final[0], own_half = lax.optimization_barrier((final[0], own_half))

    def join(mine, received):
        first = jnp.where(core == 0, mine, received)
        second = jnp.where(core == 0, received, mine)
        return jnp.concatenate([first, second], axis=1)

    out_rows = join(own_half[0], got_half[0])
    query_grad = join(own_half[1], got_half[1])

    kv_half = jax.ShapeDtypeStruct((2, BLK, HALF_KV * HEAD_DIM), BF16)
    own_kv, other_kv = call(
        functools.partial(finish_kv, n_seq), (kv_half, kv_half), 1,
        us=2, name="key_gradients",
    )(block_position, *final, *tables)
    got_kv = cross(other_kv, 1)
    key_grad = join(own_kv[0], got_kv[0])
    value_grad = join(own_kv[1], got_kv[1])
    return (out_rows, query_grad, key_grad, value_grad)


def solution(mesh):
    split = P(("grp", "seq"), None)
    return jax.shard_map(
        local,
        mesh=mesh,
        in_specs=(split, split, split, split, P(), P(), P()),
        out_specs=(split, split, split, split),
        check_vma=False,
    )
```

```python
import functools
import math

import jax
import jax.numpy as jnp
import numpy as np
from jax import lax
from jax.experimental import pallas as pl
from jax.experimental.pallas import tpu as pltpu
from jax.sharding import PartitionSpec as P

HEADS = 32
KV_HEADS = 4
HEAD_DIM = 128
BLK = 128
CORES = 2
RATIO = HEADS // KV_HEADS
HALF_KV = KV_HEADS // CORES
ROWS = RATIO * BLK
SCALE = 1.0 / math.sqrt(HEAD_DIM)
TO_LOG2 = SCALE * math.log2(math.e)
F32 = jnp.float32
BF16 = jnp.bfloat16
CHUNK = 256

VMEM_SPEC = pl.BlockSpec(memory_space=pltpu.VMEM)
SMEM_SPEC = pl.BlockSpec(memory_space=pltpu.SMEM)


def trig_tables(n_blocks):
    half = HEAD_DIM // 2
    frequency = np.power(500000.0, -np.arange(half) * (2.0 / HEAD_DIM))
    tables = []
    for places in (np.arange(n_blocks) * BLK, np.arange(BLK)):
        angles = places[:, None] * frequency
        for part in (np.cos(angles), np.sin(angles)):
            tables.append(np.concatenate([part, part], axis=1).astype(np.float32))
    return tables


def block_tables(place, block_cos, block_sin, token_cos, token_sin):
    cos_b = block_cos[pl.ds(place, 1), :]
    sin_b = block_sin[pl.ds(place, 1), :]
    cosine = cos_b * token_cos[...] - sin_b * token_sin[...]
    sine = sin_b * token_cos[...] + cos_b * token_sin[...]
    lanes = lax.broadcasted_iota(jnp.int32, sine.shape, 1)
    return cosine, jnp.where(lanes < HEAD_DIM // 2, -sine, sine)


def turn(values, cosine, signed_sine):
    return values * cosine + pltpu.roll(values, HEAD_DIM // 2, 1) * signed_sine


def dot_nt(a, b):
    return lax.dot_general(a, b, (((1,), (1,)), ((), ())), preferred_element_type=F32)


def dot_nn(a, b):
    return lax.dot_general(a, b, (((1,), (0,)), ((), ())), preferred_element_type=F32)


def here(n_seq):
    member = lax.axis_index("seq")
    group = lax.axis_index("grp")
    return group, member, lax.rem(member, CORES)


def size_of(array):
    return math.prod(array.shape) * jnp.dtype(array.dtype).itemsize


def call(kernel, out_shape, n_smem, scratch=(), us=1, name=None, spare=6):
    def run(*arrays):
        held = sum(size_of(a) for a in arrays[n_smem:])
        held += sum(size_of(a) for a in jax.tree.leaves(out_shape))
        held += sum(size_of(a) for a in scratch)
        return pl.pallas_call(
            kernel,
            out_shape=out_shape,
            in_specs=[SMEM_SPEC] * n_smem + [VMEM_SPEC] * (len(arrays) - n_smem),
            out_specs=jax.tree.map(lambda _: VMEM_SPEC, out_shape),
            scratch_shapes=list(scratch),
            compiler_params=pltpu.CompilerParams(vmem_limit_bytes=held + spare * 2**20),
            cost_estimate=pl.CostEstimate(
                flops=us * 10**9, bytes_accessed=2**20, transcendentals=0
            ),
            name=name,
        )(*arrays)

    return run


def prepare_kv(n_seq, place_ref, key, value, bc, bs, tc, ts, keep, send):
    group, member, core = here(n_seq)
    cosine, sine = block_tables(place_ref[group * n_seq + member], bc, bs, tc, ts)
    for out, half in ((keep, core), (send, 1 - core)):
        for h in range(HALF_KV):
            columns = pl.ds(pl.multiple_of((half * HALF_KV + h) * HEAD_DIM, HEAD_DIM), HEAD_DIM)
            out[0, h] = turn(key[:, columns].astype(F32), cosine, sine).astype(BF16)
            out[1, h] = value[:, columns]


def prepare_queries(n_seq, place_ref, query, grad, bc, bs, tc, ts, keep, send):
    group, member, core = here(n_seq)
    cosine, sine = block_tables(place_ref[group * n_seq + member], bc, bs, tc, ts)
    for out, half in ((keep, core), (send, 1 - core)):
        for h in range(HALF_KV):
            for r in range(RATIO):
                head = (half * HALF_KV + h) * RATIO + r
                columns = pl.ds(pl.multiple_of(head * HEAD_DIM, HEAD_DIM), HEAD_DIM)
                out[0, h, r] = turn(query[:, columns].astype(F32), cosine, sine).astype(BF16)
                out[1, h, r] = grad[:, columns]


def list_blocks(n_seq, side, block, group, member, key_blocks, key_counts, found, start=0):
    base = (group - 1 + side) * n_seq

    def look(j, n):
        offset = key_blocks[block, j] - base
        hit = jnp.logical_and(offset >= 0, offset < n_seq)

        @pl.when(hit)
        def _():
            found[n] = lax.bitwise_xor(offset, member)

        return n + hit.astype(jnp.int32)

    return lax.fori_loop(1, key_counts[block], look, jnp.int32(start))


def list_all(n_seq, block, group, member, key_blocks, key_counts, found):
    base = (group - 1) * n_seq

    def look(j, _):
        found[j] = lax.bitwise_xor(key_blocks[block, j] - base, member)
        return 0

    lax.fori_loop(1, key_counts[block], look, 0)
    return key_counts[block]


def causal():
    keys = lax.broadcasted_iota(jnp.int32, (BLK, CHUNK), 0)
    tokens = lax.rem(lax.broadcasted_iota(jnp.int32, (BLK, CHUNK), 1), BLK)
    return keys <= tokens


def chunks():
    per = CHUNK // BLK
    return [
        (slice(c * per, (c + 1) * per), slice(c * CHUNK, (c + 1) * CHUNK))
        for c in range(ROWS // CHUNK)
    ]


def heads_of(block, what, h, rows):
    return block[what, h, rows].reshape(CHUNK, HEAD_DIM)


def fill(store, pieces, first=0):
    for k, piece in enumerate(pieces):
        store[first + CORES * k : first + CORES * (k + 1)] = piece[...]


def pair_scores(store, e, h, block, rows, diagonal):
    scores = dot_nt(store[e, 0, h], heads_of(block, 0, h, rows))
    if diagonal:
        scores = jnp.where(causal(), scores, -1e30)
    return scores, dot_nt(store[e, 1, h], heads_of(block, 1, h, rows))


def gather_stats(store, e, block, stats, i, diagonal, kept=None):
    for h in range(HALF_KV):
        for rows, columns in chunks():
            scores, dprobs = pair_scores(store, e, h, block, rows, diagonal)
            if kept is not None:
                n, kept_scores, kept_dprobs = kept
                kept_scores[n, h, :, columns] = scores
                kept_dprobs[n, h, :, columns] = dprobs
            top = jnp.max(scores, axis=0, keepdims=True)
            if not diagonal:
                old_top = stats[i, h, 0:1, columns]
                top = jnp.maximum(top, old_top)
            weights = jnp.exp2((scores - top) * TO_LOG2)
            total = jnp.sum(weights, axis=0, keepdims=True)
            mixed = jnp.sum(weights * dprobs, axis=0, keepdims=True)
            if not diagonal:
                shrink = jnp.exp2((old_top - top) * TO_LOG2)
                total += stats[i, h, 1:2, columns] * shrink
                mixed += stats[i, h, 2:3, columns] * shrink
            stats[i, h, 0:1, columns] = top
            stats[i, h, 1:2, columns] = total
            stats[i, h, 2:3, columns] = mixed


def spread_grads(found, count, kept_scores, kept_dprobs, stats, i, block, acc):
    def add(n, _):
        e = found[n]
        for h in range(HALF_KV):
            dk, dv = acc[e, 0, h], acc[e, 1, h]
            for rows, columns in chunks():
                probs = jnp.exp2(
                    kept_scores[n, h, :, columns] * TO_LOG2 - stats[i, h, 0:1, columns]
                )
                dscores = probs * (kept_dprobs[n, h, :, columns] - stats[i, h, 2:3, columns])
                dv += dot_nn(probs.astype(BF16), heads_of(block, 1, h, rows))
                dk += dot_nn(dscores.astype(BF16), heads_of(block, 0, h, rows))
            acc[e, 0, h] = dk
            acc[e, 1, h] = dv
        return 0

    lax.fori_loop(0, count, add, 0)


def write_grads(acc, outs):
    for k, out in enumerate(outs):
        part = slice(CORES * k, CORES * (k + 1))
        out[:, 0] = (acc[part, 0] * SCALE).astype(out.dtype)
        out[:, 1] = acc[part, 1].astype(out.dtype)


def current_stats(n_seq, key_blocks, key_counts, own, other, *rest):
    n_pieces = n_seq // CORES
    pieces, (stats, store, found) = rest[:n_pieces], rest[n_pieces:]
    group, member, _ = here(n_seq)
    fill(store, pieces)
    for i, block in enumerate((own, other)):
        gather_stats(store, i, block, stats, i, True)
        count = list_blocks(
            n_seq, 1, group * n_seq + lax.bitwise_xor(member, i), group, member,
            key_blocks, key_counts, found,
        )

        def step(n, _):
            gather_stats(store, found[n], block, stats, i, False)
            return 0

        lax.fori_loop(0, count, step, 0)


def previous_grads(n_seq, key_blocks, key_counts, own, other, stats_in, *rest):
    n_pieces = n_seq // CORES
    pieces, outs = rest[:n_pieces], rest[n_pieces : 2 * n_pieces]
    stats, store, found, kept_scores, kept_dprobs, acc = rest[2 * n_pieces :]
    group, member, _ = here(n_seq)
    fill(store, pieces)
    acc[...] = jnp.zeros_like(acc)
    stats[...] = stats_in[...]
    for i, block in enumerate((own, other)):
        count = list_blocks(
            n_seq, 0, group * n_seq + lax.bitwise_xor(member, i), group, member,
            key_blocks, key_counts, found,
        )

        def look(n, _):
            gather_stats(store, found[n], block, stats, i, False, (n, kept_scores, kept_dprobs))
            return 0

        lax.fori_loop(0, count, look, 0)
        for h in range(HALF_KV):
            total = stats[i, h, 1:2, :]
            stats[i, h, 0:1, :] = stats[i, h, 0:1, :] * TO_LOG2 + jnp.log2(total)
            stats[i, h, 2:3, :] = stats[i, h, 2:3, :] / total

        spread_grads(found, count, kept_scores, kept_dprobs, stats, i, block, acc)
    write_grads(acc, outs)


def current_grads(n_seq, key_blocks, key_counts, own, other, stats, *rest):
    n_pieces = n_seq // CORES
    pieces, outs = rest[:n_pieces], rest[n_pieces : 2 * n_pieces]
    store, found, kept_scores, kept_dprobs, acc = rest[2 * n_pieces :]
    group, member, _ = here(n_seq)
    fill(store, pieces)
    acc[...] = jnp.zeros_like(acc)
    for i, block in enumerate((own, other)):
        found[0] = i
        count = list_blocks(
            n_seq, 1, group * n_seq + lax.bitwise_xor(member, i), group, member,
            key_blocks, key_counts, found, 1,
        )

        def look(n, diagonal):
            for h in range(HALF_KV):
                for rows, columns in chunks():
                    scores, dprobs = pair_scores(store, found[n], h, block, rows, diagonal)
                    kept_scores[n, h, :, columns] = scores
                    kept_dprobs[n, h, :, columns] = dprobs
            return 0

        look(0, True)
        lax.fori_loop(1, count, lambda n, _: look(n, False), 0)
        spread_grads(found, count, kept_scores, kept_dprobs, stats, i, block, acc)
    write_grads(acc, outs)


def query_results(n_seq, h, key_blocks, key_counts, place_ref, own, other, stats, *rest):
    n_pieces = n_seq // CORES
    pieces = rest[: 2 * n_pieces]
    (
        bc, bs, tc, ts, own_out, other_out, store, found, kept_scores, kept_dprobs, out_acc, dq_acc
    ) = rest[2 * n_pieces :]
    group, member, _ = here(n_seq)
    for k, piece in enumerate(pieces):
        store[CORES * k : CORES * (k + 1)] = piece[:, :, h : h + 1]
    for i, (block, result) in enumerate(((own, own_out), (other, other_out))):
        offset = lax.bitwise_xor(member, i)
        mine = group * n_seq + offset
        found[0] = n_seq + i
        count = list_all(n_seq, mine, group, member, key_blocks, key_counts, found)

        def look(n, diagonal):
            e = found[n]
            for rows, columns in chunks():
                scores = dot_nt(store[e, 0, 0], heads_of(block, 0, h, rows))
                if diagonal:
                    scores = jnp.where(causal(), scores, -1e30)
                kept_scores[n, :, columns] = scores
                kept_dprobs[n, :, columns] = dot_nt(store[e, 1, 0], heads_of(block, 1, h, rows))
            return 0

        look(0, True)
        lax.fori_loop(1, count, lambda n, _: look(n, False), 0)

        @pl.when(lax.rem(count, 2) == 1)
        def _():
            found[count] = 0
            kept_scores[count] = jnp.full((BLK, ROWS), -1e30, F32)
            kept_dprobs[count] = jnp.zeros((BLK, ROWS), F32)

        out_acc[...] = jnp.zeros_like(out_acc)
        dq_acc[...] = jnp.zeros_like(dq_acc)

        def add(n, _):
            pair = (2 * n, 2 * n + 1)
            keys_t = jnp.concatenate([store[found[m], 0, 0].T for m in pair], axis=1)
            values_t = jnp.concatenate([store[found[m], 1, 0].T for m in pair], axis=1)
            for _, columns in chunks():
                probs, dscores = [], []
                for m in pair:
                    part = jnp.exp2(
                        kept_scores[m, :, columns] * TO_LOG2 - stats[i, h, 0:1, columns]
                    )
                    probs.append(part.astype(BF16))
                    part *= kept_dprobs[m, :, columns] - stats[i, h, 2:3, columns]
                    dscores.append(part.astype(BF16))
                out_acc[:, columns] += dot_nn(values_t, jnp.concatenate(probs, axis=0))
                dq_acc[:, columns] += dot_nn(keys_t, jnp.concatenate(dscores, axis=0))
            return 0

        lax.fori_loop(0, lax.div(count + 1, 2), add, 0)
        cosine, sine = block_tables(place_ref[mine], bc, bs, tc, ts)
        cosine, sine = cosine.T * SCALE, sine.T * SCALE
        for r in range(RATIO):
            rows = slice(r * BLK, (r + 1) * BLK)
            columns = slice(r * HEAD_DIM, (r + 1) * HEAD_DIM)
            result[0, :, columns] = out_acc[:, rows].astype(BF16).T
            dq = dq_acc[:, rows]
            half = HEAD_DIM // 2
            turned = jnp.concatenate([dq[half:], dq[:half]], axis=0)
            result[1, :, columns] = (dq * cosine - turned * sine).astype(BF16).T


def finish_kv(n_seq, place_ref, *rest):
    *terms, bc, bs, tc, ts, keep, send = rest
    group, member, _ = here(n_seq)
    for i, result in enumerate((keep, send)):
        offset = lax.bitwise_xor(member, i)
        cosine, sine = block_tables(place_ref[group * n_seq + offset], bc, bs, tc, ts)
        for h in range(HALF_KV):
            columns = slice(h * HEAD_DIM, (h + 1) * HEAD_DIM)
            dk, dv = (sum(term[i, w, h].astype(F32) for term in terms) for w in range(2))
            result[0, :, columns] = turn(dk, cosine, -sine).astype(BF16)
            result[1, :, columns] = dv.astype(BF16)


def join_halves(n_parts, *refs):
    parts, outs = refs[: 2 * n_parts], refs[2 * n_parts :]
    core = lax.rem(lax.axis_index("seq"), CORES)
    width = parts[0].shape[-1]
    for half, which in ((core, parts[:n_parts]), (1 - core, parts[n_parts:])):
        for n, part in enumerate(which):
            start = pl.multiple_of((half * n_parts + n) * width, width)
            for w, out in enumerate(outs):
                out[:, pl.ds(start, width)] = part[w]


def local(query_input, key_input, value_input, out_grad, key_blocks, key_counts, block_position):
    n_seq = lax.axis_size("seq")
    n_grp = lax.axis_size("grp")
    n_pieces = n_seq // CORES
    n_listed = key_blocks.shape[1]

    def cross(array, by):
        return lax.ppermute(array, "seq", [(m, m ^ by) for m in range(n_seq)])

    def along(array, by):
        return cross(array, CORES * by)

    def onward(array):
        return lax.ppermute(array, "grp", [(g, g + 1) for g in range(n_grp - 1)])

    def back(array):
        return lax.ppermute(array, "grp", [(g + 1, g) for g in range(n_grp - 1)])

    tables = trig_tables(block_position.shape[0])
    n_far = min(n_seq, n_listed - 1)
    piece = (2, HALF_KV, BLK, HEAD_DIM)
    chip = (CORES, *piece)
    q_shape = jax.ShapeDtypeStruct((2, HALF_KV, RATIO, BLK, HEAD_DIM), BF16)
    kv_shape = jax.ShapeDtypeStruct(piece, BF16)
    stats_shape = jax.ShapeDtypeStruct((2, HALF_KV, 8, ROWS), F32)
    found = pltpu.SMEM((n_listed,), jnp.int32)
    store = pltpu.VMEM((n_seq, *piece), BF16)
    acc = pltpu.VMEM((n_seq, *piece), F32)
    low = jax.ShapeDtypeStruct(chip, BF16)
    high = jax.ShapeDtypeStruct(chip, F32)

    kv_keep, kv_send = call(
        functools.partial(prepare_kv, n_seq), (kv_shape, kv_shape), 1, us=2, name="rotate_keys",
        spare=61,
    )(block_position, key_input, value_input, *tables)
    kv_got = cross(kv_send, 1)
    query_late, kv_keep = lax.optimization_barrier((query_input, kv_keep))
    q_keep, q_send = call(
        functools.partial(prepare_queries, n_seq), (q_shape, q_shape), 1, us=4,
        name="rotate_queries",
    )(block_position, query_late, out_grad, *tables)
    q_send, q_keep, kv_got, kv_keep = lax.optimization_barrier((q_send, q_keep, kv_got, kv_keep))
    q_got = cross(q_send, 1)
    near = [jnp.stack([kv_keep, kv_got])]
    near += [along(near[0], k) for k in range(1, n_pieces) if k == 1 or k % 2 == 0]
    *near, first_far = lax.optimization_barrier((*near, onward(near[0])))
    near = [near[0], near[1]] + [p for even in near[2:] for p in (even, None)]
    far = [first_far, None]
    for k in range(2, n_pieces, 2):
        far += [onward(near[k]), None]
    far[1] = onward(near[1])
    for k in range(3, n_pieces, 2):
        near[k] = along(near[k - 1], 1)
        far[k] = along(far[k - 1], 1)

    stats = call(
        functools.partial(current_stats, n_seq), stats_shape, 2, [store, found],
        us=6, name="current_statistics",
    )(key_blocks, key_counts, q_keep, q_got, *near)

    kept = pltpu.VMEM((n_far, HALF_KV, BLK, ROWS), F32)
    *far_grads, stats = call(
        functools.partial(previous_grads, n_seq), (low,) * n_pieces + (stats_shape,), 2,
        [store, found, kept, kept, acc], us=14, name="previous_gradients",
    )(key_blocks, key_counts, q_keep, q_got, stats, *far)

    kept = pltpu.VMEM((min(n_seq, n_listed), HALF_KV, BLK, ROWS), F32)
    near_grads = call(
        functools.partial(current_grads, n_seq),
        tuple(low if k % 2 and k > 1 else high for k in range(n_pieces)), 2,
        [store, found, kept, kept, acc], us=10, name="current_gradients",
    )(key_blocks, key_counts, q_keep, q_got, stats, *near)

    half_out = jax.ShapeDtypeStruct((2, BLK, RATIO * HEAD_DIM), BF16)

    def results(h, after):
        stats_late, _ = lax.optimization_barrier((stats, after))
        kept = pltpu.VMEM((n_listed + 1, BLK, ROWS), F32)
        wide = pltpu.VMEM((HEAD_DIM, ROWS), F32)
        return call(
            functools.partial(query_results, n_seq, h), (half_out, half_out), 3,
            [
                pltpu.VMEM((2 * n_seq, 2, 1, BLK, HEAD_DIM), BF16),
                pltpu.SMEM((n_listed + 1,), jnp.int32), kept, kept, wide, wide,
            ],
            us=10, name="query_results",
        )(key_blocks, key_counts, block_position, q_keep, q_got, stats_late, *far, *near, *tables)

    def total(*terms):
        return sum(term.astype(F32) for term in terms).astype(BF16)

    arrived = [back(far_grads[1])]
    for k in range(2, n_pieces, 2):
        arrived.append(back(total(far_grads[k], along(far_grads[k + 1], 1))))
    merged = [total(near_grads[1], arrived[0])]
    own_halves, other_halves = [None, None], [None, None]
    own_halves[0], other_halves[0] = results(0, merged[0])
    for n, k in enumerate(range(2, n_pieces, 2)):
        ready, _ = lax.optimization_barrier((near_grads[k], other_halves[0]))
        merged.append(total(ready, arrived[1 + n], along(near_grads[k + 1], 1)))
    own_halves[1], other_halves[1] = results(1, merged[1:])
    got_halves = [cross(half, 1) for half in other_halves]
    final = [near_grads[0], back(far_grads[0]), along(merged[0], 1)]
    final += [along(merged[1 + n], k) for n, k in enumerate(range(2, n_pieces, 2))]
    final[0], own_halves[1] = lax.optimization_barrier((final[0], own_halves[1]))

    full = jax.ShapeDtypeStruct(query_input.shape, BF16)
    out_rows, query_grad = call(
        functools.partial(join_halves, HALF_KV), (full, full), 0, us=2, name="join_queries"
    )(*own_halves, *got_halves)

    kv_half = jax.ShapeDtypeStruct((2, BLK, HALF_KV * HEAD_DIM), BF16)
    own_kv, other_kv = call(
        functools.partial(finish_kv, n_seq), (kv_half, kv_half), 1,
        us=2, name="key_gradients",
    )(block_position, *final, *tables)
    got_kv = cross(other_kv, 1)
    full = jax.ShapeDtypeStruct(key_input.shape, BF16)
    key_grad, value_grad = call(
        functools.partial(join_halves, 1), (full, full), 0, us=1, name="join_keys"
    )(own_kv, got_kv)
    return (out_rows, query_grad, key_grad, value_grad)


def solution(mesh):
    split = P(("grp", "seq"), None)
    return jax.shard_map(
        local,
        mesh=mesh,
        in_specs=(split, split, split, split, P(), P(), P()),
        out_specs=(split, split, split, split),
        check_vma=False,
    )
```

```python
import functools
import math

import jax
import jax.numpy as jnp
import numpy as np
from jax import lax
from jax.experimental import pallas as pl
from jax.experimental.pallas import tpu as pltpu
from jax.sharding import PartitionSpec as P

HEADS = 32
KV_HEADS = 4
HEAD_DIM = 128
BLK = 128
CORES = 2
RATIO = HEADS // KV_HEADS
HALF_KV = KV_HEADS // CORES
ROWS = RATIO * BLK
SCALE = 1.0 / math.sqrt(HEAD_DIM)
TO_LOG2 = SCALE * math.log2(math.e)
F32 = jnp.float32
BF16 = jnp.bfloat16
CHUNK = 256

VMEM_SPEC = pl.BlockSpec(memory_space=pltpu.VMEM)
HBM_SPEC = pl.BlockSpec(memory_space=pltpu.HBM)
SMEM_SPEC = pl.BlockSpec(memory_space=pltpu.SMEM)


def trig_table(n_blocks):
    half = HEAD_DIM // 2
    frequency = np.power(500000.0, -np.arange(half) * (2.0 / HEAD_DIM))
    parts = []
    for places in (np.arange(n_blocks) * BLK, np.arange(BLK)):
        angles = places[:, None] * frequency
        for part in (np.cos(angles), np.sin(angles)):
            parts.append(np.concatenate([part, part], axis=1))
    return np.concatenate(parts, axis=0).astype(np.float32)


def block_tables(place, table):
    n_blocks = table.shape[0] // 2 - BLK
    cos_b = table[pl.ds(place, 1), :]
    sin_b = table[pl.ds(n_blocks + place, 1), :]
    cos_t = table[2 * n_blocks : 2 * n_blocks + BLK, :]
    sin_t = table[2 * n_blocks + BLK :, :]
    cosine = cos_b * cos_t - sin_b * sin_t
    sine = sin_b * cos_t + cos_b * sin_t
    lanes = lax.broadcasted_iota(jnp.int32, sine.shape, 1)
    return cosine, jnp.where(lanes < HEAD_DIM // 2, -sine, sine)


def turn(values, cosine, signed_sine):
    return values * cosine + pltpu.roll(values, HEAD_DIM // 2, 1) * signed_sine


def dot_nt(a, b):
    return lax.dot_general(a, b, (((1,), (1,)), ((), ())), preferred_element_type=F32)


def dot_nn(a, b):
    return lax.dot_general(a, b, (((1,), (0,)), ((), ())), preferred_element_type=F32)


def here(n_seq):
    member = lax.axis_index("seq")
    group = lax.axis_index("grp")
    return group, member, lax.rem(member, CORES)


def size_of(array):
    return math.prod(array.shape) * jnp.dtype(array.dtype).itemsize


def call(kernel, out_shape, n_smem, scratch=(), us=1, name=None, spare=6, n_hbm=0, hbm_out=None):
    def run(*arrays):
        n_left = n_smem + n_hbm
        outs = list(out_shape) if isinstance(out_shape, (tuple, list)) else [out_shape]
        held = sum(size_of(a) for a in arrays[n_left:])
        held += sum(size_of(a) for n, a in enumerate(outs) if n != hbm_out)
        held += sum(size_of(a) for a in scratch if a.dtype in (F32, BF16))
        out_specs = [HBM_SPEC if n == hbm_out else VMEM_SPEC for n in range(len(outs))]
        in_specs = [SMEM_SPEC] * n_smem + [HBM_SPEC] * n_hbm
        in_specs += [VMEM_SPEC] * (len(arrays) - n_left)
        pinned = [
            pltpu.with_memory_space_constraint(a, pltpu.HBM) if n < n_left else a
            for n, a in enumerate(arrays)
        ]
        results = pl.pallas_call(
            kernel,
            out_shape=[
                pltpu.HBM(a.shape, a.dtype) if n == hbm_out else a for n, a in enumerate(outs)
            ],
            in_specs=in_specs,
            out_specs=out_specs,
            scratch_shapes=list(scratch),
            compiler_params=pltpu.CompilerParams(vmem_limit_bytes=held + spare * 2**20),
            cost_estimate=pl.CostEstimate(
                flops=us * 10**9, bytes_accessed=2**20, transcendentals=0
            ),
            name=name,
        )(*pinned)
        return results if isinstance(out_shape, (tuple, list)) else results[0]

    return run


def fetch(sources, places, sems):
    copies = [
        pltpu.make_async_copy(source, place, sems.at[n])
        for n, (source, place) in enumerate(zip(sources, places))
    ]
    for copy in copies:
        copy.start()
    for copy in copies:
        copy.wait()


def prepare_kv(n_seq, place_ref, *refs):
    sources, (keep, send), (key, value, table, sems) = refs[:3], refs[3:5], refs[5:]
    fetch(sources, (key, value, table), sems)
    group, member, core = here(n_seq)
    cosine, sine = block_tables(place_ref[group * n_seq + member], table)
    for out, half in ((keep, core), (send, 1 - core)):
        for h in range(HALF_KV):
            columns = pl.ds(pl.multiple_of((half * HALF_KV + h) * HEAD_DIM, HEAD_DIM), HEAD_DIM)
            out[0, h] = turn(key[:, columns].astype(F32), cosine, sine).astype(BF16)
            out[1, h] = value[:, columns]


def prepare_queries(n_seq, place_ref, *refs):
    sources, (keep, send), (query, grad, table, sems) = refs[:3], refs[3:5], refs[5:]
    fetch(sources, (query, grad, table), sems)
    group, member, core = here(n_seq)
    cosine, sine = block_tables(place_ref[group * n_seq + member], table)
    for out, half in ((keep, core), (send, 1 - core)):
        for h in range(HALF_KV):
            for r in range(RATIO):
                head = (half * HALF_KV + h) * RATIO + r
                columns = pl.ds(pl.multiple_of(head * HEAD_DIM, HEAD_DIM), HEAD_DIM)
                out[0, h, r] = turn(query[:, columns].astype(F32), cosine, sine).astype(BF16)
                out[1, h, r] = grad[:, columns]


def list_blocks(
    n_seq, side, block, group, member, key_blocks, key_counts, found, start=0, shift=0
):
    base = (group - 1 + side) * n_seq

    def look(j, n):
        offset = key_blocks[block, j] - base
        hit = jnp.logical_and(offset >= 0, offset < n_seq)

        @pl.when(hit)
        def _():
            found[n] = lax.bitwise_xor(offset, member) + shift

        return n + hit.astype(jnp.int32)

    return lax.fori_loop(1, key_counts[block], look, jnp.int32(start))


def causal():
    keys = lax.broadcasted_iota(jnp.int32, (BLK, CHUNK), 0)
    tokens = lax.rem(lax.broadcasted_iota(jnp.int32, (BLK, CHUNK), 1), BLK)
    return keys <= tokens


def chunks():
    per = CHUNK // BLK
    return [
        (slice(c * per, (c + 1) * per), slice(c * CHUNK, (c + 1) * CHUNK))
        for c in range(ROWS // CHUNK)
    ]


def heads_of(block, what, h, rows):
    return block[what, h, rows].reshape(CHUNK, HEAD_DIM)


def fill(store, pieces, first=0):
    for k, piece in enumerate(pieces):
        store[first + CORES * k : first + CORES * (k + 1)] = piece[...]


def pair_scores(store, e, h, block, rows, diagonal):
    scores = dot_nt(store[e, 0, h], heads_of(block, 0, h, rows))
    if diagonal:
        scores = jnp.where(causal(), scores, -1e30)
    return scores, dot_nt(store[e, 1, h], heads_of(block, 1, h, rows))


def gather_stats(store, e, block, stats, i, diagonal, kept=None):
    for h in range(HALF_KV):
        for rows, columns in chunks():
            scores, dprobs = pair_scores(store, e, h, block, rows, diagonal)
            if kept is not None:
                n, kept_scores, kept_dprobs = kept
                kept_scores[n, h, :, columns] = scores
                kept_dprobs[n, h, :, columns] = dprobs
            top = jnp.max(scores, axis=0, keepdims=True)
            if not diagonal:
                old_top = stats[i, h, 0:1, columns]
                top = jnp.maximum(top, old_top)
            weights = jnp.exp2((scores - top) * TO_LOG2)
            total = jnp.sum(weights, axis=0, keepdims=True)
            mixed = jnp.sum(weights * dprobs, axis=0, keepdims=True)
            if not diagonal:
                shrink = jnp.exp2((old_top - top) * TO_LOG2)
                total += stats[i, h, 1:2, columns] * shrink
                mixed += stats[i, h, 2:3, columns] * shrink
            stats[i, h, 0:1, columns] = top
            stats[i, h, 1:2, columns] = total
            stats[i, h, 2:3, columns] = mixed


def spread_grads(found, count, kept_scores, kept_dprobs, stats, i, block, acc, saved, low, sent):
    def copy(n):
        return pltpu.make_async_copy(low.at[n], saved.at[i, n], sent.at[n])

    def add(n, _):
        e = found[n]
        for h in range(HALF_KV):
            dk, dv = acc[e, 0, h], acc[e, 1, h]
            for rows, columns in chunks():
                probs = jnp.exp2(
                    kept_scores[n, h, :, columns] * TO_LOG2 - stats[i, h, 0:1, columns]
                )
                dscores = probs * (kept_dprobs[n, h, :, columns] - stats[i, h, 2:3, columns])
                probs, dscores = probs.astype(BF16), dscores.astype(BF16)
                low[n, h, 0, :, columns] = probs
                low[n, h, 1, :, columns] = dscores
                dv += dot_nn(probs, heads_of(block, 1, h, rows))
                dk += dot_nn(dscores, heads_of(block, 0, h, rows))
            acc[e, 0, h] = dk
            acc[e, 1, h] = dv
        copy(n).start()
        return 0

    def finish(n, _):
        copy(n).wait()
        return 0

    lax.fori_loop(0, count, add, 0)
    lax.fori_loop(0, count, finish, 0)


def write_grads(acc, outs):
    for k, out in enumerate(outs):
        part = slice(CORES * k, CORES * (k + 1))
        out[:, 0] = (acc[part, 0] * SCALE).astype(out.dtype)
        out[:, 1] = acc[part, 1].astype(out.dtype)


def current_stats(n_seq, key_blocks, key_counts, own, other, *rest):
    n_pieces = n_seq // CORES
    pieces, (stats, store, found) = rest[:n_pieces], rest[n_pieces:]
    group, member, _ = here(n_seq)
    fill(store, pieces)
    for i, block in enumerate((own, other)):
        gather_stats(store, i, block, stats, i, True)
        count = list_blocks(
            n_seq, 1, group * n_seq + lax.bitwise_xor(member, i), group, member,
            key_blocks, key_counts, found,
        )

        def step(n, _):
            gather_stats(store, found[n], block, stats, i, False)
            return 0

        lax.fori_loop(0, count, step, 0)


def previous_grads(n_seq, key_blocks, key_counts, own, other, stats_in, *rest):
    n_pieces = n_seq // CORES
    pieces, outs = rest[:n_pieces], rest[n_pieces : 2 * n_pieces]
    saved, stats, store, found, kept_scores, kept_dprobs, acc, low, sent = rest[2 * n_pieces :]
    group, member, _ = here(n_seq)
    fill(store, pieces)
    acc[...] = jnp.zeros_like(acc)
    stats[...] = stats_in[...]
    for i, block in enumerate((own, other)):
        count = list_blocks(
            n_seq, 0, group * n_seq + lax.bitwise_xor(member, i), group, member,
            key_blocks, key_counts, found,
        )

        def look(n, _):
            gather_stats(store, found[n], block, stats, i, False, (n, kept_scores, kept_dprobs))
            return 0

        lax.fori_loop(0, count, look, 0)
        for h in range(HALF_KV):
            total = stats[i, h, 1:2, :]
            stats[i, h, 0:1, :] = stats[i, h, 0:1, :] * TO_LOG2 + jnp.log2(total)
            stats[i, h, 2:3, :] = stats[i, h, 2:3, :] / total

        spread_grads(
            found, count, kept_scores, kept_dprobs, stats, i, block, acc, saved, low, sent
        )
    write_grads(acc, outs)


def current_grads(n_seq, key_blocks, key_counts, own, other, stats, *rest):
    n_pieces = n_seq // CORES
    pieces, outs = rest[:n_pieces], rest[n_pieces : 2 * n_pieces]
    saved, store, found, kept_scores, kept_dprobs, acc, low, sent = rest[2 * n_pieces :]
    group, member, _ = here(n_seq)
    fill(store, pieces)
    acc[...] = jnp.zeros_like(acc)
    for i, block in enumerate((own, other)):
        found[0] = i
        count = list_blocks(
            n_seq, 1, group * n_seq + lax.bitwise_xor(member, i), group, member,
            key_blocks, key_counts, found, 1,
        )

        def look(n, diagonal):
            for h in range(HALF_KV):
                for rows, columns in chunks():
                    scores, dprobs = pair_scores(store, found[n], h, block, rows, diagonal)
                    kept_scores[n, h, :, columns] = scores
                    kept_dprobs[n, h, :, columns] = dprobs
            return 0

        look(0, True)
        lax.fori_loop(1, count, lambda n, _: look(n, False), 0)
        spread_grads(
            found, count, kept_scores, kept_dprobs, stats, i, block, acc, saved, low, sent
        )
    write_grads(acc, outs)


def query_results(n_seq, h, key_blocks, key_counts, place_ref, far_saved, near_saved, *rest):
    n_pieces = n_seq // CORES
    pieces = rest[: 2 * n_pieces]
    (
        table, own_out, other_out, store, found, low, out_acc, dq_acc, got
    ) = rest[2 * n_pieces :]
    group, member, _ = here(n_seq)
    outs = (own_out, other_out)

    def far_copy(i, n, _):
        return pltpu.make_async_copy(far_saved.at[i, n, h], low.at[i, n], got.at[i, n])

    def near_copy(i, n, count):
        return pltpu.make_async_copy(near_saved.at[i, n - count, h], low.at[i, n], got.at[i, n])

    counts = []
    for i in range(2):
        block = group * n_seq + lax.bitwise_xor(member, i)
        lists = (block, group, member, key_blocks, key_counts, found.at[i])
        far = list_blocks(n_seq, 0, *lists)
        found[i, far] = n_seq + i
        total = list_blocks(n_seq, 1, *lists, far + 1, n_seq)
        counts.append((far, total))

        def fetch_far(n, _):
            far_copy(i, n, 0).start()
            return 0

        def fetch_near(n, _):
            near_copy(i, n, far).start()
            return 0

        lax.fori_loop(0, far, fetch_far, 0)
        lax.fori_loop(far, total, fetch_near, 0)
    for k, piece in enumerate(pieces):
        store[CORES * k : CORES * (k + 1)] = piece[:, :, h : h + 1]
    for i, (far, total) in enumerate(counts):
        mine = group * n_seq + lax.bitwise_xor(member, i)

        @pl.when(lax.rem(total, 2) == 1)
        def _():
            found[i, total] = 0
            low[i, total] = jnp.zeros((2, BLK, ROWS), BF16)

        out_acc[...] = jnp.zeros_like(out_acc)
        dq_acc[...] = jnp.zeros_like(dq_acc)

        def add(n, _):
            pair = (2 * n, 2 * n + 1)
            for m in pair:

                @pl.when(m < far)
                def _():
                    far_copy(i, m, 0).wait()

                @pl.when(jnp.logical_and(m >= far, m < total))
                def _():
                    near_copy(i, m, far).wait()

            keys_t = jnp.concatenate([store[found[i, m], 0, 0].T for m in pair], axis=1)
            values_t = jnp.concatenate([store[found[i, m], 1, 0].T for m in pair], axis=1)
            for _, columns in chunks():
                probs = jnp.concatenate([low[i, m, 0, :, columns] for m in pair], axis=0)
                dscores = jnp.concatenate([low[i, m, 1, :, columns] for m in pair], axis=0)
                out_acc[:, columns] += dot_nn(values_t, probs)
                dq_acc[:, columns] += dot_nn(keys_t, dscores)
            return 0

        lax.fori_loop(0, lax.div(total + 1, 2), add, 0)
        cosine, sine = block_tables(place_ref[mine], table)
        cosine, sine = cosine.T * SCALE, sine.T * SCALE
        for r in range(RATIO):
            rows = slice(r * BLK, (r + 1) * BLK)
            columns = slice(r * HEAD_DIM, (r + 1) * HEAD_DIM)
            outs[i][0, :, columns] = out_acc[:, rows].astype(BF16).T
            dq = dq_acc[:, rows]
            half = HEAD_DIM // 2
            turned = jnp.concatenate([dq[half:], dq[:half]], axis=0)
            outs[i][1, :, columns] = (dq * cosine - turned * sine).astype(BF16).T


def finish_kv(n_seq, place_ref, *rest):
    *terms, table, keep, send = rest
    group, member, _ = here(n_seq)
    for i, result in enumerate((keep, send)):
        offset = lax.bitwise_xor(member, i)
        cosine, sine = block_tables(place_ref[group * n_seq + offset], table)
        for h in range(HALF_KV):
            columns = slice(h * HEAD_DIM, (h + 1) * HEAD_DIM)
            dk, dv = (sum(term[i, w, h].astype(F32) for term in terms) for w in range(2))
            result[0, :, columns] = turn(dk, cosine, -sine).astype(BF16)
            result[1, :, columns] = dv.astype(BF16)


def join_halves(n_parts, *refs):
    parts, outs = refs[: 2 * n_parts], refs[2 * n_parts :]
    core = lax.rem(lax.axis_index("seq"), CORES)
    width = parts[0].shape[-1]
    for half, which in ((core, parts[:n_parts]), (1 - core, parts[n_parts:])):
        for n, part in enumerate(which):
            start = pl.multiple_of((half * n_parts + n) * width, width)
            for w, out in enumerate(outs):
                out[:, pl.ds(start, width)] = part[w]


def local(query_input, key_input, value_input, out_grad, key_blocks, key_counts, block_position):
    n_seq = lax.axis_size("seq")
    n_grp = lax.axis_size("grp")
    n_pieces = n_seq // CORES
    n_listed = key_blocks.shape[1]

    def cross(array, by):
        return lax.ppermute(array, "seq", [(m, m ^ by) for m in range(n_seq)])

    def along(array, by):
        return cross(array, CORES * by)

    def onward(array):
        return lax.ppermute(array, "grp", [(g, g + 1) for g in range(n_grp - 1)])

    def back(array):
        return lax.ppermute(array, "grp", [(g + 1, g) for g in range(n_grp - 1)])

    table = trig_table(block_position.shape[0])
    n_far = min(n_seq, n_listed - 1)
    piece = (2, HALF_KV, BLK, HEAD_DIM)
    chip = (CORES, *piece)
    q_shape = jax.ShapeDtypeStruct((2, HALF_KV, RATIO, BLK, HEAD_DIM), BF16)
    kv_shape = jax.ShapeDtypeStruct(piece, BF16)
    stats_shape = jax.ShapeDtypeStruct((2, HALF_KV, 8, ROWS), F32)
    found = pltpu.SMEM((n_listed,), jnp.int32)
    store = pltpu.VMEM((n_seq, *piece), BF16)
    acc = pltpu.VMEM((n_seq, *piece), F32)
    low = jax.ShapeDtypeStruct(chip, BF16)
    high = jax.ShapeDtypeStruct(chip, F32)

    def prepared(kernel, shape, first, second, name):
        held = [pltpu.VMEM(a.shape, a.dtype) for a in (first, second, table)]
        return call(
            functools.partial(kernel, n_seq), (shape, shape), 1,
            [*held, pltpu.SemaphoreType.DMA((3,))], us=1, name=name, n_hbm=3,
        )(block_position, first, second, table)

    kv_keep, kv_send = prepared(prepare_kv, kv_shape, key_input, value_input, "rotate_keys")
    kv_got = cross(kv_send, 1)
    query_late, kv_keep = lax.optimization_barrier((query_input, kv_keep))
    q_keep, q_send = prepared(prepare_queries, q_shape, query_late, out_grad, "rotate_queries")
    q_send, q_keep, kv_got, kv_keep = lax.optimization_barrier((q_send, q_keep, kv_got, kv_keep))
    q_got = cross(q_send, 1)
    near = [jnp.stack([kv_keep, kv_got])]
    near += [along(near[0], 1)]
    ready, first_far = lax.optimization_barrier((near[1], onward(near[0])))
    far = [first_far, onward(ready)]
    for k in range(2, n_pieces, 2):
        piece_k, _ = lax.optimization_barrier((along(near[0], k), ready))
        near.append(piece_k)
        far.append(onward(near[k]))
        near.append(along(near[k], 1))
        far.append(along(far[k], 1))

    stats = call(
        functools.partial(current_stats, n_seq), stats_shape, 2, [store, found],
        us=6, name="current_statistics",
    )(key_blocks, key_counts, q_keep, q_got, *near)

    def grads_call(kernel, n_slots, outs, us, name):
        kept = pltpu.VMEM((n_slots, HALF_KV, BLK, ROWS), F32)
        pair = (n_slots, HALF_KV, 2, BLK, ROWS)
        saved = jax.ShapeDtypeStruct((2, *pair), BF16)
        return call(
            functools.partial(kernel, n_seq), (*outs[:n_pieces], saved, *outs[n_pieces:]), 2,
            [
                store, found, kept, kept, acc, pltpu.VMEM(pair, BF16),
                pltpu.SemaphoreType.DMA((n_slots,)),
            ],
            us=us, name=name, hbm_out=n_pieces,
        )

    *far_grads, far_saved, stats = grads_call(
        previous_grads, n_far, (low,) * n_pieces + (stats_shape,), 14, "previous_gradients"
    )(key_blocks, key_counts, q_keep, q_got, stats, *far)
    *near_grads, near_saved = grads_call(
        current_grads, min(n_seq, n_listed),
        tuple(low if k % 2 and k > 1 else high for k in range(n_pieces)), 10, "current_gradients",
    )(key_blocks, key_counts, q_keep, q_got, stats, *near)

    half_out = jax.ShapeDtypeStruct((2, BLK, RATIO * HEAD_DIM), BF16)

    def results(h, after):
        place_late, _ = lax.optimization_barrier((block_position, after))
        wide = pltpu.VMEM((HEAD_DIM, ROWS), F32)
        return call(
            functools.partial(query_results, n_seq, h), (half_out, half_out), 3,
            [
                pltpu.VMEM((2 * n_seq, 2, 1, BLK, HEAD_DIM), BF16),
                pltpu.SMEM((2, n_listed + 1), jnp.int32),
                pltpu.VMEM((2, n_listed + 1, 2, BLK, ROWS), BF16), wide, wide,
                pltpu.SemaphoreType.DMA((2, n_listed)),
            ],
            us=20, name="query_results", n_hbm=2,
        )(key_blocks, key_counts, place_late, far_saved, near_saved, *far, *near, table)

    def total(*terms):
        return sum(term.astype(F32) for term in terms).astype(BF16)

    arrived = [back(far_grads[1])]
    last = far_grads[0]
    for k in range(2, n_pieces, 2):
        gathered = total(far_grads[k], along(far_grads[k + 1], 1))
        last, gathered = lax.optimization_barrier((last, gathered))
        arrived.append(back(gathered))
    last = back(last)
    merged = [total(near_grads[1], arrived[0])]
    own_halves, other_halves = [None, None], [None, None]
    own_halves[0], other_halves[0] = results(0, merged[0])
    for n, k in enumerate(range(2, n_pieces, 2)):
        ready, _ = lax.optimization_barrier((near_grads[k], other_halves[0]))
        merged.append(total(ready, arrived[1 + n], along(near_grads[k + 1], 1)))
    own_halves[1], other_halves[1] = results(1, merged[1:])
    got_halves = [cross(half, 1) for half in other_halves]
    final = [near_grads[0], last, along(merged[0], 1)]
    final += [along(merged[1 + n], k) for n, k in enumerate(range(2, n_pieces, 2))]
    final[0], own_halves[1] = lax.optimization_barrier((final[0], own_halves[1]))
    full = jax.ShapeDtypeStruct(query_input.shape, BF16)
    out_rows, query_grad = call(
        functools.partial(join_halves, HALF_KV), (full, full), 0, us=2, name="join_queries"
    )(*own_halves, *got_halves)
    kv_half = jax.ShapeDtypeStruct((2, BLK, HALF_KV * HEAD_DIM), BF16)
    own_kv, other_kv = call(
        functools.partial(finish_kv, n_seq), (kv_half, kv_half), 1,
        us=2, name="key_gradients",
    )(block_position, *final, table)
    got_kv = cross(other_kv, 1)
    full = jax.ShapeDtypeStruct(key_input.shape, BF16)
    key_grad, value_grad = call(
        functools.partial(join_halves, 1), (full, full), 0, us=1, name="join_keys"
    )(own_kv, got_kv)
    return (out_rows, query_grad, key_grad, value_grad)


def solution(mesh):
    split = P(("grp", "seq"), None)
    return jax.shard_map(
        local,
        mesh=mesh,
        in_specs=(split, split, split, split, P(), P(), P()),
        out_specs=(split, split, split, split),
        check_vma=False,
    )
```

```python
import functools
import math

import jax
import jax.numpy as jnp
import numpy as np
from jax import lax
from jax.experimental import pallas as pl
from jax.experimental.pallas import tpu as pltpu
from jax.sharding import PartitionSpec as P

HEADS = 32
KV_HEADS = 4
HEAD_DIM = 128
BLK = 128
CORES = 2
RATIO = HEADS // KV_HEADS
HALF_KV = KV_HEADS // CORES
ROWS = RATIO * BLK
SCALE = 1.0 / math.sqrt(HEAD_DIM)
TO_LOG2 = SCALE * math.log2(math.e)
F32 = jnp.float32
BF16 = jnp.bfloat16
CHUNK = 256

VMEM_SPEC = pl.BlockSpec(memory_space=pltpu.VMEM)
HBM_SPEC = pl.BlockSpec(memory_space=pltpu.HBM)
SMEM_SPEC = pl.BlockSpec(memory_space=pltpu.SMEM)


def trig_table(n_blocks):
    half = HEAD_DIM // 2
    frequency = np.power(500000.0, -np.arange(half) * (2.0 / HEAD_DIM))
    parts = []
    for places in (np.arange(n_blocks) * BLK, np.arange(BLK)):
        angles = places[:, None] * frequency
        for part in (np.cos(angles), np.sin(angles)):
            parts.append(np.concatenate([part, part], axis=1))
    return np.concatenate(parts, axis=0).astype(np.float32)


def block_tables(place, table):
    n_blocks = table.shape[0] // 2 - BLK
    cos_b = table[pl.ds(place, 1), :]
    sin_b = table[pl.ds(n_blocks + place, 1), :]
    cos_t = table[2 * n_blocks : 2 * n_blocks + BLK, :]
    sin_t = table[2 * n_blocks + BLK :, :]
    cosine = cos_b * cos_t - sin_b * sin_t
    sine = sin_b * cos_t + cos_b * sin_t
    lanes = lax.broadcasted_iota(jnp.int32, sine.shape, 1)
    return cosine, jnp.where(lanes < HEAD_DIM // 2, -sine, sine)


def turn(values, cosine, signed_sine):
    return values * cosine + pltpu.roll(values, HEAD_DIM // 2, 1) * signed_sine


def dot_nt(a, b):
    return lax.dot_general(a, b, (((1,), (1,)), ((), ())), preferred_element_type=F32)


def dot_nn(a, b):
    return lax.dot_general(a, b, (((1,), (0,)), ((), ())), preferred_element_type=F32)


def here(n_seq):
    member = lax.axis_index("seq")
    group = lax.axis_index("grp")
    return group, member, lax.rem(member, CORES)


def size_of(array):
    return math.prod(array.shape) * jnp.dtype(array.dtype).itemsize


def call(kernel, out_shape, n_smem, scratch=(), us=1, name=None, spare=6, n_hbm=0, hbm_out=None):
    def run(*arrays):
        n_left = n_smem + n_hbm
        outs = list(out_shape) if isinstance(out_shape, (tuple, list)) else [out_shape]
        held = sum(size_of(a) for a in arrays[n_left:])
        held += sum(size_of(a) for n, a in enumerate(outs) if n != hbm_out)
        held += sum(size_of(a) for a in scratch if a.dtype in (F32, BF16))
        out_specs = [HBM_SPEC if n == hbm_out else VMEM_SPEC for n in range(len(outs))]
        in_specs = [SMEM_SPEC] * n_smem + [HBM_SPEC] * n_hbm
        in_specs += [VMEM_SPEC] * (len(arrays) - n_left)
        pinned = [
            pltpu.with_memory_space_constraint(a, pltpu.HBM) if n < n_left else a
            for n, a in enumerate(arrays)
        ]
        results = pl.pallas_call(
            kernel,
            out_shape=[
                pltpu.HBM(a.shape, a.dtype) if n == hbm_out else a for n, a in enumerate(outs)
            ],
            in_specs=in_specs,
            out_specs=out_specs,
            scratch_shapes=list(scratch),
            compiler_params=pltpu.CompilerParams(vmem_limit_bytes=held + spare * 2**20),
            cost_estimate=pl.CostEstimate(
                flops=us * 10**9, bytes_accessed=2**20, transcendentals=0
            ),
            name=name,
        )(*pinned)
        return results if isinstance(out_shape, (tuple, list)) else results[0]

    return run


def fetch(sources, places, sems):
    copies = [
        pltpu.make_async_copy(source, place, sems.at[n])
        for n, (source, place) in enumerate(zip(sources, places))
    ]
    for copy in copies:
        copy.start()
    for copy in copies:
        copy.wait()


def prepare_kv(n_seq, place_ref, *refs):
    sources, (keep, send), (key, value, table, sems) = refs[:3], refs[3:5], refs[5:]
    fetch(sources, (key, value, table), sems)
    group, member, core = here(n_seq)
    cosine, sine = block_tables(place_ref[group * n_seq + member], table)
    for out, half in ((keep, core), (send, 1 - core)):
        for h in range(HALF_KV):
            columns = pl.ds(pl.multiple_of((half * HALF_KV + h) * HEAD_DIM, HEAD_DIM), HEAD_DIM)
            out[0, h] = turn(key[:, columns].astype(F32), cosine, sine).astype(BF16)
            out[1, h] = value[:, columns]


def prepare_queries(n_seq, place_ref, *refs):
    sources, (keep, send), (query, grad, table, sems) = refs[:3], refs[3:5], refs[5:]
    fetch(sources, (query, grad, table), sems)
    group, member, core = here(n_seq)
    cosine, sine = block_tables(place_ref[group * n_seq + member], table)
    for out, half in ((keep, core), (send, 1 - core)):
        for h in range(HALF_KV):
            for r in range(RATIO):
                head = (half * HALF_KV + h) * RATIO + r
                columns = pl.ds(pl.multiple_of(head * HEAD_DIM, HEAD_DIM), HEAD_DIM)
                out[0, h, r] = turn(query[:, columns].astype(F32), cosine, sine).astype(BF16)
                out[1, h, r] = grad[:, columns]


def list_blocks(
    n_seq, side, block, group, member, key_blocks, key_counts, found, start=0, shift=0
):
    base = (group - 1 + side) * n_seq

    def look(j, n):
        offset = key_blocks[block, j] - base
        hit = jnp.logical_and(offset >= 0, offset < n_seq)

        @pl.when(hit)
        def _():
            found[n] = lax.bitwise_xor(offset, member) + shift

        return n + hit.astype(jnp.int32)

    return lax.fori_loop(1, key_counts[block], look, jnp.int32(start))


def causal():
    keys = lax.broadcasted_iota(jnp.int32, (BLK, CHUNK), 0)
    tokens = lax.rem(lax.broadcasted_iota(jnp.int32, (BLK, CHUNK), 1), BLK)
    return keys <= tokens


def chunks():
    per = CHUNK // BLK
    return [
        (slice(c * per, (c + 1) * per), slice(c * CHUNK, (c + 1) * CHUNK))
        for c in range(ROWS // CHUNK)
    ]


def heads_of(block, what, h, rows):
    return block[what, h, rows].reshape(CHUNK, HEAD_DIM)


def fill(store, pieces, first=0):
    for k, piece in enumerate(pieces):
        store[first + CORES * k : first + CORES * (k + 1)] = piece[...]


def pair_scores(store, e, h, turned, i, columns, diagonal):
    scores = dot_nn(store[e, 0, h], turned[i, 0, h, :, columns])
    if diagonal:
        scores = jnp.where(causal(), scores, -1e30)
    return scores, dot_nn(store[e, 1, h], turned[i, 1, h, :, columns])


def gather_stats(store, e, turned, stats, i, diagonal, kept=None):
    for h in range(HALF_KV):
        for _, columns in chunks():
            scores, dprobs = pair_scores(store, e, h, turned, i, columns, diagonal)
            if kept is not None:
                n, kept_scores, kept_dprobs = kept
                kept_scores[n, h, :, columns] = scores
                kept_dprobs[n, h, :, columns] = dprobs
            top = jnp.max(scores, axis=0, keepdims=True)
            if not diagonal:
                old_top = stats[i, h, 0:1, columns]
                top = jnp.maximum(top, old_top)
            weights = jnp.exp2((scores - top) * TO_LOG2)
            total = jnp.sum(weights, axis=0, keepdims=True)
            mixed = jnp.sum(weights * dprobs, axis=0, keepdims=True)
            if not diagonal:
                shrink = jnp.exp2((old_top - top) * TO_LOG2)
                total += stats[i, h, 1:2, columns] * shrink
                mixed += stats[i, h, 2:3, columns] * shrink
            stats[i, h, 0:1, columns] = top
            stats[i, h, 1:2, columns] = total
            stats[i, h, 2:3, columns] = mixed


def spread_grads(found, count, kept_scores, kept_dprobs, stats, i, block, acc, saved, low, sent):
    def copy(n):
        return pltpu.make_async_copy(low.at[n], saved.at[i, n], sent.at[n])

    def add(n, _):
        e = found[n]
        for h in range(HALF_KV):
            dk, dv = acc[e, 0, h], acc[e, 1, h]
            for rows, columns in chunks():
                probs = jnp.exp2(
                    kept_scores[n, h, :, columns] * TO_LOG2 - stats[i, h, 0:1, columns]
                )
                dscores = probs * (kept_dprobs[n, h, :, columns] - stats[i, h, 2:3, columns])
                probs, dscores = probs.astype(BF16), dscores.astype(BF16)
                low[n, h, 0, :, columns] = probs
                low[n, h, 1, :, columns] = dscores
                dv += dot_nn(probs, heads_of(block, 1, h, rows))
                dk += dot_nn(dscores, heads_of(block, 0, h, rows))
            acc[e, 0, h] = dk
            acc[e, 1, h] = dv
        copy(n).start()
        return 0

    def finish(n, _):
        copy(n).wait()
        return 0

    lax.fori_loop(0, count, add, 0)
    lax.fori_loop(0, count, finish, 0)


def write_grads(acc, outs):
    for k, out in enumerate(outs):
        part = slice(CORES * k, CORES * (k + 1))
        out[:, 0] = (acc[part, 0] * SCALE).astype(out.dtype)
        out[:, 1] = acc[part, 1].astype(out.dtype)


def current_stats(n_seq, key_blocks, key_counts, own, other, *rest):
    n_pieces = n_seq // CORES
    pieces, (turned, stats, store, found) = rest[:n_pieces], rest[n_pieces:]
    group, member, _ = here(n_seq)
    fill(store, pieces)
    for i, block in enumerate((own, other)):
        for w in range(2):
            for h in range(HALF_KV):
                for r in range(RATIO):
                    turned[i, w, h, :, r * BLK : (r + 1) * BLK] = block[w, h, r].T
        gather_stats(store, i, turned, stats, i, True)
        count = list_blocks(
            n_seq, 1, group * n_seq + lax.bitwise_xor(member, i), group, member,
            key_blocks, key_counts, found,
        )

        def step(n, _):
            gather_stats(store, found[n], turned, stats, i, False)
            return 0

        lax.fori_loop(0, count, step, 0)


def previous_grads(n_seq, key_blocks, key_counts, own, other, turned, stats_in, *rest):
    n_pieces = n_seq // CORES
    pieces, outs = rest[:n_pieces], rest[n_pieces : 2 * n_pieces]
    saved, stats, store, found, kept_scores, kept_dprobs, acc, low, sent = rest[2 * n_pieces :]
    group, member, _ = here(n_seq)
    fill(store, pieces)
    acc[...] = jnp.zeros_like(acc)
    stats[...] = stats_in[...]
    for i, block in enumerate((own, other)):
        count = list_blocks(
            n_seq, 0, group * n_seq + lax.bitwise_xor(member, i), group, member,
            key_blocks, key_counts, found,
        )

        def look(n, _):
            gather_stats(store, found[n], turned, stats, i, False, (n, kept_scores, kept_dprobs))
            return 0

        lax.fori_loop(0, count, look, 0)
        for h in range(HALF_KV):
            total = stats[i, h, 1:2, :]
            stats[i, h, 0:1, :] = stats[i, h, 0:1, :] * TO_LOG2 + jnp.log2(total)
            stats[i, h, 2:3, :] = stats[i, h, 2:3, :] / total

        spread_grads(
            found, count, kept_scores, kept_dprobs, stats, i, block, acc, saved, low, sent
        )
    write_grads(acc, outs)


def current_grads(n_seq, key_blocks, key_counts, own, other, turned, stats, *rest):
    n_pieces = n_seq // CORES
    pieces, outs = rest[:n_pieces], rest[n_pieces : 2 * n_pieces]
    saved, store, found, kept_scores, kept_dprobs, acc, low, sent = rest[2 * n_pieces :]
    group, member, _ = here(n_seq)
    fill(store, pieces)
    acc[...] = jnp.zeros_like(acc)
    for i, block in enumerate((own, other)):
        found[0] = i
        count = list_blocks(
            n_seq, 1, group * n_seq + lax.bitwise_xor(member, i), group, member,
            key_blocks, key_counts, found, 1,
        )

        def look(n, diagonal):
            for h in range(HALF_KV):
                for _, columns in chunks():
                    scores, dprobs = pair_scores(
                        store, found[n], h, turned, i, columns, diagonal
                    )
                    kept_scores[n, h, :, columns] = scores
                    kept_dprobs[n, h, :, columns] = dprobs
            return 0

        look(0, True)
        lax.fori_loop(1, count, lambda n, _: look(n, False), 0)
        spread_grads(
            found, count, kept_scores, kept_dprobs, stats, i, block, acc, saved, low, sent
        )
    write_grads(acc, outs)


def query_results(n_seq, h, key_blocks, key_counts, place_ref, far_saved, near_saved, *rest):
    n_pieces = n_seq // CORES
    pieces = rest[: 2 * n_pieces]
    (
        table, own_out, other_out, store, found, low, out_acc, dq_acc, got
    ) = rest[2 * n_pieces :]
    group, member, _ = here(n_seq)
    outs = (own_out, other_out)

    def far_copy(i, n, _):
        return pltpu.make_async_copy(far_saved.at[i, n, h], low.at[i, n], got.at[i, n])

    def near_copy(i, n, count):
        return pltpu.make_async_copy(near_saved.at[i, n - count, h], low.at[i, n], got.at[i, n])

    counts = []
    for i in range(2):
        block = group * n_seq + lax.bitwise_xor(member, i)
        lists = (block, group, member, key_blocks, key_counts, found.at[i])
        far = list_blocks(n_seq, 0, *lists)
        found[i, far] = n_seq + i
        total = list_blocks(n_seq, 1, *lists, far + 1, n_seq)
        counts.append((far, total))

        def fetch_far(n, _):
            far_copy(i, n, 0).start()
            return 0

        def fetch_near(n, _):
            near_copy(i, n, far).start()
            return 0

        lax.fori_loop(0, far, fetch_far, 0)
        lax.fori_loop(far, total, fetch_near, 0)
    for k, piece in enumerate(pieces):
        store[CORES * k : CORES * (k + 1)] = piece[:, :, h : h + 1]
    for i, (far, total) in enumerate(counts):
        mine = group * n_seq + lax.bitwise_xor(member, i)

        @pl.when(lax.rem(total, 2) == 1)
        def _():
            found[i, total] = 0
            low[i, total] = jnp.zeros((2, BLK, ROWS), BF16)

        out_acc[...] = jnp.zeros_like(out_acc)
        dq_acc[...] = jnp.zeros_like(dq_acc)

        def add(n, _):
            pair = (2 * n, 2 * n + 1)
            for m in pair:

                @pl.when(m < far)
                def _():
                    far_copy(i, m, 0).wait()

                @pl.when(jnp.logical_and(m >= far, m < total))
                def _():
                    near_copy(i, m, far).wait()

            keys_t = jnp.concatenate([store[found[i, m], 0, 0].T for m in pair], axis=1)
            values_t = jnp.concatenate([store[found[i, m], 1, 0].T for m in pair], axis=1)
            for _, columns in chunks():
                probs = jnp.concatenate([low[i, m, 0, :, columns] for m in pair], axis=0)
                dscores = jnp.concatenate([low[i, m, 1, :, columns] for m in pair], axis=0)
                out_acc[:, columns] += dot_nn(values_t, probs)
                dq_acc[:, columns] += dot_nn(keys_t, dscores)
            return 0

        lax.fori_loop(0, lax.div(total + 1, 2), add, 0)
        cosine, sine = block_tables(place_ref[mine], table)
        cosine, sine = cosine.T * SCALE, sine.T * SCALE
        for r in range(RATIO):
            rows = slice(r * BLK, (r + 1) * BLK)
            columns = slice(r * HEAD_DIM, (r + 1) * HEAD_DIM)
            outs[i][0, :, columns] = out_acc[:, rows].astype(BF16).T
            dq = dq_acc[:, rows]
            half = HEAD_DIM // 2
            turned = jnp.concatenate([dq[half:], dq[:half]], axis=0)
            outs[i][1, :, columns] = (dq * cosine - turned * sine).astype(BF16).T


def finish_kv(n_seq, place_ref, *rest):
    *terms, table, keep, send = rest
    group, member, _ = here(n_seq)
    for i, result in enumerate((keep, send)):
        offset = lax.bitwise_xor(member, i)
        cosine, sine = block_tables(place_ref[group * n_seq + offset], table)
        for h in range(HALF_KV):
            columns = slice(h * HEAD_DIM, (h + 1) * HEAD_DIM)
            dk, dv = (sum(term[i, w, h].astype(F32) for term in terms) for w in range(2))
            result[0, :, columns] = turn(dk, cosine, -sine).astype(BF16)
            result[1, :, columns] = dv.astype(BF16)


def join_halves(n_parts, *refs):
    parts, outs = refs[: 2 * n_parts], refs[2 * n_parts :]
    core = lax.rem(lax.axis_index("seq"), CORES)
    width = parts[0].shape[-1]
    for half, which in ((core, parts[:n_parts]), (1 - core, parts[n_parts:])):
        for n, part in enumerate(which):
            start = pl.multiple_of((half * n_parts + n) * width, width)
            for w, out in enumerate(outs):
                out[:, pl.ds(start, width)] = part[w]


def local(query_input, key_input, value_input, out_grad, key_blocks, key_counts, block_position):
    n_seq = lax.axis_size("seq")
    n_grp = lax.axis_size("grp")
    n_pieces = n_seq // CORES
    n_listed = key_blocks.shape[1]

    def cross(array, by):
        return lax.ppermute(array, "seq", [(m, m ^ by) for m in range(n_seq)])

    def along(array, by):
        return cross(array, CORES * by)

    def onward(array):
        return lax.ppermute(array, "grp", [(g, g + 1) for g in range(n_grp - 1)])

    def back(array):
        return lax.ppermute(array, "grp", [(g + 1, g) for g in range(n_grp - 1)])

    table = trig_table(block_position.shape[0])
    n_far = min(n_seq, n_listed - 1)
    piece = (2, HALF_KV, BLK, HEAD_DIM)
    chip = (CORES, *piece)
    q_shape = jax.ShapeDtypeStruct((2, HALF_KV, RATIO, BLK, HEAD_DIM), BF16)
    kv_shape = jax.ShapeDtypeStruct(piece, BF16)
    stats_shape = jax.ShapeDtypeStruct((2, HALF_KV, 8, ROWS), F32)
    found = pltpu.SMEM((n_listed,), jnp.int32)
    store = pltpu.VMEM((n_seq, *piece), BF16)
    acc = pltpu.VMEM((n_seq, *piece), F32)
    low = jax.ShapeDtypeStruct(chip, BF16)
    high = jax.ShapeDtypeStruct(chip, F32)

    def prepared(kernel, shape, first, second, name):
        held = [pltpu.VMEM(a.shape, a.dtype) for a in (first, second, table)]
        return call(
            functools.partial(kernel, n_seq), (shape, shape), 1,
            [*held, pltpu.SemaphoreType.DMA((3,))], us=1, name=name, n_hbm=3,
        )(block_position, first, second, table)

    kv_keep, kv_send = prepared(prepare_kv, kv_shape, key_input, value_input, "rotate_keys")
    kv_got = cross(kv_send, 1)
    query_late, kv_keep = lax.optimization_barrier((query_input, kv_keep))
    q_keep, q_send = prepared(prepare_queries, q_shape, query_late, out_grad, "rotate_queries")
    q_send, q_keep, kv_got, kv_keep = lax.optimization_barrier((q_send, q_keep, kv_got, kv_keep))
    q_got = cross(q_send, 1)
    near = [jnp.stack([kv_keep, kv_got])]
    near.append(along(near[0], 1))
    ready, first_far = lax.optimization_barrier((near[1], onward(near[0])))
    far = [first_far, None]
    for k in range(2, n_pieces, 2):
        piece_k, _ = lax.optimization_barrier((along(near[0], k), ready))
        near += [piece_k, along(piece_k, 1)]
        far.append(onward(piece_k))
        far.append(along(far[k], 1))
    ready, far[2] = lax.optimization_barrier((ready, far[2]))
    far[1] = onward(ready)

    turned_shape = jax.ShapeDtypeStruct((2, 2, HALF_KV, HEAD_DIM, ROWS), BF16)
    turned, stats = call(
        functools.partial(current_stats, n_seq), (turned_shape, stats_shape), 2, [store, found],
        us=6, name="current_statistics",
    )(key_blocks, key_counts, q_keep, q_got, *near)

    def grads_call(kernel, n_slots, outs, us, name):
        kept = pltpu.VMEM((n_slots, HALF_KV, BLK, ROWS), F32)
        pair = (n_slots, HALF_KV, 2, BLK, ROWS)
        saved = jax.ShapeDtypeStruct((2, *pair), BF16)
        return call(
            functools.partial(kernel, n_seq), (*outs[:n_pieces], saved, *outs[n_pieces:]), 2,
            [
                store, found, kept, kept, acc, pltpu.VMEM(pair, BF16),
                pltpu.SemaphoreType.DMA((n_slots,)),
            ],
            us=us, name=name, hbm_out=n_pieces,
        )

    *far_grads, far_saved, stats = grads_call(
        previous_grads, n_far, (low,) * n_pieces + (stats_shape,), 14, "previous_gradients"
    )(key_blocks, key_counts, q_keep, q_got, turned, stats, *far)
    *near_grads, near_saved = grads_call(
        current_grads, min(n_seq, n_listed),
        tuple(low if k % 2 and k > 1 else high for k in range(n_pieces)), 10, "current_gradients",
    )(key_blocks, key_counts, q_keep, q_got, turned, stats, *near)

    half_out = jax.ShapeDtypeStruct((2, BLK, RATIO * HEAD_DIM), BF16)

    def results(h, after):
        place_late, _ = lax.optimization_barrier((block_position, after))
        wide = pltpu.VMEM((HEAD_DIM, ROWS), F32)
        return call(
            functools.partial(query_results, n_seq, h), (half_out, half_out), 3,
            [
                pltpu.VMEM((2 * n_seq, 2, 1, BLK, HEAD_DIM), BF16),
                pltpu.SMEM((2, n_listed + 1), jnp.int32),
                pltpu.VMEM((2, n_listed + 1, 2, BLK, ROWS), BF16), wide, wide,
                pltpu.SemaphoreType.DMA((2, n_listed)),
            ],
            us=20, name="query_results", n_hbm=2,
        )(key_blocks, key_counts, place_late, far_saved, near_saved, *far, *near, table)

    def total(*terms):
        return sum(term.astype(F32) for term in terms).astype(BF16)

    arrived = [back(far_grads[1])]
    last = far_grads[0]
    for k in range(2, n_pieces, 2):
        gathered = total(far_grads[k], along(far_grads[k + 1], 1))
        last, gathered = lax.optimization_barrier((last, gathered))
        arrived.append(back(gathered))
    last = back(last)
    merged = [total(near_grads[1], arrived[0])]
    own_halves, other_halves = [None, None], [None, None]
    own_halves[0], other_halves[0] = results(0, merged[0])
    for n, k in enumerate(range(2, n_pieces, 2)):
        ready, _ = lax.optimization_barrier((near_grads[k], other_halves[0]))
        merged.append(total(ready, arrived[1 + n], along(near_grads[k + 1], 1)))
    own_halves[1], other_halves[1] = results(1, merged[1:])
    got_halves = [cross(half, 1) for half in other_halves]
    final = [near_grads[0], last, along(merged[0], 1)]
    final += [along(merged[1 + n], k) for n, k in enumerate(range(2, n_pieces, 2))]
    final[0], own_halves[1] = lax.optimization_barrier((final[0], own_halves[1]))
    full = jax.ShapeDtypeStruct(query_input.shape, BF16)
    out_rows, query_grad = call(
        functools.partial(join_halves, HALF_KV), (full, full), 0, us=2, name="join_queries"
    )(*own_halves, *got_halves)
    kv_half = jax.ShapeDtypeStruct((2, BLK, HALF_KV * HEAD_DIM), BF16)
    own_kv, other_kv = call(
        functools.partial(finish_kv, n_seq), (kv_half, kv_half), 1,
        us=2, name="key_gradients",
    )(block_position, *final, table)
    got_kv = cross(other_kv, 1)
    full = jax.ShapeDtypeStruct(key_input.shape, BF16)
    key_grad, value_grad = call(
        functools.partial(join_halves, 1), (full, full), 0, us=1, name="join_keys"
    )(own_kv, got_kv)
    return (out_rows, query_grad, key_grad, value_grad)


def solution(mesh):
    split = P(("grp", "seq"), None)
    return jax.shard_map(
        local,
        mesh=mesh,
        in_specs=(split, split, split, split, P(), P(), P()),
        out_specs=(split, split, split, split),
        check_vma=False,
    )
```

```python
import functools
import math

import jax
import jax.numpy as jnp
import numpy as np
from jax import lax
from jax.experimental import pallas as pl
from jax.experimental.pallas import tpu as pltpu
from jax.sharding import PartitionSpec as P

HEADS = 32
KV_HEADS = 4
HEAD_DIM = 128
BLK = 128
CORES = 2
RATIO = HEADS // KV_HEADS
HALF_KV = KV_HEADS // CORES
ROWS = RATIO * BLK
SCALE = 1.0 / math.sqrt(HEAD_DIM)
TO_LOG2 = SCALE * math.log2(math.e)
F32 = jnp.float32
BF16 = jnp.bfloat16
CHUNK = 256

VMEM_SPEC = pl.BlockSpec(memory_space=pltpu.VMEM)
HBM_SPEC = pl.BlockSpec(memory_space=pltpu.HBM)
SMEM_SPEC = pl.BlockSpec(memory_space=pltpu.SMEM)


def trig_table(n_blocks):
    half = HEAD_DIM // 2
    frequency = np.power(500000.0, -np.arange(half) * (2.0 / HEAD_DIM))
    parts = []
    for places in (np.arange(n_blocks) * BLK, np.arange(BLK)):
        angles = places[:, None] * frequency
        for part in (np.cos(angles), np.sin(angles)):
            parts.append(np.concatenate([part, part], axis=1))
    return np.concatenate(parts, axis=0).astype(np.float32)


def block_tables(place, table):
    n_blocks = table.shape[0] // 2 - BLK
    cos_b = table[pl.ds(place, 1), :]
    sin_b = table[pl.ds(n_blocks + place, 1), :]
    cos_t = table[2 * n_blocks : 2 * n_blocks + BLK, :]
    sin_t = table[2 * n_blocks + BLK :, :]
    cosine = cos_b * cos_t - sin_b * sin_t
    sine = sin_b * cos_t + cos_b * sin_t
    lanes = lax.broadcasted_iota(jnp.int32, sine.shape, 1)
    return cosine, jnp.where(lanes < HEAD_DIM // 2, -sine, sine)


def turn(values, cosine, signed_sine):
    return values * cosine + pltpu.roll(values, HEAD_DIM // 2, 1) * signed_sine


def dot_nt(a, b):
    return lax.dot_general(a, b, (((1,), (1,)), ((), ())), preferred_element_type=F32)


def dot_nn(a, b):
    return lax.dot_general(a, b, (((1,), (0,)), ((), ())), preferred_element_type=F32)


def here(n_seq):
    member = lax.axis_index("seq")
    group = lax.axis_index("grp")
    return group, member, lax.rem(member, CORES)


def size_of(array):
    return math.prod(array.shape) * jnp.dtype(array.dtype).itemsize


def call(kernel, out_shape, n_smem, scratch=(), us=1, name=None, spare=6, n_hbm=0, hbm_out=None):
    def run(*arrays):
        n_left = n_smem + n_hbm
        outs = list(out_shape) if isinstance(out_shape, (tuple, list)) else [out_shape]
        held = sum(size_of(a) for a in arrays[n_left:])
        held += sum(size_of(a) for n, a in enumerate(outs) if n != hbm_out)
        held += sum(size_of(a) for a in scratch if a.dtype in (F32, BF16))
        out_specs = [HBM_SPEC if n == hbm_out else VMEM_SPEC for n in range(len(outs))]
        in_specs = [SMEM_SPEC] * n_smem + [HBM_SPEC] * n_hbm
        in_specs += [VMEM_SPEC] * (len(arrays) - n_left)
        pinned = [
            pltpu.with_memory_space_constraint(a, pltpu.HBM) if n < n_left else a
            for n, a in enumerate(arrays)
        ]
        results = pl.pallas_call(
            kernel,
            out_shape=[
                pltpu.HBM(a.shape, a.dtype) if n == hbm_out else a for n, a in enumerate(outs)
            ],
            in_specs=in_specs,
            out_specs=out_specs,
            scratch_shapes=list(scratch),
            compiler_params=pltpu.CompilerParams(vmem_limit_bytes=held + spare * 2**20),
            cost_estimate=pl.CostEstimate(
                flops=us * 10**9, bytes_accessed=2**20, transcendentals=0
            ),
            name=name,
        )(*pinned)
        return results if isinstance(out_shape, (tuple, list)) else results[0]

    return run


def fetch(sources, places, sems):
    copies = [
        pltpu.make_async_copy(source, place, sems.at[n])
        for n, (source, place) in enumerate(zip(sources, places))
    ]
    for copy in copies:
        copy.start()
    for copy in copies:
        copy.wait()


def prepare_kv(n_seq, place_ref, *refs):
    sources, (keep, send), (key, value, table, sems) = refs[:3], refs[3:5], refs[5:]
    fetch(sources, (key, value, table), sems)
    group, member, core = here(n_seq)
    cosine, sine = block_tables(place_ref[group * n_seq + member], table)
    for out, half in ((keep, core), (send, 1 - core)):
        for h in range(HALF_KV):
            columns = pl.ds(pl.multiple_of((half * HALF_KV + h) * HEAD_DIM, HEAD_DIM), HEAD_DIM)
            out[0, h] = turn(key[:, columns].astype(F32), cosine, sine).astype(BF16)
            out[1, h] = value[:, columns]


def prepare_queries(n_seq, place_ref, *refs):
    sources, (keep, send), (query, grad, table, sems) = refs[:3], refs[3:5], refs[5:]
    fetch(sources, (query, grad, table), sems)
    group, member, core = here(n_seq)
    cosine, sine = block_tables(place_ref[group * n_seq + member], table)
    for out, half in ((keep, core), (send, 1 - core)):
        for h in range(HALF_KV):
            for r in range(RATIO):
                head = (half * HALF_KV + h) * RATIO + r
                columns = pl.ds(pl.multiple_of(head * HEAD_DIM, HEAD_DIM), HEAD_DIM)
                out[0, h, r] = turn(query[:, columns].astype(F32), cosine, sine).astype(BF16)
                out[1, h, r] = grad[:, columns]


def list_blocks(
    n_seq, side, block, group, member, key_blocks, key_counts, found, start=0, shift=0
):
    base = (group - 1 + side) * n_seq

    def look(j, n):
        offset = key_blocks[block, j] - base
        hit = jnp.logical_and(offset >= 0, offset < n_seq)

        @pl.when(hit)
        def _():
            found[n] = lax.bitwise_xor(offset, member) + shift

        return n + hit.astype(jnp.int32)

    return lax.fori_loop(1, key_counts[block], look, jnp.int32(start))


def causal():
    keys = lax.broadcasted_iota(jnp.int32, (BLK, CHUNK), 0)
    tokens = lax.rem(lax.broadcasted_iota(jnp.int32, (BLK, CHUNK), 1), BLK)
    return keys <= tokens


def chunks():
    per = CHUNK // BLK
    return [
        (slice(c * per, (c + 1) * per), slice(c * CHUNK, (c + 1) * CHUNK))
        for c in range(ROWS // CHUNK)
    ]


def heads_of(block, what, h, rows):
    return block[what, h, rows].reshape(CHUNK, HEAD_DIM)


def fill(store, pieces, first=0):
    for k, piece in enumerate(pieces):
        store[first + CORES * k : first + CORES * (k + 1)] = piece[...]


def pair_scores(store, e, h, block, rows, diagonal):
    scores = dot_nt(store[e, 0, h], heads_of(block, 0, h, rows))
    if diagonal:
        scores = jnp.where(causal(), scores, -1e30)
    return scores, dot_nt(store[e, 1, h], heads_of(block, 1, h, rows))


def gather_stats(store, e, block, stats, i, diagonal, kept=None):
    for h in range(HALF_KV):
        for rows, columns in chunks():
            scores, dprobs = pair_scores(store, e, h, block, rows, diagonal)
            if kept is not None:
                n, kept_scores, kept_dprobs = kept
                kept_scores[n, h, :, columns] = scores
                kept_dprobs[n, h, :, columns] = dprobs
            top = jnp.max(scores, axis=0, keepdims=True)
            if not diagonal:
                old_top = stats[i, h, 0:1, columns]
                top = jnp.maximum(top, old_top)
            weights = jnp.exp2((scores - top) * TO_LOG2)
            total = jnp.sum(weights, axis=0, keepdims=True)
            mixed = jnp.sum(weights * dprobs, axis=0, keepdims=True)
            if not diagonal:
                shrink = jnp.exp2((old_top - top) * TO_LOG2)
                total += stats[i, h, 1:2, columns] * shrink
                mixed += stats[i, h, 2:3, columns] * shrink
            stats[i, h, 0:1, columns] = top
            stats[i, h, 1:2, columns] = total
            stats[i, h, 2:3, columns] = mixed


def spread_grads(found, count, kept_scores, kept_dprobs, stats, i, block, acc, saved, low, sent):
    def copy(n):
        return pltpu.make_async_copy(low.at[n], saved.at[i, n], sent.at[n])

    def add(n, _):
        e = found[n]
        for h in range(HALF_KV):
            dk, dv = acc[e, 0, h], acc[e, 1, h]
            for rows, columns in chunks():
                probs = jnp.exp2(
                    kept_scores[n, h, :, columns] * TO_LOG2 - stats[i, h, 0:1, columns]
                )
                dscores = probs * (kept_dprobs[n, h, :, columns] - stats[i, h, 2:3, columns])
                probs, dscores = probs.astype(BF16), dscores.astype(BF16)
                low[n, h, 0, :, columns] = probs
                low[n, h, 1, :, columns] = dscores
                dv += dot_nn(probs, heads_of(block, 1, h, rows))
                dk += dot_nn(dscores, heads_of(block, 0, h, rows))
            acc[e, 0, h] = dk
            acc[e, 1, h] = dv
        copy(n).start()
        return 0

    def finish(n, _):
        copy(n).wait()
        return 0

    lax.fori_loop(0, count, add, 0)
    lax.fori_loop(0, count, finish, 0)


def write_grads(acc, outs):
    for k, out in enumerate(outs):
        part = slice(CORES * k, CORES * (k + 1))
        out[:, 0] = (acc[part, 0] * SCALE).astype(out.dtype)
        out[:, 1] = acc[part, 1].astype(out.dtype)


def current_stats(n_seq, key_blocks, key_counts, own, other, *rest):
    n_pieces = n_seq // CORES
    pieces, (stats, store, found) = rest[:n_pieces], rest[n_pieces:]
    group, member, _ = here(n_seq)
    fill(store, pieces)
    for i, block in enumerate((own, other)):
        gather_stats(store, i, block, stats, i, True)
        count = list_blocks(
            n_seq, 1, group * n_seq + lax.bitwise_xor(member, i), group, member,
            key_blocks, key_counts, found,
        )

        def step(n, _):
            gather_stats(store, found[n], block, stats, i, False)
            return 0

        lax.fori_loop(0, count, step, 0)


def previous_grads(n_seq, key_blocks, key_counts, own, other, stats_in, *rest):
    n_pieces = n_seq // CORES
    pieces, outs = rest[:n_pieces], rest[n_pieces : 2 * n_pieces]
    saved, stats, store, found, kept_scores, kept_dprobs, acc, low, sent = rest[2 * n_pieces :]
    group, member, _ = here(n_seq)
    fill(store, pieces)
    acc[...] = jnp.zeros_like(acc)
    stats[...] = stats_in[...]
    for i, block in enumerate((own, other)):
        count = list_blocks(
            n_seq, 0, group * n_seq + lax.bitwise_xor(member, i), group, member,
            key_blocks, key_counts, found,
        )

        def look(n, _):
            gather_stats(store, found[n], block, stats, i, False, (n, kept_scores, kept_dprobs))
            return 0

        lax.fori_loop(0, count, look, 0)
        for h in range(HALF_KV):
            total = stats[i, h, 1:2, :]
            stats[i, h, 0:1, :] = stats[i, h, 0:1, :] * TO_LOG2 + jnp.log2(total)
            stats[i, h, 2:3, :] = stats[i, h, 2:3, :] / total

        spread_grads(
            found, count, kept_scores, kept_dprobs, stats, i, block, acc, saved, low, sent
        )
    write_grads(acc, outs)


def current_grads(n_seq, key_blocks, key_counts, own, other, stats, *rest):
    n_pieces = n_seq // CORES
    pieces, outs = rest[:n_pieces], rest[n_pieces : 2 * n_pieces]
    saved, store, found, acc, low, sent = rest[2 * n_pieces :]
    group, member, _ = here(n_seq)
    fill(store, pieces)
    acc[...] = jnp.zeros_like(acc)
    for i, block in enumerate((own, other)):
        found[0] = i
        count = list_blocks(
            n_seq, 1, group * n_seq + lax.bitwise_xor(member, i), group, member,
            key_blocks, key_counts, found, 1,
        )

        def copy(n):
            return pltpu.make_async_copy(low.at[n], saved.at[i, n], sent.at[n])

        def look(n, diagonal):
            e = found[n]
            for h in range(HALF_KV):
                for rows, columns in chunks():
                    scores, dprobs = pair_scores(store, e, h, block, rows, diagonal)
                    probs = jnp.exp2(scores * TO_LOG2 - stats[i, h, 0:1, columns])
                    low[n, h, 0, :, columns] = probs.astype(BF16)
                    dscores = probs * (dprobs - stats[i, h, 2:3, columns])
                    low[n, h, 1, :, columns] = dscores.astype(BF16)
            copy(n).start()
            return 0

        def add(n, _):
            e = found[n]
            for h in range(HALF_KV):
                for w in range(2):
                    right = block[1 - w, h].reshape(ROWS, HEAD_DIM)
                    acc[e, 1 - w, h] += dot_nn(low[n, h, w], right)
            return 0

        def finish(n, _):
            copy(n).wait()
            return 0

        look(0, True)
        lax.fori_loop(1, count, lambda n, _: look(n, False), 0)
        lax.fori_loop(0, count, add, 0)
        lax.fori_loop(0, count, finish, 0)
    write_grads(acc, outs)


def query_results(n_seq, h, key_blocks, key_counts, place_ref, far_saved, near_saved, *rest):
    n_pieces = n_seq // CORES
    pieces = rest[: 2 * n_pieces]
    (
        table, own_out, other_out, store, found, low, out_acc, dq_acc, got
    ) = rest[2 * n_pieces :]
    group, member, _ = here(n_seq)
    outs = (own_out, other_out)

    def far_copy(i, n, _):
        return pltpu.make_async_copy(far_saved.at[i, n, h], low.at[i, n], got.at[i, n])

    def near_copy(i, n, count):
        return pltpu.make_async_copy(near_saved.at[i, n - count, h], low.at[i, n], got.at[i, n])

    counts = []
    for i in range(2):
        block = group * n_seq + lax.bitwise_xor(member, i)
        lists = (block, group, member, key_blocks, key_counts, found.at[i])
        far = list_blocks(n_seq, 0, *lists)
        found[i, far] = n_seq + i
        total = list_blocks(n_seq, 1, *lists, far + 1, n_seq)
        counts.append((far, total))

        def fetch_far(n, _):
            far_copy(i, n, 0).start()
            return 0

        def fetch_near(n, _):
            near_copy(i, n, far).start()
            return 0

        lax.fori_loop(0, far, fetch_far, 0)
        lax.fori_loop(far, total, fetch_near, 0)
    for k, piece in enumerate(pieces):
        store[CORES * k : CORES * (k + 1)] = piece[:, :, h : h + 1]
    for i, (far, total) in enumerate(counts):
        mine = group * n_seq + lax.bitwise_xor(member, i)

        @pl.when(lax.rem(total, 2) == 1)
        def _():
            found[i, total] = 0
            low[i, total] = jnp.zeros((2, BLK, ROWS), BF16)

        out_acc[...] = jnp.zeros_like(out_acc)
        dq_acc[...] = jnp.zeros_like(dq_acc)

        def add(n, _):
            pair = (2 * n, 2 * n + 1)
            for m in pair:

                @pl.when(m < far)
                def _():
                    far_copy(i, m, 0).wait()

                @pl.when(jnp.logical_and(m >= far, m < total))
                def _():
                    near_copy(i, m, far).wait()

            keys_t = jnp.concatenate([store[found[i, m], 0, 0].T for m in pair], axis=1)
            values_t = jnp.concatenate([store[found[i, m], 1, 0].T for m in pair], axis=1)
            for _, columns in chunks():
                probs = jnp.concatenate([low[i, m, 0, :, columns] for m in pair], axis=0)
                dscores = jnp.concatenate([low[i, m, 1, :, columns] for m in pair], axis=0)
                out_acc[:, columns] += dot_nn(values_t, probs)
                dq_acc[:, columns] += dot_nn(keys_t, dscores)
            return 0

        lax.fori_loop(0, lax.div(total + 1, 2), add, 0)
        cosine, sine = block_tables(place_ref[mine], table)
        cosine, sine = cosine.T * SCALE, sine.T * SCALE
        for r in range(RATIO):
            rows = slice(r * BLK, (r + 1) * BLK)
            columns = slice(r * HEAD_DIM, (r + 1) * HEAD_DIM)
            outs[i][0, :, columns] = out_acc[:, rows].astype(BF16).T
            dq = dq_acc[:, rows]
            half = HEAD_DIM // 2
            turned = jnp.concatenate([dq[half:], dq[:half]], axis=0)
            outs[i][1, :, columns] = (dq * cosine - turned * sine).astype(BF16).T


def finish_kv(n_seq, place_ref, *rest):
    *terms, table, keep, send = rest
    group, member, _ = here(n_seq)
    for i, result in enumerate((keep, send)):
        offset = lax.bitwise_xor(member, i)
        cosine, sine = block_tables(place_ref[group * n_seq + offset], table)
        for h in range(HALF_KV):
            columns = slice(h * HEAD_DIM, (h + 1) * HEAD_DIM)
            dk, dv = (sum(term[i, w, h].astype(F32) for term in terms) for w in range(2))
            result[0, :, columns] = turn(dk, cosine, -sine).astype(BF16)
            result[1, :, columns] = dv.astype(BF16)


def join_halves(n_parts, *refs):
    parts, outs = refs[: 2 * n_parts], refs[2 * n_parts :]
    core = lax.rem(lax.axis_index("seq"), CORES)
    width = parts[0].shape[-1]
    for half, which in ((core, parts[:n_parts]), (1 - core, parts[n_parts:])):
        for n, part in enumerate(which):
            start = pl.multiple_of((half * n_parts + n) * width, width)
            for w, out in enumerate(outs):
                out[:, pl.ds(start, width)] = part[w]


def local(query_input, key_input, value_input, out_grad, key_blocks, key_counts, block_position):
    n_seq = lax.axis_size("seq")
    n_grp = lax.axis_size("grp")
    n_pieces = n_seq // CORES
    n_listed = key_blocks.shape[1]

    def cross(array, by):
        return lax.ppermute(array, "seq", [(m, m ^ by) for m in range(n_seq)])

    def along(array, by):
        return cross(array, CORES * by)

    def onward(array):
        return lax.ppermute(array, "grp", [(g, g + 1) for g in range(n_grp - 1)])

    def back(array):
        return lax.ppermute(array, "grp", [(g + 1, g) for g in range(n_grp - 1)])

    table = trig_table(block_position.shape[0])
    n_far = min(n_seq, n_listed - 1)
    piece = (2, HALF_KV, BLK, HEAD_DIM)
    chip = (CORES, *piece)
    q_shape = jax.ShapeDtypeStruct((2, HALF_KV, RATIO, BLK, HEAD_DIM), BF16)
    kv_shape = jax.ShapeDtypeStruct(piece, BF16)
    stats_shape = jax.ShapeDtypeStruct((2, HALF_KV, 8, ROWS), F32)
    found = pltpu.SMEM((n_listed,), jnp.int32)
    store = pltpu.VMEM((n_seq, *piece), BF16)
    acc = pltpu.VMEM((n_seq, *piece), F32)
    low = jax.ShapeDtypeStruct(chip, BF16)
    high = jax.ShapeDtypeStruct(chip, F32)

    def prepared(kernel, shape, first, second, name):
        held = [pltpu.VMEM(a.shape, a.dtype) for a in (first, second, table)]
        return call(
            functools.partial(kernel, n_seq), (shape, shape), 1,
            [*held, pltpu.SemaphoreType.DMA((3,))], us=1, name=name, n_hbm=3,
        )(block_position, first, second, table)

    kv_keep, kv_send = prepared(prepare_kv, kv_shape, key_input, value_input, "rotate_keys")
    kv_got = cross(kv_send, 1)
    query_late, kv_keep = lax.optimization_barrier((query_input, kv_keep))
    q_keep, q_send = prepared(prepare_queries, q_shape, query_late, out_grad, "rotate_queries")
    q_send, q_keep, kv_got, kv_keep = lax.optimization_barrier((q_send, q_keep, kv_got, kv_keep))
    q_got = cross(q_send, 1)
    near = [jnp.stack([kv_keep, kv_got])]
    near.append(along(near[0], 1))
    ready, first_far = lax.optimization_barrier((near[1], onward(near[0])))
    far = [first_far, None]
    for k in range(2, n_pieces, 2):
        piece_k, _ = lax.optimization_barrier((along(near[0], k), ready))
        near += [piece_k, along(piece_k, 1)]
        far.append(onward(piece_k))
        far.append(along(far[k], 1))
    ready, far[2] = lax.optimization_barrier((ready, far[2]))
    far[1] = onward(ready)

    stats = call(
        functools.partial(current_stats, n_seq), stats_shape, 2, [store, found],
        us=6, name="current_statistics",
    )(key_blocks, key_counts, q_keep, q_got, *near)

    def grads_call(kernel, n_slots, outs, us, name, kept=()):
        pair = (n_slots, HALF_KV, 2, BLK, ROWS)
        saved = jax.ShapeDtypeStruct((2, *pair), BF16)
        return call(
            functools.partial(kernel, n_seq), (*outs[:n_pieces], saved, *outs[n_pieces:]), 2,
            [store, found, *kept, acc, pltpu.VMEM(pair, BF16), pltpu.SemaphoreType.DMA((n_slots,))],
            us=us, name=name, hbm_out=n_pieces,
        )

    kept = pltpu.VMEM((n_far, HALF_KV, BLK, ROWS), F32)
    *far_grads, far_saved, stats = grads_call(
        previous_grads, n_far, (low,) * n_pieces + (stats_shape,), 14, "previous_gradients",
        (kept, kept),
    )(key_blocks, key_counts, q_keep, q_got, stats, *far)
    *near_grads, near_saved = grads_call(
        current_grads, min(n_seq, n_listed),
        tuple(low if k % 2 and k > 1 else high for k in range(n_pieces)), 10, "current_gradients",
    )(key_blocks, key_counts, q_keep, q_got, stats, *near)

    half_out = jax.ShapeDtypeStruct((2, BLK, RATIO * HEAD_DIM), BF16)

    def results(h, after):
        place_late, _ = lax.optimization_barrier((block_position, after))
        wide = pltpu.VMEM((HEAD_DIM, ROWS), F32)
        return call(
            functools.partial(query_results, n_seq, h), (half_out, half_out), 3,
            [
                pltpu.VMEM((2 * n_seq, 2, 1, BLK, HEAD_DIM), BF16),
                pltpu.SMEM((2, n_listed + 1), jnp.int32),
                pltpu.VMEM((2, n_listed + 1, 2, BLK, ROWS), BF16), wide, wide,
                pltpu.SemaphoreType.DMA((2, n_listed)),
            ],
            us=20, name="query_results", n_hbm=2,
        )(key_blocks, key_counts, place_late, far_saved, near_saved, *far, *near, table)

    def total(*terms):
        return sum(term.astype(F32) for term in terms).astype(BF16)

    arrived = [back(far_grads[1])]
    last = far_grads[0]
    for k in range(2, n_pieces, 2):
        gathered = total(far_grads[k], along(far_grads[k + 1], 1))
        arrived.append(back(gathered))
    last, arrived[-1] = lax.optimization_barrier((last, arrived[-1]))
    last = back(last)
    merged = [total(near_grads[1], arrived[0])]
    for n, k in enumerate(range(2, n_pieces, 2)):
        merged.append(total(near_grads[k], arrived[1 + n], along(near_grads[k + 1], 1)))
    own_halves, other_halves = zip(*[results(h, merged) for h in range(HALF_KV)])
    own_halves = list(own_halves)
    got_halves = [cross(half, 1) for half in other_halves]
    final = [near_grads[0], last, along(merged[0], 1)]
    final += [along(merged[1 + n], k) for n, k in enumerate(range(2, n_pieces, 2))]
    final[0], own_halves[1] = lax.optimization_barrier((final[0], own_halves[1]))
    full = jax.ShapeDtypeStruct(query_input.shape, BF16)
    out_rows, query_grad = call(
        functools.partial(join_halves, HALF_KV), (full, full), 0, us=2, name="join_queries"
    )(*own_halves, *got_halves)
    kv_half = jax.ShapeDtypeStruct((2, BLK, HALF_KV * HEAD_DIM), BF16)
    own_kv, other_kv = call(
        functools.partial(finish_kv, n_seq), (kv_half, kv_half), 1,
        us=2, name="key_gradients",
    )(block_position, *final, table)
    got_kv = cross(other_kv, 1)
    full = jax.ShapeDtypeStruct(key_input.shape, BF16)
    key_grad, value_grad = call(
        functools.partial(join_halves, 1), (full, full), 0, us=1, name="join_keys"
    )(own_kv, got_kv)
    return (out_rows, query_grad, key_grad, value_grad)


def solution(mesh):
    split = P(("grp", "seq"), None)
    return jax.shard_map(
        local,
        mesh=mesh,
        in_specs=(split, split, split, split, P(), P(), P()),
        out_specs=(split, split, split, split),
        check_vma=False,
    )
```

```python
import functools
import math

import jax
import jax.numpy as jnp
import numpy as np
from jax import lax
from jax.experimental import pallas as pl
from jax.experimental.pallas import tpu as pltpu
from jax.sharding import PartitionSpec as P

HEADS = 32
KV_HEADS = 4
HEAD_DIM = 128
BLK = 128
CORES = 2
RATIO = HEADS // KV_HEADS
HALF_KV = KV_HEADS // CORES
ROWS = RATIO * BLK
SCALE = 1.0 / math.sqrt(HEAD_DIM)
TO_LOG2 = SCALE * math.log2(math.e)
F32 = jnp.float32
BF16 = jnp.bfloat16
CHUNK = 256

VMEM_SPEC = pl.BlockSpec(memory_space=pltpu.VMEM)
HBM_SPEC = pl.BlockSpec(memory_space=pltpu.HBM)
SMEM_SPEC = pl.BlockSpec(memory_space=pltpu.SMEM)


def trig_table(n_blocks):
    half = HEAD_DIM // 2
    frequency = np.power(500000.0, -np.arange(half) * (2.0 / HEAD_DIM))
    parts = []
    for places in (np.arange(n_blocks) * BLK, np.arange(BLK)):
        angles = places[:, None] * frequency
        for part in (np.cos(angles), np.sin(angles)):
            parts.append(np.concatenate([part, part], axis=1))
    return np.concatenate(parts, axis=0).astype(np.float32)


def block_tables(place, table):
    n_blocks = table.shape[0] // 2 - BLK
    cos_b = table[pl.ds(place, 1), :]
    sin_b = table[pl.ds(n_blocks + place, 1), :]
    cos_t = table[2 * n_blocks : 2 * n_blocks + BLK, :]
    sin_t = table[2 * n_blocks + BLK :, :]
    cosine = cos_b * cos_t - sin_b * sin_t
    sine = sin_b * cos_t + cos_b * sin_t
    lanes = lax.broadcasted_iota(jnp.int32, sine.shape, 1)
    return cosine, jnp.where(lanes < HEAD_DIM // 2, -sine, sine)


def turn(values, cosine, signed_sine):
    return values * cosine + pltpu.roll(values, HEAD_DIM // 2, 1) * signed_sine


def dot_nt(a, b):
    return lax.dot_general(a, b, (((1,), (1,)), ((), ())), preferred_element_type=F32)


def dot_nn(a, b):
    return lax.dot_general(a, b, (((1,), (0,)), ((), ())), preferred_element_type=F32)


def here(n_seq):
    member = lax.axis_index("seq")
    group = lax.axis_index("grp")
    return group, member, lax.rem(member, CORES)


def size_of(array):
    return math.prod(array.shape) * jnp.dtype(array.dtype).itemsize


def call(kernel, out_shape, n_smem, scratch=(), us=1, name=None, spare=6, n_hbm=0, hbm_out=None):
    def run(*arrays):
        n_left = n_smem + n_hbm
        outs = list(out_shape) if isinstance(out_shape, (tuple, list)) else [out_shape]
        held = sum(size_of(a) for a in arrays[n_left:])
        held += sum(size_of(a) for n, a in enumerate(outs) if n != hbm_out)
        held += sum(size_of(a) for a in scratch if a.dtype in (F32, BF16))
        out_specs = [HBM_SPEC if n == hbm_out else VMEM_SPEC for n in range(len(outs))]
        in_specs = [SMEM_SPEC] * n_smem + [HBM_SPEC] * n_hbm
        in_specs += [VMEM_SPEC] * (len(arrays) - n_left)
        pinned = [
            pltpu.with_memory_space_constraint(a, pltpu.HBM) if n < n_left else a
            for n, a in enumerate(arrays)
        ]
        results = pl.pallas_call(
            kernel,
            out_shape=[
                pltpu.HBM(a.shape, a.dtype) if n == hbm_out else a for n, a in enumerate(outs)
            ],
            in_specs=in_specs,
            out_specs=out_specs,
            scratch_shapes=list(scratch),
            compiler_params=pltpu.CompilerParams(vmem_limit_bytes=held + spare * 2**20),
            cost_estimate=pl.CostEstimate(
                flops=us * 10**9, bytes_accessed=2**20, transcendentals=0
            ),
            name=name,
        )(*pinned)
        return results if isinstance(out_shape, (tuple, list)) else results[0]

    return run


def fetch(sources, places, sems):
    copies = [
        pltpu.make_async_copy(source, place, sems.at[n])
        for n, (source, place) in enumerate(zip(sources, places))
    ]
    for copy in copies:
        copy.start()
    for copy in copies:
        copy.wait()


def prepare_kv(n_seq, place_ref, *refs):
    sources, (keep, send), (key, value, table, sems) = refs[:3], refs[3:5], refs[5:]
    fetch(sources, (key, value, table), sems)
    group, member, core = here(n_seq)
    cosine, sine = block_tables(place_ref[group * n_seq + member], table)
    for out, half in ((keep, core), (send, 1 - core)):
        for h in range(HALF_KV):
            columns = pl.ds(pl.multiple_of((half * HALF_KV + h) * HEAD_DIM, HEAD_DIM), HEAD_DIM)
            out[0, h] = turn(key[:, columns].astype(F32), cosine, sine).astype(BF16)
            out[1, h] = value[:, columns]


def prepare_queries(n_seq, place_ref, *refs):
    sources, (keep, send), (query, grad, table, sems) = refs[:3], refs[3:5], refs[5:]
    fetch(sources, (query, grad, table), sems)
    group, member, core = here(n_seq)
    cosine, sine = block_tables(place_ref[group * n_seq + member], table)
    for out, half in ((keep, core), (send, 1 - core)):
        for h in range(HALF_KV):
            for r in range(RATIO):
                head = (half * HALF_KV + h) * RATIO + r
                columns = pl.ds(pl.multiple_of(head * HEAD_DIM, HEAD_DIM), HEAD_DIM)
                out[0, h, r] = turn(query[:, columns].astype(F32), cosine, sine).astype(BF16)
                out[1, h, r] = grad[:, columns]


def list_blocks(
    n_seq, side, block, group, member, key_blocks, key_counts, found, start=0, shift=0, span=None
):
    base = (group - 1 + side) * n_seq
    low, high = span or (0, n_seq)

    def look(j, n):
        offset = key_blocks[block, j] - base
        place = lax.bitwise_xor(jnp.clip(offset, 0, n_seq - 1), member)
        hit = jnp.logical_and(offset >= 0, offset < n_seq)
        hit = jnp.logical_and(hit, jnp.logical_and(place >= low, place < high))

        @pl.when(hit)
        def _():
            found[n] = place - low + shift

        return n + hit.astype(jnp.int32)

    return lax.fori_loop(1, key_counts[block], look, jnp.int32(start))


def causal():
    keys = lax.broadcasted_iota(jnp.int32, (BLK, CHUNK), 0)
    tokens = lax.rem(lax.broadcasted_iota(jnp.int32, (BLK, CHUNK), 1), BLK)
    return keys <= tokens


def chunks():
    per = CHUNK // BLK
    return [
        (slice(c * per, (c + 1) * per), slice(c * CHUNK, (c + 1) * CHUNK))
        for c in range(ROWS // CHUNK)
    ]


def heads_of(block, what, h, rows):
    return block[what, h, rows].reshape(CHUNK, HEAD_DIM)


def fill(store, pieces, first=0):
    for k, piece in enumerate(pieces):
        store[first + CORES * k : first + CORES * (k + 1)] = piece[...]


def pair_scores(store, e, h, block, rows, diagonal):
    scores = dot_nt(store[e, 0, h], heads_of(block, 0, h, rows))
    if diagonal:
        scores = jnp.where(causal(), scores, -1e30)
    return scores, dot_nt(store[e, 1, h], heads_of(block, 1, h, rows))


def gather_stats(store, e, block, stats, i, diagonal, kept=None):
    for h in range(HALF_KV):
        for rows, columns in chunks():
            scores, dprobs = pair_scores(store, e, h, block, rows, diagonal)
            if kept is not None:
                n, kept_scores, kept_dprobs = kept
                kept_scores[n, h, :, columns] = scores
                kept_dprobs[n, h, :, columns] = dprobs
            top = jnp.max(scores, axis=0, keepdims=True)
            if not diagonal:
                old_top = stats[i, h, 0:1, columns]
                top = jnp.maximum(top, old_top)
            weights = jnp.exp2((scores - top) * TO_LOG2)
            total = jnp.sum(weights, axis=0, keepdims=True)
            mixed = jnp.sum(weights * dprobs, axis=0, keepdims=True)
            if not diagonal:
                shrink = jnp.exp2((old_top - top) * TO_LOG2)
                total += stats[i, h, 1:2, columns] * shrink
                mixed += stats[i, h, 2:3, columns] * shrink
            stats[i, h, 0:1, columns] = top
            stats[i, h, 1:2, columns] = total
            stats[i, h, 2:3, columns] = mixed


def spread_grads(found, count, kept_scores, kept_dprobs, stats, i, block, acc, saved, low, sent):
    def copy(n):
        return pltpu.make_async_copy(low.at[n], saved.at[i, n], sent.at[n])

    def add(n, _):
        e = found[n]
        for h in range(HALF_KV):
            dk, dv = acc[e, 0, h], acc[e, 1, h]
            for rows, columns in chunks():
                probs = jnp.exp2(
                    kept_scores[n, h, :, columns] * TO_LOG2 - stats[i, h, 0:1, columns]
                )
                dscores = probs * (kept_dprobs[n, h, :, columns] - stats[i, h, 2:3, columns])
                probs, dscores = probs.astype(BF16), dscores.astype(BF16)
                low[n, h, 0, :, columns] = probs
                low[n, h, 1, :, columns] = dscores
                dv += dot_nn(probs, heads_of(block, 1, h, rows))
                dk += dot_nn(dscores, heads_of(block, 0, h, rows))
            acc[e, 0, h] = dk
            acc[e, 1, h] = dv
        copy(n).start()
        return 0

    def finish(n, _):
        copy(n).wait()
        return 0

    lax.fori_loop(0, count, add, 0)
    lax.fori_loop(0, count, finish, 0)


def write_grads(acc, outs):
    start = 0
    for out in outs:
        part = slice(start, start + out.shape[0])
        out[:, 0] = (acc[part, 0] * SCALE).astype(out.dtype)
        out[:, 1] = acc[part, 1].astype(out.dtype)
        start += out.shape[0]


def current_stats(n_seq, key_blocks, key_counts, own, other, *rest):
    n_pieces = n_seq // CORES
    pieces, (stats, store, found) = rest[:n_pieces], rest[n_pieces:]
    group, member, _ = here(n_seq)
    fill(store, pieces)
    for i, block in enumerate((own, other)):
        gather_stats(store, i, block, stats, i, True)
        count = list_blocks(
            n_seq, 1, group * n_seq + lax.bitwise_xor(member, i), group, member,
            key_blocks, key_counts, found,
        )

        def step(n, _):
            gather_stats(store, found[n], block, stats, i, False)
            return 0

        lax.fori_loop(0, count, step, 0)


def previous_grads(n_seq, key_blocks, key_counts, own, other, stats_in, *rest):
    n_pieces = n_seq // CORES
    n_ends = 2 * n_pieces - 1
    pieces, outs = rest[:n_pieces], rest[n_pieces:n_ends]
    saved, stats, store, found, kept_scores, kept_dprobs, acc, low, sent = rest[n_ends:]
    group, member, _ = here(n_seq)
    fill(store, pieces)
    acc[...] = jnp.zeros_like(acc)
    stats[...] = stats_in[...]
    for i, block in enumerate((own, other)):
        count = list_blocks(
            n_seq, 0, group * n_seq + lax.bitwise_xor(member, i), group, member,
            key_blocks, key_counts, found,
        )

        def look(n, _):
            gather_stats(store, found[n], block, stats, i, False, (n, kept_scores, kept_dprobs))
            return 0

        lax.fori_loop(0, count, look, 0)
        for h in range(HALF_KV):
            total = stats[i, h, 1:2, :]
            stats[i, h, 0:1, :] = stats[i, h, 0:1, :] * TO_LOG2 + jnp.log2(total)
            stats[i, h, 2:3, :] = stats[i, h, 2:3, :] / total

        spread_grads(
            found, count, kept_scores, kept_dprobs, stats, i, block, acc, saved, low, sent
        )
    write_grads(acc, outs)


def current_grads(n_seq, span, key_blocks, key_counts, own, other, stats, *rest):
    n_pieces = (span[1] - span[0]) // CORES
    diagonal_too = span[0] == 0
    pieces, outs = rest[:n_pieces], rest[n_pieces : 2 * n_pieces]
    saved, store, found, acc, low, sent = rest[2 * n_pieces :]
    group, member, _ = here(n_seq)
    fill(store, pieces)
    acc[...] = jnp.zeros_like(acc)
    for i, block in enumerate((own, other)):
        if diagonal_too:
            found[0] = i
        count = list_blocks(
            n_seq, 1, group * n_seq + lax.bitwise_xor(member, i), group, member,
            key_blocks, key_counts, found, int(diagonal_too), 0, span,
        )

        def copy(n):
            return pltpu.make_async_copy(low.at[n], saved.at[i, n], sent.at[n])

        def look(n, diagonal):
            e = found[n]
            for h in range(HALF_KV):
                for rows, columns in chunks():
                    scores, dprobs = pair_scores(store, e, h, block, rows, diagonal)
                    probs = jnp.exp2(scores * TO_LOG2 - stats[i, h, 0:1, columns])
                    low[n, h, 0, :, columns] = probs.astype(BF16)
                    dscores = probs * (dprobs - stats[i, h, 2:3, columns])
                    low[n, h, 1, :, columns] = dscores.astype(BF16)
            copy(n).start()
            return 0

        def add(n, _):
            e = found[n]
            for h in range(HALF_KV):
                for w in range(2):
                    right = block[1 - w, h].reshape(ROWS, HEAD_DIM)
                    acc[e, 1 - w, h] += dot_nn(low[n, h, w], right)
            return 0

        def finish(n, _):
            copy(n).wait()
            return 0

        if diagonal_too:
            look(0, True)
        lax.fori_loop(int(diagonal_too), count, lambda n, _: look(n, False), 0)
        lax.fori_loop(0, count, add, 0)
        lax.fori_loop(0, count, finish, 0)
    write_grads(acc, outs)


def query_results(n_seq, h, spans, key_blocks, key_counts, place_ref, *rest):
    n_saved = len(spans)
    n_pieces = n_seq // CORES
    saved, pieces, rest = rest[:n_saved], rest[n_saved:][: 2 * n_pieces], rest[n_saved + 2 * n_pieces :]
    table, own_out, other_out, store, found, low, out_acc, dq_acc, got = rest
    group, member, _ = here(n_seq)
    outs = (own_out, other_out)

    def copy(source, i, n, first):
        return pltpu.make_async_copy(source.at[i, n - first, h], low.at[i, n], got.at[i, n])

    ends = []
    for i in range(2):
        block = group * n_seq + lax.bitwise_xor(member, i)
        stops = [jnp.int32(0)]
        for source, (side, *span) in zip(saved, spans):
            first = start = stops[-1]
            shift = side * n_seq + span[0]
            if side == 1 and span[0] == 0:
                found[i, first] = n_seq + i
                start = first + 1
            stop = list_blocks(
                n_seq, side, block, group, member, key_blocks, key_counts, found.at[i], start,
                shift, span,
            )

            def fetch_one(n, _):
                copy(source, i, n, first).start()
                return 0

            lax.fori_loop(first, stop, fetch_one, 0)
            stops.append(stop)
        ends.append(stops)
    for k, piece in enumerate(pieces):
        store[CORES * k : CORES * (k + 1)] = piece[:, :, h : h + 1]
    for i, stops in enumerate(ends):
        mine = group * n_seq + lax.bitwise_xor(member, i)
        total = stops[-1]

        @pl.when(lax.rem(total, 2) == 1)
        def _():
            found[i, total] = 0
            low[i, total] = jnp.zeros((2, BLK, ROWS), BF16)

        out_acc[...] = jnp.zeros_like(out_acc)
        dq_acc[...] = jnp.zeros_like(dq_acc)

        def add(n, _):
            pair = (2 * n, 2 * n + 1)
            for m in pair:
                for source, first, stop in zip(saved, stops, stops[1:]):

                    @pl.when(jnp.logical_and(m >= first, m < stop))
                    def _():
                        copy(source, i, m, first).wait()

            keys_t = jnp.concatenate([store[found[i, m], 0, 0].T for m in pair], axis=1)
            values_t = jnp.concatenate([store[found[i, m], 1, 0].T for m in pair], axis=1)
            for _, columns in chunks():
                probs = jnp.concatenate([low[i, m, 0, :, columns] for m in pair], axis=0)
                dscores = jnp.concatenate([low[i, m, 1, :, columns] for m in pair], axis=0)
                out_acc[:, columns] += dot_nn(values_t, probs)
                dq_acc[:, columns] += dot_nn(keys_t, dscores)
            return 0

        lax.fori_loop(0, lax.div(total + 1, 2), add, 0)
        cosine, sine = block_tables(place_ref[mine], table)
        cosine, sine = cosine.T * SCALE, sine.T * SCALE
        for r in range(RATIO):
            rows = slice(r * BLK, (r + 1) * BLK)
            columns = slice(r * HEAD_DIM, (r + 1) * HEAD_DIM)
            outs[i][0, :, columns] = out_acc[:, rows].astype(BF16).T
            dq = dq_acc[:, rows]
            half = HEAD_DIM // 2
            turned = jnp.concatenate([dq[half:], dq[:half]], axis=0)
            outs[i][1, :, columns] = (dq * cosine - turned * sine).astype(BF16).T


def finish_kv(n_seq, place_ref, *rest):
    *terms, table, keep, send = rest
    group, member, _ = here(n_seq)
    for i, result in enumerate((keep, send)):
        offset = lax.bitwise_xor(member, i)
        cosine, sine = block_tables(place_ref[group * n_seq + offset], table)
        for h in range(HALF_KV):
            columns = slice(h * HEAD_DIM, (h + 1) * HEAD_DIM)
            dk, dv = (sum(term[i, w, h].astype(F32) for term in terms) for w in range(2))
            result[0, :, columns] = turn(dk, cosine, -sine).astype(BF16)
            result[1, :, columns] = dv.astype(BF16)


def join_halves(n_parts, *refs):
    parts, outs = refs[: 2 * n_parts], refs[2 * n_parts :]
    core = lax.rem(lax.axis_index("seq"), CORES)
    width = parts[0].shape[-1]
    for half, which in ((core, parts[:n_parts]), (1 - core, parts[n_parts:])):
        for n, part in enumerate(which):
            start = pl.multiple_of((half * n_parts + n) * width, width)
            for w, out in enumerate(outs):
                out[:, pl.ds(start, width)] = part[w]


def local(query_input, key_input, value_input, out_grad, key_blocks, key_counts, block_position):
    n_seq = lax.axis_size("seq")
    n_grp = lax.axis_size("grp")
    n_pieces = n_seq // CORES
    n_listed = key_blocks.shape[1]

    def cross(array, by):
        return lax.ppermute(array, "seq", [(m, m ^ by) for m in range(n_seq)])

    def along(array, by):
        return cross(array, CORES * by)

    def onward(array):
        return lax.ppermute(array, "grp", [(g, g + 1) for g in range(n_grp - 1)])

    def back(array):
        return lax.ppermute(array, "grp", [(g + 1, g) for g in range(n_grp - 1)])

    table = trig_table(block_position.shape[0])
    n_far = min(n_seq, n_listed - 1)
    piece = (2, HALF_KV, BLK, HEAD_DIM)
    chip = (CORES, *piece)
    q_shape = jax.ShapeDtypeStruct((2, HALF_KV, RATIO, BLK, HEAD_DIM), BF16)
    kv_shape = jax.ShapeDtypeStruct(piece, BF16)
    stats_shape = jax.ShapeDtypeStruct((2, HALF_KV, 8, ROWS), F32)
    found = pltpu.SMEM((n_listed,), jnp.int32)
    store = pltpu.VMEM((n_seq, *piece), BF16)
    low = jax.ShapeDtypeStruct(chip, BF16)
    high = jax.ShapeDtypeStruct(chip, F32)

    def prepared(kernel, shape, first, second, name):
        held = [pltpu.VMEM(a.shape, a.dtype) for a in (first, second, table)]
        return call(
            functools.partial(kernel, n_seq), (shape, shape), 1,
            [*held, pltpu.SemaphoreType.DMA((3,))], us=1, name=name, n_hbm=3,
        )(block_position, first, second, table)

    kv_keep, kv_send = prepared(prepare_kv, kv_shape, key_input, value_input, "rotate_keys")
    kv_got = cross(kv_send, 1)
    query_late, kv_keep = lax.optimization_barrier((query_input, kv_keep))
    q_keep, q_send = prepared(prepare_queries, q_shape, query_late, out_grad, "rotate_queries")
    q_send, q_keep, kv_got, kv_keep = lax.optimization_barrier((q_send, q_keep, kv_got, kv_keep))
    q_got = cross(q_send, 1)
    near = [jnp.stack([kv_keep, kv_got])]
    near.append(along(near[0], 1))
    ready, first_far = lax.optimization_barrier((near[1], onward(near[0])))
    far = [first_far, None]
    for k in range(2, n_pieces, 2):
        piece_k, _ = lax.optimization_barrier((along(near[0], k), ready))
        near += [piece_k, along(piece_k, 1)]
        far.append(onward(piece_k))
        far.append(along(far[k], 1))
    ready, far[2] = lax.optimization_barrier((ready, far[2]))
    far[1] = onward(ready)

    stats = call(
        functools.partial(current_stats, n_seq), stats_shape, 2, [store, found],
        us=6, name="current_statistics",
    )(key_blocks, key_counts, q_keep, q_got, *near)

    def grads_call(kernel, n_slots, n_store, outs, us, name, kept=(), more=()):
        pair = (n_slots, HALF_KV, 2, BLK, ROWS)
        saved = jax.ShapeDtypeStruct((2, *pair), BF16)
        return call(
            kernel, (*outs, saved, *more), 2,
            [
                pltpu.VMEM((n_store, *piece), BF16), found, *kept,
                pltpu.VMEM((n_store, *piece), F32), pltpu.VMEM(pair, BF16),
                pltpu.SemaphoreType.DMA((n_slots,)),
            ],
            us=us, name=name, hbm_out=len(outs),
        )

    kept = pltpu.VMEM((n_far, HALF_KV, BLK, ROWS), F32)
    two = jax.ShapeDtypeStruct((2 * CORES, *piece), BF16)
    first_far, *far_grads, far_saved, stats = grads_call(
        functools.partial(previous_grads, n_seq), n_far, n_seq, (two,) + (low,) * (n_pieces - 2),
        14, "previous_gradients", (kept, kept), (stats_shape,),
    )(key_blocks, key_counts, q_keep, q_got, stats, *far)

    split = 2 * CORES
    spans = ((0, 0, n_seq), (1, 0, split), (1, split, n_seq))

    def current_call(span, outs, name, pieces, after):
        stats_late, _ = lax.optimization_barrier((stats, after))
        n_slots = min(span[1] - span[0], n_listed)
        *grads, saved = grads_call(
            functools.partial(current_grads, n_seq, span), n_slots, span[1] - span[0], outs, 6, name
        )(key_blocks, key_counts, q_keep, q_got, stats_late, *pieces)
        return grads, saved

    half_out = jax.ShapeDtypeStruct((2, BLK, RATIO * HEAD_DIM), BF16)

    def results(h, after):
        place_late, _ = lax.optimization_barrier((block_position, after))
        wide = pltpu.VMEM((HEAD_DIM, ROWS), F32)
        return call(
            functools.partial(query_results, n_seq, h, spans), (half_out, half_out), 3,
            [
                pltpu.VMEM((2 * n_seq, 2, 1, BLK, HEAD_DIM), BF16),
                pltpu.SMEM((2, n_listed + 1), jnp.int32),
                pltpu.VMEM((2, n_listed + 1, 2, BLK, ROWS), BF16), wide, wide,
                pltpu.SemaphoreType.DMA((2, n_listed)),
            ],
            us=20, name="query_results", n_hbm=len(spans),
        )(
            key_blocks, key_counts, place_late, far_saved, low_saved, high_saved, *far, *near, table
        )

    def total(*terms):
        return sum(term.astype(F32) for term in terms).astype(BF16)

    from_far = back(first_far)
    crossing = [along(grad, 1) for grad in far_grads[1::2]]
    high_grads, high_saved = current_call(
        (split, n_seq), [high, low] * (n_pieces // 2 - 1), "far_current_gradients",
        near[2:], far_grads[0],
    )
    crossing, high_grads = lax.optimization_barrier((crossing, high_grads))
    arrived = [
        back(total(grad, extra)) for grad, extra in zip(far_grads[0::2], crossing)
    ]
    swapped = [along(grad, 1) for grad in high_grads[1::2]]
    low_grads, low_saved = current_call(
        (0, split), [high, high], "near_current_gradients", near[:2], high_grads[0]
    )
    low_grads, from_far = lax.optimization_barrier((low_grads, from_far))
    from_next = along(total(low_grads[1], from_far[CORES:]), 1)
    merged = [
        total(*terms) for terms in zip(high_grads[0::2], arrived, swapped)
    ]
    own_halves, other_halves = zip(*[results(h, merged) for h in range(HALF_KV)])
    own_halves, other_halves = list(own_halves), lax.optimization_barrier(list(other_halves))
    got_halves = [cross(half, 1) for half in other_halves]
    final = [low_grads[0], from_far[:CORES], from_next]
    final += [along(part, 2 + 2 * n) for n, part in enumerate(merged)]
    final[0], own_halves[1] = lax.optimization_barrier((final[0], own_halves[1]))
    full = jax.ShapeDtypeStruct(query_input.shape, BF16)
    out_rows, query_grad = call(
        functools.partial(join_halves, HALF_KV), (full, full), 0, us=2, name="join_queries"
    )(*own_halves, *got_halves)

    kv_half = jax.ShapeDtypeStruct((2, BLK, HALF_KV * HEAD_DIM), BF16)
    own_kv, other_kv = call(
        functools.partial(finish_kv, n_seq), (kv_half, kv_half), 1,
        us=2, name="key_gradients",
    )(block_position, *final, table)
    got_kv = cross(other_kv, 1)
    full = jax.ShapeDtypeStruct(key_input.shape, BF16)
    key_grad, value_grad = call(
        functools.partial(join_halves, 1), (full, full), 0, us=1, name="join_keys"
    )(own_kv, got_kv)
    return (out_rows, query_grad, key_grad, value_grad)


def solution(mesh):
    split = P(("grp", "seq"), None)
    return jax.shard_map(
        local,
        mesh=mesh,
        in_specs=(split, split, split, split, P(), P(), P()),
        out_specs=(split, split, split, split),
        check_vma=False,
    )
```

```python
import functools
import math

import jax
import jax.numpy as jnp
import numpy as np
from jax import lax
from jax.experimental import pallas as pl
from jax.experimental.pallas import tpu as pltpu
from jax.sharding import PartitionSpec as P

HEADS = 32
KV_HEADS = 4
HEAD_DIM = 128
BLK = 128
CORES = 2
RATIO = HEADS // KV_HEADS
HALF_KV = KV_HEADS // CORES
ROWS = RATIO * BLK
SCALE = 1.0 / math.sqrt(HEAD_DIM)
TO_LOG2 = SCALE * math.log2(math.e)
F32 = jnp.float32
BF16 = jnp.bfloat16
CHUNK = 256

VMEM_SPEC = pl.BlockSpec(memory_space=pltpu.VMEM)
HBM_SPEC = pl.BlockSpec(memory_space=pltpu.HBM)
SMEM_SPEC = pl.BlockSpec(memory_space=pltpu.SMEM)


def trig_table(n_blocks):
    half = HEAD_DIM // 2
    frequency = np.power(500000.0, -np.arange(half) * (2.0 / HEAD_DIM))
    parts = []
    for places in (np.arange(n_blocks) * BLK, np.arange(BLK)):
        angles = places[:, None] * frequency
        for part in (np.cos(angles), np.sin(angles)):
            parts.append(np.concatenate([part, part], axis=1))
    return np.concatenate(parts, axis=0).astype(np.float32)


def block_tables(place, table):
    n_blocks = table.shape[0] // 2 - BLK
    cos_b = table[pl.ds(place, 1), :]
    sin_b = table[pl.ds(n_blocks + place, 1), :]
    cos_t = table[2 * n_blocks : 2 * n_blocks + BLK, :]
    sin_t = table[2 * n_blocks + BLK :, :]
    cosine = cos_b * cos_t - sin_b * sin_t
    sine = sin_b * cos_t + cos_b * sin_t
    lanes = lax.broadcasted_iota(jnp.int32, sine.shape, 1)
    return cosine, jnp.where(lanes < HEAD_DIM // 2, -sine, sine)


def turn(values, cosine, signed_sine):
    return values * cosine + pltpu.roll(values, HEAD_DIM // 2, 1) * signed_sine


def dot_nt(a, b):
    return lax.dot_general(a, b, (((1,), (1,)), ((), ())), preferred_element_type=F32)


def dot_nn(a, b):
    return lax.dot_general(a, b, (((1,), (0,)), ((), ())), preferred_element_type=F32)


def here(n_seq):
    member = lax.axis_index("seq")
    group = lax.axis_index("grp")
    return group, member, lax.rem(member, CORES)


def size_of(array):
    return math.prod(array.shape) * jnp.dtype(array.dtype).itemsize


def call(kernel, out_shape, n_smem, scratch=(), us=1, name=None, n_hbm=0, hbm_out=None, pin=False):
    def placed(n, a):
        if n == hbm_out:
            return pltpu.HBM(a.shape, a.dtype)
        return pltpu.VMEM(a.shape, a.dtype) if pin else a

    def spec(n, a):
        if a.dtype == jnp.int32:
            return SMEM_SPEC
        return HBM_SPEC if n == hbm_out else VMEM_SPEC

    def run(*arrays):
        n_left = n_smem + n_hbm
        outs = list(out_shape) if isinstance(out_shape, (tuple, list)) else [out_shape]
        held = sum(size_of(a) for a in arrays[n_left:])
        held += sum(size_of(a) for n, a in enumerate(outs) if n != hbm_out)
        held += sum(size_of(a) for a in scratch if a.dtype in (F32, BF16))
        in_specs = [SMEM_SPEC] * n_smem + [HBM_SPEC] * n_hbm
        in_specs += [VMEM_SPEC] * (len(arrays) - n_left)
        pinned = [
            pltpu.with_memory_space_constraint(a, pltpu.HBM) if n < n_left else a
            for n, a in enumerate(arrays)
        ]
        results = pl.pallas_call(
            kernel,
            out_shape=[placed(n, a) for n, a in enumerate(outs)],
            in_specs=in_specs,
            out_specs=[spec(n, a) for n, a in enumerate(outs)],
            scratch_shapes=list(scratch),
            compiler_params=pltpu.CompilerParams(vmem_limit_bytes=held + 6 * 2**20),
            cost_estimate=pl.CostEstimate(
                flops=us * 10**9, bytes_accessed=2**20, transcendentals=0
            ),
            name=name,
        )(*pinned)
        return results if isinstance(out_shape, (tuple, list)) else results[0]

    return run


def fetch(sources, places, sems):
    copies = [
        pltpu.make_async_copy(source, place, sems.at[n])
        for n, (source, place) in enumerate(zip(sources, places))
    ]
    for copy in copies:
        copy.start()
    for copy in copies:
        copy.wait()


def prepare_kv(n_seq, place_ref, *refs):
    sources, (keep, send), (key, value, table, sems) = refs[:3], refs[3:5], refs[5:]
    fetch(sources, (key, value, table), sems)
    group, member, core = here(n_seq)
    cosine, sine = block_tables(place_ref[group * n_seq + member], table)
    for out, half in ((keep, core), (send, 1 - core)):
        for h in range(HALF_KV):
            columns = pl.ds(pl.multiple_of((half * HALF_KV + h) * HEAD_DIM, HEAD_DIM), HEAD_DIM)
            out[0, h] = turn(key[:, columns].astype(F32), cosine, sine).astype(BF16)
            out[1, h] = value[:, columns]


def prepare_queries(n_seq, place_ref, *refs):
    sources, (keep, send), (query, grad, table, sems) = refs[:3], refs[3:5], refs[5:]
    fetch(sources, (query, grad, table), sems)
    group, member, core = here(n_seq)
    cosine, sine = block_tables(place_ref[group * n_seq + member], table)
    for out, half in ((keep, core), (send, 1 - core)):
        for h in range(HALF_KV):
            for r in range(RATIO):
                head = (half * HALF_KV + h) * RATIO + r
                columns = pl.ds(pl.multiple_of(head * HEAD_DIM, HEAD_DIM), HEAD_DIM)
                out[0, h, r] = turn(query[:, columns].astype(F32), cosine, sine).astype(BF16)
                out[1, h, r] = grad[:, columns]


def make_lists(n_seq, split, key_blocks, key_counts, lists, counts):
    group, member, _ = here(n_seq)
    for i in range(2):
        block = group * n_seq + lax.bitwise_xor(member, i)
        for section in range(3):
            counts[i, section] = int(section == 1)
        lists[i, 1, 0] = i

        def look(j, _):
            place = lax.bitwise_xor(key_blocks[block, j] - (group - 1) * n_seq, member)
            section = (place >= n_seq).astype(jnp.int32)
            section += (place >= n_seq + split).astype(jnp.int32)
            n = counts[i, section]
            lists[i, section, n] = place - jnp.where(section == 0, 0, n_seq) - jnp.where(
                section == 2, split, 0
            )
            counts[i, section] = n + 1
            return 0

        lax.fori_loop(1, key_counts[block], look, 0)
        total = 0
        for section, base in enumerate((0, n_seq, n_seq + split)):

            def append(n, m):
                lists[i, 3, m] = lists[i, section, n] + base
                return m + 1

            total = lax.fori_loop(0, counts[i, section], append, jnp.int32(total))
        counts[i, 3] = total
        lists[i, 3, total] = 0


def causal():
    keys = lax.broadcasted_iota(jnp.int32, (BLK, CHUNK), 0)
    tokens = lax.rem(lax.broadcasted_iota(jnp.int32, (BLK, CHUNK), 1), BLK)
    return keys <= tokens


def chunks():
    per = CHUNK // BLK
    return [
        (slice(c * per, (c + 1) * per), slice(c * CHUNK, (c + 1) * CHUNK))
        for c in range(ROWS // CHUNK)
    ]


def heads_of(block, what, h, rows):
    return block[what, h, rows].reshape(CHUNK, HEAD_DIM)


def fill(store, pieces, first=0):
    for k, piece in enumerate(pieces):
        store[first + CORES * k : first + CORES * (k + 1)] = piece[...]


def pair_scores(store, e, h, block, rows, diagonal):
    scores = dot_nt(store[e, 0, h], heads_of(block, 0, h, rows))
    if diagonal:
        scores = jnp.where(causal(), scores, -1e30)
    return scores, dot_nt(store[e, 1, h], heads_of(block, 1, h, rows))


def gather_stats(store, e, block, stats, i, diagonal, kept=None):
    for h in range(HALF_KV):
        for rows, columns in chunks():
            scores, dprobs = pair_scores(store, e, h, block, rows, diagonal)
            if kept is not None:
                n, kept_scores, kept_dprobs = kept
                kept_scores[n, h, :, columns] = scores
                kept_dprobs[n, h, :, columns] = dprobs
            top = jnp.max(scores, axis=0, keepdims=True)
            if not diagonal:
                old_top = stats[i, h, 0:1, columns]
                top = jnp.maximum(top, old_top)
            weights = jnp.exp2((scores - top) * TO_LOG2)
            total = jnp.sum(weights, axis=0, keepdims=True)
            mixed = jnp.sum(weights * dprobs, axis=0, keepdims=True)
            if not diagonal:
                shrink = jnp.exp2((old_top - top) * TO_LOG2)
                total += stats[i, h, 1:2, columns] * shrink
                mixed += stats[i, h, 2:3, columns] * shrink
            stats[i, h, 0:1, columns] = top
            stats[i, h, 1:2, columns] = total
            stats[i, h, 2:3, columns] = mixed


def spread_grads(found, count, kept_scores, kept_dprobs, stats, i, block, acc, saved, low, sent):
    def copy(n):
        return pltpu.make_async_copy(low.at[n], saved.at[i, n], sent.at[n])

    def add(n, _):
        e = found[n]
        for h in range(HALF_KV):
            dk, dv = acc[e, 0, h], acc[e, 1, h]
            for rows, columns in chunks():
                probs = jnp.exp2(
                    kept_scores[n, h, :, columns] * TO_LOG2 - stats[i, h, 0:1, columns]
                )
                dscores = probs * (kept_dprobs[n, h, :, columns] - stats[i, h, 2:3, columns])
                probs, dscores = probs.astype(BF16), dscores.astype(BF16)
                low[n, h, 0, :, columns] = probs
                low[n, h, 1, :, columns] = dscores
                dv += dot_nn(probs, heads_of(block, 1, h, rows))
                dk += dot_nn(dscores, heads_of(block, 0, h, rows))
            acc[e, 0, h] = dk
            acc[e, 1, h] = dv
        copy(n).start()
        return 0

    def finish(n, _):
        copy(n).wait()
        return 0

    lax.fori_loop(0, count, add, 0)
    lax.fori_loop(0, count, finish, 0)


def write_grads(acc, outs):
    start = 0
    for out in outs:
        part = slice(start, start + out.shape[0])
        out[:, 0] = (acc[part, 0] * SCALE).astype(out.dtype)
        out[:, 1] = acc[part, 1].astype(out.dtype)
        start += out.shape[0]


def current_stats(section, lists, counts, own, other, *rest):
    *pieces, stats, store = rest
    first = section == 1
    if not first:
        stats_in, *pieces = pieces
        stats[...] = stats_in[...]
    fill(store, pieces)
    for i, block in enumerate((own, other)):
        if first:
            gather_stats(store, i, block, stats, i, True)

        def step(n, _):
            gather_stats(store, lists[i, section, n], block, stats, i, False)
            return 0

        lax.fori_loop(int(first), counts[i, section], step, 0)


def previous_grads(n_pieces, lists, counts, own, other, stats_in, *rest):
    n_ends = 2 * n_pieces - 1
    pieces, outs = rest[:n_pieces], rest[n_pieces:n_ends]
    saved, stats, store, acc, low, sent, kept_scores, kept_dprobs = rest[n_ends:]
    fill(store, pieces)
    acc[...] = jnp.zeros_like(acc)
    stats[...] = stats_in[...]
    for i, block in enumerate((own, other)):
        count = counts[i, 0]

        def look(n, _):
            gather_stats(
                store, lists[i, 0, n], block, stats, i, False, (n, kept_scores, kept_dprobs)
            )
            return 0

        lax.fori_loop(0, count, look, 0)
        for h in range(HALF_KV):
            total = stats[i, h, 1:2, :]
            stats[i, h, 0:1, :] = stats[i, h, 0:1, :] * TO_LOG2 + jnp.log2(total)
            stats[i, h, 2:3, :] = stats[i, h, 2:3, :] / total

        def copy(n):
            return pltpu.make_async_copy(low.at[n], saved.at[i, n], sent.at[n])

        def add(n, _):
            e = lists[i, 0, n]
            for h in range(HALF_KV):
                dk, dv = acc[e, 0, h], acc[e, 1, h]
                for rows, columns in chunks():
                    probs = jnp.exp2(
                        kept_scores[n, h, :, columns] * TO_LOG2 - stats[i, h, 0:1, columns]
                    )
                    dscores = probs * (kept_dprobs[n, h, :, columns] - stats[i, h, 2:3, columns])
                    probs, dscores = probs.astype(BF16), dscores.astype(BF16)
                    low[n, h, 0, :, columns] = probs
                    low[n, h, 1, :, columns] = dscores
                    dv += dot_nn(probs, heads_of(block, 1, h, rows))
                    dk += dot_nn(dscores, heads_of(block, 0, h, rows))
                acc[e, 0, h] = dk
                acc[e, 1, h] = dv
            copy(n).start()
            return 0

        def finish(n, _):
            copy(n).wait()
            return 0

        lax.fori_loop(0, count, add, 0)
        lax.fori_loop(0, count, finish, 0)
    write_grads(acc, outs)


def current_grads(section, n_pieces, lists, counts, own, other, stats, *rest):
    pieces, outs = rest[:n_pieces], rest[n_pieces : 2 * n_pieces]
    saved, store, acc, low, sent = rest[2 * n_pieces :]
    first = section == 1
    fill(store, pieces)
    acc[...] = jnp.zeros_like(acc)
    for i, block in enumerate((own, other)):
        count = counts[i, section]

        def copy(n):
            return pltpu.make_async_copy(low.at[n], saved.at[i, n], sent.at[n])

        def look(n, diagonal):
            e = lists[i, section, n]
            for h in range(HALF_KV):
                for rows, columns in chunks():
                    scores, dprobs = pair_scores(store, e, h, block, rows, diagonal)
                    probs = jnp.exp2(scores * TO_LOG2 - stats[i, h, 0:1, columns])
                    low[n, h, 0, :, columns] = probs.astype(BF16)
                    dscores = probs * (dprobs - stats[i, h, 2:3, columns])
                    low[n, h, 1, :, columns] = dscores.astype(BF16)
            copy(n).start()
            return 0

        def add(n, _):
            e = lists[i, section, n]
            for h in range(HALF_KV):
                for w in range(2):
                    right = block[1 - w, h].reshape(ROWS, HEAD_DIM)
                    acc[e, 1 - w, h] += dot_nn(low[n, h, w], right)
            return 0

        def finish(n, _):
            copy(n).wait()
            return 0

        if first:
            look(0, True)
        lax.fori_loop(int(first), count, lambda n, _: look(n, False), 0)
        lax.fori_loop(0, count, add, 0)
        lax.fori_loop(0, count, finish, 0)
    write_grads(acc, outs)


def query_results(n_seq, lists, counts, place_ref, *rest):
    n_saved = 3
    n_pieces = n_seq // CORES
    saved, pieces, rest = rest[:n_saved], rest[n_saved:][: 2 * n_pieces], rest[n_saved + 2 * n_pieces :]
    table, *rest = rest
    outs, (store, low, out_acc, dq_acc, got) = rest[: 2 * HALF_KV], rest[2 * HALF_KV :]
    group, member, _ = here(n_seq)

    def copy(source, h, i, n, first):
        return pltpu.make_async_copy(source.at[i, n - first, h], low.at[h, i, n], got.at[h, i, n])

    ends = []
    for i in range(2):
        stops = [0]
        for section in range(n_saved):
            stops.append(stops[-1] + counts[i, section])
        ends.append(stops)
    for h in range(HALF_KV):
        for i, stops in enumerate(ends):
            for source, first, stop in zip(saved, stops, stops[1:]):

                def fetch_one(n, _):
                    copy(source, h, i, n, first).start()
                    return 0

                lax.fori_loop(first, stop, fetch_one, 0)
    fill(store, pieces)
    tables = []
    for i in range(2):
        mine = group * n_seq + lax.bitwise_xor(member, i)
        cosine, sine = block_tables(place_ref[mine], table)
        tables.append((cosine.T * SCALE, sine.T * SCALE))
    for h, (i, stops) in ((h, pair) for h in range(HALF_KV) for pair in enumerate(ends)):
        total = stops[-1]
        result = outs[i * HALF_KV + h]

        @pl.when(lax.rem(total, 2) == 1)
        def _():
            low[h, i, total] = jnp.zeros((2, BLK, ROWS), BF16)

        out_acc[...] = jnp.zeros_like(out_acc)
        dq_acc[...] = jnp.zeros_like(dq_acc)

        def add(n, _):
            pair = (2 * n, 2 * n + 1)
            for m in pair:
                for source, first, stop in zip(saved, stops, stops[1:]):

                    @pl.when(jnp.logical_and(m >= first, m < stop))
                    def _():
                        copy(source, h, i, m, first).wait()

            found = [lists[i, 3, m] for m in pair]
            keys_t = jnp.concatenate([store[e, 0, h].T for e in found], axis=1)
            values_t = jnp.concatenate([store[e, 1, h].T for e in found], axis=1)
            for _, columns in chunks():
                probs = jnp.concatenate([low[h, i, m, 0, :, columns] for m in pair], axis=0)
                dscores = jnp.concatenate([low[h, i, m, 1, :, columns] for m in pair], axis=0)
                out_acc[:, columns] += dot_nn(values_t, probs)
                dq_acc[:, columns] += dot_nn(keys_t, dscores)
            return 0

        lax.fori_loop(0, lax.div(total + 1, 2), add, 0)
        cosine, sine = tables[i]
        for r in range(RATIO):
            rows = slice(r * BLK, (r + 1) * BLK)
            columns = slice(r * HEAD_DIM, (r + 1) * HEAD_DIM)
            result[0, :, columns] = out_acc[:, rows].astype(BF16).T
            dq = dq_acc[:, rows]
            half = HEAD_DIM // 2
            turned = jnp.concatenate([dq[half:], dq[:half]], axis=0)
            result[1, :, columns] = (dq * cosine - turned * sine).astype(BF16).T


def finish_kv(n_seq, place_ref, *rest):
    *terms, table, keep, send = rest
    group, member, _ = here(n_seq)
    for i, result in enumerate((keep, send)):
        offset = lax.bitwise_xor(member, i)
        cosine, sine = block_tables(place_ref[group * n_seq + offset], table)
        for h in range(HALF_KV):
            columns = slice(h * HEAD_DIM, (h + 1) * HEAD_DIM)
            dk, dv = (sum(term[i, w, h].astype(F32) for term in terms) for w in range(2))
            result[0, :, columns] = turn(dk, cosine, -sine).astype(BF16)
            result[1, :, columns] = dv.astype(BF16)


def join_halves(*refs):
    core = lax.rem(lax.axis_index("seq"), CORES)
    own_q, got_q, (own_kv, got_kv) = refs[:HALF_KV], refs[HALF_KV:][:HALF_KV], refs[2 * HALF_KV :][:2]
    outs = refs[2 * HALF_KV + 2 :]
    for own, got, results in ((own_q, got_q, outs[:2]), ([own_kv], [got_kv], outs[2:])):
        width = own[0].shape[-1]
        for half, parts in ((core, own), (1 - core, got)):
            for n, part in enumerate(parts):
                start = pl.multiple_of((half * len(parts) + n) * width, width)
                for w, out in enumerate(results):
                    out[:, pl.ds(start, width)] = part[w]


def local(query_input, key_input, value_input, out_grad, key_blocks, key_counts, block_position):
    n_seq = lax.axis_size("seq")
    n_grp = lax.axis_size("grp")
    n_pieces = n_seq // CORES
    n_listed = key_blocks.shape[1]

    def cross(array, by):
        return lax.ppermute(array, "seq", [(m, m ^ by) for m in range(n_seq)])

    def along(array, by):
        return cross(array, CORES * by)

    def onward(array):
        return lax.ppermute(array, "grp", [(g, g + 1) for g in range(n_grp - 1)])

    def back(array):
        return lax.ppermute(array, "grp", [(g + 1, g) for g in range(n_grp - 1)])

    table = trig_table(block_position.shape[0])
    n_far = min(n_seq, n_listed - 1)
    split = 2 * CORES
    piece = (2, HALF_KV, BLK, HEAD_DIM)
    chip = (CORES, *piece)
    q_shape = jax.ShapeDtypeStruct((2, HALF_KV, RATIO, BLK, HEAD_DIM), BF16)
    kv_shape = jax.ShapeDtypeStruct(piece, BF16)
    stats_shape = jax.ShapeDtypeStruct((2, HALF_KV, 8, ROWS), F32)
    low = jax.ShapeDtypeStruct(chip, BF16)
    high = jax.ShapeDtypeStruct(chip, F32)
    lists, counts = call(
        functools.partial(make_lists, n_seq, split),
        (
            jax.ShapeDtypeStruct((2, 4, n_listed + 1), jnp.int32),
            jax.ShapeDtypeStruct((2, 4), jnp.int32),
        ),
        2, us=2, name="block_lists",
    )(key_blocks, key_counts)

    def prepared(kernel, shape, first, second, name):
        held = [pltpu.VMEM(a.shape, a.dtype) for a in (first, second, table)]
        return call(
            functools.partial(kernel, n_seq), (shape, shape), 1,
            [*held, pltpu.SemaphoreType.DMA((3,))], us=1, name=name, n_hbm=3, pin=True,
        )(block_position, first, second, table)

    kv_keep, kv_send = prepared(prepare_kv, kv_shape, key_input, value_input, "rotate_keys")
    kv_got = cross(kv_send, 1)
    query_late, kv_keep = lax.optimization_barrier((query_input, kv_keep))
    q_keep, q_send = prepared(prepare_queries, q_shape, query_late, out_grad, "rotate_queries")
    q_send, q_keep, kv_got, kv_keep = lax.optimization_barrier((q_send, q_keep, kv_got, kv_keep))
    q_got = cross(q_send, 1)
    near = [jnp.stack([kv_keep, kv_got])]
    near.append(along(near[0], 1))
    ready, first_far = lax.optimization_barrier((near[1], onward(near[0])))
    far = [first_far, None]
    for k in range(2, n_pieces, 2):
        piece_k, _ = lax.optimization_barrier((along(near[0], k), ready))
        near += [piece_k, along(piece_k, 1)]
        far += [onward(piece_k), None]
    stats = call(
        functools.partial(current_stats, 1), stats_shape, 2, [pltpu.VMEM((split, *piece), BF16)],
        us=4, name="near_statistics",
    )(lists, counts, q_keep, q_got, *near[:2])
    ready, far[2], stats = lax.optimization_barrier((ready, far[2], stats))
    far[1] = onward(ready)
    for k in range(2, n_pieces, 2):
        far[k + 1] = along(far[k], 1)
    stats = call(
        functools.partial(current_stats, 2), stats_shape, 2,
        [pltpu.VMEM((n_seq - split, *piece), BF16)], us=4, name="far_statistics",
    )(lists, counts, q_keep, q_got, stats, *near[2:])

    def grads_call(kernel, n_slots, n_store, outs, us, name, kept=(), more=()):
        pair = (n_slots, HALF_KV, 2, BLK, ROWS)
        saved = jax.ShapeDtypeStruct((2, *pair), BF16)
        return call(
            kernel, (*outs, saved, *more), 2,
            [
                pltpu.VMEM((n_store, *piece), BF16), pltpu.VMEM((n_store, *piece), F32),
                pltpu.VMEM(pair, BF16), pltpu.SemaphoreType.DMA((n_slots,)), *kept,
            ],
            us=us, name=name, hbm_out=len(outs),
        )

    kept = pltpu.VMEM((n_far, HALF_KV, BLK, ROWS), F32)
    two = jax.ShapeDtypeStruct((2 * CORES, *piece), BF16)
    first_far, *far_grads, far_saved, stats = grads_call(
        functools.partial(previous_grads, n_pieces), n_far, n_seq, (two,) + (low,) * (n_pieces - 2),
        14, "previous_gradients", (kept, kept), (stats_shape,),
    )(lists, counts, q_keep, q_got, stats, *far)

    def current_call(section, outs, name, pieces, after):
        stats_late, _ = lax.optimization_barrier((stats, after))
        n_store = CORES * len(pieces)
        *grads, saved = grads_call(
            functools.partial(current_grads, section, len(pieces)), min(n_store, n_listed), n_store,
            outs, 6, name,
        )(lists, counts, q_keep, q_got, stats_late, *pieces)
        return grads, saved

    def total(*terms):
        return sum(term.astype(F32) for term in terms).astype(BF16)

    from_far = back(first_far)
    crossing = [along(grad, 1) for grad in far_grads[1::2]]
    high_grads, high_saved = current_call(
        2, [high, low] * (n_pieces // 2 - 1), "far_current_gradients", near[2:], far_grads[0]
    )
    crossing, high_grads = lax.optimization_barrier((crossing, high_grads))
    arrived = [
        back(total(grad, extra)) for grad, extra in zip(far_grads[0::2], crossing)
    ]
    swapped = [along(grad, 1) for grad in high_grads[1::2]]
    low_grads, low_saved = current_call(
        1, [high, high], "near_current_gradients", near[:2], high_grads[0]
    )
    low_grads, from_far = lax.optimization_barrier((low_grads, from_far))
    from_next = along(total(low_grads[1], from_far[CORES:]), 1)
    merged = [
        total(*terms) for terms in zip(high_grads[0::2], arrived, swapped)
    ]
    half_out = jax.ShapeDtypeStruct((2, BLK, RATIO * HEAD_DIM), BF16)
    place_late, _ = lax.optimization_barrier((block_position, merged))
    wide = pltpu.VMEM((HEAD_DIM, ROWS), F32)
    slots = (HALF_KV, 2, n_listed + 1)
    halves = call(
        functools.partial(query_results, n_seq), (half_out,) * (2 * HALF_KV), 3,
        [
            pltpu.VMEM((2 * n_seq, *piece), BF16), pltpu.VMEM((*slots, 2, BLK, ROWS), BF16),
            wide, wide, pltpu.SemaphoreType.DMA(slots),
        ],
        us=20, name="query_results", n_hbm=3,
    )(lists, counts, place_late, far_saved, low_saved, high_saved, *far, *near, table)
    own_halves, other_halves = halves[:HALF_KV], halves[HALF_KV:]
    other_halves = lax.optimization_barrier(list(other_halves))
    got_halves = [cross(half, 1) for half in other_halves]
    final = [low_grads[0], from_far[:CORES], from_next]
    final += [along(part, 2 + 2 * n) for n, part in enumerate(merged)]
    own_halves = list(own_halves)
    final[0], own_halves[1] = lax.optimization_barrier((final[0], own_halves[1]))
    kv_half = jax.ShapeDtypeStruct((2, BLK, HALF_KV * HEAD_DIM), BF16)
    own_kv, other_kv = call(
        functools.partial(finish_kv, n_seq), (kv_half, kv_half), 1, us=2, name="key_gradients"
    )(block_position, *final, table)
    got_kv = cross(other_kv, 1)
    q_out = jax.ShapeDtypeStruct(query_input.shape, BF16)
    kv_out = jax.ShapeDtypeStruct(key_input.shape, BF16)
    out_rows, query_grad, key_grad, value_grad = call(
        join_halves, (q_out, q_out, kv_out, kv_out), 0, us=2, name="join_halves"
    )(*own_halves, *got_halves, own_kv, got_kv)
    return (out_rows, query_grad, key_grad, value_grad)


def solution(mesh):
    split = P(("grp", "seq"), None)
    return jax.shard_map(
        local,
        mesh=mesh,
        in_specs=(split, split, split, split, P(), P(), P()),
        out_specs=(split, split, split, split),
        check_vma=False,
    )
```

```python
import functools
import math

import jax
import jax.numpy as jnp
import numpy as np
from jax import lax
from jax.experimental import pallas as pl
from jax.experimental.pallas import tpu as pltpu
from jax.sharding import PartitionSpec as P

HEADS = 32
KV_HEADS = 4
HEAD_DIM = 128
BLK = 128
CORES = 2
RATIO = HEADS // KV_HEADS
HALF_KV = KV_HEADS // CORES
ROWS = RATIO * BLK
SCALE = 1.0 / math.sqrt(HEAD_DIM)
TO_LOG2 = SCALE * math.log2(math.e)
F32 = jnp.float32
BF16 = jnp.bfloat16
CHUNK = 256

VMEM_SPEC = pl.BlockSpec(memory_space=pltpu.VMEM)
HBM_SPEC = pl.BlockSpec(memory_space=pltpu.HBM)
SMEM_SPEC = pl.BlockSpec(memory_space=pltpu.SMEM)


def trig_table(n_blocks):
    half = HEAD_DIM // 2
    frequency = np.power(500000.0, -np.arange(half) * (2.0 / HEAD_DIM))
    parts = []
    for places in (np.arange(n_blocks) * BLK, np.arange(BLK)):
        angles = places[:, None] * frequency
        for part in (np.cos(angles), np.sin(angles)):
            parts.append(np.concatenate([part, part], axis=1))
    return np.concatenate(parts, axis=0).astype(np.float32)


def block_tables(place, table):
    n_blocks = table.shape[0] // 2 - BLK
    cos_b = table[pl.ds(place, 1), :]
    sin_b = table[pl.ds(n_blocks + place, 1), :]
    cos_t = table[2 * n_blocks : 2 * n_blocks + BLK, :]
    sin_t = table[2 * n_blocks + BLK :, :]
    cosine = cos_b * cos_t - sin_b * sin_t
    sine = sin_b * cos_t + cos_b * sin_t
    lanes = lax.broadcasted_iota(jnp.int32, sine.shape, 1)
    return cosine, jnp.where(lanes < HEAD_DIM // 2, -sine, sine)


def turn(values, cosine, signed_sine):
    return values * cosine + pltpu.roll(values, HEAD_DIM // 2, 1) * signed_sine


def dot_nt(a, b):
    return lax.dot_general(a, b, (((1,), (1,)), ((), ())), preferred_element_type=F32)


def dot_nn(a, b):
    return lax.dot_general(a, b, (((1,), (0,)), ((), ())), preferred_element_type=F32)


def here(n_seq):
    member = lax.axis_index("seq")
    group = lax.axis_index("grp")
    return group, member, lax.rem(member, CORES)


def size_of(array):
    return math.prod(array.shape) * jnp.dtype(array.dtype).itemsize


def call(kernel, out_shape, n_smem, scratch=(), us=1, name=None, n_hbm=0, hbm_out=None, away=None):
    def placed(n, a):
        return pltpu.HBM(a.shape, a.dtype) if n in (hbm_out, away) else a

    def spec(n, a):
        if a.dtype == jnp.int32:
            return SMEM_SPEC
        return HBM_SPEC if n == hbm_out else VMEM_SPEC

    def run(*arrays):
        n_left = n_smem + n_hbm
        outs = list(out_shape) if isinstance(out_shape, (tuple, list)) else [out_shape]
        held = sum(size_of(a) for a in arrays[n_left:])
        held += sum(size_of(a) for n, a in enumerate(outs) if n != hbm_out)
        held += sum(size_of(a) for a in scratch if a.dtype in (F32, BF16))
        in_specs = [SMEM_SPEC] * n_smem + [HBM_SPEC] * n_hbm
        in_specs += [VMEM_SPEC] * (len(arrays) - n_left)
        pinned = [
            pltpu.with_memory_space_constraint(a, pltpu.HBM) if n < n_left else a
            for n, a in enumerate(arrays)
        ]
        results = pl.pallas_call(
            kernel,
            out_shape=[placed(n, a) for n, a in enumerate(outs)],
            in_specs=in_specs,
            out_specs=[spec(n, a) for n, a in enumerate(outs)],
            scratch_shapes=list(scratch),
            compiler_params=pltpu.CompilerParams(vmem_limit_bytes=held + 6 * 2**20),
            cost_estimate=pl.CostEstimate(
                flops=us * 10**9, bytes_accessed=2**20, transcendentals=0
            ),
            name=name,
        )(*pinned)
        return results if isinstance(out_shape, (tuple, list)) else results[0]

    return run


def fetch(sources, places, sems):
    copies = [
        pltpu.make_async_copy(source, place, sems.at[n])
        for n, (source, place) in enumerate(zip(sources, places))
    ]
    for copy in copies:
        copy.start()
    for copy in copies:
        copy.wait()


def prepare_kv(n_seq, place_ref, *refs):
    sources, (keep, send), (key, value, table, sems) = refs[:3], refs[3:5], refs[5:]
    fetch(sources, (key, value, table), sems)
    group, member, core = here(n_seq)
    cosine, sine = block_tables(place_ref[group * n_seq + member], table)
    for out, half in ((keep, core), (send, 1 - core)):
        for h in range(HALF_KV):
            columns = pl.ds(pl.multiple_of((half * HALF_KV + h) * HEAD_DIM, HEAD_DIM), HEAD_DIM)
            out[0, h] = turn(key[:, columns].astype(F32), cosine, sine).astype(BF16)
            out[1, h] = value[:, columns]


def prepare_queries(n_seq, place_ref, *refs):
    sources, (keep, send), (query, grad, table, sems) = refs[:3], refs[3:5], refs[5:]
    fetch(sources, (query, grad, table), sems)
    group, member, core = here(n_seq)
    cosine, sine = block_tables(place_ref[group * n_seq + member], table)
    for out, half in ((keep, core), (send, 1 - core)):
        for h in range(HALF_KV):
            for r in range(RATIO):
                head = (half * HALF_KV + h) * RATIO + r
                columns = pl.ds(pl.multiple_of(head * HEAD_DIM, HEAD_DIM), HEAD_DIM)
                out[0, h, r] = turn(query[:, columns].astype(F32), cosine, sine).astype(BF16)
                out[1, h, r] = grad[:, columns]


FAR_HIGH, FAR_LOW, NEAR_HIGH, NEAR_LOW, ALL = range(5)


def make_lists(n_seq, split, key_blocks, key_counts, lists, counts):
    group, member, _ = here(n_seq)
    bases = (split, 0, n_seq + split, n_seq)
    for i in range(2):
        block = group * n_seq + lax.bitwise_xor(member, i)
        for section in range(4):
            counts[i, section] = int(section == NEAR_LOW)
        lists[i, NEAR_LOW, 0] = i

        def look(j, _):
            place = lax.bitwise_xor(key_blocks[block, j] - (group - 1) * n_seq, member)
            near = (place >= n_seq).astype(jnp.int32)
            inner = place - n_seq * near
            low = (inner < split).astype(jnp.int32)
            section = 2 * near + low
            n = counts[i, section]
            lists[i, section, n] = inner - split * (1 - low)
            counts[i, section] = n + 1
            return 0

        lax.fori_loop(1, key_counts[block], look, 0)
        total = jnp.int32(0)
        for section, base in enumerate(bases):

            def append(n, m):
                lists[i, ALL, m] = lists[i, section, n] + base
                return m + 1

            total = lax.fori_loop(0, counts[i, section], append, total)
        counts[i, ALL] = total
        lists[i, ALL, total] = 0


def causal():
    keys = lax.broadcasted_iota(jnp.int32, (BLK, CHUNK), 0)
    tokens = lax.rem(lax.broadcasted_iota(jnp.int32, (BLK, CHUNK), 1), BLK)
    return keys <= tokens


def chunks():
    per = CHUNK // BLK
    return [
        (slice(c * per, (c + 1) * per), slice(c * CHUNK, (c + 1) * CHUNK))
        for c in range(ROWS // CHUNK)
    ]


def heads_of(block, what, h, rows):
    return block[what, h, rows].reshape(CHUNK, HEAD_DIM)


def fill(store, pieces, first=0):
    for k, piece in enumerate(pieces):
        store[first + CORES * k : first + CORES * (k + 1)] = piece[...]


def pair_scores(store, e, h, block, rows, diagonal):
    scores = dot_nt(store[e, 0, h], heads_of(block, 0, h, rows))
    if diagonal:
        scores = jnp.where(causal(), scores, -1e30)
    return scores, dot_nt(store[e, 1, h], heads_of(block, 1, h, rows))


def gather_stats(store, e, block, stats, i, diagonal, kept=None):
    for h in range(HALF_KV):
        for rows, columns in chunks():
            scores, dprobs = pair_scores(store, e, h, block, rows, diagonal)
            if kept is not None:
                n, kept_scores, kept_dprobs = kept
                kept_scores[n, h, :, columns] = scores
                kept_dprobs[n, h, :, columns] = dprobs
            top = jnp.max(scores, axis=0, keepdims=True)
            if not diagonal:
                old_top = stats[i, h, 0:1, columns]
                top = jnp.maximum(top, old_top)
            weights = jnp.exp2((scores - top) * TO_LOG2)
            total = jnp.sum(weights, axis=0, keepdims=True)
            mixed = jnp.sum(weights * dprobs, axis=0, keepdims=True)
            if not diagonal:
                shrink = jnp.exp2((old_top - top) * TO_LOG2)
                total += stats[i, h, 1:2, columns] * shrink
                mixed += stats[i, h, 2:3, columns] * shrink
            stats[i, h, 0:1, columns] = top
            stats[i, h, 1:2, columns] = total
            stats[i, h, 2:3, columns] = mixed


def spread_grads(found, count, kept_scores, kept_dprobs, stats, i, block, acc, saved, low, sent):
    def copy(n):
        return pltpu.make_async_copy(low.at[n], saved.at[i, n], sent.at[n])

    def add(n, _):
        e = found[n]
        for h in range(HALF_KV):
            dk, dv = acc[e, 0, h], acc[e, 1, h]
            for rows, columns in chunks():
                probs = jnp.exp2(
                    kept_scores[n, h, :, columns] * TO_LOG2 - stats[i, h, 0:1, columns]
                )
                dscores = probs * (kept_dprobs[n, h, :, columns] - stats[i, h, 2:3, columns])
                probs, dscores = probs.astype(BF16), dscores.astype(BF16)
                low[n, h, 0, :, columns] = probs
                low[n, h, 1, :, columns] = dscores
                dv += dot_nn(probs, heads_of(block, 1, h, rows))
                dk += dot_nn(dscores, heads_of(block, 0, h, rows))
            acc[e, 0, h] = dk
            acc[e, 1, h] = dv
        copy(n).start()
        return 0

    def finish(n, _):
        copy(n).wait()
        return 0

    lax.fori_loop(0, count, add, 0)
    lax.fori_loop(0, count, finish, 0)


def write_grads(acc, outs):
    start = 0
    for out in outs:
        part = slice(start, start + out.shape[0])
        out[:, 0] = (acc[part, 0] * SCALE).astype(out.dtype)
        out[:, 1] = acc[part, 1].astype(out.dtype)
        start += out.shape[0]


def current_stats(section, lists, counts, own, other, *rest):
    *pieces, stats, store = rest
    first = section == NEAR_LOW
    if not first:
        stats_in, *pieces = pieces
        stats[...] = stats_in[...]
    fill(store, pieces)
    for i, block in enumerate((own, other)):
        if first:
            gather_stats(store, i, block, stats, i, True)

        def step(n, _):
            gather_stats(store, lists[i, section, n], block, stats, i, False)
            return 0

        lax.fori_loop(int(first), counts[i, section], step, 0)


def previous_grads(n_pieces, lists, counts, own, other, stats_in, *rest):
    n_ends = 2 * n_pieces - 2
    pieces, outs = rest[:n_pieces], rest[n_pieces:n_ends]
    saved, stats, store, acc, low, sent, kept_scores, kept_dprobs, low_store = rest[n_ends:]
    fill(low_store, pieces[:2])
    fill(store, pieces[2:])
    acc[...] = jnp.zeros_like(acc)
    stats[...] = stats_in[...]
    for i, block in enumerate((own, other)):
        count = counts[i, FAR_HIGH]

        def look_low(n, _):
            gather_stats(low_store, lists[i, FAR_LOW, n], block, stats, i, False)
            return 0

        def look(n, _):
            e = lists[i, FAR_HIGH, n]
            gather_stats(store, e, block, stats, i, False, (n, kept_scores, kept_dprobs))
            return 0

        lax.fori_loop(0, counts[i, FAR_LOW], look_low, 0)
        lax.fori_loop(0, count, look, 0)
        for h in range(HALF_KV):
            total = stats[i, h, 1:2, :]
            stats[i, h, 0:1, :] = stats[i, h, 0:1, :] * TO_LOG2 + jnp.log2(total)
            stats[i, h, 2:3, :] = stats[i, h, 2:3, :] / total

        def copy(n):
            return pltpu.make_async_copy(low.at[n], saved.at[i, n], sent.at[n])

        def add(n, _):
            e = lists[i, FAR_HIGH, n]
            for h in range(HALF_KV):
                dk, dv = acc[e, 0, h], acc[e, 1, h]
                for rows, columns in chunks():
                    probs = jnp.exp2(
                        kept_scores[n, h, :, columns] * TO_LOG2 - stats[i, h, 0:1, columns]
                    )
                    dscores = probs * (kept_dprobs[n, h, :, columns] - stats[i, h, 2:3, columns])
                    probs, dscores = probs.astype(BF16), dscores.astype(BF16)
                    low[n, h, 0, :, columns] = probs
                    low[n, h, 1, :, columns] = dscores
                    dv += dot_nn(probs, heads_of(block, 1, h, rows))
                    dk += dot_nn(dscores, heads_of(block, 0, h, rows))
                acc[e, 0, h] = dk
                acc[e, 1, h] = dv
            copy(n).start()
            return 0

        def finish(n, _):
            copy(n).wait()
            return 0

        lax.fori_loop(0, count, add, 0)
        lax.fori_loop(0, count, finish, 0)
    write_grads(acc, outs)


def section_grads(section, n_pieces, lists, counts, own, other, stats, *rest):
    pieces, (*outs, saved, store, acc, low, sent) = rest[:n_pieces], rest[n_pieces:]
    first = section == NEAR_LOW
    fill(store, pieces)
    acc[...] = jnp.zeros_like(acc)
    for i, block in enumerate((own, other)):
        count = counts[i, section]

        def copy(n):
            return pltpu.make_async_copy(low.at[n], saved.at[i, n], sent.at[n])

        def look(n, diagonal):
            e = lists[i, section, n]
            for h in range(HALF_KV):
                for rows, columns in chunks():
                    scores, dprobs = pair_scores(store, e, h, block, rows, diagonal)
                    probs = jnp.exp2(scores * TO_LOG2 - stats[i, h, 0:1, columns])
                    low[n, h, 0, :, columns] = probs.astype(BF16)
                    dscores = probs * (dprobs - stats[i, h, 2:3, columns])
                    low[n, h, 1, :, columns] = dscores.astype(BF16)
            copy(n).start()
            return 0

        def add(n, _):
            e = lists[i, section, n]
            for h in range(HALF_KV):
                for w in range(2):
                    right = block[1 - w, h].reshape(ROWS, HEAD_DIM)
                    acc[e, 1 - w, h] += dot_nn(low[n, h, w], right)
            return 0

        def finish(n, _):
            copy(n).wait()
            return 0

        if first:
            look(0, True)
        lax.fori_loop(int(first), count, lambda n, _: look(n, False), 0)
        lax.fori_loop(0, count, add, 0)
        lax.fori_loop(0, count, finish, 0)
    write_grads(acc, outs)


def query_results(n_seq, lists, counts, place_ref, *rest):
    n_saved = 4
    n_pieces = n_seq // CORES
    saved, pieces, rest = rest[:n_saved], rest[n_saved:][: 2 * n_pieces], rest[n_saved + 2 * n_pieces :]
    table, *rest = rest
    outs, (store, low, out_acc, dq_acc, got) = rest[: 2 * HALF_KV], rest[2 * HALF_KV :]
    group, member, _ = here(n_seq)

    def copy(source, h, i, n, first):
        return pltpu.make_async_copy(source.at[i, n - first, h], low.at[h, i, n], got.at[h, i, n])

    ends = []
    for i in range(2):
        stops = [0]
        for section in range(n_saved):
            stops.append(stops[-1] + counts[i, section])
        ends.append(stops)
    for h in range(HALF_KV):
        for i, stops in enumerate(ends):
            for source, first, stop in zip(saved, stops, stops[1:]):

                def fetch_one(n, _):
                    copy(source, h, i, n, first).start()
                    return 0

                lax.fori_loop(first, stop, fetch_one, 0)
    fill(store, pieces)
    tables = []
    for i in range(2):
        mine = group * n_seq + lax.bitwise_xor(member, i)
        cosine, sine = block_tables(place_ref[mine], table)
        tables.append((cosine.T * SCALE, sine.T * SCALE))
    for h, (i, stops) in ((h, pair) for h in range(HALF_KV) for pair in enumerate(ends)):
        total = stops[-1]
        result = outs[i * HALF_KV + h]

        @pl.when(lax.rem(total, 2) == 1)
        def _():
            low[h, i, total] = jnp.zeros((2, BLK, ROWS), BF16)

        out_acc[...] = jnp.zeros_like(out_acc)
        dq_acc[...] = jnp.zeros_like(dq_acc)

        def add(n, _):
            pair = (2 * n, 2 * n + 1)
            for m in pair:
                for source, first, stop in zip(saved, stops, stops[1:]):

                    @pl.when(jnp.logical_and(m >= first, m < stop))
                    def _():
                        copy(source, h, i, m, first).wait()

            found = [lists[i, ALL, m] for m in pair]
            keys_t = jnp.concatenate([store[e, 0, h].T for e in found], axis=1)
            values_t = jnp.concatenate([store[e, 1, h].T for e in found], axis=1)
            for _, columns in chunks():
                probs = jnp.concatenate([low[h, i, m, 0, :, columns] for m in pair], axis=0)
                dscores = jnp.concatenate([low[h, i, m, 1, :, columns] for m in pair], axis=0)
                out_acc[:, columns] += dot_nn(values_t, probs)
                dq_acc[:, columns] += dot_nn(keys_t, dscores)
            return 0

        lax.fori_loop(0, lax.div(total + 1, 2), add, 0)
        cosine, sine = tables[i]
        for r in range(RATIO):
            rows = slice(r * BLK, (r + 1) * BLK)
            columns = slice(r * HEAD_DIM, (r + 1) * HEAD_DIM)
            result[0, :, columns] = out_acc[:, rows].astype(BF16).T
            dq = dq_acc[:, rows]
            half = HEAD_DIM // 2
            turned = jnp.concatenate([dq[half:], dq[:half]], axis=0)
            result[1, :, columns] = (dq * cosine - turned * sine).astype(BF16).T


def finish_kv(n_seq, place_ref, *rest):
    *terms, table, keep, send = rest
    group, member, _ = here(n_seq)
    for i, result in enumerate((keep, send)):
        offset = lax.bitwise_xor(member, i)
        cosine, sine = block_tables(place_ref[group * n_seq + offset], table)
        for h in range(HALF_KV):
            columns = slice(h * HEAD_DIM, (h + 1) * HEAD_DIM)
            dk, dv = (sum(term[i, w, h].astype(F32) for term in terms) for w in range(2))
            result[0, :, columns] = turn(dk, cosine, -sine).astype(BF16)
            result[1, :, columns] = dv.astype(BF16)


def join_halves(*refs):
    core = lax.rem(lax.axis_index("seq"), CORES)
    own_q, got_q, (own_kv, got_kv) = refs[:HALF_KV], refs[HALF_KV:][:HALF_KV], refs[2 * HALF_KV :][:2]
    outs = refs[2 * HALF_KV + 2 :]
    for own, got, results in ((own_q, got_q, outs[:2]), ([own_kv], [got_kv], outs[2:])):
        width = own[0].shape[-1]
        for half, parts in ((core, own), (1 - core, got)):
            for n, part in enumerate(parts):
                start = pl.multiple_of((half * len(parts) + n) * width, width)
                for w, out in enumerate(results):
                    out[:, pl.ds(start, width)] = part[w]


def local(query_input, key_input, value_input, out_grad, key_blocks, key_counts, block_position):
    n_seq = lax.axis_size("seq")
    n_grp = lax.axis_size("grp")
    n_pieces = n_seq // CORES
    n_listed = key_blocks.shape[1]

    def cross(array, by):
        return lax.ppermute(array, "seq", [(m, m ^ by) for m in range(n_seq)])

    def along(array, by):
        return cross(array, CORES * by)

    def onward(array):
        return lax.ppermute(array, "grp", [(g, g + 1) for g in range(n_grp - 1)])

    def back(array):
        return lax.ppermute(array, "grp", [(g + 1, g) for g in range(n_grp - 1)])

    table = trig_table(block_position.shape[0])
    n_far = min(n_seq, n_listed - 1)
    split = 2 * CORES
    piece = (2, HALF_KV, BLK, HEAD_DIM)
    chip = (CORES, *piece)
    q_shape = jax.ShapeDtypeStruct((2, HALF_KV, RATIO, BLK, HEAD_DIM), BF16)
    kv_shape = jax.ShapeDtypeStruct(piece, BF16)
    stats_shape = jax.ShapeDtypeStruct((2, HALF_KV, 8, ROWS), F32)
    low = jax.ShapeDtypeStruct(chip, BF16)
    high = jax.ShapeDtypeStruct(chip, F32)
    lists, counts = call(
        functools.partial(make_lists, n_seq, split),
        (
            jax.ShapeDtypeStruct((2, 5, n_listed + 1), jnp.int32),
            jax.ShapeDtypeStruct((2, 5), jnp.int32),
        ),
        2, us=2, name="block_lists",
    )(key_blocks, key_counts)

    def prepared(kernel, shape, first, second, name, away=None):
        held = [pltpu.VMEM(a.shape, a.dtype) for a in (first, second, table)]
        return call(
            functools.partial(kernel, n_seq), (shape, shape), 1,
            [*held, pltpu.SemaphoreType.DMA((3,))], us=1, name=name, n_hbm=3, away=away,
        )(block_position, first, second, table)

    kv_keep, kv_send = prepared(prepare_kv, kv_shape, key_input, value_input, "rotate_keys")
    kv_got = cross(kv_send, 1)
    query_late, kv_keep = lax.optimization_barrier((query_input, kv_keep))
    q_keep, q_send = prepared(prepare_queries, q_shape, query_late, out_grad, "rotate_queries", 0)
    q_send, q_keep, kv_got, kv_keep = lax.optimization_barrier((q_send, q_keep, kv_got, kv_keep))
    q_got = cross(q_send, 1)
    near = [jnp.stack([kv_keep, kv_got])]
    near.append(along(near[0], 1))
    ready, first_far = lax.optimization_barrier((near[1], onward(near[0])))
    far = [first_far, None]
    for k in range(2, n_pieces, 2):
        piece_k, _ = lax.optimization_barrier((along(near[0], k), ready))
        near += [piece_k, along(piece_k, 1)]
        far += [onward(piece_k), None]
    stats = call(
        functools.partial(current_stats, NEAR_LOW), stats_shape, 2, [pltpu.VMEM((split, *piece), BF16)],
        us=4, name="near_statistics",
    )(lists, counts, q_keep, q_got, *near[:2])
    ready, far[2], stats = lax.optimization_barrier((ready, far[2], stats))
    far[1] = onward(ready)
    for k in range(2, n_pieces, 2):
        far[k + 1] = along(far[k], 1)
    stats = call(
        functools.partial(current_stats, NEAR_HIGH), stats_shape, 2,
        [pltpu.VMEM((n_seq - split, *piece), BF16)], us=4, name="far_statistics",
    )(lists, counts, q_keep, q_got, stats, *near[2:])

    def grads_call(kernel, n_slots, n_store, outs, us, name, kept=(), more=()):
        pair = (n_slots, HALF_KV, 2, BLK, ROWS)
        saved = jax.ShapeDtypeStruct((2, *pair), BF16)
        return call(
            kernel, (*outs, saved, *more), 2,
            [
                pltpu.VMEM((n_store, *piece), BF16), pltpu.VMEM((n_store, *piece), F32),
                pltpu.VMEM(pair, BF16), pltpu.SemaphoreType.DMA((n_slots,)), *kept,
            ],
            us=us, name=name, hbm_out=len(outs),
        )

    n_high = n_seq - split
    kept = pltpu.VMEM((min(n_high, n_listed - 1), HALF_KV, BLK, ROWS), F32)
    *far_grads, far_high_saved, stats = grads_call(
        functools.partial(previous_grads, n_pieces), min(n_high, n_listed - 1), n_high,
        (low,) * (n_pieces - 2), 14, "previous_gradients",
        (kept, kept, pltpu.VMEM((split, *piece), BF16)), (stats_shape,),
    )(lists, counts, q_keep, q_got, stats, *far)

    def section_call(section, outs, name, pieces, after):
        stats_late, _ = lax.optimization_barrier((stats, after))
        n_store = CORES * len(pieces)
        *grads, saved = grads_call(
            functools.partial(section_grads, section, len(pieces)), min(n_store, n_listed), n_store,
            outs, 6, name,
        )(lists, counts, q_keep, q_got, stats_late, *pieces)
        return grads, saved

    def total(*terms):
        return sum(term.astype(F32) for term in terms).astype(BF16)

    crossing = [along(grad, 1) for grad in far_grads[1::2]]
    high_grads, near_high_saved = section_call(
        NEAR_HIGH, [high, low] * (n_pieces // 2 - 1), "current_high_gradients", near[2:],
        far_grads[0],
    )
    crossing, high_grads = lax.optimization_barrier((crossing, high_grads))
    arrived = [back(total(grad, extra)) for grad, extra in zip(far_grads[0::2], crossing)]
    swapped = [along(grad, 1) for grad in high_grads[1::2]]
    first_far, far_low_saved = section_call(
        FAR_LOW, [low, low], "previous_low_gradients", far[:2], high_grads[0]
    )
    arrived, swapped, first_far = lax.optimization_barrier((arrived, swapped, first_far))
    merged = [total(*terms) for terms in zip(high_grads[0::2], arrived, swapped)]
    second = back(first_far[1])
    low_grads, near_low_saved = section_call(
        NEAR_LOW, [high, high], "current_low_gradients", near[:2], merged
    )
    low_grads, second = lax.optimization_barrier((low_grads, second))
    next_part = total(low_grads[1], second)
    first, next_part = lax.optimization_barrier((first_far[0], next_part))
    half_out = jax.ShapeDtypeStruct((2, BLK, RATIO * HEAD_DIM), BF16)
    place_late, _ = lax.optimization_barrier((block_position, next_part))
    wide = pltpu.VMEM((HEAD_DIM, ROWS), F32)
    slots = (HALF_KV, 2, n_listed + 1)
    halves = call(
        functools.partial(query_results, n_seq), (half_out,) * (2 * HALF_KV), 3,
        [
            pltpu.VMEM((2 * n_seq, *piece), BF16), pltpu.VMEM((*slots, 2, BLK, ROWS), BF16),
            wide, wide, pltpu.SemaphoreType.DMA(slots),
        ],
        us=20, name="query_results", n_hbm=4,
    )(lists, counts, place_late, far_high_saved, far_low_saved, near_high_saved, near_low_saved, *far, *near, table)
    own_halves, other_halves = halves[:HALF_KV], halves[HALF_KV:]
    other_halves = lax.optimization_barrier(list(other_halves))
    got_halves = [cross(half, 1) for half in other_halves]
    final = [low_grads[0], back(first), along(next_part, 1)]
    final += [along(part, 2 + 2 * n) for n, part in enumerate(merged)]
    own_halves = list(own_halves)
    final[0], own_halves[1] = lax.optimization_barrier((final[0], own_halves[1]))
    kv_half = jax.ShapeDtypeStruct((2, BLK, HALF_KV * HEAD_DIM), BF16)
    own_kv, other_kv = call(
        functools.partial(finish_kv, n_seq), (kv_half, kv_half), 1, us=2, name="key_gradients"
    )(block_position, *final, table)
    got_kv = cross(other_kv, 1)
    q_out = jax.ShapeDtypeStruct(query_input.shape, BF16)
    kv_out = jax.ShapeDtypeStruct(key_input.shape, BF16)
    out_rows, query_grad, key_grad, value_grad = call(
        join_halves, (q_out, q_out, kv_out, kv_out), 0, us=2, name="join_halves"
    )(*own_halves, *got_halves, own_kv, got_kv)
    return (out_rows, query_grad, key_grad, value_grad)


def solution(mesh):
    split = P(("grp", "seq"), None)
    return jax.shard_map(
        local,
        mesh=mesh,
        in_specs=(split, split, split, split, P(), P(), P()),
        out_specs=(split, split, split, split),
        check_vma=False,
    )
```

```python
import functools
import math

import jax
import jax.numpy as jnp
import numpy as np
from jax import lax
from jax.experimental import pallas as pl
from jax.experimental.pallas import tpu as pltpu
from jax.sharding import PartitionSpec as P

HEADS = 32
KV_HEADS = 4
HEAD_DIM = 128
BLK = 128
CORES = 2
RATIO = HEADS // KV_HEADS
HALF_KV = KV_HEADS // CORES
ROWS = RATIO * BLK
SCALE = 1.0 / math.sqrt(HEAD_DIM)
TO_LOG2 = SCALE * math.log2(math.e)
F32 = jnp.float32
BF16 = jnp.bfloat16
CHUNK = 256

VMEM_SPEC = pl.BlockSpec(memory_space=pltpu.VMEM)
HBM_SPEC = pl.BlockSpec(memory_space=pltpu.HBM)
SMEM_SPEC = pl.BlockSpec(memory_space=pltpu.SMEM)


def trig_table(n_blocks):
    half = HEAD_DIM // 2
    frequency = np.power(500000.0, -np.arange(half) * (2.0 / HEAD_DIM))
    parts = []
    for places in (np.arange(n_blocks) * BLK, np.arange(BLK)):
        angles = places[:, None] * frequency
        for part in (np.cos(angles), np.sin(angles)):
            parts.append(np.concatenate([part, part], axis=1))
    return np.concatenate(parts, axis=0).astype(np.float32)


def block_tables(place, table):
    n_blocks = table.shape[0] // 2 - BLK
    cos_b = table[pl.ds(place, 1), :]
    sin_b = table[pl.ds(n_blocks + place, 1), :]
    cos_t = table[2 * n_blocks : 2 * n_blocks + BLK, :]
    sin_t = table[2 * n_blocks + BLK :, :]
    cosine = cos_b * cos_t - sin_b * sin_t
    sine = sin_b * cos_t + cos_b * sin_t
    lanes = lax.broadcasted_iota(jnp.int32, sine.shape, 1)
    return cosine, jnp.where(lanes < HEAD_DIM // 2, -sine, sine)


def turn(values, cosine, signed_sine):
    return values * cosine + pltpu.roll(values, HEAD_DIM // 2, 1) * signed_sine


def dot_nt(a, b):
    return lax.dot_general(a, b, (((1,), (1,)), ((), ())), preferred_element_type=F32)


def dot_nn(a, b):
    return lax.dot_general(a, b, (((1,), (0,)), ((), ())), preferred_element_type=F32)


def here(n_seq):
    member = lax.axis_index("seq")
    group = lax.axis_index("grp")
    return group, member, lax.rem(member, CORES)


def size_of(array):
    return math.prod(array.shape) * jnp.dtype(array.dtype).itemsize


def call(kernel, out_shape, n_smem, scratch=(), us=1, name=None, n_hbm=0, hbm_out=None, pin=False):
    def placed(n, a):
        if n == hbm_out:
            return pltpu.HBM(a.shape, a.dtype)
        return pltpu.VMEM(a.shape, a.dtype) if pin else a

    def spec(n, a):
        if a.dtype == jnp.int32:
            return SMEM_SPEC
        return HBM_SPEC if n == hbm_out else VMEM_SPEC

    def run(*arrays):
        n_left = n_smem + n_hbm
        outs = list(out_shape) if isinstance(out_shape, (tuple, list)) else [out_shape]
        held = sum(size_of(a) for a in arrays[n_left:])
        held += sum(size_of(a) for n, a in enumerate(outs) if n != hbm_out)
        held += sum(size_of(a) for a in scratch if a.dtype in (F32, BF16))
        in_specs = [SMEM_SPEC] * n_smem + [HBM_SPEC] * n_hbm
        in_specs += [VMEM_SPEC] * (len(arrays) - n_left)
        pinned = [
            pltpu.with_memory_space_constraint(a, pltpu.HBM) if n < n_left else a
            for n, a in enumerate(arrays)
        ]
        results = pl.pallas_call(
            kernel,
            out_shape=[placed(n, a) for n, a in enumerate(outs)],
            in_specs=in_specs,
            out_specs=[spec(n, a) for n, a in enumerate(outs)],
            scratch_shapes=list(scratch),
            compiler_params=pltpu.CompilerParams(vmem_limit_bytes=held + 6 * 2**20),
            cost_estimate=pl.CostEstimate(
                flops=us * 10**9, bytes_accessed=2**20, transcendentals=0
            ),
            name=name,
        )(*pinned)
        return results if isinstance(out_shape, (tuple, list)) else results[0]

    return run


def fetch(sources, places, sems):
    copies = [
        pltpu.make_async_copy(source, place, sems.at[n])
        for n, (source, place) in enumerate(zip(sources, places))
    ]
    for copy in copies:
        copy.start()
    for copy in copies:
        copy.wait()


def prepare_kv(n_seq, place_ref, *refs):
    sources, (keep, send), (key, value, table, sems) = refs[:3], refs[3:5], refs[5:]
    fetch(sources, (key, value, table), sems)
    group, member, core = here(n_seq)
    cosine, sine = block_tables(place_ref[group * n_seq + member], table)
    for out, half in ((keep, core), (send, 1 - core)):
        for h in range(HALF_KV):
            columns = pl.ds(pl.multiple_of((half * HALF_KV + h) * HEAD_DIM, HEAD_DIM), HEAD_DIM)
            out[0, h] = turn(key[:, columns].astype(F32), cosine, sine).astype(BF16)
            out[1, h] = value[:, columns]


def prepare_queries(n_seq, place_ref, *refs):
    sources, (keep, send), (query, grad, table, sems) = refs[:3], refs[3:5], refs[5:]
    fetch(sources, (query, grad, table), sems)
    group, member, core = here(n_seq)
    cosine, sine = block_tables(place_ref[group * n_seq + member], table)
    for out, half in ((keep, core), (send, 1 - core)):
        for h in range(HALF_KV):
            for r in range(RATIO):
                head = (half * HALF_KV + h) * RATIO + r
                columns = pl.ds(pl.multiple_of(head * HEAD_DIM, HEAD_DIM), HEAD_DIM)
                out[0, h, r] = turn(query[:, columns].astype(F32), cosine, sine).astype(BF16)
                out[1, h, r] = grad[:, columns]


def make_lists(n_seq, split, key_blocks, key_counts, lists, counts):
    group, member, _ = here(n_seq)
    for i in range(2):
        block = group * n_seq + lax.bitwise_xor(member, i)
        for section in range(3):
            counts[i, section] = int(section == 1)
        lists[i, 1, 0] = i

        def look(j, _):
            place = lax.bitwise_xor(key_blocks[block, j] - (group - 1) * n_seq, member)
            section = (place >= n_seq).astype(jnp.int32)
            section += (place >= n_seq + split).astype(jnp.int32)
            n = counts[i, section]
            lists[i, section, n] = place - jnp.where(section == 0, 0, n_seq) - jnp.where(
                section == 2, split, 0
            )
            counts[i, section] = n + 1
            return 0

        lax.fori_loop(1, key_counts[block], look, 0)
        total = 0
        for section, base in enumerate((0, n_seq, n_seq + split)):

            def append(n, m):
                lists[i, 3, m] = lists[i, section, n] + base
                return m + 1

            total = lax.fori_loop(0, counts[i, section], append, jnp.int32(total))
        counts[i, 3] = total
        lists[i, 3, total] = 0


def causal():
    keys = lax.broadcasted_iota(jnp.int32, (BLK, CHUNK), 0)
    tokens = lax.rem(lax.broadcasted_iota(jnp.int32, (BLK, CHUNK), 1), BLK)
    return keys <= tokens


def chunks():
    per = CHUNK // BLK
    return [
        (slice(c * per, (c + 1) * per), slice(c * CHUNK, (c + 1) * CHUNK))
        for c in range(ROWS // CHUNK)
    ]


def heads_of(block, what, h, rows):
    return block[what, h, rows].reshape(CHUNK, HEAD_DIM)


def fill(store, pieces, first=0):
    pieces = list(pieces)
    while pieces:
        part = slice(first, first + CORES)
        piece = pieces.pop(0)
        whole = len(piece.shape) == 5
        store[part, 0] = piece[0] if whole else piece[...]
        store[part, 1] = piece[1] if whole else pieces.pop(0)[...]
        first += CORES


def pair_scores(store, e, h, block, rows, diagonal):
    scores = dot_nt(store[e, 0, h], heads_of(block, 0, h, rows))
    if diagonal:
        scores = jnp.where(causal(), scores, -1e30)
    return scores, dot_nt(store[e, 1, h], heads_of(block, 1, h, rows))


def gather_stats(store, e, block, stats, i, diagonal, kept=None):
    for h in range(HALF_KV):
        for rows, columns in chunks():
            scores, dprobs = pair_scores(store, e, h, block, rows, diagonal)
            if kept is not None:
                n, kept_scores, kept_dprobs = kept
                kept_scores[n, h, :, columns] = scores
                kept_dprobs[n, h, :, columns] = dprobs
            top = jnp.max(scores, axis=0, keepdims=True)
            if not diagonal:
                old_top = stats[i, h, 0:1, columns]
                top = jnp.maximum(top, old_top)
            weights = jnp.exp2((scores - top) * TO_LOG2)
            total = jnp.sum(weights, axis=0, keepdims=True)
            mixed = jnp.sum(weights * dprobs, axis=0, keepdims=True)
            if not diagonal:
                shrink = jnp.exp2((old_top - top) * TO_LOG2)
                total += stats[i, h, 1:2, columns] * shrink
                mixed += stats[i, h, 2:3, columns] * shrink
            stats[i, h, 0:1, columns] = top
            stats[i, h, 1:2, columns] = total
            stats[i, h, 2:3, columns] = mixed


def spread_grads(found, count, kept_scores, kept_dprobs, stats, i, block, acc, saved, low, sent):
    def copy(n):
        return pltpu.make_async_copy(low.at[n], saved.at[i, n], sent.at[n])

    def add(n, _):
        e = found[n]
        for h in range(HALF_KV):
            dk, dv = acc[e, 0, h], acc[e, 1, h]
            for rows, columns in chunks():
                probs = jnp.exp2(
                    kept_scores[n, h, :, columns] * TO_LOG2 - stats[i, h, 0:1, columns]
                )
                dscores = probs * (kept_dprobs[n, h, :, columns] - stats[i, h, 2:3, columns])
                probs, dscores = probs.astype(BF16), dscores.astype(BF16)
                low[n, h, 0, :, columns] = probs
                low[n, h, 1, :, columns] = dscores
                dv += dot_nn(probs, heads_of(block, 1, h, rows))
                dk += dot_nn(dscores, heads_of(block, 0, h, rows))
            acc[e, 0, h] = dk
            acc[e, 1, h] = dv
        copy(n).start()
        return 0

    def finish(n, _):
        copy(n).wait()
        return 0

    lax.fori_loop(0, count, add, 0)
    lax.fori_loop(0, count, finish, 0)


def write_grads(acc, outs):
    start = 0
    for out in outs:
        part = slice(start, start + out.shape[0])
        out[:, 0] = (acc[part, 0] * SCALE).astype(out.dtype)
        out[:, 1] = acc[part, 1].astype(out.dtype)
        start += out.shape[0]


def current_stats(section, lists, counts, own, other, *rest):
    *pieces, stats, store = rest
    first = section == 1
    if not first:
        stats_in, *pieces = pieces
        stats[...] = stats_in[...]
    fill(store, pieces)
    for i, block in enumerate((own, other)):
        if first:
            gather_stats(store, i, block, stats, i, True)

        def step(n, _):
            gather_stats(store, lists[i, section, n], block, stats, i, False)
            return 0

        lax.fori_loop(int(first), counts[i, section], step, 0)


def previous_grads(n_pieces, lists, counts, own, other, stats_in, *rest):
    n_refs = 2 * n_pieces - 2
    n_ends = n_refs + n_pieces - 1
    pieces, outs = rest[:n_refs], rest[n_refs:n_ends]
    saved, stats, store, acc, low, sent, kept_scores, kept_dprobs = rest[n_ends:]
    fill(store, pieces)
    acc[...] = jnp.zeros_like(acc)
    stats[...] = stats_in[...]
    for i, block in enumerate((own, other)):
        count = counts[i, 0]

        def look(n, _):
            gather_stats(
                store, lists[i, 0, n], block, stats, i, False, (n, kept_scores, kept_dprobs)
            )
            return 0

        lax.fori_loop(0, count, look, 0)
        for h in range(HALF_KV):
            total = stats[i, h, 1:2, :]
            stats[i, h, 0:1, :] = stats[i, h, 0:1, :] * TO_LOG2 + jnp.log2(total)
            stats[i, h, 2:3, :] = stats[i, h, 2:3, :] / total

        def copy(n):
            return pltpu.make_async_copy(low.at[n], saved.at[i, n], sent.at[n])

        def add(n, _):
            e = lists[i, 0, n]
            for h in range(HALF_KV):
                dk, dv = acc[e, 0, h], acc[e, 1, h]
                for rows, columns in chunks():
                    probs = jnp.exp2(
                        kept_scores[n, h, :, columns] * TO_LOG2 - stats[i, h, 0:1, columns]
                    )
                    dscores = probs * (kept_dprobs[n, h, :, columns] - stats[i, h, 2:3, columns])
                    probs, dscores = probs.astype(BF16), dscores.astype(BF16)
                    low[n, h, 0, :, columns] = probs
                    low[n, h, 1, :, columns] = dscores
                    dv += dot_nn(probs, heads_of(block, 1, h, rows))
                    dk += dot_nn(dscores, heads_of(block, 0, h, rows))
                acc[e, 0, h] = dk
                acc[e, 1, h] = dv
            copy(n).start()
            return 0

        def finish(n, _):
            copy(n).wait()
            return 0

        lax.fori_loop(0, count, add, 0)
        lax.fori_loop(0, count, finish, 0)
    write_grads(acc, outs)


def current_grads(section, n_refs, lists, counts, own, other, stats, *rest):
    pieces, (*outs, saved, store, acc, low, sent) = rest[:n_refs], rest[n_refs:]
    first = section == 1
    fill(store, pieces)
    acc[...] = jnp.zeros_like(acc)
    for i, block in enumerate((own, other)):
        count = counts[i, section]

        def copy(n):
            return pltpu.make_async_copy(low.at[n], saved.at[i, n], sent.at[n])

        def look(n, diagonal):
            e = lists[i, section, n]
            for h in range(HALF_KV):
                for rows, columns in chunks():
                    scores, dprobs = pair_scores(store, e, h, block, rows, diagonal)
                    probs = jnp.exp2(scores * TO_LOG2 - stats[i, h, 0:1, columns])
                    low[n, h, 0, :, columns] = probs.astype(BF16)
                    dscores = probs * (dprobs - stats[i, h, 2:3, columns])
                    low[n, h, 1, :, columns] = dscores.astype(BF16)
            copy(n).start()
            return 0

        def add(n, _):
            e = lists[i, section, n]
            for h in range(HALF_KV):
                for w in range(2):
                    right = block[1 - w, h].reshape(ROWS, HEAD_DIM)
                    acc[e, 1 - w, h] += dot_nn(low[n, h, w], right)
            return 0

        def finish(n, _):
            copy(n).wait()
            return 0

        if first:
            look(0, True)
        lax.fori_loop(int(first), count, lambda n, _: look(n, False), 0)
        lax.fori_loop(0, count, add, 0)
        lax.fori_loop(0, count, finish, 0)
    write_grads(acc, outs)


def query_results(n_seq, lists, counts, place_ref, *rest):
    n_saved = 3
    n_refs = 2 * (n_seq - 2)
    saved, pieces, rest = rest[:n_saved], rest[n_saved:][:n_refs], rest[n_saved + n_refs :]
    table, *rest = rest
    outs, (store, low, out_acc, dq_acc, got) = rest[: 2 * HALF_KV], rest[2 * HALF_KV :]
    group, member, _ = here(n_seq)

    def copy(source, h, i, n, first):
        return pltpu.make_async_copy(source.at[i, n - first, h], low.at[h, i, n], got.at[h, i, n])

    ends = []
    for i in range(2):
        stops = [0]
        for section in range(n_saved):
            stops.append(stops[-1] + counts[i, section])
        ends.append(stops)
    for h in range(HALF_KV):
        for i, stops in enumerate(ends):
            for source, first, stop in zip(saved, stops, stops[1:]):

                def fetch_one(n, _):
                    copy(source, h, i, n, first).start()
                    return 0

                lax.fori_loop(first, stop, fetch_one, 0)
    fill(store, pieces)
    tables = []
    for i in range(2):
        mine = group * n_seq + lax.bitwise_xor(member, i)
        cosine, sine = block_tables(place_ref[mine], table)
        tables.append((cosine.T * SCALE, sine.T * SCALE))
    for h, (i, stops) in ((h, pair) for h in range(HALF_KV) for pair in enumerate(ends)):
        total = stops[-1]
        result = outs[i * HALF_KV + h]

        @pl.when(lax.rem(total, 2) == 1)
        def _():
            low[h, i, total] = jnp.zeros((2, BLK, ROWS), BF16)

        out_acc[...] = jnp.zeros_like(out_acc)
        dq_acc[...] = jnp.zeros_like(dq_acc)

        def add(n, _):
            pair = (2 * n, 2 * n + 1)
            for m in pair:
                for source, first, stop in zip(saved, stops, stops[1:]):

                    @pl.when(jnp.logical_and(m >= first, m < stop))
                    def _():
                        copy(source, h, i, m, first).wait()

            found = [lists[i, 3, m] for m in pair]
            keys_t = jnp.concatenate([store[e, 0, h].T for e in found], axis=1)
            values_t = jnp.concatenate([store[e, 1, h].T for e in found], axis=1)
            for _, columns in chunks():
                probs = jnp.concatenate([low[h, i, m, 0, :, columns] for m in pair], axis=0)
                dscores = jnp.concatenate([low[h, i, m, 1, :, columns] for m in pair], axis=0)
                out_acc[:, columns] += dot_nn(values_t, probs)
                dq_acc[:, columns] += dot_nn(keys_t, dscores)
            return 0

        lax.fori_loop(0, lax.div(total + 1, 2), add, 0)
        cosine, sine = tables[i]
        for r in range(RATIO):
            rows = slice(r * BLK, (r + 1) * BLK)
            columns = slice(r * HEAD_DIM, (r + 1) * HEAD_DIM)
            result[0, :, columns] = out_acc[:, rows].astype(BF16).T
            dq = dq_acc[:, rows]
            half = HEAD_DIM // 2
            turned = jnp.concatenate([dq[half:], dq[:half]], axis=0)
            result[1, :, columns] = (dq * cosine - turned * sine).astype(BF16).T


def finish_kv(n_seq, place_ref, *rest):
    *terms, table, keep, send = rest
    group, member, _ = here(n_seq)
    for i, result in enumerate((keep, send)):
        offset = lax.bitwise_xor(member, i)
        cosine, sine = block_tables(place_ref[group * n_seq + offset], table)
        for h in range(HALF_KV):
            columns = slice(h * HEAD_DIM, (h + 1) * HEAD_DIM)
            dk, dv = (sum(term[i, w, h].astype(F32) for term in terms) for w in range(2))
            result[0, :, columns] = turn(dk, cosine, -sine).astype(BF16)
            result[1, :, columns] = dv.astype(BF16)


def join_halves(*refs):
    core = lax.rem(lax.axis_index("seq"), CORES)
    own_q, got_q, (own_kv, got_kv) = refs[:HALF_KV], refs[HALF_KV:][:HALF_KV], refs[2 * HALF_KV :][:2]
    outs = refs[2 * HALF_KV + 2 :]
    for own, got, results in ((own_q, got_q, outs[:2]), ([own_kv], [got_kv], outs[2:])):
        width = own[0].shape[-1]
        for half, parts in ((core, own), (1 - core, got)):
            for n, part in enumerate(parts):
                start = pl.multiple_of((half * len(parts) + n) * width, width)
                for w, out in enumerate(results):
                    out[:, pl.ds(start, width)] = part[w]


def local(query_input, key_input, value_input, out_grad, key_blocks, key_counts, block_position):
    n_seq = lax.axis_size("seq")
    n_grp = lax.axis_size("grp")
    n_pieces = n_seq // CORES
    n_listed = key_blocks.shape[1]

    def cross(array, by):
        return lax.ppermute(array, "seq", [(m, m ^ by) for m in range(n_seq)])

    def along(array, by):
        return cross(array, CORES * by)

    def onward(array):
        return lax.ppermute(array, "grp", [(g, g + 1) for g in range(n_grp - 1)])

    def back(array):
        return lax.ppermute(array, "grp", [(g + 1, g) for g in range(n_grp - 1)])

    table = trig_table(block_position.shape[0])
    n_far = min(n_seq, n_listed - 1)
    split = 2 * CORES
    piece = (2, HALF_KV, BLK, HEAD_DIM)
    chip = (CORES, *piece)
    q_shape = jax.ShapeDtypeStruct((2, HALF_KV, RATIO, BLK, HEAD_DIM), BF16)
    kv_shape = jax.ShapeDtypeStruct(piece, BF16)
    stats_shape = jax.ShapeDtypeStruct((2, HALF_KV, 8, ROWS), F32)
    low = jax.ShapeDtypeStruct(chip, BF16)
    high = jax.ShapeDtypeStruct(chip, F32)
    lists, counts = call(
        functools.partial(make_lists, n_seq, split),
        (
            jax.ShapeDtypeStruct((2, 4, n_listed + 1), jnp.int32),
            jax.ShapeDtypeStruct((2, 4), jnp.int32),
        ),
        2, us=2, name="block_lists",
    )(key_blocks, key_counts)

    def prepared(kernel, shape, first, second, name):
        held = [pltpu.VMEM(a.shape, a.dtype) for a in (first, second, table)]
        return call(
            functools.partial(kernel, n_seq), (shape, shape), 1,
            [*held, pltpu.SemaphoreType.DMA((3,))], us=1, name=name, n_hbm=3, pin=True,
        )(block_position, first, second, table)

    kv_keep, kv_send = prepared(prepare_kv, kv_shape, key_input, value_input, "rotate_keys")
    kv_got = cross(kv_send, 1)
    query_late, kv_keep = lax.optimization_barrier((query_input, kv_keep))
    q_keep, q_send = prepared(prepare_queries, q_shape, query_late, out_grad, "rotate_queries")
    q_send, q_keep, kv_got, kv_keep = lax.optimization_barrier((q_send, q_keep, kv_got, kv_keep))
    q_got = cross(q_send, 1)
    here_kv = jnp.stack([kv_keep, kv_got], axis=1)
    near, far = [here_kv, along(here_kv, 1)], [onward(here_kv), None]
    ready, far[0] = lax.optimization_barrier((near[1], far[0]))
    for k in range(2, n_pieces, 2):
        keys, _ = lax.optimization_barrier((along(here_kv[0], k), ready))
        values, _ = lax.optimization_barrier((along(here_kv[1], k), keys))
        near += [keys, values, along(keys, 1), along(values, 1)]
        far += [onward(keys), onward(values), None, None]
    stats = call(
        functools.partial(current_stats, 1), stats_shape, 2, [pltpu.VMEM((split, *piece), BF16)],
        us=4, name="near_statistics",
    )(lists, counts, q_keep, q_got, *near[:2])
    ready, far[3], stats = lax.optimization_barrier((ready, far[3], stats))
    for k in range(2, 2 * n_pieces - 2, 4):
        far[k + 2], far[k + 3] = along(far[k], 1), along(far[k + 1], 1)
    far[1] = onward(ready)
    stats = call(
        functools.partial(current_stats, 2), stats_shape, 2,
        [pltpu.VMEM((n_seq - split, *piece), BF16)], us=4, name="far_statistics",
    )(lists, counts, q_keep, q_got, stats, *near[2:])

    def grads_call(kernel, n_slots, n_store, outs, us, name, kept=(), more=()):
        pair = (n_slots, HALF_KV, 2, BLK, ROWS)
        saved = jax.ShapeDtypeStruct((2, *pair), BF16)
        return call(
            kernel, (*outs, saved, *more), 2,
            [
                pltpu.VMEM((n_store, *piece), BF16), pltpu.VMEM((n_store, *piece), F32),
                pltpu.VMEM(pair, BF16), pltpu.SemaphoreType.DMA((n_slots,)), *kept,
            ],
            us=us, name=name, hbm_out=len(outs),
        )

    kept = pltpu.VMEM((n_far, HALF_KV, BLK, ROWS), F32)
    two = jax.ShapeDtypeStruct((2 * CORES, *piece), BF16)
    first_far, *far_grads, far_saved, stats = grads_call(
        functools.partial(previous_grads, n_pieces), n_far, n_seq, (two,) + (low,) * (n_pieces - 2),
        14, "previous_gradients", (kept, kept), (stats_shape,),
    )(lists, counts, q_keep, q_got, stats, *far)

    def current_call(section, outs, name, pieces, after):
        stats_late, _ = lax.optimization_barrier((stats, after))
        n_store = n_seq - split if section == 2 else split
        *grads, saved = grads_call(
            functools.partial(current_grads, section, len(pieces)), min(n_store, n_listed), n_store,
            outs, 6, name,
        )(lists, counts, q_keep, q_got, stats_late, *pieces)
        return grads, saved

    def total(*terms):
        return sum(term.astype(F32) for term in terms).astype(BF16)

    from_far = back(first_far)
    crossing = [along(grad, 1) for grad in far_grads[1::2]]
    high_grads, high_saved = current_call(
        2, [high, low] * (n_pieces // 2 - 1), "far_current_gradients", near[2:], far_grads[0]
    )
    crossing, high_grads = lax.optimization_barrier((crossing, high_grads))
    arrived = [
        back(total(grad, extra)) for grad, extra in zip(far_grads[0::2], crossing)
    ]
    swapped = [along(grad, 1) for grad in high_grads[1::2]]
    low_grads, low_saved = current_call(
        1, [high, high], "near_current_gradients", near[:2], high_grads[0]
    )
    low_grads, from_far = lax.optimization_barrier((low_grads, from_far))
    from_next = along(total(low_grads[1], from_far[CORES:]), 1)
    merged = [
        total(*terms) for terms in zip(high_grads[0::2], arrived, swapped)
    ]
    half_out = jax.ShapeDtypeStruct((2, BLK, RATIO * HEAD_DIM), BF16)
    place_late, _ = lax.optimization_barrier((block_position, merged))
    wide = pltpu.VMEM((HEAD_DIM, ROWS), F32)
    slots = (HALF_KV, 2, n_listed + 1)
    halves = call(
        functools.partial(query_results, n_seq), (half_out,) * (2 * HALF_KV), 3,
        [
            pltpu.VMEM((2 * n_seq, *piece), BF16), pltpu.VMEM((*slots, 2, BLK, ROWS), BF16),
            wide, wide, pltpu.SemaphoreType.DMA(slots),
        ],
        us=20, name="query_results", n_hbm=3,
    )(lists, counts, place_late, far_saved, low_saved, high_saved, *far, *near, table)
    own_halves, other_halves = halves[:HALF_KV], halves[HALF_KV:]
    other_halves = lax.optimization_barrier(list(other_halves))
    got_halves = [cross(half, 1) for half in other_halves]
    final = [low_grads[0], from_far[:CORES], from_next]
    final += [along(part, 2 + 2 * n) for n, part in enumerate(merged)]
    own_halves = list(own_halves)
    final[0], own_halves[1] = lax.optimization_barrier((final[0], own_halves[1]))
    kv_half = jax.ShapeDtypeStruct((2, BLK, HALF_KV * HEAD_DIM), BF16)
    own_kv, other_kv = call(
        functools.partial(finish_kv, n_seq), (kv_half, kv_half), 1, us=2, name="key_gradients"
    )(block_position, *final, table)
    got_kv = cross(other_kv, 1)
    q_out = jax.ShapeDtypeStruct(query_input.shape, BF16)
    kv_out = jax.ShapeDtypeStruct(key_input.shape, BF16)
    out_rows, query_grad, key_grad, value_grad = call(
        join_halves, (q_out, q_out, kv_out, kv_out), 0, us=2, name="join_halves"
    )(*own_halves, *got_halves, own_kv, got_kv)
    return (out_rows, query_grad, key_grad, value_grad)


def solution(mesh):
    split = P(("grp", "seq"), None)
    return jax.shard_map(
        local,
        mesh=mesh,
        in_specs=(split, split, split, split, P(), P(), P()),
        out_specs=(split, split, split, split),
        check_vma=False,
    )
```

```python
import functools
import math

import jax
import jax.numpy as jnp
import numpy as np
from jax import lax
from jax.experimental import pallas as pl
from jax.experimental.pallas import tpu as pltpu
from jax.sharding import PartitionSpec as P

HEADS = 32
KV_HEADS = 4
HEAD_DIM = 128
BLK = 128
CORES = 2
RATIO = HEADS // KV_HEADS
HALF_KV = KV_HEADS // CORES
ROWS = RATIO * BLK
SCALE = 1.0 / math.sqrt(HEAD_DIM)
TO_LOG2 = SCALE * math.log2(math.e)
F32 = jnp.float32
BF16 = jnp.bfloat16
CHUNK = 256

VMEM_SPEC = pl.BlockSpec(memory_space=pltpu.VMEM)
HBM_SPEC = pl.BlockSpec(memory_space=pltpu.HBM)
SMEM_SPEC = pl.BlockSpec(memory_space=pltpu.SMEM)


def trig_table(n_blocks):
    half = HEAD_DIM // 2
    frequency = np.power(500000.0, -np.arange(half) * (2.0 / HEAD_DIM))
    parts = []
    for places in (np.arange(n_blocks) * BLK, np.arange(BLK)):
        angles = places[:, None] * frequency
        for part in (np.cos(angles), np.sin(angles)):
            parts.append(np.concatenate([part, part], axis=1))
    return np.concatenate(parts, axis=0).astype(np.float32)


def block_tables(place, table):
    n_blocks = table.shape[0] // 2 - BLK
    cos_b = table[pl.ds(place, 1), :]
    sin_b = table[pl.ds(n_blocks + place, 1), :]
    cos_t = table[2 * n_blocks : 2 * n_blocks + BLK, :]
    sin_t = table[2 * n_blocks + BLK :, :]
    cosine = cos_b * cos_t - sin_b * sin_t
    sine = sin_b * cos_t + cos_b * sin_t
    lanes = lax.broadcasted_iota(jnp.int32, sine.shape, 1)
    return cosine, jnp.where(lanes < HEAD_DIM // 2, -sine, sine)


def turn(values, cosine, signed_sine):
    return values * cosine + pltpu.roll(values, HEAD_DIM // 2, 1) * signed_sine


def dot_nt(a, b):
    return lax.dot_general(a, b, (((1,), (1,)), ((), ())), preferred_element_type=F32)


def dot_nn(a, b):
    return lax.dot_general(a, b, (((1,), (0,)), ((), ())), preferred_element_type=F32)


def here(n_seq):
    member = lax.axis_index("seq")
    group = lax.axis_index("grp")
    return group, member, lax.rem(member, CORES)


def size_of(array):
    return math.prod(array.shape) * jnp.dtype(array.dtype).itemsize


def call(kernel, out_shape, n_smem, scratch=(), us=1, name=None, n_hbm=0, hbm_out=None, pin=False):
    def placed(n, a):
        if n == hbm_out:
            return pltpu.HBM(a.shape, a.dtype)
        return pltpu.VMEM(a.shape, a.dtype) if pin else a

    def spec(n, a):
        if a.dtype == jnp.int32:
            return SMEM_SPEC
        return HBM_SPEC if n == hbm_out else VMEM_SPEC

    def run(*arrays):
        n_left = n_smem + n_hbm
        outs = list(out_shape) if isinstance(out_shape, (tuple, list)) else [out_shape]
        held = sum(size_of(a) for a in arrays[n_left:])
        held += sum(size_of(a) for n, a in enumerate(outs) if n != hbm_out)
        held += sum(size_of(a) for a in scratch if a.dtype in (F32, BF16))
        in_specs = [SMEM_SPEC] * n_smem + [HBM_SPEC] * n_hbm
        in_specs += [VMEM_SPEC] * (len(arrays) - n_left)
        pinned = [
            pltpu.with_memory_space_constraint(a, pltpu.HBM) if n < n_left else a
            for n, a in enumerate(arrays)
        ]
        results = pl.pallas_call(
            kernel,
            out_shape=[placed(n, a) for n, a in enumerate(outs)],
            in_specs=in_specs,
            out_specs=[spec(n, a) for n, a in enumerate(outs)],
            scratch_shapes=list(scratch),
            compiler_params=pltpu.CompilerParams(vmem_limit_bytes=held + 6 * 2**20),
            cost_estimate=pl.CostEstimate(
                flops=us * 10**9, bytes_accessed=2**20, transcendentals=0
            ),
            name=name,
        )(*pinned)
        return results if isinstance(out_shape, (tuple, list)) else results[0]

    return run


def fetch(sources, places, sems):
    copies = [
        pltpu.make_async_copy(source, place, sems.at[n])
        for n, (source, place) in enumerate(zip(sources, places))
    ]
    for copy in copies:
        copy.start()
    for copy in copies:
        copy.wait()


def prepare_kv(n_seq, place_ref, *refs):
    sources, (keep, send), (key, value, table, sems) = refs[:3], refs[3:5], refs[5:]
    fetch(sources, (key, value, table), sems)
    group, member, core = here(n_seq)
    cosine, sine = block_tables(place_ref[group * n_seq + member], table)
    for out, half in ((keep, core), (send, 1 - core)):
        for h in range(HALF_KV):
            columns = pl.ds(pl.multiple_of((half * HALF_KV + h) * HEAD_DIM, HEAD_DIM), HEAD_DIM)
            out[0, h] = turn(key[:, columns].astype(F32), cosine, sine).astype(BF16)
            out[1, h] = value[:, columns]


def prepare_queries(n_seq, place_ref, *refs):
    sources, (keep, send), (query, grad, table, sems) = refs[:3], refs[3:5], refs[5:]
    fetch(sources, (query, grad, table), sems)
    group, member, core = here(n_seq)
    cosine, sine = block_tables(place_ref[group * n_seq + member], table)
    for out, half in ((keep, core), (send, 1 - core)):
        for h in range(HALF_KV):
            for r in range(RATIO):
                head = (half * HALF_KV + h) * RATIO + r
                columns = pl.ds(pl.multiple_of(head * HEAD_DIM, HEAD_DIM), HEAD_DIM)
                out[0, h, r] = turn(query[:, columns].astype(F32), cosine, sine).astype(BF16)
                out[1, h, r] = grad[:, columns]


def make_lists(n_seq, split, key_blocks, key_counts, lists, counts):
    group, member, _ = here(n_seq)
    for i in range(2):
        block = group * n_seq + lax.bitwise_xor(member, i)
        for section in range(3):
            counts[i, section] = int(section == 1)
        lists[i, 1, 0] = i

        def look(j, _):
            place = lax.bitwise_xor(key_blocks[block, j] - (group - 1) * n_seq, member)
            section = (place >= n_seq).astype(jnp.int32)
            section += (place >= n_seq + split).astype(jnp.int32)
            n = counts[i, section]
            lists[i, section, n] = place - jnp.where(section == 0, 0, n_seq) - jnp.where(
                section == 2, split, 0
            )
            counts[i, section] = n + 1
            return 0

        lax.fori_loop(1, key_counts[block], look, 0)
        total = 0
        for section, base in enumerate((0, n_seq, n_seq + split)):

            def append(n, m):
                lists[i, 3, m] = lists[i, section, n] + base
                return m + 1

            total = lax.fori_loop(0, counts[i, section], append, jnp.int32(total))
        counts[i, 3] = total
        lists[i, 3, total] = 0


def causal():
    keys = lax.broadcasted_iota(jnp.int32, (BLK, CHUNK), 0)
    tokens = lax.rem(lax.broadcasted_iota(jnp.int32, (BLK, CHUNK), 1), BLK)
    return keys <= tokens


def chunks():
    per = CHUNK // BLK
    return [
        (slice(c * per, (c + 1) * per), slice(c * CHUNK, (c + 1) * CHUNK))
        for c in range(ROWS // CHUNK)
    ]


def heads_of(block, what, h, rows):
    return block[what, h, rows].reshape(CHUNK, HEAD_DIM)


def fill(store, pieces, first=0):
    for k, piece in enumerate(pieces):
        store[first + CORES * k : first + CORES * (k + 1)] = piece[...]


def pair_scores(store, e, h, block, rows, diagonal):
    scores = dot_nt(store[e, 0, h], heads_of(block, 0, h, rows))
    if diagonal:
        scores = jnp.where(causal(), scores, -1e30)
    return scores, dot_nt(store[e, 1, h], heads_of(block, 1, h, rows))


def gather_stats(store, e, block, stats, i, diagonal, kept=None):
    for h in range(HALF_KV):
        for rows, columns in chunks():
            scores, dprobs = pair_scores(store, e, h, block, rows, diagonal)
            top = jnp.max(scores, axis=0, keepdims=True)
            if not diagonal:
                old_top = stats[i, h, 0:1, columns]
                top = jnp.maximum(top, old_top)
            weights = jnp.exp2((scores - top) * TO_LOG2)
            if kept is not None:
                n, kept_weights, kept_dprobs, tops = kept
                kept_weights[n, h, :, columns] = weights
                kept_dprobs[n, h, :, columns] = dprobs
                tops[n, h, 0:1, columns] = top * TO_LOG2
            total = jnp.sum(weights, axis=0, keepdims=True)
            mixed = jnp.sum(weights * dprobs, axis=0, keepdims=True)
            if not diagonal:
                shrink = jnp.exp2((old_top - top) * TO_LOG2)
                total += stats[i, h, 1:2, columns] * shrink
                mixed += stats[i, h, 2:3, columns] * shrink
            stats[i, h, 0:1, columns] = top
            stats[i, h, 1:2, columns] = total
            stats[i, h, 2:3, columns] = mixed


def spread_grads(found, count, kept_scores, kept_dprobs, stats, i, block, acc, saved, low, sent):
    def copy(n):
        return pltpu.make_async_copy(low.at[n], saved.at[i, n], sent.at[n])

    def add(n, _):
        e = found[n]
        for h in range(HALF_KV):
            dk, dv = acc[e, 0, h], acc[e, 1, h]
            for rows, columns in chunks():
                probs = jnp.exp2(
                    kept_scores[n, h, :, columns] * TO_LOG2 - stats[i, h, 0:1, columns]
                )
                dscores = probs * (kept_dprobs[n, h, :, columns] - stats[i, h, 2:3, columns])
                probs, dscores = probs.astype(BF16), dscores.astype(BF16)
                low[n, h, 0, :, columns] = probs
                low[n, h, 1, :, columns] = dscores
                dv += dot_nn(probs, heads_of(block, 1, h, rows))
                dk += dot_nn(dscores, heads_of(block, 0, h, rows))
            acc[e, 0, h] = dk
            acc[e, 1, h] = dv
        copy(n).start()
        return 0

    def finish(n, _):
        copy(n).wait()
        return 0

    lax.fori_loop(0, count, add, 0)
    lax.fori_loop(0, count, finish, 0)


def write_grads(acc, outs):
    start = 0
    for out in outs:
        part = slice(start, start + out.shape[0])
        out[:, 0] = (acc[part, 0] * SCALE).astype(out.dtype)
        out[:, 1] = acc[part, 1].astype(out.dtype)
        start += out.shape[0]


def current_stats(section, lists, counts, own, other, *rest):
    *pieces, stats, store = rest
    first = section == 1
    if not first:
        stats_in, *pieces = pieces
        stats[...] = stats_in[...]
    fill(store, pieces)
    for i, block in enumerate((own, other)):
        if first:
            gather_stats(store, i, block, stats, i, True)

        def step(n, _):
            gather_stats(store, lists[i, section, n], block, stats, i, False)
            return 0

        lax.fori_loop(int(first), counts[i, section], step, 0)


def previous_grads(n_pieces, lists, counts, own, other, stats_in, *rest):
    n_ends = 2 * n_pieces - 1
    pieces, outs = rest[:n_pieces], rest[n_pieces:n_ends]
    saved, stats, store, acc, low, sent, kept_weights, kept_dprobs, tops = rest[n_ends:]
    fill(store, pieces)
    acc[...] = jnp.zeros_like(acc)
    stats[...] = stats_in[...]
    for i, block in enumerate((own, other)):
        count = counts[i, 0]

        def look(n, _):
            kept = (n, kept_weights, kept_dprobs, tops)
            gather_stats(store, lists[i, 0, n], block, stats, i, False, kept)
            return 0

        lax.fori_loop(0, count, look, 0)
        for h in range(HALF_KV):
            total = stats[i, h, 1:2, :]
            stats[i, h, 0:1, :] = stats[i, h, 0:1, :] * TO_LOG2 + jnp.log2(total)
            stats[i, h, 2:3, :] = stats[i, h, 2:3, :] / total

        def copy(n):
            return pltpu.make_async_copy(low.at[n], saved.at[i, n], sent.at[n])

        def add(n, _):
            e = lists[i, 0, n]
            for h in range(HALF_KV):
                dk, dv = acc[e, 0, h], acc[e, 1, h]
                for rows, columns in chunks():
                    share = jnp.exp2(tops[n, h, 0:1, columns] - stats[i, h, 0:1, columns])
                    probs = kept_weights[n, h, :, columns] * share
                    dscores = probs * (kept_dprobs[n, h, :, columns] - stats[i, h, 2:3, columns])
                    probs, dscores = probs.astype(BF16), dscores.astype(BF16)
                    low[n, h, 0, :, columns] = probs
                    low[n, h, 1, :, columns] = dscores
                    dv += dot_nn(probs, heads_of(block, 1, h, rows))
                    dk += dot_nn(dscores, heads_of(block, 0, h, rows))
                acc[e, 0, h] = dk
                acc[e, 1, h] = dv
            copy(n).start()
            return 0

        def finish(n, _):
            copy(n).wait()
            return 0

        lax.fori_loop(0, count, add, 0)
        lax.fori_loop(0, count, finish, 0)
    write_grads(acc, outs)


def current_grads(section, n_pieces, lists, counts, own, other, stats, *rest):
    pieces, outs = rest[:n_pieces], rest[n_pieces : 2 * n_pieces]
    saved, store, acc, low, sent = rest[2 * n_pieces :]
    first = section == 1
    fill(store, pieces)
    acc[...] = jnp.zeros_like(acc)
    for i, block in enumerate((own, other)):
        count = counts[i, section]

        def copy(n):
            return pltpu.make_async_copy(low.at[n], saved.at[i, n], sent.at[n])

        def look(n, diagonal):
            e = lists[i, section, n]
            for h in range(HALF_KV):
                for rows, columns in chunks():
                    scores, dprobs = pair_scores(store, e, h, block, rows, diagonal)
                    probs = jnp.exp2(scores * TO_LOG2 - stats[i, h, 0:1, columns])
                    low[n, h, 0, :, columns] = probs.astype(BF16)
                    dscores = probs * (dprobs - stats[i, h, 2:3, columns])
                    low[n, h, 1, :, columns] = dscores.astype(BF16)
            copy(n).start()
            return 0

        def add(n, _):
            e = lists[i, section, n]
            for h in range(HALF_KV):
                for w in range(2):
                    right = block[1 - w, h].reshape(ROWS, HEAD_DIM)
                    acc[e, 1 - w, h] += dot_nn(low[n, h, w], right)
            return 0

        def finish(n, _):
            copy(n).wait()
            return 0

        if first:
            look(0, True)
        lax.fori_loop(int(first), count, lambda n, _: look(n, False), 0)
        lax.fori_loop(0, count, add, 0)
        lax.fori_loop(0, count, finish, 0)
    write_grads(acc, outs)


def query_results(n_seq, lists, counts, place_ref, *rest):
    n_saved = 3
    n_pieces = n_seq // CORES
    saved, pieces, rest = rest[:n_saved], rest[n_saved:][: 2 * n_pieces], rest[n_saved + 2 * n_pieces :]
    table, *rest = rest
    outs, (store, low, out_acc, dq_acc, got) = rest[: 2 * HALF_KV], rest[2 * HALF_KV :]
    group, member, _ = here(n_seq)

    def copy(source, h, i, n, first):
        return pltpu.make_async_copy(source.at[i, n - first, h], low.at[h, i, n], got.at[h, i, n])

    ends = []
    for i in range(2):
        stops = [0]
        for section in range(n_saved):
            stops.append(stops[-1] + counts[i, section])
        ends.append(stops)
    for h in range(HALF_KV):
        for i, stops in enumerate(ends):
            for source, first, stop in zip(saved, stops, stops[1:]):

                def fetch_one(n, _):
                    copy(source, h, i, n, first).start()
                    return 0

                lax.fori_loop(first, stop, fetch_one, 0)
    fill(store, pieces)
    tables = []
    for i in range(2):
        mine = group * n_seq + lax.bitwise_xor(member, i)
        cosine, sine = block_tables(place_ref[mine], table)
        tables.append((cosine.T * SCALE, sine.T * SCALE))
    for h, (i, stops) in ((h, pair) for h in range(HALF_KV) for pair in enumerate(ends)):
        total = stops[-1]
        result = outs[i * HALF_KV + h]

        @pl.when(lax.rem(total, 2) == 1)
        def _():
            low[h, i, total] = jnp.zeros((2, BLK, ROWS), BF16)

        out_acc[...] = jnp.zeros_like(out_acc)
        dq_acc[...] = jnp.zeros_like(dq_acc)

        def add(n, _):
            pair = (2 * n, 2 * n + 1)
            for m in pair:
                for source, first, stop in zip(saved, stops, stops[1:]):

                    @pl.when(jnp.logical_and(m >= first, m < stop))
                    def _():
                        copy(source, h, i, m, first).wait()

            found = [lists[i, 3, m] for m in pair]
            keys_t = jnp.concatenate([store[e, 0, h].T for e in found], axis=1)
            values_t = jnp.concatenate([store[e, 1, h].T for e in found], axis=1)
            for _, columns in chunks():
                probs = jnp.concatenate([low[h, i, m, 0, :, columns] for m in pair], axis=0)
                dscores = jnp.concatenate([low[h, i, m, 1, :, columns] for m in pair], axis=0)
                out_acc[:, columns] += dot_nn(values_t, probs)
                dq_acc[:, columns] += dot_nn(keys_t, dscores)
            return 0

        lax.fori_loop(0, lax.div(total + 1, 2), add, 0)
        cosine, sine = tables[i]
        for r in range(RATIO):
            rows = slice(r * BLK, (r + 1) * BLK)
            columns = slice(r * HEAD_DIM, (r + 1) * HEAD_DIM)
            result[0, :, columns] = out_acc[:, rows].astype(BF16).T
            dq = dq_acc[:, rows]
            half = HEAD_DIM // 2
            turned = jnp.concatenate([dq[half:], dq[:half]], axis=0)
            result[1, :, columns] = (dq * cosine - turned * sine).astype(BF16).T


def finish_kv(n_seq, place_ref, *rest):
    *terms, table, keep, send = rest
    group, member, _ = here(n_seq)
    for i, result in enumerate((keep, send)):
        offset = lax.bitwise_xor(member, i)
        cosine, sine = block_tables(place_ref[group * n_seq + offset], table)
        for h in range(HALF_KV):
            columns = slice(h * HEAD_DIM, (h + 1) * HEAD_DIM)
            dk, dv = (sum(term[i, w, h].astype(F32) for term in terms) for w in range(2))
            result[0, :, columns] = turn(dk, cosine, -sine).astype(BF16)
            result[1, :, columns] = dv.astype(BF16)


def join_halves(*refs):
    core = lax.rem(lax.axis_index("seq"), CORES)
    own_q, got_q, (own_kv, got_kv) = refs[:HALF_KV], refs[HALF_KV:][:HALF_KV], refs[2 * HALF_KV :][:2]
    outs = refs[2 * HALF_KV + 2 :]
    for own, got, results in ((own_q, got_q, outs[:2]), ([own_kv], [got_kv], outs[2:])):
        width = own[0].shape[-1]
        for half, parts in ((core, own), (1 - core, got)):
            for n, part in enumerate(parts):
                start = pl.multiple_of((half * len(parts) + n) * width, width)
                for w, out in enumerate(results):
                    out[:, pl.ds(start, width)] = part[w]


def local(query_input, key_input, value_input, out_grad, key_blocks, key_counts, block_position):
    n_seq = lax.axis_size("seq")
    n_grp = lax.axis_size("grp")
    n_pieces = n_seq // CORES
    n_listed = key_blocks.shape[1]

    def cross(array, by):
        return lax.ppermute(array, "seq", [(m, m ^ by) for m in range(n_seq)])

    def along(array, by):
        return cross(array, CORES * by)

    def onward(array):
        return lax.ppermute(array, "grp", [(g, g + 1) for g in range(n_grp - 1)])

    def back(array):
        return lax.ppermute(array, "grp", [(g + 1, g) for g in range(n_grp - 1)])

    table = trig_table(block_position.shape[0])
    n_far = min(n_seq, n_listed - 1)
    split = 2 * CORES
    piece = (2, HALF_KV, BLK, HEAD_DIM)
    chip = (CORES, *piece)
    q_shape = jax.ShapeDtypeStruct((2, HALF_KV, RATIO, BLK, HEAD_DIM), BF16)
    kv_shape = jax.ShapeDtypeStruct(piece, BF16)
    stats_shape = jax.ShapeDtypeStruct((2, HALF_KV, 8, ROWS), F32)
    low = jax.ShapeDtypeStruct(chip, BF16)
    high = jax.ShapeDtypeStruct(chip, F32)
    lists, counts = call(
        functools.partial(make_lists, n_seq, split),
        (
            jax.ShapeDtypeStruct((2, 4, n_listed + 1), jnp.int32),
            jax.ShapeDtypeStruct((2, 4), jnp.int32),
        ),
        2, us=2, name="block_lists",
    )(key_blocks, key_counts)

    def prepared(kernel, shape, first, second, name):
        held = [pltpu.VMEM(a.shape, a.dtype) for a in (first, second, table)]
        return call(
            functools.partial(kernel, n_seq), (shape, shape), 1,
            [*held, pltpu.SemaphoreType.DMA((3,))], us=1, name=name, n_hbm=3,
        )(block_position, first, second, table)

    kv_keep, kv_send = prepared(prepare_kv, kv_shape, key_input, value_input, "rotate_keys")
    kv_got = cross(kv_send, 1)
    near = [jnp.stack([kv_keep, kv_got])]
    near.append(along(near[0], 1))
    ready, first_far = lax.optimization_barrier((near[1], onward(near[0])))
    query_late, _ = lax.optimization_barrier((query_input, near[0]))
    q_keep, q_send = prepared(prepare_queries, q_shape, query_late, out_grad, "rotate_queries")
    far = [first_far, None]
    for k in range(2, n_pieces, 2):
        piece_k, q_send, lists, counts, _ = lax.optimization_barrier(
            (along(near[0], k), q_send, lists, counts, ready)
        )
        near += [piece_k, along(piece_k, 1)]
        far += [onward(piece_k), None]
    q_got = cross(q_send, 1)
    stats = call(
        functools.partial(current_stats, 1), stats_shape, 2, [pltpu.VMEM((split, *piece), BF16)],
        us=4, name="near_statistics",
    )(lists, counts, q_keep, q_got, *near[:2])
    ready, far[2], stats = lax.optimization_barrier((ready, far[2], stats))
    far[1] = onward(ready)
    for k in range(2, n_pieces, 2):
        far[k + 1] = along(far[k], 1)
    stats = call(
        functools.partial(current_stats, 2), stats_shape, 2,
        [pltpu.VMEM((n_seq - split, *piece), BF16)], us=4, name="far_statistics",
    )(lists, counts, q_keep, q_got, stats, *near[2:])

    def grads_call(kernel, n_slots, n_store, outs, us, name, kept=(), more=()):
        pair = (n_slots, HALF_KV, 2, BLK, ROWS)
        saved = jax.ShapeDtypeStruct((2, *pair), BF16)
        return call(
            kernel, (*outs, saved, *more), 2,
            [
                pltpu.VMEM((n_store, *piece), BF16), pltpu.VMEM((n_store, *piece), F32),
                pltpu.VMEM(pair, BF16), pltpu.SemaphoreType.DMA((n_slots,)), *kept,
            ],
            us=us, name=name, hbm_out=len(outs),
        )

    kept = pltpu.VMEM((n_far, HALF_KV, BLK, ROWS), F32)
    two = jax.ShapeDtypeStruct((2 * CORES, *piece), BF16)
    first_far, *far_grads, far_saved, stats = grads_call(
        functools.partial(previous_grads, n_pieces), n_far, n_seq, (two,) + (low,) * (n_pieces - 2),
        14, "previous_gradients", (kept, kept, pltpu.VMEM((n_far, HALF_KV, 8, ROWS), F32)), (stats_shape,),
    )(lists, counts, q_keep, q_got, stats, *far)

    def current_call(section, outs, name, pieces, after):
        stats_late, _ = lax.optimization_barrier((stats, after))
        n_store = CORES * len(pieces)
        *grads, saved = grads_call(
            functools.partial(current_grads, section, len(pieces)), min(n_store, n_listed), n_store,
            outs, 6, name,
        )(lists, counts, q_keep, q_got, stats_late, *pieces)
        return grads, saved

    def total(*terms):
        return sum(term.astype(F32) for term in terms).astype(BF16)

    from_far = back(first_far)
    crossing = [along(grad, 1) for grad in far_grads[1::2]]
    high_grads, high_saved = current_call(
        2, [high, low] * (n_pieces // 2 - 1), "far_current_gradients", near[2:], far_grads[0]
    )
    crossing, high_grads = lax.optimization_barrier((crossing, high_grads))
    arrived = [
        back(total(grad, extra)) for grad, extra in zip(far_grads[0::2], crossing)
    ]
    swapped = [along(grad, 1) for grad in high_grads[1::2]]
    low_grads, low_saved = current_call(
        1, [high, high], "near_current_gradients", near[:2], high_grads[0]
    )
    low_grads, from_far = lax.optimization_barrier((low_grads, from_far))
    from_next = along(total(low_grads[1], from_far[CORES:]), 1)
    merged = [
        total(*terms) for terms in zip(high_grads[0::2], arrived, swapped)
    ]
    half_out = jax.ShapeDtypeStruct((2, BLK, RATIO * HEAD_DIM), BF16)
    place_late, _ = lax.optimization_barrier((block_position, merged))
    wide = pltpu.VMEM((HEAD_DIM, ROWS), F32)
    slots = (HALF_KV, 2, n_listed + 1)
    halves = call(
        functools.partial(query_results, n_seq), (half_out,) * (2 * HALF_KV), 3,
        [
            pltpu.VMEM((2 * n_seq, *piece), BF16), pltpu.VMEM((*slots, 2, BLK, ROWS), BF16),
            wide, wide, pltpu.SemaphoreType.DMA(slots),
        ],
        us=20, name="query_results", n_hbm=3,
    )(lists, counts, place_late, far_saved, low_saved, high_saved, *far, *near, table)
    own_halves, other_halves = halves[:HALF_KV], halves[HALF_KV:]
    other_halves = lax.optimization_barrier(list(other_halves))
    got_halves = [cross(half, 1) for half in other_halves]
    final = [low_grads[0], from_far[:CORES], from_next]
    final += [along(part, 2 + 2 * n) for n, part in enumerate(merged)]
    own_halves = list(own_halves)
    final[0], own_halves[1] = lax.optimization_barrier((final[0], own_halves[1]))
    kv_half = jax.ShapeDtypeStruct((2, BLK, HALF_KV * HEAD_DIM), BF16)
    own_kv, other_kv = call(
        functools.partial(finish_kv, n_seq), (kv_half, kv_half), 1, us=2, name="key_gradients"
    )(block_position, *final, table)
    got_kv = cross(other_kv, 1)
    q_out = jax.ShapeDtypeStruct(query_input.shape, BF16)
    kv_out = jax.ShapeDtypeStruct(key_input.shape, BF16)
    out_rows, query_grad, key_grad, value_grad = call(
        join_halves, (q_out, q_out, kv_out, kv_out), 0, us=2, name="join_halves"
    )(*own_halves, *got_halves, own_kv, got_kv)
    return (out_rows, query_grad, key_grad, value_grad)


def solution(mesh):
    split = P(("grp", "seq"), None)
    return jax.shard_map(
        local,
        mesh=mesh,
        in_specs=(split, split, split, split, P(), P(), P()),
        out_specs=(split, split, split, split),
        check_vma=False,
    )
```

```python
import functools
import math

import jax
import jax.numpy as jnp
import numpy as np
from jax import lax
from jax.experimental import pallas as pl
from jax.experimental.pallas import tpu as pltpu
from jax.sharding import PartitionSpec as P

HEADS = 32
KV_HEADS = 4
HEAD_DIM = 128
BLK = 128
CORES = 2
RATIO = HEADS // KV_HEADS
HALF_KV = KV_HEADS // CORES
ROWS = RATIO * BLK
SCALE = 1.0 / math.sqrt(HEAD_DIM)
TO_LOG2 = SCALE * math.log2(math.e)
F32 = jnp.float32
BF16 = jnp.bfloat16
CHUNK = 256

VMEM_SPEC = pl.BlockSpec(memory_space=pltpu.VMEM)
HBM_SPEC = pl.BlockSpec(memory_space=pltpu.HBM)
SMEM_SPEC = pl.BlockSpec(memory_space=pltpu.SMEM)


def trig_table(n_blocks):
    half = HEAD_DIM // 2
    frequency = np.power(500000.0, -np.arange(half) * (2.0 / HEAD_DIM))
    parts = []
    for places in (np.arange(n_blocks) * BLK, np.arange(BLK)):
        angles = places[:, None] * frequency
        for part in (np.cos(angles), np.sin(angles)):
            parts.append(np.concatenate([part, part], axis=1))
    return np.concatenate(parts, axis=0).astype(np.float32)


def block_tables(place, table):
    n_blocks = table.shape[0] // 2 - BLK
    cos_b = table[pl.ds(place, 1), :]
    sin_b = table[pl.ds(n_blocks + place, 1), :]
    cos_t = table[2 * n_blocks : 2 * n_blocks + BLK, :]
    sin_t = table[2 * n_blocks + BLK :, :]
    cosine = cos_b * cos_t - sin_b * sin_t
    sine = sin_b * cos_t + cos_b * sin_t
    lanes = lax.broadcasted_iota(jnp.int32, sine.shape, 1)
    return cosine, jnp.where(lanes < HEAD_DIM // 2, -sine, sine)


def turn(values, cosine, signed_sine):
    return values * cosine + pltpu.roll(values, HEAD_DIM // 2, 1) * signed_sine


def dot_nt(a, b):
    return lax.dot_general(a, b, (((1,), (1,)), ((), ())), preferred_element_type=F32)


def dot_nn(a, b):
    return lax.dot_general(a, b, (((1,), (0,)), ((), ())), preferred_element_type=F32)


def here(n_seq):
    member = lax.axis_index("seq")
    group = lax.axis_index("grp")
    return group, member, lax.rem(member, CORES)


def size_of(array):
    return math.prod(array.shape) * jnp.dtype(array.dtype).itemsize


def call(kernel, out_shape, n_smem, scratch=(), us=1, name=None, n_hbm=0, hbm_out=None, hold=()):
    def placed(n, a):
        if n == hbm_out:
            return pltpu.HBM(a.shape, a.dtype)
        return a

    def spec(n, a):
        if a.dtype == jnp.int32:
            return SMEM_SPEC
        return HBM_SPEC if n == hbm_out else VMEM_SPEC

    def run(*arrays):
        n_left = n_smem + n_hbm
        outs = list(out_shape) if isinstance(out_shape, (tuple, list)) else [out_shape]
        held = sum(size_of(a) for a in arrays[n_left:])
        held += sum(size_of(a) for n, a in enumerate(outs) if n != hbm_out)
        held += sum(size_of(a) for a in scratch if a.dtype in (F32, BF16))
        in_specs = [SMEM_SPEC] * n_smem + [HBM_SPEC] * n_hbm
        in_specs += [VMEM_SPEC] * (len(arrays) - n_left)
        pinned = [
            pltpu.with_memory_space_constraint(a, pltpu.HBM) if n < n_left or n in hold else a
            for n, a in enumerate(arrays)
        ]
        results = pl.pallas_call(
            kernel,
            out_shape=[placed(n, a) for n, a in enumerate(outs)],
            in_specs=in_specs,
            out_specs=[spec(n, a) for n, a in enumerate(outs)],
            scratch_shapes=list(scratch),
            compiler_params=pltpu.CompilerParams(vmem_limit_bytes=held + 6 * 2**20),
            cost_estimate=pl.CostEstimate(
                flops=us * 10**9, bytes_accessed=2**20, transcendentals=0
            ),
            name=name,
        )(*pinned)
        return results if isinstance(out_shape, (tuple, list)) else results[0]

    return run


def prepare(n_seq, place_ref, *refs):
    key, value, query, grad, table_hbm, kv_keep, kv_send, q_keep, q_send = refs[:9]
    key_here, table, query_here, kept, sems = refs[9:]
    group, member, core = here(n_seq)
    width = HEADS // CORES * HEAD_DIM
    started = []

    def start(source, place):
        copy = pltpu.make_async_copy(source, place, sems.at[len(started)])
        copy.start()
        started.append(copy)
        return copy

    def columns(first, count=1):
        return pl.ds(pl.multiple_of(first * HEAD_DIM, HEAD_DIM), count * HEAD_DIM)

    waits = [start(key, key_here), start(table_hbm, table)]
    halves = (1 - core, core)
    loads = []
    for n, half in enumerate(halves):
        loads.append(start(query.at[:, columns(half * (HEADS // CORES), HEADS // CORES)], query_here.at[n]))
    late = []
    for half, kv_out, q_out in ((halves[0], kv_send, q_send), (halves[1], kv_keep, q_keep)):
        for h in range(HALF_KV):
            head = half * HALF_KV + h
            late.append(start(value.at[:, columns(head)], kv_out.at[1, h]))
            for r in range(RATIO):
                late.append(start(grad.at[:, columns(head * RATIO + r)], q_out.at[1, h, r]))
    for copy in waits:
        copy.wait()
    cosine, sine = block_tables(place_ref[group * n_seq + member], table)
    for half, out in ((halves[0], kv_send), (halves[1], kv_keep)):
        for h in range(HALF_KV):
            part = key_here[:, columns(half * HALF_KV + h)]
            out[0, h] = turn(part.astype(F32), cosine, sine).astype(BF16)
    for n, out in enumerate((q_send.at[0], kept)):
        loads[n].wait()
        for h in range(HALF_KV):
            for r in range(RATIO):
                at = (h * RATIO + r) * HEAD_DIM
                part = query_here[n, :, at : at + HEAD_DIM].astype(F32)
                out[h, r] = turn(part, cosine, sine).astype(BF16)
    late.append(start(kept, q_keep.at[0]))
    for copy in late:
        copy.wait()


def make_lists(n_seq, split, key_blocks, key_counts, lists, counts):
    group, member, _ = here(n_seq)
    for i in range(2):
        block = group * n_seq + lax.bitwise_xor(member, i)
        for section in range(3):
            counts[i, section] = int(section == 1)
        lists[i, 1, 0] = i

        def look(j, _):
            place = lax.bitwise_xor(key_blocks[block, j] - (group - 1) * n_seq, member)
            section = (place >= n_seq).astype(jnp.int32)
            section += (place >= n_seq + split).astype(jnp.int32)
            n = counts[i, section]
            lists[i, section, n] = place - jnp.where(section == 0, 0, n_seq) - jnp.where(
                section == 2, split, 0
            )
            counts[i, section] = n + 1
            return 0

        lax.fori_loop(1, key_counts[block], look, 0)
        total = 0
        for section, base in enumerate((0, n_seq, n_seq + split)):

            def append(n, m):
                lists[i, 3, m] = lists[i, section, n] + base
                return m + 1

            total = lax.fori_loop(0, counts[i, section], append, jnp.int32(total))
        counts[i, 3] = total
        lists[i, 3, total] = 0


def causal():
    keys = lax.broadcasted_iota(jnp.int32, (BLK, CHUNK), 0)
    tokens = lax.rem(lax.broadcasted_iota(jnp.int32, (BLK, CHUNK), 1), BLK)
    return keys <= tokens


def chunks():
    per = CHUNK // BLK
    return [
        (slice(c * per, (c + 1) * per), slice(c * CHUNK, (c + 1) * CHUNK))
        for c in range(ROWS // CHUNK)
    ]


def heads_of(block, what, h, rows):
    return block[what, h, rows].reshape(CHUNK, HEAD_DIM)


def fill(store, pieces, first=0):
    for k, piece in enumerate(pieces):
        store[first + CORES * k : first + CORES * (k + 1)] = piece[...]


def pair_scores(store, e, h, block, rows, diagonal):
    scores = dot_nt(store[e, 0, h], heads_of(block, 0, h, rows))
    if diagonal:
        scores = jnp.where(causal(), scores, -1e30)
    return scores, dot_nt(store[e, 1, h], heads_of(block, 1, h, rows))


def gather_stats(store, e, block, stats, i, diagonal, kept=None):
    for h in range(HALF_KV):
        for rows, columns in chunks():
            scores, dprobs = pair_scores(store, e, h, block, rows, diagonal)
            if kept is not None:
                n, kept_scores, kept_dprobs = kept
                kept_scores[n, h, :, columns] = scores
                kept_dprobs[n, h, :, columns] = dprobs
            top = jnp.max(scores, axis=0, keepdims=True)
            if not diagonal:
                old_top = stats[i, h, 0:1, columns]
                top = jnp.maximum(top, old_top)
            weights = jnp.exp2((scores - top) * TO_LOG2)
            total = jnp.sum(weights, axis=0, keepdims=True)
            mixed = jnp.sum(weights * dprobs, axis=0, keepdims=True)
            if not diagonal:
                shrink = jnp.exp2((old_top - top) * TO_LOG2)
                total += stats[i, h, 1:2, columns] * shrink
                mixed += stats[i, h, 2:3, columns] * shrink
            stats[i, h, 0:1, columns] = top
            stats[i, h, 1:2, columns] = total
            stats[i, h, 2:3, columns] = mixed


def spread_grads(found, count, kept_scores, kept_dprobs, stats, i, block, acc, saved, low, sent):
    def copy(n):
        return pltpu.make_async_copy(low.at[n], saved.at[i, n], sent.at[n])

    def add(n, _):
        e = found[n]
        for h in range(HALF_KV):
            dk, dv = acc[e, 0, h], acc[e, 1, h]
            for rows, columns in chunks():
                probs = jnp.exp2(
                    kept_scores[n, h, :, columns] * TO_LOG2 - stats[i, h, 0:1, columns]
                )
                dscores = probs * (kept_dprobs[n, h, :, columns] - stats[i, h, 2:3, columns])
                probs, dscores = probs.astype(BF16), dscores.astype(BF16)
                low[n, h, 0, :, columns] = probs
                low[n, h, 1, :, columns] = dscores
                dv += dot_nn(probs, heads_of(block, 1, h, rows))
                dk += dot_nn(dscores, heads_of(block, 0, h, rows))
            acc[e, 0, h] = dk
            acc[e, 1, h] = dv
        copy(n).start()
        return 0

    def finish(n, _):
        copy(n).wait()
        return 0

    lax.fori_loop(0, count, add, 0)
    lax.fori_loop(0, count, finish, 0)


def write_grads(acc, outs):
    start = 0
    for out in outs:
        part = slice(start, start + out.shape[0])
        out[:, 0] = (acc[part, 0] * SCALE).astype(out.dtype)
        out[:, 1] = acc[part, 1].astype(out.dtype)
        start += out.shape[0]


def current_stats(section, lists, counts, own, other, *rest):
    *pieces, stats, store = rest
    first = section == 1
    if not first:
        stats_in, *pieces = pieces
        stats[...] = stats_in[...]
    fill(store, pieces)
    for i, block in enumerate((own, other)):
        if first:
            gather_stats(store, i, block, stats, i, True)

        def step(n, _):
            gather_stats(store, lists[i, section, n], block, stats, i, False)
            return 0

        lax.fori_loop(int(first), counts[i, section], step, 0)


def previous_grads(n_pieces, lists, counts, own, other, stats_in, *rest):
    n_ends = 2 * n_pieces - 1
    pieces, outs = rest[:n_pieces], rest[n_pieces:n_ends]
    saved, stats, store, acc, low, sent, kept_scores, kept_dprobs = rest[n_ends:]
    fill(store, pieces)
    acc[...] = jnp.zeros_like(acc)
    stats[...] = stats_in[...]
    for i, block in enumerate((own, other)):
        count = counts[i, 0]

        def look(n, _):
            gather_stats(
                store, lists[i, 0, n], block, stats, i, False, (n, kept_scores, kept_dprobs)
            )
            return 0

        lax.fori_loop(0, count, look, 0)
        for h in range(HALF_KV):
            total = stats[i, h, 1:2, :]
            stats[i, h, 0:1, :] = stats[i, h, 0:1, :] * TO_LOG2 + jnp.log2(total)
            stats[i, h, 2:3, :] = stats[i, h, 2:3, :] / total

        def copy(n):
            return pltpu.make_async_copy(low.at[n], saved.at[i, n], sent.at[n])

        def add(n, _):
            e = lists[i, 0, n]
            for h in range(HALF_KV):
                dk, dv = acc[e, 0, h], acc[e, 1, h]
                for rows, columns in chunks():
                    probs = jnp.exp2(
                        kept_scores[n, h, :, columns] * TO_LOG2 - stats[i, h, 0:1, columns]
                    )
                    dscores = probs * (kept_dprobs[n, h, :, columns] - stats[i, h, 2:3, columns])
                    probs, dscores = probs.astype(BF16), dscores.astype(BF16)
                    low[n, h, 0, :, columns] = probs
                    low[n, h, 1, :, columns] = dscores
                    dv += dot_nn(probs, heads_of(block, 1, h, rows))
                    dk += dot_nn(dscores, heads_of(block, 0, h, rows))
                acc[e, 0, h] = dk
                acc[e, 1, h] = dv
            copy(n).start()
            return 0

        def finish(n, _):
            copy(n).wait()
            return 0

        lax.fori_loop(0, count, add, 0)
        lax.fori_loop(0, count, finish, 0)
    write_grads(acc, outs)


def current_grads(section, n_pieces, lists, counts, own, other, stats, *rest):
    pieces, outs = rest[:n_pieces], rest[n_pieces : 2 * n_pieces]
    saved, store, acc, low, sent = rest[2 * n_pieces :]
    first = section == 1
    fill(store, pieces)
    acc[...] = jnp.zeros_like(acc)
    for i, block in enumerate((own, other)):
        count = counts[i, section]

        def copy(n):
            return pltpu.make_async_copy(low.at[n], saved.at[i, n], sent.at[n])

        def look(n, diagonal):
            e = lists[i, section, n]
            for h in range(HALF_KV):
                for rows, columns in chunks():
                    scores, dprobs = pair_scores(store, e, h, block, rows, diagonal)
                    probs = jnp.exp2(scores * TO_LOG2 - stats[i, h, 0:1, columns])
                    low[n, h, 0, :, columns] = probs.astype(BF16)
                    dscores = probs * (dprobs - stats[i, h, 2:3, columns])
                    low[n, h, 1, :, columns] = dscores.astype(BF16)
            copy(n).start()
            return 0

        def add(n, _):
            e = lists[i, section, n]
            for h in range(HALF_KV):
                for w in range(2):
                    right = block[1 - w, h].reshape(ROWS, HEAD_DIM)
                    acc[e, 1 - w, h] += dot_nn(low[n, h, w], right)
            return 0

        def finish(n, _):
            copy(n).wait()
            return 0

        if first:
            look(0, True)
        lax.fori_loop(int(first), count, lambda n, _: look(n, False), 0)
        lax.fori_loop(0, count, add, 0)
        lax.fori_loop(0, count, finish, 0)
    write_grads(acc, outs)


def query_results(n_seq, lists, counts, place_ref, *rest):
    n_saved = 3
    n_pieces = n_seq // CORES
    saved, pieces, rest = rest[:n_saved], rest[n_saved:][: 2 * n_pieces], rest[n_saved + 2 * n_pieces :]
    table, *rest = rest
    outs, (store, low, out_acc, dq_acc, got) = rest[: 2 * HALF_KV], rest[2 * HALF_KV :]
    group, member, _ = here(n_seq)

    def copy(source, h, i, n, first):
        return pltpu.make_async_copy(source.at[i, n - first, h], low.at[h, i, n], got.at[h, i, n])

    ends = []
    for i in range(2):
        stops = [0]
        for section in range(n_saved):
            stops.append(stops[-1] + counts[i, section])
        ends.append(stops)
    for h in range(HALF_KV):
        for i, stops in enumerate(ends):
            for source, first, stop in zip(saved, stops, stops[1:]):

                def fetch_one(n, _):
                    copy(source, h, i, n, first).start()
                    return 0

                lax.fori_loop(first, stop, fetch_one, 0)
    fill(store, pieces)
    tables = []
    for i in range(2):
        mine = group * n_seq + lax.bitwise_xor(member, i)
        cosine, sine = block_tables(place_ref[mine], table)
        tables.append((cosine.T * SCALE, sine.T * SCALE))
    for h, (i, stops) in ((h, pair) for h in range(HALF_KV) for pair in enumerate(ends)):
        total = stops[-1]
        result = outs[i * HALF_KV + h]

        @pl.when(lax.rem(total, 2) == 1)
        def _():
            low[h, i, total] = jnp.zeros((2, BLK, ROWS), BF16)

        out_acc[...] = jnp.zeros_like(out_acc)
        dq_acc[...] = jnp.zeros_like(dq_acc)

        def add(n, _):
            pair = (2 * n, 2 * n + 1)
            for m in pair:
                for source, first, stop in zip(saved, stops, stops[1:]):

                    @pl.when(jnp.logical_and(m >= first, m < stop))
                    def _():
                        copy(source, h, i, m, first).wait()

            found = [lists[i, 3, m] for m in pair]
            keys_t = jnp.concatenate([store[e, 0, h].T for e in found], axis=1)
            values_t = jnp.concatenate([store[e, 1, h].T for e in found], axis=1)
            for _, columns in chunks():
                probs = jnp.concatenate([low[h, i, m, 0, :, columns] for m in pair], axis=0)
                dscores = jnp.concatenate([low[h, i, m, 1, :, columns] for m in pair], axis=0)
                out_acc[:, columns] += dot_nn(values_t, probs)
                dq_acc[:, columns] += dot_nn(keys_t, dscores)
            return 0

        lax.fori_loop(0, lax.div(total + 1, 2), add, 0)
        cosine, sine = tables[i]
        for r in range(RATIO):
            rows = slice(r * BLK, (r + 1) * BLK)
            columns = slice(r * HEAD_DIM, (r + 1) * HEAD_DIM)
            result[0, :, columns] = out_acc[:, rows].astype(BF16).T
            dq = dq_acc[:, rows]
            half = HEAD_DIM // 2
            turned = jnp.concatenate([dq[half:], dq[:half]], axis=0)
            result[1, :, columns] = (dq * cosine - turned * sine).astype(BF16).T


def finish_kv(n_seq, place_ref, *rest):
    *terms, table, keep, send = rest
    group, member, _ = here(n_seq)
    for i, result in enumerate((keep, send)):
        offset = lax.bitwise_xor(member, i)
        cosine, sine = block_tables(place_ref[group * n_seq + offset], table)
        for h in range(HALF_KV):
            columns = slice(h * HEAD_DIM, (h + 1) * HEAD_DIM)
            dk, dv = (sum(term[i, w, h].astype(F32) for term in terms) for w in range(2))
            result[0, :, columns] = turn(dk, cosine, -sine).astype(BF16)
            result[1, :, columns] = dv.astype(BF16)


def join_halves(*refs):
    core = lax.rem(lax.axis_index("seq"), CORES)
    own_q, got_q, (own_kv, got_kv) = refs[:HALF_KV], refs[HALF_KV:][:HALF_KV], refs[2 * HALF_KV :][:2]
    outs = refs[2 * HALF_KV + 2 :]
    for own, got, results in ((own_q, got_q, outs[:2]), ([own_kv], [got_kv], outs[2:])):
        width = own[0].shape[-1]
        for half, parts in ((core, own), (1 - core, got)):
            for n, part in enumerate(parts):
                start = pl.multiple_of((half * len(parts) + n) * width, width)
                for w, out in enumerate(results):
                    out[:, pl.ds(start, width)] = part[w]


def local(query_input, key_input, value_input, out_grad, key_blocks, key_counts, block_position):
    n_seq = lax.axis_size("seq")
    n_grp = lax.axis_size("grp")
    n_pieces = n_seq // CORES
    n_listed = key_blocks.shape[1]

    def cross(array, by):
        return lax.ppermute(array, "seq", [(m, m ^ by) for m in range(n_seq)])

    def along(array, by):
        return cross(array, CORES * by)

    def onward(array):
        return lax.ppermute(array, "grp", [(g, g + 1) for g in range(n_grp - 1)])

    def back(array):
        return lax.ppermute(array, "grp", [(g + 1, g) for g in range(n_grp - 1)])

    table = trig_table(block_position.shape[0])
    n_far = min(n_seq, n_listed - 1)
    split = 2 * CORES
    piece = (2, HALF_KV, BLK, HEAD_DIM)
    chip = (CORES, *piece)
    q_shape = jax.ShapeDtypeStruct((2, HALF_KV, RATIO, BLK, HEAD_DIM), BF16)
    kv_shape = jax.ShapeDtypeStruct(piece, BF16)
    stats_shape = jax.ShapeDtypeStruct((2, HALF_KV, 8, ROWS), F32)
    low = jax.ShapeDtypeStruct(chip, BF16)
    high = jax.ShapeDtypeStruct(chip, F32)
    lists, counts = call(
        functools.partial(make_lists, n_seq, split),
        (
            jax.ShapeDtypeStruct((2, 4, n_listed + 1), jnp.int32),
            jax.ShapeDtypeStruct((2, 4), jnp.int32),
        ),
        2, us=2, name="block_lists",
    )(key_blocks, key_counts)

    tokens = query_input.shape[0]
    n_copies = 5 + 2 * HALF_KV * (1 + RATIO)
    kv_keep, kv_send, q_keep, q_send = call(
        functools.partial(prepare, n_seq), (kv_shape, kv_shape, q_shape, q_shape), 1,
        [
            pltpu.VMEM(key_input.shape, BF16), pltpu.VMEM(table.shape, F32),
            pltpu.VMEM((CORES, tokens, HEADS // CORES * HEAD_DIM), BF16),
            pltpu.VMEM(q_shape.shape[1:], BF16), pltpu.SemaphoreType.DMA((n_copies,)),
        ],
        us=3, name="prepare", n_hbm=5, hbm_out=2,
    )(block_position, key_input, value_input, query_input, out_grad, table)
    kv_got = cross(kv_send, 1)
    q_send, kv_got = lax.optimization_barrier((q_send, kv_got))
    q_got = cross(q_send, 1)
    near = [jnp.stack([kv_keep, kv_got])]
    near.append(along(near[0], 1))
    ready, first_far = lax.optimization_barrier((near[1], onward(near[0])))
    far = [first_far, None]
    for k in range(2, n_pieces, 2):
        piece_k, lists, counts, _ = lax.optimization_barrier(
            (along(near[0], k), lists, counts, ready)
        )
        near += [piece_k, along(piece_k, 1)]
        far += [onward(piece_k), None]
    stats = call(
        functools.partial(current_stats, 1), stats_shape, 2, [pltpu.VMEM((split, *piece), BF16)],
        us=4, name="near_statistics", hold=(2,),
    )(lists, counts, q_keep, q_got, *near[:2])
    ready, far[2], stats = lax.optimization_barrier((ready, far[2], stats))
    far[1] = onward(ready)
    for k in range(2, n_pieces, 2):
        far[k + 1] = along(far[k], 1)
    stats = call(
        functools.partial(current_stats, 2), stats_shape, 2,
        [pltpu.VMEM((n_seq - split, *piece), BF16)], us=4, name="far_statistics",
    )(lists, counts, q_keep, q_got, stats, *near[2:])

    def grads_call(kernel, n_slots, n_store, outs, us, name, kept=(), more=()):
        pair = (n_slots, HALF_KV, 2, BLK, ROWS)
        saved = jax.ShapeDtypeStruct((2, *pair), BF16)
        return call(
            kernel, (*outs, saved, *more), 2,
            [
                pltpu.VMEM((n_store, *piece), BF16), pltpu.VMEM((n_store, *piece), F32),
                pltpu.VMEM(pair, BF16), pltpu.SemaphoreType.DMA((n_slots,)), *kept,
            ],
            us=us, name=name, hbm_out=len(outs),
        )

    kept = pltpu.VMEM((n_far, HALF_KV, BLK, ROWS), F32)
    two = jax.ShapeDtypeStruct((2 * CORES, *piece), BF16)
    first_far, *far_grads, far_saved, stats = grads_call(
        functools.partial(previous_grads, n_pieces), n_far, n_seq, (two,) + (low,) * (n_pieces - 2),
        14, "previous_gradients", (kept, kept), (stats_shape,),
    )(lists, counts, q_keep, q_got, stats, *far)

    def current_call(section, outs, name, pieces, after):
        stats_late, _ = lax.optimization_barrier((stats, after))
        n_store = CORES * len(pieces)
        *grads, saved = grads_call(
            functools.partial(current_grads, section, len(pieces)), min(n_store, n_listed), n_store,
            outs, 6, name,
        )(lists, counts, q_keep, q_got, stats_late, *pieces)
        return grads, saved

    def total(*terms):
        return sum(term.astype(F32) for term in terms).astype(BF16)

    from_far = back(first_far)
    crossing = [along(grad, 1) for grad in far_grads[1::2]]
    high_grads, high_saved = current_call(
        2, [high, low] * (n_pieces // 2 - 1), "far_current_gradients", near[2:], far_grads[0]
    )
    crossing, high_grads = lax.optimization_barrier((crossing, high_grads))
    arrived = [
        back(total(grad, extra)) for grad, extra in zip(far_grads[0::2], crossing)
    ]
    swapped = [along(grad, 1) for grad in high_grads[1::2]]
    low_grads, low_saved = current_call(
        1, [high, high], "near_current_gradients", near[:2], high_grads[0]
    )
    low_grads, from_far = lax.optimization_barrier((low_grads, from_far))
    from_next = along(total(low_grads[1], from_far[CORES:]), 1)
    merged = [
        total(*terms) for terms in zip(high_grads[0::2], arrived, swapped)
    ]
    half_out = jax.ShapeDtypeStruct((2, BLK, RATIO * HEAD_DIM), BF16)
    place_late, _ = lax.optimization_barrier((block_position, merged))
    wide = pltpu.VMEM((HEAD_DIM, ROWS), F32)
    slots = (HALF_KV, 2, n_listed + 1)
    halves = call(
        functools.partial(query_results, n_seq), (half_out,) * (2 * HALF_KV), 3,
        [
            pltpu.VMEM((2 * n_seq, *piece), BF16), pltpu.VMEM((*slots, 2, BLK, ROWS), BF16),
            wide, wide, pltpu.SemaphoreType.DMA(slots),
        ],
        us=20, name="query_results", n_hbm=3,
    )(lists, counts, place_late, far_saved, low_saved, high_saved, *far, *near, table)
    own_halves, other_halves = halves[:HALF_KV], halves[HALF_KV:]
    other_halves = lax.optimization_barrier(list(other_halves))
    got_halves = [cross(half, 1) for half in other_halves]
    final = [low_grads[0], from_far[:CORES], from_next]
    final += [along(part, 2 + 2 * n) for n, part in enumerate(merged)]
    own_halves = list(own_halves)
    final[0], own_halves[1] = lax.optimization_barrier((final[0], own_halves[1]))
    kv_half = jax.ShapeDtypeStruct((2, BLK, HALF_KV * HEAD_DIM), BF16)
    own_kv, other_kv = call(
        functools.partial(finish_kv, n_seq), (kv_half, kv_half), 1, us=2, name="key_gradients"
    )(block_position, *final, table)
    got_kv = cross(other_kv, 1)
    q_out = jax.ShapeDtypeStruct(query_input.shape, BF16)
    kv_out = jax.ShapeDtypeStruct(key_input.shape, BF16)
    out_rows, query_grad, key_grad, value_grad = call(
        join_halves, (q_out, q_out, kv_out, kv_out), 0, us=2, name="join_halves"
    )(*own_halves, *got_halves, own_kv, got_kv)
    return (out_rows, query_grad, key_grad, value_grad)


def solution(mesh):
    split = P(("grp", "seq"), None)
    return jax.shard_map(
        local,
        mesh=mesh,
        in_specs=(split, split, split, split, P(), P(), P()),
        out_specs=(split, split, split, split),
        check_vma=False,
    )
```

```python
import functools
import math

import jax
import jax.numpy as jnp
import numpy as np
from jax import lax
from jax.experimental import pallas as pl
from jax.experimental.pallas import tpu as pltpu
from jax.sharding import PartitionSpec as P

HEADS = 32
KV_HEADS = 4
HEAD_DIM = 128
BLK = 128
CORES = 2
RATIO = HEADS // KV_HEADS
HALF_KV = KV_HEADS // CORES
ROWS = RATIO * BLK
SCALE = 1.0 / math.sqrt(HEAD_DIM)
TO_LOG2 = SCALE * math.log2(math.e)
F32 = jnp.float32
BF16 = jnp.bfloat16
CHUNK = 256

VMEM_SPEC = pl.BlockSpec(memory_space=pltpu.VMEM)
HBM_SPEC = pl.BlockSpec(memory_space=pltpu.HBM)
SMEM_SPEC = pl.BlockSpec(memory_space=pltpu.SMEM)


def trig_table(n_blocks):
    half = HEAD_DIM // 2
    frequency = np.power(500000.0, -np.arange(half) * (2.0 / HEAD_DIM))
    parts = []
    for places in (np.arange(n_blocks) * BLK, np.arange(BLK)):
        angles = places[:, None] * frequency
        for part in (np.cos(angles), np.sin(angles)):
            parts.append(np.concatenate([part, part], axis=1))
    return np.concatenate(parts, axis=0).astype(np.float32)


def block_tables(place, table):
    n_blocks = table.shape[0] // 2 - BLK
    cos_b = table[pl.ds(place, 1), :]
    sin_b = table[pl.ds(n_blocks + place, 1), :]
    cos_t = table[2 * n_blocks : 2 * n_blocks + BLK, :]
    sin_t = table[2 * n_blocks + BLK :, :]
    cosine = cos_b * cos_t - sin_b * sin_t
    sine = sin_b * cos_t + cos_b * sin_t
    lanes = lax.broadcasted_iota(jnp.int32, sine.shape, 1)
    return cosine, jnp.where(lanes < HEAD_DIM // 2, -sine, sine)


def turn(values, cosine, signed_sine):
    return values * cosine + pltpu.roll(values, HEAD_DIM // 2, 1) * signed_sine


def dot_nt(a, b):
    return lax.dot_general(a, b, (((1,), (1,)), ((), ())), preferred_element_type=F32)


def dot_nn(a, b):
    return lax.dot_general(a, b, (((1,), (0,)), ((), ())), preferred_element_type=F32)


def here(n_seq):
    member = lax.axis_index("seq")
    group = lax.axis_index("grp")
    return group, member, lax.rem(member, CORES)


def size_of(array):
    return math.prod(array.shape) * jnp.dtype(array.dtype).itemsize


def call(kernel, out_shape, n_smem, scratch=(), us=1, name=None, n_hbm=0, hbm_out=None, hold=()):
    def placed(n, a):
        if n == hbm_out:
            return pltpu.HBM(a.shape, a.dtype)
        return a

    def spec(n, a):
        if a.dtype == jnp.int32:
            return SMEM_SPEC
        return HBM_SPEC if n == hbm_out else VMEM_SPEC

    def run(*arrays):
        n_left = n_smem + n_hbm
        outs = list(out_shape) if isinstance(out_shape, (tuple, list)) else [out_shape]
        held = sum(size_of(a) for a in arrays[n_left:])
        held += sum(size_of(a) for n, a in enumerate(outs) if n != hbm_out)
        held += sum(size_of(a) for a in scratch if a.dtype in (F32, BF16))
        in_specs = [SMEM_SPEC] * n_smem + [HBM_SPEC] * n_hbm
        in_specs += [VMEM_SPEC] * (len(arrays) - n_left)
        pinned = [
            pltpu.with_memory_space_constraint(a, pltpu.HBM) if n < n_left or n in hold else a
            for n, a in enumerate(arrays)
        ]
        results = pl.pallas_call(
            kernel,
            out_shape=[placed(n, a) for n, a in enumerate(outs)],
            in_specs=in_specs,
            out_specs=[spec(n, a) for n, a in enumerate(outs)],
            scratch_shapes=list(scratch),
            compiler_params=pltpu.CompilerParams(vmem_limit_bytes=held + 6 * 2**20),
            cost_estimate=pl.CostEstimate(
                flops=us * 10**9, bytes_accessed=2**20, transcendentals=0
            ),
            name=name,
        )(*pinned)
        return results if isinstance(out_shape, (tuple, list)) else results[0]

    return run


def prepare(n_seq, place_ref, *refs):
    key, value, query, grad, table_hbm, kv_keep, kv_send, q_keep, q_send = refs[:9]
    key_here, value_here, table, query_here, grad_here, kept, sems = refs[9:]
    group, member, core = here(n_seq)
    half_heads = HEADS // CORES
    halves = (1 - core, core)

    def copy(n, source, place):
        return pltpu.make_async_copy(source, place, sems.at[n])

    def columns(first, count=1):
        return pl.ds(pl.multiple_of(first * HEAD_DIM, HEAD_DIM), count * HEAD_DIM)

    loads = [copy(0, key, key_here), copy(1, table_hbm, table), copy(2, value, value_here)]
    for n, half in enumerate(halves):
        part = columns(half * half_heads, half_heads)
        loads.append(copy(3 + 2 * n, query.at[:, part], query_here.at[n]))
        loads.append(copy(4 + 2 * n, grad.at[:, part], grad_here.at[n]))
    for load in loads:
        load.start()
    for load in loads[:3]:
        load.wait()
    cosine, sine = block_tables(place_ref[group * n_seq + member], table)
    for half, out in zip(halves, (kv_send, kv_keep)):
        for h in range(HALF_KV):
            at = columns(half * HALF_KV + h)
            out[0, h] = turn(key_here[:, at].astype(F32), cosine, sine).astype(BF16)
            out[1, h] = value_here[:, at]
    for n, out in enumerate((q_send, kept)):
        loads[3 + 2 * n].wait()
        loads[4 + 2 * n].wait()
        for h in range(HALF_KV):
            for r in range(RATIO):
                at = slice((h * RATIO + r) * HEAD_DIM, (h * RATIO + r + 1) * HEAD_DIM)
                part = query_here[n, :, at].astype(F32)
                out[0, h, r] = turn(part, cosine, sine).astype(BF16)
                out[1, h, r] = grad_here[n, :, at]
    away = copy(7, kept, q_keep)
    away.start()
    away.wait()


def make_lists(n_seq, split, key_blocks, key_counts, lists, counts):
    group, member, _ = here(n_seq)
    for i in range(2):
        block = group * n_seq + lax.bitwise_xor(member, i)
        for section in range(3):
            counts[i, section] = int(section == 1)
        lists[i, 1, 0] = i

        def look(j, _):
            place = lax.bitwise_xor(key_blocks[block, j] - (group - 1) * n_seq, member)
            section = (place >= n_seq).astype(jnp.int32)
            section += (place >= n_seq + split).astype(jnp.int32)
            n = counts[i, section]
            lists[i, section, n] = place - jnp.where(section == 0, 0, n_seq) - jnp.where(
                section == 2, split, 0
            )
            counts[i, section] = n + 1
            return 0

        lax.fori_loop(1, key_counts[block], look, 0)
        total = 0
        for section, base in enumerate((0, n_seq, n_seq + split)):

            def append(n, m):
                lists[i, 3, m] = lists[i, section, n] + base
                return m + 1

            total = lax.fori_loop(0, counts[i, section], append, jnp.int32(total))
        counts[i, 3] = total
        lists[i, 3, total] = 0


def causal():
    keys = lax.broadcasted_iota(jnp.int32, (BLK, CHUNK), 0)
    tokens = lax.rem(lax.broadcasted_iota(jnp.int32, (BLK, CHUNK), 1), BLK)
    return keys <= tokens


def chunks():
    per = CHUNK // BLK
    return [
        (slice(c * per, (c + 1) * per), slice(c * CHUNK, (c + 1) * CHUNK))
        for c in range(ROWS // CHUNK)
    ]


def heads_of(block, what, h, rows):
    return block[what, h, rows].reshape(CHUNK, HEAD_DIM)


def fill(store, pieces, first=0):
    for k, piece in enumerate(pieces):
        store[first + CORES * k : first + CORES * (k + 1)] = piece[...]


def pair_scores(store, e, h, block, rows, diagonal):
    scores = dot_nt(store[e, 0, h], heads_of(block, 0, h, rows))
    if diagonal:
        scores = jnp.where(causal(), scores, -1e30)
    return scores, dot_nt(store[e, 1, h], heads_of(block, 1, h, rows))


def gather_stats(store, e, block, stats, i, diagonal, kept=None):
    for h in range(HALF_KV):
        for rows, columns in chunks():
            scores, dprobs = pair_scores(store, e, h, block, rows, diagonal)
            if kept is not None:
                n, kept_scores, kept_dprobs = kept
                kept_scores[n, h, :, columns] = scores
                kept_dprobs[n, h, :, columns] = dprobs
            top = jnp.max(scores, axis=0, keepdims=True)
            if not diagonal:
                old_top = stats[i, h, 0:1, columns]
                top = jnp.maximum(top, old_top)
            weights = jnp.exp2((scores - top) * TO_LOG2)
            total = jnp.sum(weights, axis=0, keepdims=True)
            mixed = jnp.sum(weights * dprobs, axis=0, keepdims=True)
            if not diagonal:
                shrink = jnp.exp2((old_top - top) * TO_LOG2)
                total += stats[i, h, 1:2, columns] * shrink
                mixed += stats[i, h, 2:3, columns] * shrink
            stats[i, h, 0:1, columns] = top
            stats[i, h, 1:2, columns] = total
            stats[i, h, 2:3, columns] = mixed


def spread_grads(found, count, kept_scores, kept_dprobs, stats, i, block, acc, saved, low, sent):
    def copy(n):
        return pltpu.make_async_copy(low.at[n], saved.at[i, n], sent.at[n])

    def add(n, _):
        e = found[n]
        for h in range(HALF_KV):
            dk, dv = acc[e, 0, h], acc[e, 1, h]
            for rows, columns in chunks():
                probs = jnp.exp2(
                    kept_scores[n, h, :, columns] * TO_LOG2 - stats[i, h, 0:1, columns]
                )
                dscores = probs * (kept_dprobs[n, h, :, columns] - stats[i, h, 2:3, columns])
                probs, dscores = probs.astype(BF16), dscores.astype(BF16)
                low[n, h, 0, :, columns] = probs
                low[n, h, 1, :, columns] = dscores
                dv += dot_nn(probs, heads_of(block, 1, h, rows))
                dk += dot_nn(dscores, heads_of(block, 0, h, rows))
            acc[e, 0, h] = dk
            acc[e, 1, h] = dv
        copy(n).start()
        return 0

    def finish(n, _):
        copy(n).wait()
        return 0

    lax.fori_loop(0, count, add, 0)
    lax.fori_loop(0, count, finish, 0)


def write_grads(acc, outs):
    start = 0
    for out in outs:
        part = slice(start, start + out.shape[0])
        out[:, 0] = (acc[part, 0] * SCALE).astype(out.dtype)
        out[:, 1] = acc[part, 1].astype(out.dtype)
        start += out.shape[0]


def current_stats(section, lists, counts, own, other, *rest):
    *pieces, stats, store = rest
    first = section == 1
    if not first:
        stats_in, *pieces = pieces
        stats[...] = stats_in[...]
    fill(store, pieces)
    for i, block in enumerate((own, other)):
        if first:
            gather_stats(store, i, block, stats, i, True)

        def step(n, _):
            gather_stats(store, lists[i, section, n], block, stats, i, False)
            return 0

        lax.fori_loop(int(first), counts[i, section], step, 0)


def previous_grads(n_pieces, lists, counts, own, other, stats_in, *rest):
    n_ends = 2 * n_pieces - 1
    pieces, outs = rest[:n_pieces], rest[n_pieces:n_ends]
    saved, stats, store, acc, low, sent, kept_scores, kept_dprobs = rest[n_ends:]
    fill(store, pieces)
    acc[...] = jnp.zeros_like(acc)
    stats[...] = stats_in[...]
    for i, block in enumerate((own, other)):
        count = counts[i, 0]

        def look(n, _):
            gather_stats(
                store, lists[i, 0, n], block, stats, i, False, (n, kept_scores, kept_dprobs)
            )
            return 0

        lax.fori_loop(0, count, look, 0)
        for h in range(HALF_KV):
            total = stats[i, h, 1:2, :]
            stats[i, h, 0:1, :] = stats[i, h, 0:1, :] * TO_LOG2 + jnp.log2(total)
            stats[i, h, 2:3, :] = stats[i, h, 2:3, :] / total

        def copy(n):
            return pltpu.make_async_copy(low.at[n], saved.at[i, n], sent.at[n])

        def add(n, _):
            e = lists[i, 0, n]
            for h in range(HALF_KV):
                dk, dv = acc[e, 0, h], acc[e, 1, h]
                for rows, columns in chunks():
                    probs = jnp.exp2(
                        kept_scores[n, h, :, columns] * TO_LOG2 - stats[i, h, 0:1, columns]
                    )
                    dscores = probs * (kept_dprobs[n, h, :, columns] - stats[i, h, 2:3, columns])
                    probs, dscores = probs.astype(BF16), dscores.astype(BF16)
                    low[n, h, 0, :, columns] = probs
                    low[n, h, 1, :, columns] = dscores
                    dv += dot_nn(probs, heads_of(block, 1, h, rows))
                    dk += dot_nn(dscores, heads_of(block, 0, h, rows))
                acc[e, 0, h] = dk
                acc[e, 1, h] = dv
            copy(n).start()
            return 0

        def finish(n, _):
            copy(n).wait()
            return 0

        lax.fori_loop(0, count, add, 0)
        lax.fori_loop(0, count, finish, 0)
    write_grads(acc, outs)


def current_grads(section, n_pieces, lists, counts, own, other, stats, *rest):
    pieces, outs = rest[:n_pieces], rest[n_pieces : 2 * n_pieces]
    saved, store, acc, low, sent = rest[2 * n_pieces :]
    first = section == 1
    fill(store, pieces)
    acc[...] = jnp.zeros_like(acc)
    for i, block in enumerate((own, other)):
        count = counts[i, section]

        def copy(n):
            return pltpu.make_async_copy(low.at[n], saved.at[i, n], sent.at[n])

        def look(n, diagonal):
            e = lists[i, section, n]
            for h in range(HALF_KV):
                for rows, columns in chunks():
                    scores, dprobs = pair_scores(store, e, h, block, rows, diagonal)
                    probs = jnp.exp2(scores * TO_LOG2 - stats[i, h, 0:1, columns])
                    low[n, h, 0, :, columns] = probs.astype(BF16)
                    dscores = probs * (dprobs - stats[i, h, 2:3, columns])
                    low[n, h, 1, :, columns] = dscores.astype(BF16)
            copy(n).start()
            return 0

        def add(n, _):
            e = lists[i, section, n]
            for h in range(HALF_KV):
                for w in range(2):
                    right = block[1 - w, h].reshape(ROWS, HEAD_DIM)
                    acc[e, 1 - w, h] += dot_nn(low[n, h, w], right)
            return 0

        def finish(n, _):
            copy(n).wait()
            return 0

        if first:
            look(0, True)
        lax.fori_loop(int(first), count, lambda n, _: look(n, False), 0)
        lax.fori_loop(0, count, add, 0)
        lax.fori_loop(0, count, finish, 0)
    write_grads(acc, outs)


def query_results(n_seq, lists, counts, place_ref, *rest):
    n_saved = 3
    n_pieces = n_seq // CORES
    saved, pieces, rest = rest[:n_saved], rest[n_saved:][: 2 * n_pieces], rest[n_saved + 2 * n_pieces :]
    table, *rest = rest
    outs, (store, low, out_acc, dq_acc, got) = rest[: 2 * HALF_KV], rest[2 * HALF_KV :]
    group, member, _ = here(n_seq)

    def copy(source, h, i, n, first):
        return pltpu.make_async_copy(source.at[i, n - first, h], low.at[h, i, n], got.at[h, i, n])

    ends = []
    for i in range(2):
        stops = [0]
        for section in range(n_saved):
            stops.append(stops[-1] + counts[i, section])
        ends.append(stops)
    for h in range(HALF_KV):
        for i, stops in enumerate(ends):
            for source, first, stop in zip(saved, stops, stops[1:]):

                def fetch_one(n, _):
                    copy(source, h, i, n, first).start()
                    return 0

                lax.fori_loop(first, stop, fetch_one, 0)
    fill(store, pieces)
    tables = []
    for i in range(2):
        mine = group * n_seq + lax.bitwise_xor(member, i)
        cosine, sine = block_tables(place_ref[mine], table)
        tables.append((cosine.T * SCALE, sine.T * SCALE))
    for h, (i, stops) in ((h, pair) for h in range(HALF_KV) for pair in enumerate(ends)):
        total = stops[-1]
        result = outs[i * HALF_KV + h]

        @pl.when(lax.rem(total, 2) == 1)
        def _():
            low[h, i, total] = jnp.zeros((2, BLK, ROWS), BF16)

        out_acc[...] = jnp.zeros_like(out_acc)
        dq_acc[...] = jnp.zeros_like(dq_acc)

        def add(n, _):
            pair = (2 * n, 2 * n + 1)
            for m in pair:
                for source, first, stop in zip(saved, stops, stops[1:]):

                    @pl.when(jnp.logical_and(m >= first, m < stop))
                    def _():
                        copy(source, h, i, m, first).wait()

            found = [lists[i, 3, m] for m in pair]
            keys_t = jnp.concatenate([store[e, 0, h].T for e in found], axis=1)
            values_t = jnp.concatenate([store[e, 1, h].T for e in found], axis=1)
            for _, columns in chunks():
                probs = jnp.concatenate([low[h, i, m, 0, :, columns] for m in pair], axis=0)
                dscores = jnp.concatenate([low[h, i, m, 1, :, columns] for m in pair], axis=0)
                out_acc[:, columns] += dot_nn(values_t, probs)
                dq_acc[:, columns] += dot_nn(keys_t, dscores)
            return 0

        lax.fori_loop(0, lax.div(total + 1, 2), add, 0)
        cosine, sine = tables[i]
        for r in range(RATIO):
            rows = slice(r * BLK, (r + 1) * BLK)
            columns = slice(r * HEAD_DIM, (r + 1) * HEAD_DIM)
            result[0, :, columns] = out_acc[:, rows].astype(BF16).T
            dq = dq_acc[:, rows]
            half = HEAD_DIM // 2
            turned = jnp.concatenate([dq[half:], dq[:half]], axis=0)
            result[1, :, columns] = (dq * cosine - turned * sine).astype(BF16).T


def finish_kv(n_seq, place_ref, *rest):
    *terms, table, keep, send = rest
    group, member, _ = here(n_seq)
    for i, result in enumerate((keep, send)):
        offset = lax.bitwise_xor(member, i)
        cosine, sine = block_tables(place_ref[group * n_seq + offset], table)
        for h in range(HALF_KV):
            columns = slice(h * HEAD_DIM, (h + 1) * HEAD_DIM)
            dk, dv = (sum(term[i, w, h].astype(F32) for term in terms) for w in range(2))
            result[0, :, columns] = turn(dk, cosine, -sine).astype(BF16)
            result[1, :, columns] = dv.astype(BF16)


def join_halves(*refs):
    core = lax.rem(lax.axis_index("seq"), CORES)
    own_q, got_q, (own_kv, got_kv) = refs[:HALF_KV], refs[HALF_KV:][:HALF_KV], refs[2 * HALF_KV :][:2]
    outs = refs[2 * HALF_KV + 2 :]
    for own, got, results in ((own_q, got_q, outs[:2]), ([own_kv], [got_kv], outs[2:])):
        width = own[0].shape[-1]
        for half, parts in ((core, own), (1 - core, got)):
            for n, part in enumerate(parts):
                start = pl.multiple_of((half * len(parts) + n) * width, width)
                for w, out in enumerate(results):
                    out[:, pl.ds(start, width)] = part[w]


def local(query_input, key_input, value_input, out_grad, key_blocks, key_counts, block_position):
    n_seq = lax.axis_size("seq")
    n_grp = lax.axis_size("grp")
    n_pieces = n_seq // CORES
    n_listed = key_blocks.shape[1]

    def cross(array, by):
        return lax.ppermute(array, "seq", [(m, m ^ by) for m in range(n_seq)])

    def along(array, by):
        return cross(array, CORES * by)

    def onward(array):
        return lax.ppermute(array, "grp", [(g, g + 1) for g in range(n_grp - 1)])

    def back(array):
        return lax.ppermute(array, "grp", [(g + 1, g) for g in range(n_grp - 1)])

    table = trig_table(block_position.shape[0])
    n_far = min(n_seq, n_listed - 1)
    split = 2 * CORES
    piece = (2, HALF_KV, BLK, HEAD_DIM)
    chip = (CORES, *piece)
    q_shape = jax.ShapeDtypeStruct((2, HALF_KV, RATIO, BLK, HEAD_DIM), BF16)
    kv_shape = jax.ShapeDtypeStruct(piece, BF16)
    stats_shape = jax.ShapeDtypeStruct((2, HALF_KV, 8, ROWS), F32)
    low = jax.ShapeDtypeStruct(chip, BF16)
    high = jax.ShapeDtypeStruct(chip, F32)
    lists, counts = call(
        functools.partial(make_lists, n_seq, split),
        (
            jax.ShapeDtypeStruct((2, 4, n_listed + 1), jnp.int32),
            jax.ShapeDtypeStruct((2, 4), jnp.int32),
        ),
        2, us=2, name="block_lists",
    )(key_blocks, key_counts)

    halves = pltpu.VMEM((CORES, query_input.shape[0], HEADS // CORES * HEAD_DIM), BF16)
    kv_keep, kv_send, q_keep, q_send = call(
        functools.partial(prepare, n_seq), (kv_shape, kv_shape, q_shape, q_shape), 1,
        [
            pltpu.VMEM(key_input.shape, BF16), pltpu.VMEM(value_input.shape, BF16),
            pltpu.VMEM(table.shape, F32), halves, halves, pltpu.VMEM(q_shape.shape, BF16),
            pltpu.SemaphoreType.DMA((8,)),
        ],
        us=3, name="prepare", n_hbm=5, hbm_out=2,
    )(block_position, key_input, value_input, query_input, out_grad, table)
    kv_got = cross(kv_send, 1)
    q_send, kv_got = lax.optimization_barrier((q_send, kv_got))
    q_got = cross(q_send, 1)
    near = [jnp.stack([kv_keep, kv_got])]
    near.append(along(near[0], 1))
    ready, first_far = lax.optimization_barrier((near[1], onward(near[0])))
    far = [first_far, None]
    for k in range(2, n_pieces, 2):
        piece_k, lists, counts, _ = lax.optimization_barrier(
            (along(near[0], k), lists, counts, ready)
        )
        near += [piece_k, along(piece_k, 1)]
        far += [onward(piece_k), None]
    stats = call(
        functools.partial(current_stats, 1), stats_shape, 2, [pltpu.VMEM((split, *piece), BF16)],
        us=4, name="near_statistics", hold=(2,),
    )(lists, counts, q_keep, q_got, *near[:2])
    ready, far[2], stats = lax.optimization_barrier((ready, far[2], stats))
    far[1] = onward(ready)
    for k in range(2, n_pieces, 2):
        far[k + 1] = along(far[k], 1)
    stats = call(
        functools.partial(current_stats, 2), stats_shape, 2,
        [pltpu.VMEM((n_seq - split, *piece), BF16)], us=4, name="far_statistics",
    )(lists, counts, q_keep, q_got, stats, *near[2:])

    def grads_call(kernel, n_slots, n_store, outs, us, name, kept=(), more=()):
        pair = (n_slots, HALF_KV, 2, BLK, ROWS)
        saved = jax.ShapeDtypeStruct((2, *pair), BF16)
        return call(
            kernel, (*outs, saved, *more), 2,
            [
                pltpu.VMEM((n_store, *piece), BF16), pltpu.VMEM((n_store, *piece), F32),
                pltpu.VMEM(pair, BF16), pltpu.SemaphoreType.DMA((n_slots,)), *kept,
            ],
            us=us, name=name, hbm_out=len(outs),
        )

    kept = pltpu.VMEM((n_far, HALF_KV, BLK, ROWS), F32)
    two = jax.ShapeDtypeStruct((2 * CORES, *piece), BF16)
    first_far, *far_grads, far_saved, stats = grads_call(
        functools.partial(previous_grads, n_pieces), n_far, n_seq, (two,) + (low,) * (n_pieces - 2),
        14, "previous_gradients", (kept, kept), (stats_shape,),
    )(lists, counts, q_keep, q_got, stats, *far)

    def current_call(section, outs, name, pieces, after):
        stats_late, _ = lax.optimization_barrier((stats, after))
        n_store = CORES * len(pieces)
        *grads, saved = grads_call(
            functools.partial(current_grads, section, len(pieces)), min(n_store, n_listed), n_store,
            outs, 6, name,
        )(lists, counts, q_keep, q_got, stats_late, *pieces)
        return grads, saved

    def total(*terms):
        return sum(term.astype(F32) for term in terms).astype(BF16)

    from_far = back(first_far)
    crossing = [along(grad, 1) for grad in far_grads[1::2]]
    high_grads, high_saved = current_call(
        2, [high, low] * (n_pieces // 2 - 1), "far_current_gradients", near[2:], far_grads[0]
    )
    crossing, high_grads = lax.optimization_barrier((crossing, high_grads))
    arrived = [
        back(total(grad, extra)) for grad, extra in zip(far_grads[0::2], crossing)
    ]
    swapped = [along(grad, 1) for grad in high_grads[1::2]]
    low_grads, low_saved = current_call(
        1, [high, high], "near_current_gradients", near[:2], high_grads[0]
    )
    low_grads, from_far = lax.optimization_barrier((low_grads, from_far))
    from_next = along(total(low_grads[1], from_far[CORES:]), 1)
    merged = [
        total(*terms) for terms in zip(high_grads[0::2], arrived, swapped)
    ]
    half_out = jax.ShapeDtypeStruct((2, BLK, RATIO * HEAD_DIM), BF16)
    place_late, _ = lax.optimization_barrier((block_position, merged))
    wide = pltpu.VMEM((HEAD_DIM, ROWS), F32)
    slots = (HALF_KV, 2, n_listed + 1)
    halves = call(
        functools.partial(query_results, n_seq), (half_out,) * (2 * HALF_KV), 3,
        [
            pltpu.VMEM((2 * n_seq, *piece), BF16), pltpu.VMEM((*slots, 2, BLK, ROWS), BF16),
            wide, wide, pltpu.SemaphoreType.DMA(slots),
        ],
        us=20, name="query_results", n_hbm=3,
    )(lists, counts, place_late, far_saved, low_saved, high_saved, *far, *near, table)
    own_halves, other_halves = halves[:HALF_KV], halves[HALF_KV:]
    other_halves = lax.optimization_barrier(list(other_halves))
    got_halves = [cross(half, 1) for half in other_halves]
    final = [low_grads[0], from_far[:CORES], from_next]
    final += [along(part, 2 + 2 * n) for n, part in enumerate(merged)]
    own_halves = list(own_halves)
    final[0], own_halves[1] = lax.optimization_barrier((final[0], own_halves[1]))
    kv_half = jax.ShapeDtypeStruct((2, BLK, HALF_KV * HEAD_DIM), BF16)
    own_kv, other_kv = call(
        functools.partial(finish_kv, n_seq), (kv_half, kv_half), 1, us=2, name="key_gradients"
    )(block_position, *final, table)
    got_kv = cross(other_kv, 1)
    q_out = jax.ShapeDtypeStruct(query_input.shape, BF16)
    kv_out = jax.ShapeDtypeStruct(key_input.shape, BF16)
    out_rows, query_grad, key_grad, value_grad = call(
        join_halves, (q_out, q_out, kv_out, kv_out), 0, us=2, name="join_halves"
    )(*own_halves, *got_halves, own_kv, got_kv)
    return (out_rows, query_grad, key_grad, value_grad)


def solution(mesh):
    split = P(("grp", "seq"), None)
    return jax.shard_map(
        local,
        mesh=mesh,
        in_specs=(split, split, split, split, P(), P(), P()),
        out_specs=(split, split, split, split),
        check_vma=False,
    )
```

```python
import functools
import math

import jax
import jax.numpy as jnp
import numpy as np
from jax import lax
from jax.experimental import pallas as pl
from jax.experimental.pallas import tpu as pltpu
from jax.sharding import PartitionSpec as P

HEADS = 32
KV_HEADS = 4
HEAD_DIM = 128
BLK = 128
CORES = 2
RATIO = HEADS // KV_HEADS
HALF_KV = KV_HEADS // CORES
ROWS = RATIO * BLK
SCALE = 1.0 / math.sqrt(HEAD_DIM)
TO_LOG2 = SCALE * math.log2(math.e)
F32 = jnp.float32
BF16 = jnp.bfloat16
CHUNK = 256

VMEM_SPEC = pl.BlockSpec(memory_space=pltpu.VMEM)
HBM_SPEC = pl.BlockSpec(memory_space=pltpu.HBM)
SMEM_SPEC = pl.BlockSpec(memory_space=pltpu.SMEM)


def trig_table(n_blocks):
    half = HEAD_DIM // 2
    frequency = np.power(500000.0, -np.arange(half) * (2.0 / HEAD_DIM))
    parts = []
    for places in (np.arange(n_blocks) * BLK, np.arange(BLK)):
        angles = places[:, None] * frequency
        for part in (np.cos(angles), np.sin(angles)):
            parts.append(np.concatenate([part, part], axis=1))
    return np.concatenate(parts, axis=0).astype(np.float32)


def block_tables(place, table):
    n_blocks = table.shape[0] // 2 - BLK
    cos_b = table[pl.ds(place, 1), :]
    sin_b = table[pl.ds(n_blocks + place, 1), :]
    cos_t = table[2 * n_blocks : 2 * n_blocks + BLK, :]
    sin_t = table[2 * n_blocks + BLK :, :]
    cosine = cos_b * cos_t - sin_b * sin_t
    sine = sin_b * cos_t + cos_b * sin_t
    lanes = lax.broadcasted_iota(jnp.int32, sine.shape, 1)
    return cosine, jnp.where(lanes < HEAD_DIM // 2, -sine, sine)


def turn(values, cosine, signed_sine):
    return values * cosine + pltpu.roll(values, HEAD_DIM // 2, 1) * signed_sine


def dot_nt(a, b):
    return lax.dot_general(a, b, (((1,), (1,)), ((), ())), preferred_element_type=F32)


def dot_nn(a, b):
    return lax.dot_general(a, b, (((1,), (0,)), ((), ())), preferred_element_type=F32)


def here(n_seq):
    member = lax.axis_index("seq")
    group = lax.axis_index("grp")
    return group, member, lax.rem(member, CORES)


def size_of(array):
    return math.prod(array.shape) * jnp.dtype(array.dtype).itemsize


def call(kernel, out_shape, n_smem, scratch=(), us=1, name=None, n_hbm=0, hbm_out=None, hold=()):
    def placed(n, a):
        if n == hbm_out:
            return pltpu.HBM(a.shape, a.dtype)
        return a

    def spec(n, a):
        if a.dtype == jnp.int32:
            return SMEM_SPEC
        return HBM_SPEC if n == hbm_out else VMEM_SPEC

    def run(*arrays):
        n_left = n_smem + n_hbm
        outs = list(out_shape) if isinstance(out_shape, (tuple, list)) else [out_shape]
        held = sum(size_of(a) for a in arrays[n_left:])
        held += sum(size_of(a) for n, a in enumerate(outs) if n != hbm_out)
        held += sum(size_of(a) for a in scratch if a.dtype in (F32, BF16))
        in_specs = [SMEM_SPEC] * n_smem + [HBM_SPEC] * n_hbm
        in_specs += [VMEM_SPEC] * (len(arrays) - n_left)
        pinned = [
            pltpu.with_memory_space_constraint(a, pltpu.HBM) if n < n_left or n in hold else a
            for n, a in enumerate(arrays)
        ]
        results = pl.pallas_call(
            kernel,
            out_shape=[placed(n, a) for n, a in enumerate(outs)],
            in_specs=in_specs,
            out_specs=[spec(n, a) for n, a in enumerate(outs)],
            scratch_shapes=list(scratch),
            compiler_params=pltpu.CompilerParams(vmem_limit_bytes=held + 6 * 2**20),
            cost_estimate=pl.CostEstimate(
                flops=us * 10**9, bytes_accessed=2**20, transcendentals=0
            ),
            name=name,
        )(*pinned)
        return results if isinstance(out_shape, (tuple, list)) else results[0]

    return run


def prepare(n_seq, place_ref, *refs):
    key, value, query, grad, table_hbm, kv_keep, kv_send, q_keep, q_send = refs[:9]
    key_here, value_here, table, query_here, grad_here, kept, sems = refs[9:]
    group, member, core = here(n_seq)
    half_heads = HEADS // CORES
    halves = (1 - core, core)

    def copy(n, source, place):
        return pltpu.make_async_copy(source, place, sems.at[n])

    def columns(first, count=1):
        return pl.ds(pl.multiple_of(first * HEAD_DIM, HEAD_DIM), count * HEAD_DIM)

    loads = [copy(0, key, key_here), copy(1, table_hbm, table), copy(2, value, value_here)]
    for n, half in enumerate(halves):
        part = columns(half * half_heads, half_heads)
        loads.append(copy(3 + 2 * n, query.at[:, part], query_here.at[n]))
        loads.append(copy(4 + 2 * n, grad.at[:, part], grad_here.at[n]))
    for load in (*loads[:3], *loads[5:], *loads[3:5]):
        load.start()
    for load in loads[:3]:
        load.wait()
    cosine, sine = block_tables(place_ref[group * n_seq + member], table)
    for half, out in zip(halves, (kv_send, kv_keep)):
        for h in range(HALF_KV):
            at = columns(half * HALF_KV + h)
            out[0, h] = turn(key_here[:, at].astype(F32), cosine, sine).astype(BF16)
            out[1, h] = value_here[:, at]
    away = copy(7, kept, q_keep)
    for n, out in ((1, kept), (0, q_send)):
        loads[3 + 2 * n].wait()
        loads[4 + 2 * n].wait()
        for h in range(HALF_KV):
            for r in range(RATIO):
                at = slice((h * RATIO + r) * HEAD_DIM, (h * RATIO + r + 1) * HEAD_DIM)
                part = query_here[n, :, at].astype(F32)
                out[0, h, r] = turn(part, cosine, sine).astype(BF16)
                out[1, h, r] = grad_here[n, :, at]
        if n == 1:
            away.start()
    away.wait()


def make_lists(n_seq, split, key_blocks, key_counts, lists, counts):
    group, member, _ = here(n_seq)
    for i in range(2):
        block = group * n_seq + lax.bitwise_xor(member, i)
        for section in range(3):
            counts[i, section] = int(section == 1)
        lists[i, 1, 0] = i

        def look(j, _):
            place = lax.bitwise_xor(key_blocks[block, j] - (group - 1) * n_seq, member)
            section = (place >= n_seq).astype(jnp.int32)
            section += (place >= n_seq + split).astype(jnp.int32)
            n = counts[i, section]
            lists[i, section, n] = place - jnp.where(section == 0, 0, n_seq) - jnp.where(
                section == 2, split, 0
            )
            counts[i, section] = n + 1
            return 0

        lax.fori_loop(1, key_counts[block], look, 0)
        total = 0
        for section, base in enumerate((0, n_seq, n_seq + split)):

            def append(n, m):
                lists[i, 3, m] = lists[i, section, n] + base
                return m + 1

            total = lax.fori_loop(0, counts[i, section], append, jnp.int32(total))
        counts[i, 3] = total
        lists[i, 3, total] = 0


def causal():
    keys = lax.broadcasted_iota(jnp.int32, (BLK, CHUNK), 0)
    tokens = lax.rem(lax.broadcasted_iota(jnp.int32, (BLK, CHUNK), 1), BLK)
    return keys <= tokens


def chunks():
    per = CHUNK // BLK
    return [
        (slice(c * per, (c + 1) * per), slice(c * CHUNK, (c + 1) * CHUNK))
        for c in range(ROWS // CHUNK)
    ]


def heads_of(block, what, h, rows):
    return block[what, h, rows].reshape(CHUNK, HEAD_DIM)


def fill(store, pieces, first=0):
    for k, piece in enumerate(pieces):
        store[first + CORES * k : first + CORES * (k + 1)] = piece[...]


def pair_scores(store, e, h, block, rows, diagonal):
    scores = dot_nt(store[e, 0, h], heads_of(block, 0, h, rows))
    if diagonal:
        scores = jnp.where(causal(), scores, -1e30)
    return scores, dot_nt(store[e, 1, h], heads_of(block, 1, h, rows))


def gather_stats(store, e, block, stats, i, diagonal, kept=None):
    for h in range(HALF_KV):
        for rows, columns in chunks():
            scores, dprobs = pair_scores(store, e, h, block, rows, diagonal)
            if kept is not None:
                n, kept_scores, kept_dprobs = kept
                kept_scores[n, h, :, columns] = scores
                kept_dprobs[n, h, :, columns] = dprobs
            top = jnp.max(scores, axis=0, keepdims=True)
            if not diagonal:
                old_top = stats[i, h, 0:1, columns]
                top = jnp.maximum(top, old_top)
            weights = jnp.exp2((scores - top) * TO_LOG2)
            total = jnp.sum(weights, axis=0, keepdims=True)
            mixed = jnp.sum(weights * dprobs, axis=0, keepdims=True)
            if not diagonal:
                shrink = jnp.exp2((old_top - top) * TO_LOG2)
                total += stats[i, h, 1:2, columns] * shrink
                mixed += stats[i, h, 2:3, columns] * shrink
            stats[i, h, 0:1, columns] = top
            stats[i, h, 1:2, columns] = total
            stats[i, h, 2:3, columns] = mixed


def spread_grads(found, count, kept_scores, kept_dprobs, stats, i, block, acc, saved, low, sent):
    def copy(n):
        return pltpu.make_async_copy(low.at[n], saved.at[i, n], sent.at[n])

    def add(n, _):
        e = found[n]
        for h in range(HALF_KV):
            dk, dv = acc[e, 0, h], acc[e, 1, h]
            for rows, columns in chunks():
                probs = jnp.exp2(
                    kept_scores[n, h, :, columns] * TO_LOG2 - stats[i, h, 0:1, columns]
                )
                dscores = probs * (kept_dprobs[n, h, :, columns] - stats[i, h, 2:3, columns])
                probs, dscores = probs.astype(BF16), dscores.astype(BF16)
                low[n, h, 0, :, columns] = probs
                low[n, h, 1, :, columns] = dscores
                dv += dot_nn(probs, heads_of(block, 1, h, rows))
                dk += dot_nn(dscores, heads_of(block, 0, h, rows))
            acc[e, 0, h] = dk
            acc[e, 1, h] = dv
        copy(n).start()
        return 0

    def finish(n, _):
        copy(n).wait()
        return 0

    lax.fori_loop(0, count, add, 0)
    lax.fori_loop(0, count, finish, 0)


def write_grads(acc, outs):
    start = 0
    for out in outs:
        part = slice(start, start + out.shape[0])
        out[:, 0] = (acc[part, 0] * SCALE).astype(out.dtype)
        out[:, 1] = acc[part, 1].astype(out.dtype)
        start += out.shape[0]


def current_stats(section, lists, counts, own, other, *rest):
    *pieces, stats, store = rest
    first = section == 1
    if not first:
        stats_in, *pieces = pieces
        stats[...] = stats_in[...]
    fill(store, pieces)
    for i, block in enumerate((own, other)):
        if first:
            gather_stats(store, i, block, stats, i, True)

        def step(n, _):
            gather_stats(store, lists[i, section, n], block, stats, i, False)
            return 0

        lax.fori_loop(int(first), counts[i, section], step, 0)


def previous_grads(n_pieces, lists, counts, own, other, stats_in, *rest):
    n_ends = 2 * n_pieces - 1
    pieces, outs = rest[:n_pieces], rest[n_pieces:n_ends]
    saved, stats, store, acc, low, sent, kept_scores, kept_dprobs = rest[n_ends:]
    fill(store, pieces)
    acc[...] = jnp.zeros_like(acc)
    stats[...] = stats_in[...]
    for i, block in enumerate((own, other)):
        count = counts[i, 0]

        def look(n, _):
            gather_stats(
                store, lists[i, 0, n], block, stats, i, False, (n, kept_scores, kept_dprobs)
            )
            return 0

        lax.fori_loop(0, count, look, 0)
        for h in range(HALF_KV):
            total = stats[i, h, 1:2, :]
            stats[i, h, 0:1, :] = stats[i, h, 0:1, :] * TO_LOG2 + jnp.log2(total)
            stats[i, h, 2:3, :] = stats[i, h, 2:3, :] / total

        def copy(n):
            return pltpu.make_async_copy(low.at[n], saved.at[i, n], sent.at[n])

        def add(n, _):
            e = lists[i, 0, n]
            for h in range(HALF_KV):
                dk, dv = acc[e, 0, h], acc[e, 1, h]
                for rows, columns in chunks():
                    probs = jnp.exp2(
                        kept_scores[n, h, :, columns] * TO_LOG2 - stats[i, h, 0:1, columns]
                    )
                    dscores = probs * (kept_dprobs[n, h, :, columns] - stats[i, h, 2:3, columns])
                    probs, dscores = probs.astype(BF16), dscores.astype(BF16)
                    low[n, h, 0, :, columns] = probs
                    low[n, h, 1, :, columns] = dscores
                    dv += dot_nn(probs, heads_of(block, 1, h, rows))
                    dk += dot_nn(dscores, heads_of(block, 0, h, rows))
                acc[e, 0, h] = dk
                acc[e, 1, h] = dv
            copy(n).start()
            return 0

        def finish(n, _):
            copy(n).wait()
            return 0

        lax.fori_loop(0, count, add, 0)
        lax.fori_loop(0, count, finish, 0)
    write_grads(acc, outs)


def current_grads(section, n_pieces, lists, counts, own, other, stats, *rest):
    pieces, outs = rest[:n_pieces], rest[n_pieces : 2 * n_pieces]
    saved, store, acc, low, sent = rest[2 * n_pieces :]
    first = section == 1
    fill(store, pieces)
    acc[...] = jnp.zeros_like(acc)
    for i, block in enumerate((own, other)):
        count = counts[i, section]

        def copy(n):
            return pltpu.make_async_copy(low.at[n], saved.at[i, n], sent.at[n])

        def look(n, diagonal):
            e = lists[i, section, n]
            for h in range(HALF_KV):
                for rows, columns in chunks():
                    scores, dprobs = pair_scores(store, e, h, block, rows, diagonal)
                    probs = jnp.exp2(scores * TO_LOG2 - stats[i, h, 0:1, columns])
                    low[n, h, 0, :, columns] = probs.astype(BF16)
                    dscores = probs * (dprobs - stats[i, h, 2:3, columns])
                    low[n, h, 1, :, columns] = dscores.astype(BF16)
            copy(n).start()
            return 0

        def add(n, _):
            e = lists[i, section, n]
            for h in range(HALF_KV):
                for w in range(2):
                    right = block[1 - w, h].reshape(ROWS, HEAD_DIM)
                    acc[e, 1 - w, h] += dot_nn(low[n, h, w], right)
            return 0

        def finish(n, _):
            copy(n).wait()
            return 0

        if first:
            look(0, True)
        lax.fori_loop(int(first), count, lambda n, _: look(n, False), 0)
        lax.fori_loop(0, count, add, 0)
        lax.fori_loop(0, count, finish, 0)
    write_grads(acc, outs)


def query_results(n_seq, lists, counts, place_ref, *rest):
    n_saved = 3
    n_pieces = n_seq // CORES
    saved, pieces, rest = rest[:n_saved], rest[n_saved:][: 2 * n_pieces], rest[n_saved + 2 * n_pieces :]
    table, *rest = rest
    outs, (store, low, out_acc, dq_acc, got) = rest[: 2 * HALF_KV], rest[2 * HALF_KV :]
    group, member, _ = here(n_seq)

    def copy(source, h, i, n, first):
        return pltpu.make_async_copy(source.at[i, n - first, h], low.at[h, i, n], got.at[h, i, n])

    ends = []
    for i in range(2):
        stops = [0]
        for section in range(n_saved):
            stops.append(stops[-1] + counts[i, section])
        ends.append(stops)
    for h in range(HALF_KV):
        for i, stops in enumerate(ends):
            for source, first, stop in zip(saved, stops, stops[1:]):

                def fetch_one(n, _):
                    copy(source, h, i, n, first).start()
                    return 0

                lax.fori_loop(first, stop, fetch_one, 0)
    fill(store, pieces)
    tables = []
    for i in range(2):
        mine = group * n_seq + lax.bitwise_xor(member, i)
        cosine, sine = block_tables(place_ref[mine], table)
        tables.append((cosine.T * SCALE, sine.T * SCALE))
    for h, (i, stops) in ((h, pair) for h in range(HALF_KV) for pair in enumerate(ends)):
        total = stops[-1]
        result = outs[i * HALF_KV + h]

        @pl.when(lax.rem(total, 2) == 1)
        def _():
            low[h, i, total] = jnp.zeros((2, BLK, ROWS), BF16)

        out_acc[...] = jnp.zeros_like(out_acc)
        dq_acc[...] = jnp.zeros_like(dq_acc)

        def add(n, _):
            pair = (2 * n, 2 * n + 1)
            for m in pair:
                for source, first, stop in zip(saved, stops, stops[1:]):

                    @pl.when(jnp.logical_and(m >= first, m < stop))
                    def _():
                        copy(source, h, i, m, first).wait()

            found = [lists[i, 3, m] for m in pair]
            keys_t = jnp.concatenate([store[e, 0, h].T for e in found], axis=1)
            values_t = jnp.concatenate([store[e, 1, h].T for e in found], axis=1)
            for _, columns in chunks():
                probs = jnp.concatenate([low[h, i, m, 0, :, columns] for m in pair], axis=0)
                dscores = jnp.concatenate([low[h, i, m, 1, :, columns] for m in pair], axis=0)
                out_acc[:, columns] += dot_nn(values_t, probs)
                dq_acc[:, columns] += dot_nn(keys_t, dscores)
            return 0

        lax.fori_loop(0, lax.div(total + 1, 2), add, 0)
        cosine, sine = tables[i]
        for r in range(RATIO):
            rows = slice(r * BLK, (r + 1) * BLK)
            columns = slice(r * HEAD_DIM, (r + 1) * HEAD_DIM)
            result[0, :, columns] = out_acc[:, rows].astype(BF16).T
            dq = dq_acc[:, rows]
            half = HEAD_DIM // 2
            turned = jnp.concatenate([dq[half:], dq[:half]], axis=0)
            result[1, :, columns] = (dq * cosine - turned * sine).astype(BF16).T


def finish_kv(n_seq, place_ref, *rest):
    *terms, table, keep, send = rest
    group, member, _ = here(n_seq)
    for i, result in enumerate((keep, send)):
        offset = lax.bitwise_xor(member, i)
        cosine, sine = block_tables(place_ref[group * n_seq + offset], table)
        for h in range(HALF_KV):
            columns = slice(h * HEAD_DIM, (h + 1) * HEAD_DIM)
            dk, dv = (sum(term[i, w, h].astype(F32) for term in terms) for w in range(2))
            result[0, :, columns] = turn(dk, cosine, -sine).astype(BF16)
            result[1, :, columns] = dv.astype(BF16)


def join_halves(*refs):
    core = lax.rem(lax.axis_index("seq"), CORES)
    own_q, got_q, (own_kv, got_kv) = refs[:HALF_KV], refs[HALF_KV:][:HALF_KV], refs[2 * HALF_KV :][:2]
    outs = refs[2 * HALF_KV + 2 :]
    for own, got, results in ((own_q, got_q, outs[:2]), ([own_kv], [got_kv], outs[2:])):
        width = own[0].shape[-1]
        for half, parts in ((core, own), (1 - core, got)):
            for n, part in enumerate(parts):
                start = pl.multiple_of((half * len(parts) + n) * width, width)
                for w, out in enumerate(results):
                    out[:, pl.ds(start, width)] = part[w]


def local(query_input, key_input, value_input, out_grad, key_blocks, key_counts, block_position):
    n_seq = lax.axis_size("seq")
    n_grp = lax.axis_size("grp")
    n_pieces = n_seq // CORES
    n_listed = key_blocks.shape[1]

    def cross(array, by):
        return lax.ppermute(array, "seq", [(m, m ^ by) for m in range(n_seq)])

    def along(array, by):
        return cross(array, CORES * by)

    def onward(array):
        return lax.ppermute(array, "grp", [(g, g + 1) for g in range(n_grp - 1)])

    def back(array):
        return lax.ppermute(array, "grp", [(g + 1, g) for g in range(n_grp - 1)])

    table = trig_table(block_position.shape[0])
    n_far = min(n_seq, n_listed - 1)
    split = 2 * CORES
    piece = (2, HALF_KV, BLK, HEAD_DIM)
    chip = (CORES, *piece)
    q_shape = jax.ShapeDtypeStruct((2, HALF_KV, RATIO, BLK, HEAD_DIM), BF16)
    kv_shape = jax.ShapeDtypeStruct(piece, BF16)
    stats_shape = jax.ShapeDtypeStruct((2, HALF_KV, 8, ROWS), F32)
    low = jax.ShapeDtypeStruct(chip, BF16)
    high = jax.ShapeDtypeStruct(chip, F32)
    lists, counts = call(
        functools.partial(make_lists, n_seq, split),
        (
            jax.ShapeDtypeStruct((2, 4, n_listed + 1), jnp.int32),
            jax.ShapeDtypeStruct((2, 4), jnp.int32),
        ),
        2, us=2, name="block_lists",
    )(key_blocks, key_counts)

    halves = pltpu.VMEM((CORES, query_input.shape[0], HEADS // CORES * HEAD_DIM), BF16)
    kv_keep, kv_send, q_keep, q_send = call(
        functools.partial(prepare, n_seq), (kv_shape, kv_shape, q_shape, q_shape), 1,
        [
            pltpu.VMEM(key_input.shape, BF16), pltpu.VMEM(value_input.shape, BF16),
            pltpu.VMEM(table.shape, F32), halves, halves, pltpu.VMEM(q_shape.shape, BF16),
            pltpu.SemaphoreType.DMA((8,)),
        ],
        us=3, name="prepare", n_hbm=5, hbm_out=2,
    )(block_position, key_input, value_input, query_input, out_grad, table)
    kv_got = cross(kv_send, 1)
    q_send, kv_got = lax.optimization_barrier((q_send, kv_got))
    q_got = cross(q_send, 1)
    near = [jnp.stack([kv_keep, kv_got])]
    near.append(along(near[0], 1))
    ready, first_far = lax.optimization_barrier((near[1], onward(near[0])))
    far = [first_far, None]
    for k in range(2, n_pieces, 2):
        piece_k, lists, counts, _ = lax.optimization_barrier(
            (along(near[0], k), lists, counts, ready)
        )
        near += [piece_k, along(piece_k, 1)]
        far += [onward(piece_k), None]
    stats = call(
        functools.partial(current_stats, 1), stats_shape, 2, [pltpu.VMEM((split, *piece), BF16)],
        us=4, name="near_statistics", hold=(2,),
    )(lists, counts, q_keep, q_got, *near[:2])
    ready, far[2], stats = lax.optimization_barrier((ready, far[2], stats))
    far[1] = onward(ready)
    for k in range(2, n_pieces, 2):
        far[k + 1] = along(far[k], 1)
    stats = call(
        functools.partial(current_stats, 2), stats_shape, 2,
        [pltpu.VMEM((n_seq - split, *piece), BF16)], us=4, name="far_statistics",
    )(lists, counts, q_keep, q_got, stats, *near[2:])

    def grads_call(kernel, n_slots, n_store, outs, us, name, kept=(), more=()):
        pair = (n_slots, HALF_KV, 2, BLK, ROWS)
        saved = jax.ShapeDtypeStruct((2, *pair), BF16)
        return call(
            kernel, (*outs, saved, *more), 2,
            [
                pltpu.VMEM((n_store, *piece), BF16), pltpu.VMEM((n_store, *piece), F32),
                pltpu.VMEM(pair, BF16), pltpu.SemaphoreType.DMA((n_slots,)), *kept,
            ],
            us=us, name=name, hbm_out=len(outs),
        )

    kept = pltpu.VMEM((n_far, HALF_KV, BLK, ROWS), F32)
    two = jax.ShapeDtypeStruct((2 * CORES, *piece), BF16)
    first_far, *far_grads, far_saved, stats = grads_call(
        functools.partial(previous_grads, n_pieces), n_far, n_seq, (two,) + (low,) * (n_pieces - 2),
        14, "previous_gradients", (kept, kept), (stats_shape,),
    )(lists, counts, q_keep, q_got, stats, *far)

    def current_call(section, outs, name, pieces, after):
        stats_late, _ = lax.optimization_barrier((stats, after))
        n_store = CORES * len(pieces)
        *grads, saved = grads_call(
            functools.partial(current_grads, section, len(pieces)), min(n_store, n_listed), n_store,
            outs, 6, name,
        )(lists, counts, q_keep, q_got, stats_late, *pieces)
        return grads, saved

    def total(*terms):
        return sum(term.astype(F32) for term in terms).astype(BF16)

    from_far = back(first_far)
    crossing = [along(grad, 1) for grad in far_grads[1::2]]
    high_grads, high_saved = current_call(
        2, [high, low] * (n_pieces // 2 - 1), "far_current_gradients", near[2:], far_grads[0]
    )
    crossing, high_grads = lax.optimization_barrier((crossing, high_grads))
    arrived = [
        back(total(grad, extra)) for grad, extra in zip(far_grads[0::2], crossing)
    ]
    swapped = [along(grad, 1) for grad in high_grads[1::2]]
    low_grads, low_saved = current_call(
        1, [high, high], "near_current_gradients", near[:2], high_grads[0]
    )
    low_grads, from_far = lax.optimization_barrier((low_grads, from_far))
    from_next = along(total(low_grads[1], from_far[CORES:]), 1)
    merged = [
        total(*terms) for terms in zip(high_grads[0::2], arrived, swapped)
    ]
    half_out = jax.ShapeDtypeStruct((2, BLK, RATIO * HEAD_DIM), BF16)
    place_late, _ = lax.optimization_barrier((block_position, merged))
    wide = pltpu.VMEM((HEAD_DIM, ROWS), F32)
    slots = (HALF_KV, 2, n_listed + 1)
    halves = call(
        functools.partial(query_results, n_seq), (half_out,) * (2 * HALF_KV), 3,
        [
            pltpu.VMEM((2 * n_seq, *piece), BF16), pltpu.VMEM((*slots, 2, BLK, ROWS), BF16),
            wide, wide, pltpu.SemaphoreType.DMA(slots),
        ],
        us=20, name="query_results", n_hbm=3,
    )(lists, counts, place_late, far_saved, low_saved, high_saved, *far, *near, table)
    own_halves, other_halves = halves[:HALF_KV], halves[HALF_KV:]
    other_halves = lax.optimization_barrier(list(other_halves))
    got_halves = [cross(half, 1) for half in other_halves]
    final = [low_grads[0], from_far[:CORES], from_next]
    final += [along(part, 2 + 2 * n) for n, part in enumerate(merged)]
    own_halves = list(own_halves)
    final[0], own_halves[1] = lax.optimization_barrier((final[0], own_halves[1]))
    kv_half = jax.ShapeDtypeStruct((2, BLK, HALF_KV * HEAD_DIM), BF16)
    own_kv, other_kv = call(
        functools.partial(finish_kv, n_seq), (kv_half, kv_half), 1, us=2, name="key_gradients"
    )(block_position, *final, table)
    got_kv = cross(other_kv, 1)
    q_out = jax.ShapeDtypeStruct(query_input.shape, BF16)
    kv_out = jax.ShapeDtypeStruct(key_input.shape, BF16)
    out_rows, query_grad, key_grad, value_grad = call(
        join_halves, (q_out, q_out, kv_out, kv_out), 0, us=2, name="join_halves"
    )(*own_halves, *got_halves, own_kv, got_kv)
    return (out_rows, query_grad, key_grad, value_grad)


def solution(mesh):
    split = P(("grp", "seq"), None)
    return jax.shard_map(
        local,
        mesh=mesh,
        in_specs=(split, split, split, split, P(), P(), P()),
        out_specs=(split, split, split, split),
        check_vma=False,
    )
```

```python
import functools
import math

import jax
import jax.numpy as jnp
import numpy as np
from jax import lax
from jax.experimental import pallas as pl
from jax.experimental.pallas import tpu as pltpu
from jax.sharding import PartitionSpec as P

HEADS = 32
KV_HEADS = 4
HEAD_DIM = 128
BLK = 128
CORES = 2
RATIO = HEADS // KV_HEADS
HALF_KV = KV_HEADS // CORES
ROWS = RATIO * BLK
SCALE = 1.0 / math.sqrt(HEAD_DIM)
TO_LOG2 = SCALE * math.log2(math.e)
F32 = jnp.float32
BF16 = jnp.bfloat16
CHUNK = 256

VMEM_SPEC = pl.BlockSpec(memory_space=pltpu.VMEM)
HBM_SPEC = pl.BlockSpec(memory_space=pltpu.HBM)
SMEM_SPEC = pl.BlockSpec(memory_space=pltpu.SMEM)


def trig_table(n_blocks):
    half = HEAD_DIM // 2
    frequency = np.power(500000.0, -np.arange(half) * (2.0 / HEAD_DIM))
    parts = []
    for places in (np.arange(n_blocks) * BLK, np.arange(BLK)):
        angles = places[:, None] * frequency
        for part in (np.cos(angles), np.sin(angles)):
            parts.append(np.concatenate([part, part], axis=1))
    return np.concatenate(parts, axis=0).astype(np.float32)


def block_tables(place, table):
    n_blocks = table.shape[0] // 2 - BLK
    cos_b = table[pl.ds(place, 1), :]
    sin_b = table[pl.ds(n_blocks + place, 1), :]
    cos_t = table[2 * n_blocks : 2 * n_blocks + BLK, :]
    sin_t = table[2 * n_blocks + BLK :, :]
    cosine = cos_b * cos_t - sin_b * sin_t
    sine = sin_b * cos_t + cos_b * sin_t
    lanes = lax.broadcasted_iota(jnp.int32, sine.shape, 1)
    return cosine, jnp.where(lanes < HEAD_DIM // 2, -sine, sine)


def turn(values, cosine, signed_sine):
    return values * cosine + pltpu.roll(values, HEAD_DIM // 2, 1) * signed_sine


def dot_nt(a, b):
    return lax.dot_general(a, b, (((1,), (1,)), ((), ())), preferred_element_type=F32)


def dot_nn(a, b):
    return lax.dot_general(a, b, (((1,), (0,)), ((), ())), preferred_element_type=F32)


def here(n_seq):
    member = lax.axis_index("seq")
    group = lax.axis_index("grp")
    return group, member, lax.rem(member, CORES)


def size_of(array):
    return math.prod(array.shape) * jnp.dtype(array.dtype).itemsize


def call(kernel, out_shape, n_smem, scratch=(), us=1, name=None, n_hbm=0, hbm_out=None, hold=()):
    def placed(n, a):
        if n == hbm_out:
            return pltpu.HBM(a.shape, a.dtype)
        return a

    def spec(n, a):
        if a.dtype == jnp.int32:
            return SMEM_SPEC
        return HBM_SPEC if n == hbm_out else VMEM_SPEC

    def run(*arrays):
        n_left = n_smem + n_hbm
        outs = list(out_shape) if isinstance(out_shape, (tuple, list)) else [out_shape]
        held = sum(size_of(a) for a in arrays[n_left:])
        held += sum(size_of(a) for n, a in enumerate(outs) if n != hbm_out)
        held += sum(size_of(a) for a in scratch if a.dtype in (F32, BF16))
        in_specs = [SMEM_SPEC] * n_smem + [HBM_SPEC] * n_hbm
        in_specs += [VMEM_SPEC] * (len(arrays) - n_left)
        pinned = [
            pltpu.with_memory_space_constraint(a, pltpu.HBM) if n < n_left or n in hold else a
            for n, a in enumerate(arrays)
        ]
        results = pl.pallas_call(
            kernel,
            out_shape=[placed(n, a) for n, a in enumerate(outs)],
            in_specs=in_specs,
            out_specs=[spec(n, a) for n, a in enumerate(outs)],
            scratch_shapes=list(scratch),
            compiler_params=pltpu.CompilerParams(vmem_limit_bytes=held + 6 * 2**20),
            cost_estimate=pl.CostEstimate(
                flops=us * 10**9, bytes_accessed=2**20, transcendentals=0
            ),
            name=name,
        )(*pinned)
        return results if isinstance(out_shape, (tuple, list)) else results[0]

    return run


def prepare(n_seq, place_ref, *refs):
    key, value, query, grad, table_hbm, kv_keep, kv_send, q_keep, q_send = refs[:9]
    key_here, value_here, table, query_here, grad_here, kept, sems = refs[9:]
    group, member, core = here(n_seq)
    half_heads = HEADS // CORES
    halves = (1 - core, core)

    def copy(n, source, place):
        return pltpu.make_async_copy(source, place, sems.at[n])

    def columns(first, count=1):
        return pl.ds(pl.multiple_of(first * HEAD_DIM, HEAD_DIM), count * HEAD_DIM)

    loads = [copy(0, key, key_here), copy(1, table_hbm, table), copy(2, value, value_here)]
    for n, half in enumerate(halves):
        part = columns(half * half_heads, half_heads)
        loads.append(copy(3 + 2 * n, query.at[:, part], query_here.at[n]))
        loads.append(copy(4 + 2 * n, grad.at[:, part], grad_here.at[n]))
    for load in (*loads[:3], *loads[5:], *loads[3:5]):
        load.start()
    for load in loads[:3]:
        load.wait()
    cosine, sine = block_tables(place_ref[group * n_seq + member], table)
    for half, out in zip(halves, (kv_send, kv_keep)):
        for h in range(HALF_KV):
            at = columns(half * HALF_KV + h)
            out[0, h] = turn(key_here[:, at].astype(F32), cosine, sine).astype(BF16)
            out[1, h] = value_here[:, at]
    away = copy(7, kept, q_keep)
    for n, out in ((1, kept), (0, q_send)):
        loads[3 + 2 * n].wait()
        loads[4 + 2 * n].wait()
        for h in range(HALF_KV):
            for r in range(RATIO):
                at = slice((h * RATIO + r) * HEAD_DIM, (h * RATIO + r + 1) * HEAD_DIM)
                part = query_here[n, :, at].astype(F32)
                out[0, h, r] = turn(part, cosine, sine).astype(BF16)
                out[1, h, r] = grad_here[n, :, at]
        if n == 1:
            away.start()
    away.wait()


def make_lists(n_seq, split, key_blocks, key_counts, lists, counts):
    group, member, _ = here(n_seq)
    for i in range(2):
        block = group * n_seq + lax.bitwise_xor(member, i)
        for section in range(3):
            counts[i, section] = int(section == 1)
        lists[i, 1, 0] = i

        def look(j, _):
            place = lax.bitwise_xor(key_blocks[block, j] - (group - 1) * n_seq, member)
            section = (place >= n_seq).astype(jnp.int32)
            section += (place >= n_seq + split).astype(jnp.int32)
            n = counts[i, section]
            lists[i, section, n] = place - jnp.where(section == 0, 0, n_seq) - jnp.where(
                section == 2, split, 0
            )
            counts[i, section] = n + 1
            return 0

        lax.fori_loop(1, key_counts[block], look, 0)
        total = 0
        for section, base in enumerate((0, n_seq, n_seq + split)):

            def append(n, m):
                lists[i, 3, m] = lists[i, section, n] + base
                return m + 1

            total = lax.fori_loop(0, counts[i, section], append, jnp.int32(total))
        counts[i, 3] = total
        lists[i, 3, total] = 0


def causal():
    keys = lax.broadcasted_iota(jnp.int32, (BLK, CHUNK), 0)
    tokens = lax.rem(lax.broadcasted_iota(jnp.int32, (BLK, CHUNK), 1), BLK)
    return keys <= tokens


def chunks():
    per = CHUNK // BLK
    return [
        (slice(c * per, (c + 1) * per), slice(c * CHUNK, (c + 1) * CHUNK))
        for c in range(ROWS // CHUNK)
    ]


def heads_of(block, what, h, rows):
    return block[what, h, rows].reshape(CHUNK, HEAD_DIM)


def fill(store, pieces, first=0):
    for k, piece in enumerate(pieces):
        store[first + CORES * k : first + CORES * (k + 1)] = piece[...]


def pair_scores(store, e, h, block, rows, diagonal):
    scores = dot_nt(store[e, 0, h], heads_of(block, 0, h, rows))
    if diagonal:
        scores = jnp.where(causal(), scores, -1e30)
    return scores, dot_nt(store[e, 1, h], heads_of(block, 1, h, rows))


def gather_stats(store, e, block, stats, i, diagonal, kept=None):
    for h in range(HALF_KV):
        for rows, columns in chunks():
            scores, dprobs = pair_scores(store, e, h, block, rows, diagonal)
            if kept is not None:
                n, kept_scores, kept_dprobs = kept
                kept_scores[n, h, :, columns] = scores
                kept_dprobs[n, h, :, columns] = dprobs
            top = jnp.max(scores, axis=0, keepdims=True)
            if not diagonal:
                old_top = stats[i, h, 0:1, columns]
                top = jnp.maximum(top, old_top)
            weights = jnp.exp2((scores - top) * TO_LOG2)
            total = jnp.sum(weights, axis=0, keepdims=True)
            mixed = jnp.sum(weights * dprobs, axis=0, keepdims=True)
            if not diagonal:
                shrink = jnp.exp2((old_top - top) * TO_LOG2)
                total += stats[i, h, 1:2, columns] * shrink
                mixed += stats[i, h, 2:3, columns] * shrink
            stats[i, h, 0:1, columns] = top
            stats[i, h, 1:2, columns] = total
            stats[i, h, 2:3, columns] = mixed


def spread_grads(found, count, kept_scores, kept_dprobs, stats, i, block, acc, saved, low, sent):
    def copy(n):
        return pltpu.make_async_copy(low.at[n], saved.at[i, n], sent.at[n])

    def add(n, _):
        e = found[n]
        for h in range(HALF_KV):
            dk, dv = acc[e, 0, h], acc[e, 1, h]
            for rows, columns in chunks():
                probs = jnp.exp2(
                    kept_scores[n, h, :, columns] * TO_LOG2 - stats[i, h, 0:1, columns]
                )
                dscores = probs * (kept_dprobs[n, h, :, columns] - stats[i, h, 2:3, columns])
                probs, dscores = probs.astype(BF16), dscores.astype(BF16)
                low[n, h, 0, :, columns] = probs
                low[n, h, 1, :, columns] = dscores
                dv += dot_nn(probs, heads_of(block, 1, h, rows))
                dk += dot_nn(dscores, heads_of(block, 0, h, rows))
            acc[e, 0, h] = dk
            acc[e, 1, h] = dv
        copy(n).start()
        return 0

    def finish(n, _):
        copy(n).wait()
        return 0

    lax.fori_loop(0, count, add, 0)
    lax.fori_loop(0, count, finish, 0)


def write_grads(acc, outs):
    start = 0
    for out in outs:
        part = slice(start, start + out.shape[0])
        out[:, 0] = (acc[part, 0] * SCALE).astype(out.dtype)
        out[:, 1] = acc[part, 1].astype(out.dtype)
        start += out.shape[0]


def current_stats(section, lists, counts, own, other, *rest):
    *pieces, stats, store = rest
    first = section == 1
    if not first:
        stats_in, *pieces = pieces
        stats[...] = stats_in[...]
    fill(store, pieces)
    for i, block in enumerate((own, other)):
        if first:
            gather_stats(store, i, block, stats, i, True)

        def step(n, _):
            gather_stats(store, lists[i, section, n], block, stats, i, False)
            return 0

        lax.fori_loop(int(first), counts[i, section], step, 0)


def previous_grads(n_pieces, lists, counts, own, other, stats_in, *rest):
    n_ends = 2 * n_pieces - 1
    pieces, outs = rest[:n_pieces], rest[n_pieces:n_ends]
    saved, stats, store, acc, low, sent, kept_scores, kept_dprobs = rest[n_ends:]
    fill(store, pieces)
    acc[...] = jnp.zeros_like(acc)
    stats[...] = stats_in[...]
    for i, block in enumerate((own, other)):
        count = counts[i, 0]

        def look(n, _):
            gather_stats(
                store, lists[i, 0, n], block, stats, i, False, (n, kept_scores, kept_dprobs)
            )
            return 0

        lax.fori_loop(0, count, look, 0)
        for h in range(HALF_KV):
            total = stats[i, h, 1:2, :]
            stats[i, h, 0:1, :] = stats[i, h, 0:1, :] * TO_LOG2 + jnp.log2(total)
            stats[i, h, 2:3, :] = stats[i, h, 2:3, :] / total

        def copy(n):
            return pltpu.make_async_copy(low.at[n], saved.at[i, n], sent.at[n])

        def add(n, _):
            e = lists[i, 0, n]
            for h in range(HALF_KV):
                dk, dv = acc[e, 0, h], acc[e, 1, h]
                for rows, columns in chunks():
                    probs = jnp.exp2(
                        kept_scores[n, h, :, columns] * TO_LOG2 - stats[i, h, 0:1, columns]
                    )
                    dscores = probs * (kept_dprobs[n, h, :, columns] - stats[i, h, 2:3, columns])
                    probs, dscores = probs.astype(BF16), dscores.astype(BF16)
                    low[n, h, 0, :, columns] = probs
                    low[n, h, 1, :, columns] = dscores
                    dv += dot_nn(probs, heads_of(block, 1, h, rows))
                    dk += dot_nn(dscores, heads_of(block, 0, h, rows))
                acc[e, 0, h] = dk
                acc[e, 1, h] = dv
            copy(n).start()
            return 0

        def finish(n, _):
            copy(n).wait()
            return 0

        lax.fori_loop(0, count, add, 0)
        lax.fori_loop(0, count, finish, 0)
    write_grads(acc, outs)


def current_grads(section, n_pieces, lists, counts, own, other, stats, *rest):
    pieces, outs = rest[:n_pieces], rest[n_pieces : 2 * n_pieces]
    saved, store, acc, low, sent = rest[2 * n_pieces :]
    first = section == 1
    fill(store, pieces)
    acc[...] = jnp.zeros_like(acc)
    for i, block in enumerate((own, other)):
        count = counts[i, section]

        def copy(n):
            return pltpu.make_async_copy(low.at[n], saved.at[i, n], sent.at[n])

        def look(n, diagonal):
            e = lists[i, section, n]
            for h in range(HALF_KV):
                for rows, columns in chunks():
                    scores, dprobs = pair_scores(store, e, h, block, rows, diagonal)
                    probs = jnp.exp2(scores * TO_LOG2 - stats[i, h, 0:1, columns])
                    low[n, h, 0, :, columns] = probs.astype(BF16)
                    dscores = probs * (dprobs - stats[i, h, 2:3, columns])
                    low[n, h, 1, :, columns] = dscores.astype(BF16)
            copy(n).start()
            return 0

        def add(n, _):
            e = lists[i, section, n]
            for h in range(HALF_KV):
                for w in range(2):
                    right = block[1 - w, h].reshape(ROWS, HEAD_DIM)
                    acc[e, 1 - w, h] += dot_nn(low[n, h, w], right)
            return 0

        def finish(n, _):
            copy(n).wait()
            return 0

        if first:
            look(0, True)
        lax.fori_loop(int(first), count, lambda n, _: look(n, False), 0)
        lax.fori_loop(0, count, add, 0)
        lax.fori_loop(0, count, finish, 0)
    write_grads(acc, outs)


def query_results(n_seq, lists, counts, place_ref, *rest):
    n_saved = 3
    n_pieces = n_seq // CORES
    saved, pieces, rest = rest[:n_saved], rest[n_saved:][: 2 * n_pieces], rest[n_saved + 2 * n_pieces :]
    table, *rest = rest
    outs, (store, low, out_acc, dq_acc, got) = rest[: 2 * HALF_KV], rest[2 * HALF_KV :]
    group, member, _ = here(n_seq)

    def copy(source, i, n, first):
        return pltpu.make_async_copy(source.at[i, n - first], low.at[i, n], got.at[i, n])

    totals = []
    for i in range(2):
        first = 0
        for section, source in enumerate(saved):
            stop = first + counts[i, section]

            def fetch_one(n, _):
                copy(source, i, n, first).start()
                return 0

            lax.fori_loop(first, stop, fetch_one, 0)
            first = stop
        totals.append(first)
    fill(store, pieces)
    tables = []
    for i in range(2):
        mine = group * n_seq + lax.bitwise_xor(member, i)
        cosine, sine = block_tables(place_ref[mine], table)
        tables.append((cosine.T * SCALE, sine.T * SCALE))
    for h, (i, total) in ((h, pair) for h in range(HALF_KV) for pair in enumerate(totals)):
        result = outs[i * HALF_KV + h]

        @pl.when(lax.rem(total, 2) == 1)
        def _():
            low[i, total, h] = jnp.zeros((2, BLK, ROWS), BF16)

        out_acc[...] = jnp.zeros_like(out_acc)
        dq_acc[...] = jnp.zeros_like(dq_acc)

        def add(n, _):
            pair = (2 * n, 2 * n + 1)
            if h == 0:
                for m in pair:

                    @pl.when(m < total)
                    def _():
                        copy(saved[0], i, m, m).wait()

            found = [lists[i, 3, m] for m in pair]
            keys_t = jnp.concatenate([store[e, 0, h].T for e in found], axis=1)
            values_t = jnp.concatenate([store[e, 1, h].T for e in found], axis=1)
            for _, columns in chunks():
                probs = jnp.concatenate([low[i, m, h, 0, :, columns] for m in pair], axis=0)
                dscores = jnp.concatenate([low[i, m, h, 1, :, columns] for m in pair], axis=0)
                out_acc[:, columns] += dot_nn(values_t, probs)
                dq_acc[:, columns] += dot_nn(keys_t, dscores)
            return 0

        lax.fori_loop(0, lax.div(total + 1, 2), add, 0)
        cosine, sine = tables[i]
        for r in range(RATIO):
            rows = slice(r * BLK, (r + 1) * BLK)
            columns = slice(r * HEAD_DIM, (r + 1) * HEAD_DIM)
            result[0, :, columns] = out_acc[:, rows].astype(BF16).T
            dq = dq_acc[:, rows]
            half = HEAD_DIM // 2
            turned = jnp.concatenate([dq[half:], dq[:half]], axis=0)
            result[1, :, columns] = (dq * cosine - turned * sine).astype(BF16).T


def finish_kv(n_seq, place_ref, *rest):
    *terms, table, keep, send = rest
    group, member, _ = here(n_seq)
    for i, result in enumerate((keep, send)):
        offset = lax.bitwise_xor(member, i)
        cosine, sine = block_tables(place_ref[group * n_seq + offset], table)
        for h in range(HALF_KV):
            columns = slice(h * HEAD_DIM, (h + 1) * HEAD_DIM)
            dk, dv = (sum(term[i, w, h].astype(F32) for term in terms) for w in range(2))
            result[0, :, columns] = turn(dk, cosine, -sine).astype(BF16)
            result[1, :, columns] = dv.astype(BF16)


def join_halves(*refs):
    core = lax.rem(lax.axis_index("seq"), CORES)
    own_q, got_q, (own_kv, got_kv) = refs[:HALF_KV], refs[HALF_KV:][:HALF_KV], refs[2 * HALF_KV :][:2]
    outs = refs[2 * HALF_KV + 2 :]
    for own, got, results in ((own_q, got_q, outs[:2]), ([own_kv], [got_kv], outs[2:])):
        width = own[0].shape[-1]
        for half, parts in ((core, own), (1 - core, got)):
            for n, part in enumerate(parts):
                start = pl.multiple_of((half * len(parts) + n) * width, width)
                for w, out in enumerate(results):
                    out[:, pl.ds(start, width)] = part[w]


def local(query_input, key_input, value_input, out_grad, key_blocks, key_counts, block_position):
    n_seq = lax.axis_size("seq")
    n_grp = lax.axis_size("grp")
    n_pieces = n_seq // CORES
    n_listed = key_blocks.shape[1]

    def cross(array, by):
        return lax.ppermute(array, "seq", [(m, m ^ by) for m in range(n_seq)])

    def along(array, by):
        return cross(array, CORES * by)

    def onward(array):
        return lax.ppermute(array, "grp", [(g, g + 1) for g in range(n_grp - 1)])

    def back(array):
        return lax.ppermute(array, "grp", [(g + 1, g) for g in range(n_grp - 1)])

    table = trig_table(block_position.shape[0])
    n_far = min(n_seq, n_listed - 1)
    split = 2 * CORES
    piece = (2, HALF_KV, BLK, HEAD_DIM)
    chip = (CORES, *piece)
    q_shape = jax.ShapeDtypeStruct((2, HALF_KV, RATIO, BLK, HEAD_DIM), BF16)
    kv_shape = jax.ShapeDtypeStruct(piece, BF16)
    stats_shape = jax.ShapeDtypeStruct((2, HALF_KV, 8, ROWS), F32)
    low = jax.ShapeDtypeStruct(chip, BF16)
    high = jax.ShapeDtypeStruct(chip, F32)
    lists, counts = call(
        functools.partial(make_lists, n_seq, split),
        (
            jax.ShapeDtypeStruct((2, 4, n_listed + 1), jnp.int32),
            jax.ShapeDtypeStruct((2, 4), jnp.int32),
        ),
        2, us=2, name="block_lists",
    )(key_blocks, key_counts)

    halves = pltpu.VMEM((CORES, query_input.shape[0], HEADS // CORES * HEAD_DIM), BF16)
    kv_keep, kv_send, q_keep, q_send = call(
        functools.partial(prepare, n_seq), (kv_shape, kv_shape, q_shape, q_shape), 1,
        [
            pltpu.VMEM(key_input.shape, BF16), pltpu.VMEM(value_input.shape, BF16),
            pltpu.VMEM(table.shape, F32), halves, halves, pltpu.VMEM(q_shape.shape, BF16),
            pltpu.SemaphoreType.DMA((8,)),
        ],
        us=3, name="prepare", n_hbm=5, hbm_out=2,
    )(block_position, key_input, value_input, query_input, out_grad, table)
    kv_got = cross(kv_send, 1)
    q_send, kv_got = lax.optimization_barrier((q_send, kv_got))
    q_got = cross(q_send, 1)
    near = [jnp.stack([kv_keep, kv_got])]
    near.append(along(near[0], 1))
    ready, first_far = lax.optimization_barrier((near[1], onward(near[0])))
    far = [first_far, None]
    for k in range(2, n_pieces, 2):
        piece_k, lists, counts, _ = lax.optimization_barrier(
            (along(near[0], k), lists, counts, ready)
        )
        near += [piece_k, along(piece_k, 1)]
        far += [onward(piece_k), None]
    stats = call(
        functools.partial(current_stats, 1), stats_shape, 2, [pltpu.VMEM((split, *piece), BF16)],
        us=4, name="near_statistics", hold=(2,),
    )(lists, counts, q_keep, q_got, *near[:2])
    ready, far[2], stats = lax.optimization_barrier((ready, far[2], stats))
    far[1] = onward(ready)
    for k in range(2, n_pieces, 2):
        far[k + 1] = along(far[k], 1)
    stats = call(
        functools.partial(current_stats, 2), stats_shape, 2,
        [pltpu.VMEM((n_seq - split, *piece), BF16)], us=4, name="far_statistics",
    )(lists, counts, q_keep, q_got, stats, *near[2:])

    def grads_call(kernel, n_slots, n_store, outs, us, name, kept=(), more=()):
        pair = (n_slots, HALF_KV, 2, BLK, ROWS)
        saved = jax.ShapeDtypeStruct((2, *pair), BF16)
        return call(
            kernel, (*outs, saved, *more), 2,
            [
                pltpu.VMEM((n_store, *piece), BF16), pltpu.VMEM((n_store, *piece), F32),
                pltpu.VMEM(pair, BF16), pltpu.SemaphoreType.DMA((n_slots,)), *kept,
            ],
            us=us, name=name, hbm_out=len(outs),
        )

    kept = pltpu.VMEM((n_far, HALF_KV, BLK, ROWS), F32)
    two = jax.ShapeDtypeStruct((2 * CORES, *piece), BF16)
    first_far, *far_grads, far_saved, stats = grads_call(
        functools.partial(previous_grads, n_pieces), n_far, n_seq, (two,) + (low,) * (n_pieces - 2),
        14, "previous_gradients", (kept, kept), (stats_shape,),
    )(lists, counts, q_keep, q_got, stats, *far)

    def current_call(section, outs, name, pieces, after):
        stats_late, _ = lax.optimization_barrier((stats, after))
        n_store = CORES * len(pieces)
        *grads, saved = grads_call(
            functools.partial(current_grads, section, len(pieces)), min(n_store, n_listed), n_store,
            outs, 6, name,
        )(lists, counts, q_keep, q_got, stats_late, *pieces)
        return grads, saved

    def total(*terms):
        return sum(term.astype(F32) for term in terms).astype(BF16)

    from_far = back(first_far)
    crossing = [along(grad, 1) for grad in far_grads[1::2]]
    high_grads, high_saved = current_call(
        2, [high, low] * (n_pieces // 2 - 1), "far_current_gradients", near[2:], far_grads[0]
    )
    crossing, high_grads = lax.optimization_barrier((crossing, high_grads))
    arrived = [
        back(total(grad, extra)) for grad, extra in zip(far_grads[0::2], crossing)
    ]
    swapped = [along(grad, 1) for grad in high_grads[1::2]]
    low_grads, low_saved = current_call(
        1, [high, high], "near_current_gradients", near[:2], high_grads[0]
    )
    low_grads, from_far = lax.optimization_barrier((low_grads, from_far))
    from_next = along(total(low_grads[1], from_far[CORES:]), 1)
    merged = [
        total(*terms) for terms in zip(high_grads[0::2], arrived, swapped)
    ]
    half_out = jax.ShapeDtypeStruct((2, BLK, RATIO * HEAD_DIM), BF16)
    place_late, _ = lax.optimization_barrier((block_position, merged))
    wide = pltpu.VMEM((HEAD_DIM, ROWS), F32)
    slots = (2, n_listed + 1)
    halves = call(
        functools.partial(query_results, n_seq), (half_out,) * (2 * HALF_KV), 3,
        [
            pltpu.VMEM((2 * n_seq, *piece), BF16), pltpu.VMEM((*slots, HALF_KV, 2, BLK, ROWS), BF16),
            wide, wide, pltpu.SemaphoreType.DMA(slots),
        ],
        us=20, name="query_results", n_hbm=3,
    )(lists, counts, place_late, far_saved, low_saved, high_saved, *far, *near, table)
    own_halves, other_halves = halves[:HALF_KV], halves[HALF_KV:]
    other_halves = lax.optimization_barrier(list(other_halves))
    got_halves = [cross(half, 1) for half in other_halves]
    final = [low_grads[0], from_far[:CORES], from_next]
    final += [along(part, 2 + 2 * n) for n, part in enumerate(merged)]
    own_halves = list(own_halves)
    final[0], own_halves[1] = lax.optimization_barrier((final[0], own_halves[1]))
    kv_half = jax.ShapeDtypeStruct((2, BLK, HALF_KV * HEAD_DIM), BF16)
    own_kv, other_kv = call(
        functools.partial(finish_kv, n_seq), (kv_half, kv_half), 1, us=2, name="key_gradients"
    )(block_position, *final, table)
    got_kv = cross(other_kv, 1)
    q_out = jax.ShapeDtypeStruct(query_input.shape, BF16)
    kv_out = jax.ShapeDtypeStruct(key_input.shape, BF16)
    out_rows, query_grad, key_grad, value_grad = call(
        join_halves, (q_out, q_out, kv_out, kv_out), 0, us=2, name="join_halves"
    )(*own_halves, *got_halves, own_kv, got_kv)
    return (out_rows, query_grad, key_grad, value_grad)


def solution(mesh):
    split = P(("grp", "seq"), None)
    return jax.shard_map(
        local,
        mesh=mesh,
        in_specs=(split, split, split, split, P(), P(), P()),
        out_specs=(split, split, split, split),
        check_vma=False,
    )
```

```python
import functools
import math

import jax
import jax.numpy as jnp
import numpy as np
from jax import lax
from jax.experimental import pallas as pl
from jax.experimental.pallas import tpu as pltpu
from jax.sharding import PartitionSpec as P

HEADS = 32
KV_HEADS = 4
HEAD_DIM = 128
BLK = 128
CORES = 2
RATIO = HEADS // KV_HEADS
HALF_KV = KV_HEADS // CORES
ROWS = RATIO * BLK
SCALE = 1.0 / math.sqrt(HEAD_DIM)
TO_LOG2 = SCALE * math.log2(math.e)
F32 = jnp.float32
BF16 = jnp.bfloat16
CHUNK = 256

VMEM_SPEC = pl.BlockSpec(memory_space=pltpu.VMEM)
HBM_SPEC = pl.BlockSpec(memory_space=pltpu.HBM)
SMEM_SPEC = pl.BlockSpec(memory_space=pltpu.SMEM)


def trig_table(n_blocks):
    half = HEAD_DIM // 2
    frequency = np.power(500000.0, -np.arange(half) * (2.0 / HEAD_DIM))
    parts = []
    for places in (np.arange(n_blocks) * BLK, np.arange(BLK)):
        angles = places[:, None] * frequency
        for part in (np.cos(angles), np.sin(angles)):
            parts.append(np.concatenate([part, part], axis=1))
    return np.concatenate(parts, axis=0).astype(np.float32)


def block_tables(place, table):
    n_blocks = table.shape[0] // 2 - BLK
    cos_b = table[pl.ds(place, 1), :]
    sin_b = table[pl.ds(n_blocks + place, 1), :]
    cos_t = table[2 * n_blocks : 2 * n_blocks + BLK, :]
    sin_t = table[2 * n_blocks + BLK :, :]
    cosine = cos_b * cos_t - sin_b * sin_t
    sine = sin_b * cos_t + cos_b * sin_t
    lanes = lax.broadcasted_iota(jnp.int32, sine.shape, 1)
    return cosine, jnp.where(lanes < HEAD_DIM // 2, -sine, sine)


def turn(values, cosine, signed_sine):
    return values * cosine + pltpu.roll(values, HEAD_DIM // 2, 1) * signed_sine


def dot_nt(a, b):
    return lax.dot_general(a, b, (((1,), (1,)), ((), ())), preferred_element_type=F32)


def dot_nn(a, b):
    return lax.dot_general(a, b, (((1,), (0,)), ((), ())), preferred_element_type=F32)


def here(n_seq):
    member = lax.axis_index("seq")
    group = lax.axis_index("grp")
    return group, member, lax.rem(member, CORES)


def size_of(array):
    return math.prod(array.shape) * jnp.dtype(array.dtype).itemsize


def call(kernel, out_shape, n_smem, scratch=(), us=1, name=None, n_hbm=0, hbm_out=None, hold=()):
    def placed(n, a):
        if n == hbm_out:
            return pltpu.HBM(a.shape, a.dtype)
        return a

    def spec(n, a):
        if a.dtype == jnp.int32:
            return SMEM_SPEC
        return HBM_SPEC if n == hbm_out else VMEM_SPEC

    def run(*arrays):
        n_left = n_smem + n_hbm
        outs = list(out_shape) if isinstance(out_shape, (tuple, list)) else [out_shape]
        held = sum(size_of(a) for a in arrays[n_left:])
        held += sum(size_of(a) for n, a in enumerate(outs) if n != hbm_out)
        held += sum(size_of(a) for a in scratch if a.dtype in (F32, BF16))
        in_specs = [SMEM_SPEC] * n_smem + [HBM_SPEC] * n_hbm
        in_specs += [VMEM_SPEC] * (len(arrays) - n_left)
        pinned = [
            pltpu.with_memory_space_constraint(a, pltpu.HBM) if n < n_left or n in hold else a
            for n, a in enumerate(arrays)
        ]
        results = pl.pallas_call(
            kernel,
            out_shape=[placed(n, a) for n, a in enumerate(outs)],
            in_specs=in_specs,
            out_specs=[spec(n, a) for n, a in enumerate(outs)],
            scratch_shapes=list(scratch),
            compiler_params=pltpu.CompilerParams(vmem_limit_bytes=held + 6 * 2**20),
            cost_estimate=pl.CostEstimate(
                flops=us * 10**9, bytes_accessed=2**20, transcendentals=0
            ),
            name=name,
        )(*pinned)
        return results if isinstance(out_shape, (tuple, list)) else results[0]

    return run


def prepare(n_seq, place_ref, *refs):
    key, value, query, grad, table_hbm, kv_keep, kv_send, q_keep, q_send = refs[:9]
    key_here, value_here, table, query_here, grad_here, kept, sems = refs[9:]
    group, member, core = here(n_seq)
    half_heads = HEADS // CORES
    halves = (1 - core, core)

    def copy(n, source, place):
        return pltpu.make_async_copy(source, place, sems.at[n])

    def columns(first, count=1):
        return pl.ds(pl.multiple_of(first * HEAD_DIM, HEAD_DIM), count * HEAD_DIM)

    loads = [copy(0, key, key_here), copy(1, table_hbm, table), copy(2, value, value_here)]
    for n, half in enumerate(halves):
        part = columns(half * half_heads, half_heads)
        loads.append(copy(3 + 2 * n, query.at[:, part], query_here.at[n]))
        loads.append(copy(4 + 2 * n, grad.at[:, part], grad_here.at[n]))
    for load in (*loads[:3], *loads[5:], *loads[3:5]):
        load.start()
    for load in loads[:3]:
        load.wait()
    cosine, sine = block_tables(place_ref[group * n_seq + member], table)
    for half, out in zip(halves, (kv_send, kv_keep)):
        for h in range(HALF_KV):
            at = columns(half * HALF_KV + h)
            out[0, h] = turn(key_here[:, at].astype(F32), cosine, sine).astype(BF16)
            out[1, h] = value_here[:, at]
    away = copy(7, kept, q_keep)
    for n, out in ((1, kept), (0, q_send)):
        loads[3 + 2 * n].wait()
        loads[4 + 2 * n].wait()
        for h in range(HALF_KV):
            for r in range(RATIO):
                at = slice((h * RATIO + r) * HEAD_DIM, (h * RATIO + r + 1) * HEAD_DIM)
                part = query_here[n, :, at].astype(F32)
                out[0, h, r] = turn(part, cosine, sine).astype(BF16)
                out[1, h, r] = grad_here[n, :, at]
        if n == 1:
            away.start()
    away.wait()


def make_lists(n_seq, split, key_blocks, key_counts, lists, counts):
    group, member, _ = here(n_seq)
    for i in range(2):
        block = group * n_seq + lax.bitwise_xor(member, i)
        for section in range(3):
            counts[i, section] = int(section == 1)
        lists[i, 1, 0] = i

        def look(j, _):
            place = lax.bitwise_xor(key_blocks[block, j] - (group - 1) * n_seq, member)
            section = (place >= n_seq).astype(jnp.int32)
            section += (place >= n_seq + split).astype(jnp.int32)
            n = counts[i, section]
            lists[i, section, n] = place - jnp.where(section == 0, 0, n_seq) - jnp.where(
                section == 2, split, 0
            )
            counts[i, section] = n + 1
            return 0

        lax.fori_loop(1, key_counts[block], look, 0)
        total = 0
        for section, base in enumerate((0, n_seq, n_seq + split)):

            def append(n, m):
                lists[i, 3, m] = lists[i, section, n] + base
                return m + 1

            total = lax.fori_loop(0, counts[i, section], append, jnp.int32(total))
        counts[i, 3] = total
        lists[i, 3, total] = 0


def causal():
    keys = lax.broadcasted_iota(jnp.int32, (BLK, CHUNK), 0)
    tokens = lax.rem(lax.broadcasted_iota(jnp.int32, (BLK, CHUNK), 1), BLK)
    return keys <= tokens


def chunks():
    per = CHUNK // BLK
    return [
        (slice(c * per, (c + 1) * per), slice(c * CHUNK, (c + 1) * CHUNK))
        for c in range(ROWS // CHUNK)
    ]


def heads_of(block, what, h, rows):
    return block[what, h, rows].reshape(CHUNK, HEAD_DIM)


def fill(store, pieces, first=0):
    for k, piece in enumerate(pieces):
        store[first + CORES * k : first + CORES * (k + 1)] = piece[...]


def pair_scores(store, e, h, block, rows, diagonal):
    scores = dot_nt(store[e, 0, h], heads_of(block, 0, h, rows))
    if diagonal:
        scores = jnp.where(causal(), scores, -1e30)
    return scores, dot_nt(store[e, 1, h], heads_of(block, 1, h, rows))


def gather_stats(store, e, block, stats, i, diagonal, kept=None):
    for h in range(HALF_KV):
        for rows, columns in chunks():
            scores, dprobs = pair_scores(store, e, h, block, rows, diagonal)
            if kept is not None:
                n, kept_scores, kept_dprobs = kept
                kept_scores[n, h, :, columns] = scores
                kept_dprobs[n, h, :, columns] = dprobs
            top = jnp.max(scores, axis=0, keepdims=True)
            if not diagonal:
                old_top = stats[i, h, 0:1, columns]
                top = jnp.maximum(top, old_top)
            weights = jnp.exp2((scores - top) * TO_LOG2)
            total = jnp.sum(weights, axis=0, keepdims=True)
            mixed = jnp.sum(weights * dprobs, axis=0, keepdims=True)
            if not diagonal:
                shrink = jnp.exp2((old_top - top) * TO_LOG2)
                total += stats[i, h, 1:2, columns] * shrink
                mixed += stats[i, h, 2:3, columns] * shrink
            stats[i, h, 0:1, columns] = top
            stats[i, h, 1:2, columns] = total
            stats[i, h, 2:3, columns] = mixed


def spread_grads(found, count, kept_scores, kept_dprobs, stats, i, block, acc, saved, low, sent):
    def copy(n):
        return pltpu.make_async_copy(low.at[n], saved.at[i, n], sent.at[n])

    def add(n, _):
        e = found[n]
        for h in range(HALF_KV):
            dk, dv = acc[e, 0, h], acc[e, 1, h]
            for rows, columns in chunks():
                probs = jnp.exp2(
                    kept_scores[n, h, :, columns] * TO_LOG2 - stats[i, h, 0:1, columns]
                )
                dscores = probs * (kept_dprobs[n, h, :, columns] - stats[i, h, 2:3, columns])
                probs, dscores = probs.astype(BF16), dscores.astype(BF16)
                low[n, h, 0, :, columns] = probs
                low[n, h, 1, :, columns] = dscores
                dv += dot_nn(probs, heads_of(block, 1, h, rows))
                dk += dot_nn(dscores, heads_of(block, 0, h, rows))
            acc[e, 0, h] = dk
            acc[e, 1, h] = dv
        copy(n).start()
        return 0

    def finish(n, _):
        copy(n).wait()
        return 0

    lax.fori_loop(0, count, add, 0)
    lax.fori_loop(0, count, finish, 0)


def write_grads(acc, outs):
    start = 0
    for out in outs:
        part = slice(start, start + out.shape[0])
        out[:, 0] = (acc[part, 0] * SCALE).astype(out.dtype)
        out[:, 1] = acc[part, 1].astype(out.dtype)
        start += out.shape[0]


def current_stats(section, lists, counts, own, other, *rest):
    *pieces, stats, store = rest
    first = section == 1
    if not first:
        stats_in, *pieces = pieces
        stats[...] = stats_in[...]
    fill(store, pieces)
    for i, block in enumerate((own, other)):
        if first:
            gather_stats(store, i, block, stats, i, True)

        def step(n, _):
            gather_stats(store, lists[i, section, n], block, stats, i, False)
            return 0

        lax.fori_loop(int(first), counts[i, section], step, 0)


def previous_grads(n_pieces, lists, counts, own, other, stats_in, *rest):
    n_ends = 2 * n_pieces - 1
    pieces, outs = rest[:n_pieces], rest[n_pieces:n_ends]
    saved, stats, store, acc, low, sent, kept_scores, kept_dprobs = rest[n_ends:]
    fill(store, pieces)
    acc[...] = jnp.zeros_like(acc)
    stats[...] = stats_in[...]
    for i, block in enumerate((own, other)):
        count = counts[i, 0]

        def look(n, _):
            gather_stats(
                store, lists[i, 0, n], block, stats, i, False, (n, kept_scores, kept_dprobs)
            )
            return 0

        lax.fori_loop(0, count, look, 0)
        for h in range(HALF_KV):
            total = stats[i, h, 1:2, :]
            stats[i, h, 0:1, :] = stats[i, h, 0:1, :] * TO_LOG2 + jnp.log2(total)
            stats[i, h, 2:3, :] = stats[i, h, 2:3, :] / total

        def copy(n):
            return pltpu.make_async_copy(low.at[n], saved.at[i, n], sent.at[n])

        def add(n, _):
            e = lists[i, 0, n]
            for h in range(HALF_KV):
                dk, dv = acc[e, 0, h], acc[e, 1, h]
                for rows, columns in chunks():
                    probs = jnp.exp2(
                        kept_scores[n, h, :, columns] * TO_LOG2 - stats[i, h, 0:1, columns]
                    )
                    dscores = probs * (kept_dprobs[n, h, :, columns] - stats[i, h, 2:3, columns])
                    probs, dscores = probs.astype(BF16), dscores.astype(BF16)
                    low[n, h, 0, :, columns] = probs
                    low[n, h, 1, :, columns] = dscores
                    dv += dot_nn(probs, heads_of(block, 1, h, rows))
                    dk += dot_nn(dscores, heads_of(block, 0, h, rows))
                acc[e, 0, h] = dk
                acc[e, 1, h] = dv
            copy(n).start()
            return 0

        def finish(n, _):
            copy(n).wait()
            return 0

        lax.fori_loop(0, count, add, 0)
        lax.fori_loop(0, count, finish, 0)
    write_grads(acc, outs)


def current_grads(section, n_pieces, lists, counts, own, other, stats, *rest):
    pieces, outs = rest[:n_pieces], rest[n_pieces : 2 * n_pieces]
    saved, store, acc, low, sent = rest[2 * n_pieces :]
    first = section == 1
    fill(store, pieces)
    acc[...] = jnp.zeros_like(acc)
    for i, block in enumerate((own, other)):
        count = counts[i, section]

        def copy(n):
            return pltpu.make_async_copy(low.at[n], saved.at[i, n], sent.at[n])

        def look(n, diagonal):
            e = lists[i, section, n]
            for h in range(HALF_KV):
                for rows, columns in chunks():
                    scores, dprobs = pair_scores(store, e, h, block, rows, diagonal)
                    probs = jnp.exp2(scores * TO_LOG2 - stats[i, h, 0:1, columns])
                    low[n, h, 0, :, columns] = probs.astype(BF16)
                    dscores = probs * (dprobs - stats[i, h, 2:3, columns])
                    low[n, h, 1, :, columns] = dscores.astype(BF16)
            copy(n).start()
            return 0

        def add(n, _):
            e = lists[i, section, n]
            for h in range(HALF_KV):
                for w in range(2):
                    right = block[1 - w, h].reshape(ROWS, HEAD_DIM)
                    acc[e, 1 - w, h] += dot_nn(low[n, h, w], right)
            return 0

        def finish(n, _):
            copy(n).wait()
            return 0

        if first:
            look(0, True)
        lax.fori_loop(int(first), count, lambda n, _: look(n, False), 0)
        lax.fori_loop(0, count, add, 0)
        lax.fori_loop(0, count, finish, 0)
    write_grads(acc, outs)


def query_results(n_seq, lists, counts, place_ref, *rest):
    n_saved = 3
    n_pieces = n_seq // CORES
    saved, pieces, rest = rest[:n_saved], rest[n_saved:][: 2 * n_pieces], rest[n_saved + 2 * n_pieces :]
    table, *rest = rest
    outs, (store, low, out_acc, dq_acc, got) = rest[: 2 * HALF_KV], rest[2 * HALF_KV :]
    group, member, _ = here(n_seq)

    def copy(source, h, i, n, first):
        return pltpu.make_async_copy(source.at[i, n - first, h], low.at[h, i, n], got.at[h, i, n])

    ends = []
    for i in range(2):
        stops = [0]
        for section in range(n_saved):
            stops.append(stops[-1] + counts[i, section])
        ends.append(stops)
    for h in range(HALF_KV):
        for i, stops in enumerate(ends):
            for source, first, stop in zip(saved, stops, stops[1:]):

                def fetch_one(n, _):
                    copy(source, h, i, n, first).start()
                    return 0

                lax.fori_loop(first, stop, fetch_one, 0)
    fill(store, pieces)
    tables = []
    for i in range(2):
        mine = group * n_seq + lax.bitwise_xor(member, i)
        cosine, sine = block_tables(place_ref[mine], table)
        tables.append((cosine.T * SCALE, sine.T * SCALE))
    for h, (i, stops) in ((h, pair) for h in range(HALF_KV) for pair in enumerate(ends)):
        total = stops[-1]
        result = outs[i * HALF_KV + h]

        @pl.when(lax.rem(total, 2) == 1)
        def _():
            low[h, i, total] = jnp.zeros((2, BLK, ROWS), BF16)

        out_acc[...] = jnp.zeros_like(out_acc)
        dq_acc[...] = jnp.zeros_like(dq_acc)

        def add(n, _):
            pair = (2 * n, 2 * n + 1)
            for m in pair:

                @pl.when(m < total)
                def _():
                    copy(saved[0], h, i, m, m).wait()

            found = [lists[i, 3, m] for m in pair]
            keys_t = jnp.concatenate([store[e, 0, h].T for e in found], axis=1)
            values_t = jnp.concatenate([store[e, 1, h].T for e in found], axis=1)
            for _, columns in chunks():
                probs = jnp.concatenate([low[h, i, m, 0, :, columns] for m in pair], axis=0)
                dscores = jnp.concatenate([low[h, i, m, 1, :, columns] for m in pair], axis=0)
                out_acc[:, columns] += dot_nn(values_t, probs)
                dq_acc[:, columns] += dot_nn(keys_t, dscores)
            return 0

        lax.fori_loop(0, lax.div(total + 1, 2), add, 0)
        cosine, sine = tables[i]
        for r in range(RATIO):
            rows = slice(r * BLK, (r + 1) * BLK)
            columns = slice(r * HEAD_DIM, (r + 1) * HEAD_DIM)
            result[0, :, columns] = out_acc[:, rows].astype(BF16).T
            dq = dq_acc[:, rows]
            half = HEAD_DIM // 2
            turned = jnp.concatenate([dq[half:], dq[:half]], axis=0)
            result[1, :, columns] = (dq * cosine - turned * sine).astype(BF16).T


def finish_kv(n_seq, place_ref, *rest):
    *terms, table, keep, send = rest
    group, member, _ = here(n_seq)
    for i, result in enumerate((keep, send)):
        offset = lax.bitwise_xor(member, i)
        cosine, sine = block_tables(place_ref[group * n_seq + offset], table)
        for h in range(HALF_KV):
            columns = slice(h * HEAD_DIM, (h + 1) * HEAD_DIM)
            dk, dv = (sum(term[i, w, h].astype(F32) for term in terms) for w in range(2))
            result[0, :, columns] = turn(dk, cosine, -sine).astype(BF16)
            result[1, :, columns] = dv.astype(BF16)


def join_halves(*refs):
    core = lax.rem(lax.axis_index("seq"), CORES)
    own_q, got_q, (own_kv, got_kv) = refs[:HALF_KV], refs[HALF_KV:][:HALF_KV], refs[2 * HALF_KV :][:2]
    outs = refs[2 * HALF_KV + 2 :]
    for own, got, results in ((own_q, got_q, outs[:2]), ([own_kv], [got_kv], outs[2:])):
        width = own[0].shape[-1]
        for half, parts in ((core, own), (1 - core, got)):
            for n, part in enumerate(parts):
                start = pl.multiple_of((half * len(parts) + n) * width, width)
                for w, out in enumerate(results):
                    out[:, pl.ds(start, width)] = part[w]


def local(query_input, key_input, value_input, out_grad, key_blocks, key_counts, block_position):
    n_seq = lax.axis_size("seq")
    n_grp = lax.axis_size("grp")
    n_pieces = n_seq // CORES
    n_listed = key_blocks.shape[1]

    def cross(array, by):
        return lax.ppermute(array, "seq", [(m, m ^ by) for m in range(n_seq)])

    def along(array, by):
        return cross(array, CORES * by)

    def onward(array):
        return lax.ppermute(array, "grp", [(g, g + 1) for g in range(n_grp - 1)])

    def back(array):
        return lax.ppermute(array, "grp", [(g + 1, g) for g in range(n_grp - 1)])

    table = trig_table(block_position.shape[0])
    n_far = min(n_seq, n_listed - 1)
    split = 2 * CORES
    piece = (2, HALF_KV, BLK, HEAD_DIM)
    chip = (CORES, *piece)
    q_shape = jax.ShapeDtypeStruct((2, HALF_KV, RATIO, BLK, HEAD_DIM), BF16)
    kv_shape = jax.ShapeDtypeStruct(piece, BF16)
    stats_shape = jax.ShapeDtypeStruct((2, HALF_KV, 8, ROWS), F32)
    low = jax.ShapeDtypeStruct(chip, BF16)
    high = jax.ShapeDtypeStruct(chip, F32)
    lists, counts = call(
        functools.partial(make_lists, n_seq, split),
        (
            jax.ShapeDtypeStruct((2, 4, n_listed + 1), jnp.int32),
            jax.ShapeDtypeStruct((2, 4), jnp.int32),
        ),
        2, us=2, name="block_lists",
    )(key_blocks, key_counts)

    halves = pltpu.VMEM((CORES, query_input.shape[0], HEADS // CORES * HEAD_DIM), BF16)
    kv_keep, kv_send, q_keep, q_send = call(
        functools.partial(prepare, n_seq), (kv_shape, kv_shape, q_shape, q_shape), 1,
        [
            pltpu.VMEM(key_input.shape, BF16), pltpu.VMEM(value_input.shape, BF16),
            pltpu.VMEM(table.shape, F32), halves, halves, pltpu.VMEM(q_shape.shape, BF16),
            pltpu.SemaphoreType.DMA((8,)),
        ],
        us=3, name="prepare", n_hbm=5, hbm_out=2,
    )(block_position, key_input, value_input, query_input, out_grad, table)
    kv_got = cross(kv_send, 1)
    q_send, kv_got = lax.optimization_barrier((q_send, kv_got))
    q_got = cross(q_send, 1)
    near = [jnp.stack([kv_keep, kv_got])]
    near.append(along(near[0], 1))
    ready, first_far = lax.optimization_barrier((near[1], onward(near[0])))
    far = [first_far, None]
    for k in range(2, n_pieces, 2):
        piece_k, lists, counts, _ = lax.optimization_barrier(
            (along(near[0], k), lists, counts, ready)
        )
        near += [piece_k, along(piece_k, 1)]
        far += [onward(piece_k), None]
    stats = call(
        functools.partial(current_stats, 1), stats_shape, 2, [pltpu.VMEM((split, *piece), BF16)],
        us=4, name="near_statistics", hold=(2,),
    )(lists, counts, q_keep, q_got, *near[:2])
    ready, far[2], stats = lax.optimization_barrier((ready, far[2], stats))
    far[1] = onward(ready)
    for k in range(2, n_pieces, 2):
        far[k + 1] = along(far[k], 1)
    stats = call(
        functools.partial(current_stats, 2), stats_shape, 2,
        [pltpu.VMEM((n_seq - split, *piece), BF16)], us=4, name="far_statistics",
    )(lists, counts, q_keep, q_got, stats, *near[2:])

    def grads_call(kernel, n_slots, n_store, outs, us, name, kept=(), more=()):
        pair = (n_slots, HALF_KV, 2, BLK, ROWS)
        saved = jax.ShapeDtypeStruct((2, *pair), BF16)
        return call(
            kernel, (*outs, saved, *more), 2,
            [
                pltpu.VMEM((n_store, *piece), BF16), pltpu.VMEM((n_store, *piece), F32),
                pltpu.VMEM(pair, BF16), pltpu.SemaphoreType.DMA((n_slots,)), *kept,
            ],
            us=us, name=name, hbm_out=len(outs),
        )

    kept = pltpu.VMEM((n_far, HALF_KV, BLK, ROWS), F32)
    two = jax.ShapeDtypeStruct((2 * CORES, *piece), BF16)
    first_far, *far_grads, far_saved, stats = grads_call(
        functools.partial(previous_grads, n_pieces), n_far, n_seq, (two,) + (low,) * (n_pieces - 2),
        14, "previous_gradients", (kept, kept), (stats_shape,),
    )(lists, counts, q_keep, q_got, stats, *far)

    def current_call(section, outs, name, pieces, after):
        stats_late, _ = lax.optimization_barrier((stats, after))
        n_store = CORES * len(pieces)
        *grads, saved = grads_call(
            functools.partial(current_grads, section, len(pieces)), min(n_store, n_listed), n_store,
            outs, 6, name,
        )(lists, counts, q_keep, q_got, stats_late, *pieces)
        return grads, saved

    def total(*terms):
        return sum(term.astype(F32) for term in terms).astype(BF16)

    from_far = back(first_far)
    crossing = [along(grad, 1) for grad in far_grads[1::2]]
    high_grads, high_saved = current_call(
        2, [high, low] * (n_pieces // 2 - 1), "far_current_gradients", near[2:], far_grads[0]
    )
    crossing, high_grads = lax.optimization_barrier((crossing, high_grads))
    arrived = [
        back(total(grad, extra)) for grad, extra in zip(far_grads[0::2], crossing)
    ]
    swapped = [along(grad, 1) for grad in high_grads[1::2]]
    low_grads, low_saved = current_call(
        1, [high, high], "near_current_gradients", near[:2], high_grads[0]
    )
    low_grads, from_far = lax.optimization_barrier((low_grads, from_far))
    from_next = along(total(low_grads[1], from_far[CORES:]), 1)
    merged = [
        total(*terms) for terms in zip(high_grads[0::2], arrived, swapped)
    ]
    half_out = jax.ShapeDtypeStruct((2, BLK, RATIO * HEAD_DIM), BF16)
    place_late, _ = lax.optimization_barrier((block_position, merged))
    wide = pltpu.VMEM((HEAD_DIM, ROWS), F32)
    slots = (HALF_KV, 2, n_listed + 1)
    halves = call(
        functools.partial(query_results, n_seq), (half_out,) * (2 * HALF_KV), 3,
        [
            pltpu.VMEM((2 * n_seq, *piece), BF16), pltpu.VMEM((*slots, 2, BLK, ROWS), BF16),
            wide, wide, pltpu.SemaphoreType.DMA(slots),
        ],
        us=20, name="query_results", n_hbm=3,
    )(lists, counts, place_late, far_saved, low_saved, high_saved, *far, *near, table)
    own_halves, other_halves = halves[:HALF_KV], halves[HALF_KV:]
    other_halves = lax.optimization_barrier(list(other_halves))
    got_halves = [cross(half, 1) for half in other_halves]
    final = [low_grads[0], from_far[:CORES], from_next]
    final += [along(part, 2 + 2 * n) for n, part in enumerate(merged)]
    own_halves = list(own_halves)
    final[0], own_halves[1] = lax.optimization_barrier((final[0], own_halves[1]))
    kv_half = jax.ShapeDtypeStruct((2, BLK, HALF_KV * HEAD_DIM), BF16)
    own_kv, other_kv = call(
        functools.partial(finish_kv, n_seq), (kv_half, kv_half), 1, us=2, name="key_gradients"
    )(block_position, *final, table)
    got_kv = cross(other_kv, 1)
    q_out = jax.ShapeDtypeStruct(query_input.shape, BF16)
    kv_out = jax.ShapeDtypeStruct(key_input.shape, BF16)
    out_rows, query_grad, key_grad, value_grad = call(
        join_halves, (q_out, q_out, kv_out, kv_out), 0, us=2, name="join_halves"
    )(*own_halves, *got_halves, own_kv, got_kv)
    return (out_rows, query_grad, key_grad, value_grad)


def solution(mesh):
    split = P(("grp", "seq"), None)
    return jax.shard_map(
        local,
        mesh=mesh,
        in_specs=(split, split, split, split, P(), P(), P()),
        out_specs=(split, split, split, split),
        check_vma=False,
    )
```

```python
import functools
import math

import jax
import jax.numpy as jnp
import numpy as np
from jax import lax
from jax.experimental import pallas as pl
from jax.experimental.pallas import tpu as pltpu
from jax.sharding import PartitionSpec as P

HEADS = 32
KV_HEADS = 4
HEAD_DIM = 128
BLK = 128
CORES = 2
RATIO = HEADS // KV_HEADS
HALF_KV = KV_HEADS // CORES
ROWS = RATIO * BLK
SCALE = 1.0 / math.sqrt(HEAD_DIM)
TO_LOG2 = SCALE * math.log2(math.e)
F32 = jnp.float32
BF16 = jnp.bfloat16
CHUNK = 256

VMEM_SPEC = pl.BlockSpec(memory_space=pltpu.VMEM)
HBM_SPEC = pl.BlockSpec(memory_space=pltpu.HBM)
SMEM_SPEC = pl.BlockSpec(memory_space=pltpu.SMEM)


def trig_table(n_blocks):
    half = HEAD_DIM // 2
    frequency = np.power(500000.0, -np.arange(half) * (2.0 / HEAD_DIM))
    parts = []
    for places in (np.arange(n_blocks) * BLK, np.arange(BLK)):
        angles = places[:, None] * frequency
        for part in (np.cos(angles), np.sin(angles)):
            parts.append(np.concatenate([part, part], axis=1))
    return np.concatenate(parts, axis=0).astype(np.float32)


def block_tables(place, table):
    n_blocks = table.shape[0] // 2 - BLK
    cos_b = table[pl.ds(place, 1), :]
    sin_b = table[pl.ds(n_blocks + place, 1), :]
    cos_t = table[2 * n_blocks : 2 * n_blocks + BLK, :]
    sin_t = table[2 * n_blocks + BLK :, :]
    cosine = cos_b * cos_t - sin_b * sin_t
    sine = sin_b * cos_t + cos_b * sin_t
    lanes = lax.broadcasted_iota(jnp.int32, sine.shape, 1)
    return cosine, jnp.where(lanes < HEAD_DIM // 2, -sine, sine)


def turn(values, cosine, signed_sine):
    return values * cosine + pltpu.roll(values, HEAD_DIM // 2, 1) * signed_sine


def dot_nt(a, b):
    return lax.dot_general(a, b, (((1,), (1,)), ((), ())), preferred_element_type=F32)


def dot_nn(a, b):
    return lax.dot_general(a, b, (((1,), (0,)), ((), ())), preferred_element_type=F32)


def here(n_seq):
    member = lax.axis_index("seq")
    group = lax.axis_index("grp")
    return group, member, lax.rem(member, CORES)


def size_of(array):
    return math.prod(array.shape) * jnp.dtype(array.dtype).itemsize


def call(kernel, out_shape, n_smem, scratch=(), us=1, name=None, n_hbm=0, hbm_out=None, hold=()):
    def placed(n, a):
        if n == hbm_out:
            return pltpu.HBM(a.shape, a.dtype)
        return a

    def spec(n, a):
        if a.dtype == jnp.int32:
            return SMEM_SPEC
        return HBM_SPEC if n == hbm_out else VMEM_SPEC

    def run(*arrays):
        n_left = n_smem + n_hbm
        outs = list(out_shape) if isinstance(out_shape, (tuple, list)) else [out_shape]
        held = sum(size_of(a) for a in arrays[n_left:])
        held += sum(size_of(a) for n, a in enumerate(outs) if n != hbm_out)
        held += sum(size_of(a) for a in scratch if a.dtype in (F32, BF16))
        in_specs = [SMEM_SPEC] * n_smem + [HBM_SPEC] * n_hbm
        in_specs += [VMEM_SPEC] * (len(arrays) - n_left)
        pinned = [
            pltpu.with_memory_space_constraint(a, pltpu.HBM) if n < n_left or n in hold else a
            for n, a in enumerate(arrays)
        ]
        results = pl.pallas_call(
            kernel,
            out_shape=[placed(n, a) for n, a in enumerate(outs)],
            in_specs=in_specs,
            out_specs=[spec(n, a) for n, a in enumerate(outs)],
            scratch_shapes=list(scratch),
            compiler_params=pltpu.CompilerParams(vmem_limit_bytes=held + 6 * 2**20),
            cost_estimate=pl.CostEstimate(
                flops=us * 10**9, bytes_accessed=2**20, transcendentals=0
            ),
            name=name,
        )(*pinned)
        return results if isinstance(out_shape, (tuple, list)) else results[0]

    return run


def prepare(n_seq, place_ref, *refs):
    key, value, query, grad, table_hbm, kv_keep, kv_send, q_keep, q_send = refs[:9]
    key_here, value_here, table, query_here, grad_here, kept, sems = refs[9:]
    group, member, core = here(n_seq)
    half_heads = HEADS // CORES
    halves = (1 - core, core)

    def copy(n, source, place):
        return pltpu.make_async_copy(source, place, sems.at[n])

    def columns(first, count=1):
        return pl.ds(pl.multiple_of(first * HEAD_DIM, HEAD_DIM), count * HEAD_DIM)

    loads = [copy(0, key, key_here), copy(1, table_hbm, table), copy(2, value, value_here)]
    for n, half in enumerate(halves):
        part = columns(half * half_heads, half_heads)
        loads.append(copy(3 + 2 * n, query.at[:, part], query_here.at[n]))
        loads.append(copy(4 + 2 * n, grad.at[:, part], grad_here.at[n]))
    for load in (*loads[:3], *loads[5:], *loads[3:5]):
        load.start()
    for load in loads[:3]:
        load.wait()
    cosine, sine = block_tables(place_ref[group * n_seq + member], table)
    for half, out in zip(halves, (kv_send, kv_keep)):
        for h in range(HALF_KV):
            at = columns(half * HALF_KV + h)
            out[0, h] = turn(key_here[:, at].astype(F32), cosine, sine).astype(BF16)
            out[1, h] = value_here[:, at]
    away = copy(7, kept, q_keep)
    for n, out in ((1, kept), (0, q_send)):
        loads[3 + 2 * n].wait()
        loads[4 + 2 * n].wait()
        for h in range(HALF_KV):
            for r in range(RATIO):
                at = slice((h * RATIO + r) * HEAD_DIM, (h * RATIO + r + 1) * HEAD_DIM)
                part = query_here[n, :, at].astype(F32)
                out[0, h, r] = turn(part, cosine, sine).astype(BF16)
                out[1, h, r] = grad_here[n, :, at]
        if n == 1:
            away.start()
    away.wait()


def make_lists(n_seq, split, key_blocks, key_counts, lists, counts):
    group, member, _ = here(n_seq)
    for i in range(2):
        block = group * n_seq + lax.bitwise_xor(member, i)
        for section in range(3):
            counts[i, section] = int(section == 1)
        lists[i, 1, 0] = i

        def look(j, _):
            place = lax.bitwise_xor(key_blocks[block, j] - (group - 1) * n_seq, member)
            section = (place >= n_seq).astype(jnp.int32)
            section += (place >= n_seq + split).astype(jnp.int32)
            n = counts[i, section]
            lists[i, section, n] = place - jnp.where(section == 0, 0, n_seq) - jnp.where(
                section == 2, split, 0
            )
            counts[i, section] = n + 1
            return 0

        lax.fori_loop(1, key_counts[block], look, 0)
        total = 0
        for section, base in enumerate((0, n_seq, n_seq + split)):

            def append(n, m):
                lists[i, 3, m] = lists[i, section, n] + base
                return m + 1

            total = lax.fori_loop(0, counts[i, section], append, jnp.int32(total))
        counts[i, 3] = total
        lists[i, 3, total] = 0


def causal():
    keys = lax.broadcasted_iota(jnp.int32, (BLK, CHUNK), 0)
    tokens = lax.rem(lax.broadcasted_iota(jnp.int32, (BLK, CHUNK), 1), BLK)
    return keys <= tokens


def chunks():
    per = CHUNK // BLK
    return [
        (slice(c * per, (c + 1) * per), slice(c * CHUNK, (c + 1) * CHUNK))
        for c in range(ROWS // CHUNK)
    ]


def heads_of(block, what, h, rows):
    return block[what, h, rows].reshape(CHUNK, HEAD_DIM)


def fill(store, pieces, first=0):
    for k, piece in enumerate(pieces):
        store[first + CORES * k : first + CORES * (k + 1)] = piece[...]


def pair_scores(store, e, h, block, rows, diagonal):
    scores = dot_nt(store[e, 0, h], heads_of(block, 0, h, rows))
    if diagonal:
        scores = jnp.where(causal(), scores, -1e30)
    return scores, dot_nt(store[e, 1, h], heads_of(block, 1, h, rows))


def gather_stats(store, e, block, stats, i, diagonal, kept=None):
    for h in range(HALF_KV):
        for rows, columns in chunks():
            scores, dprobs = pair_scores(store, e, h, block, rows, diagonal)
            if kept is not None:
                n, kept_scores, kept_dprobs = kept
                kept_scores[n, h, :, columns] = scores
                kept_dprobs[n, h, :, columns] = dprobs
            top = jnp.max(scores, axis=0, keepdims=True)
            if not diagonal:
                old_top = stats[i, h, 0:1, columns]
                top = jnp.maximum(top, old_top)
            weights = jnp.exp2((scores - top) * TO_LOG2)
            total = jnp.sum(weights, axis=0, keepdims=True)
            mixed = jnp.sum(weights * dprobs, axis=0, keepdims=True)
            if not diagonal:
                shrink = jnp.exp2((old_top - top) * TO_LOG2)
                total += stats[i, h, 1:2, columns] * shrink
                mixed += stats[i, h, 2:3, columns] * shrink
            stats[i, h, 0:1, columns] = top
            stats[i, h, 1:2, columns] = total
            stats[i, h, 2:3, columns] = mixed


def spread_grads(found, count, kept_scores, kept_dprobs, stats, i, block, acc, saved, low, sent):
    def copy(n):
        return pltpu.make_async_copy(low.at[n], saved.at[i, n], sent.at[n])

    def add(n, _):
        e = found[n]
        for h in range(HALF_KV):
            dk, dv = acc[e, 0, h], acc[e, 1, h]
            for rows, columns in chunks():
                probs = jnp.exp2(
                    kept_scores[n, h, :, columns] * TO_LOG2 - stats[i, h, 0:1, columns]
                )
                dscores = probs * (kept_dprobs[n, h, :, columns] - stats[i, h, 2:3, columns])
                probs, dscores = probs.astype(BF16), dscores.astype(BF16)
                low[n, h, 0, :, columns] = probs
                low[n, h, 1, :, columns] = dscores
                dv += dot_nn(probs, heads_of(block, 1, h, rows))
                dk += dot_nn(dscores, heads_of(block, 0, h, rows))
            acc[e, 0, h] = dk
            acc[e, 1, h] = dv
        copy(n).start()
        return 0

    def finish(n, _):
        copy(n).wait()
        return 0

    lax.fori_loop(0, count, add, 0)
    lax.fori_loop(0, count, finish, 0)


def write_grads(acc, outs):
    start = 0
    for out in outs:
        part = slice(start, start + out.shape[0])
        out[:, 0] = (acc[part, 0] * SCALE).astype(out.dtype)
        out[:, 1] = acc[part, 1].astype(out.dtype)
        start += out.shape[0]


def current_stats(section, lists, counts, own, other, *rest):
    *pieces, stats, store = rest
    first = section == 1
    if not first:
        stats_in, *pieces = pieces
        stats[...] = stats_in[...]
    fill(store, pieces)
    for i, block in enumerate((own, other)):
        if first:
            gather_stats(store, i, block, stats, i, True)

        def step(n, _):
            gather_stats(store, lists[i, section, n], block, stats, i, False)
            return 0

        lax.fori_loop(int(first), counts[i, section], step, 0)


def previous_grads(n_pieces, lists, counts, own, other, stats_in, *rest):
    n_ends = 2 * n_pieces - 1
    pieces, outs = rest[:n_pieces], rest[n_pieces:n_ends]
    saved, stats, store, acc, low, sent, kept_scores, kept_dprobs = rest[n_ends:]
    fill(store, pieces)
    acc[...] = jnp.zeros_like(acc)
    stats[...] = stats_in[...]
    for i, block in enumerate((own, other)):
        count = counts[i, 0]

        def look(n, _):
            gather_stats(
                store, lists[i, 0, n], block, stats, i, False, (n, kept_scores, kept_dprobs)
            )
            return 0

        lax.fori_loop(0, count, look, 0)
        for h in range(HALF_KV):
            total = stats[i, h, 1:2, :]
            stats[i, h, 0:1, :] = stats[i, h, 0:1, :] * TO_LOG2 + jnp.log2(total)
            stats[i, h, 2:3, :] = stats[i, h, 2:3, :] / total

        def copy(n):
            return pltpu.make_async_copy(low.at[n], saved.at[i, n], sent.at[n])

        def add(n, _):
            e = lists[i, 0, n]
            for h in range(HALF_KV):
                dk, dv = acc[e, 0, h], acc[e, 1, h]
                for rows, columns in chunks():
                    probs = jnp.exp2(
                        kept_scores[n, h, :, columns] * TO_LOG2 - stats[i, h, 0:1, columns]
                    )
                    dscores = probs * (kept_dprobs[n, h, :, columns] - stats[i, h, 2:3, columns])
                    probs, dscores = probs.astype(BF16), dscores.astype(BF16)
                    low[n, h, 0, :, columns] = probs
                    low[n, h, 1, :, columns] = dscores
                    dv += dot_nn(probs, heads_of(block, 1, h, rows))
                    dk += dot_nn(dscores, heads_of(block, 0, h, rows))
                acc[e, 0, h] = dk
                acc[e, 1, h] = dv
            copy(n).start()
            return 0

        def finish(n, _):
            copy(n).wait()
            return 0

        lax.fori_loop(0, count, add, 0)
        lax.fori_loop(0, count, finish, 0)
    write_grads(acc, outs)


def current_grads(section, n_pieces, lists, counts, own, other, stats, *rest):
    pieces, outs = rest[:n_pieces], rest[n_pieces : 2 * n_pieces]
    saved, store, acc, low, sent = rest[2 * n_pieces :]
    first = section == 1
    fill(store, pieces)
    acc[...] = jnp.zeros_like(acc)
    for i, block in enumerate((own, other)):
        count = counts[i, section]

        def copy(n):
            return pltpu.make_async_copy(low.at[n], saved.at[i, n], sent.at[n])

        def look(n, diagonal):
            e = lists[i, section, n]
            for h in range(HALF_KV):
                for rows, columns in chunks():
                    scores, dprobs = pair_scores(store, e, h, block, rows, diagonal)
                    probs = jnp.exp2(scores * TO_LOG2 - stats[i, h, 0:1, columns])
                    low[n, h, 0, :, columns] = probs.astype(BF16)
                    dscores = probs * (dprobs - stats[i, h, 2:3, columns])
                    low[n, h, 1, :, columns] = dscores.astype(BF16)
            copy(n).start()
            return 0

        def add(n, _):
            e = lists[i, section, n]
            for h in range(HALF_KV):
                for w in range(2):
                    right = block[1 - w, h].reshape(ROWS, HEAD_DIM)
                    acc[e, 1 - w, h] += dot_nn(low[n, h, w], right)
            return 0

        def finish(n, _):
            copy(n).wait()
            return 0

        if first:
            look(0, True)
        lax.fori_loop(int(first), count, lambda n, _: look(n, False), 0)
        lax.fori_loop(0, count, add, 0)
        lax.fori_loop(0, count, finish, 0)
    write_grads(acc, outs)


def query_results(n_seq, lists, counts, place_ref, *rest):
    n_saved = 3
    n_pieces = n_seq // CORES
    saved, pieces, rest = rest[:n_saved], rest[n_saved:][: 2 * n_pieces], rest[n_saved + 2 * n_pieces :]
    table, *rest = rest
    outs, (store, low, out_acc, dq_acc, got) = rest[: 2 * HALF_KV], rest[2 * HALF_KV :]
    group, member, _ = here(n_seq)

    def copy(source, h, i, n, first):
        return pltpu.make_async_copy(source.at[i, n - first, h], low.at[h, i, n], got.at[h, i, n])

    ends = []
    for i in range(2):
        stops = [0]
        for section in range(n_saved):
            stops.append(stops[-1] + counts[i, section])
        ends.append(stops)
    for h in range(HALF_KV):
        for i, stops in enumerate(ends):
            for source, first, stop in zip(saved, stops, stops[1:]):

                def fetch_one(n, _):
                    copy(source, h, i, n, first).start()
                    return 0

                lax.fori_loop(first, stop, fetch_one, 0)
    fill(store, pieces)
    tables = []
    for i in range(2):
        mine = group * n_seq + lax.bitwise_xor(member, i)
        cosine, sine = block_tables(place_ref[mine], table)
        tables.append((cosine.T * SCALE, sine.T * SCALE))
    for h, (i, stops) in ((h, pair) for h in range(HALF_KV) for pair in enumerate(ends)):
        total = stops[-1]
        result = outs[i * HALF_KV + h]

        filled = lax.div(total + 3, 4) * 4
        for extra in range(3):

            @pl.when(total + extra < filled)
            def _():
                low[h, i, total + extra] = jnp.zeros((2, BLK, ROWS), BF16)

        out_acc[...] = jnp.zeros_like(out_acc)
        dq_acc[...] = jnp.zeros_like(dq_acc)

        def add(n, _):
            pair = [4 * n + m for m in range(4)]
            for m in pair:
                for source, first, stop in zip(saved, stops, stops[1:]):

                    @pl.when(jnp.logical_and(m >= first, m < stop))
                    def _():
                        copy(source, h, i, m, first).wait()

            found = [jnp.where(m < total, lists[i, 3, jnp.minimum(m, total)], 0) for m in pair]
            keys_t = jnp.concatenate([store[e, 0, h].T for e in found], axis=1)
            values_t = jnp.concatenate([store[e, 1, h].T for e in found], axis=1)
            for _, columns in chunks():
                probs = jnp.concatenate([low[h, i, m, 0, :, columns] for m in pair], axis=0)
                dscores = jnp.concatenate([low[h, i, m, 1, :, columns] for m in pair], axis=0)
                out_acc[:, columns] += dot_nn(values_t, probs)
                dq_acc[:, columns] += dot_nn(keys_t, dscores)
            return 0

        lax.fori_loop(0, lax.div(filled, 4), add, 0)
        cosine, sine = tables[i]
        for r in range(RATIO):
            rows = slice(r * BLK, (r + 1) * BLK)
            columns = slice(r * HEAD_DIM, (r + 1) * HEAD_DIM)
            result[0, :, columns] = out_acc[:, rows].astype(BF16).T
            dq = dq_acc[:, rows]
            half = HEAD_DIM // 2
            turned = jnp.concatenate([dq[half:], dq[:half]], axis=0)
            result[1, :, columns] = (dq * cosine - turned * sine).astype(BF16).T


def finish_kv(n_seq, place_ref, *rest):
    *terms, table, keep, send = rest
    group, member, _ = here(n_seq)
    for i, result in enumerate((keep, send)):
        offset = lax.bitwise_xor(member, i)
        cosine, sine = block_tables(place_ref[group * n_seq + offset], table)
        for h in range(HALF_KV):
            columns = slice(h * HEAD_DIM, (h + 1) * HEAD_DIM)
            dk, dv = (sum(term[i, w, h].astype(F32) for term in terms) for w in range(2))
            result[0, :, columns] = turn(dk, cosine, -sine).astype(BF16)
            result[1, :, columns] = dv.astype(BF16)


def join_halves(*refs):
    core = lax.rem(lax.axis_index("seq"), CORES)
    own_q, got_q, (own_kv, got_kv) = refs[:HALF_KV], refs[HALF_KV:][:HALF_KV], refs[2 * HALF_KV :][:2]
    outs = refs[2 * HALF_KV + 2 :]
    for own, got, results in ((own_q, got_q, outs[:2]), ([own_kv], [got_kv], outs[2:])):
        width = own[0].shape[-1]
        for half, parts in ((core, own), (1 - core, got)):
            for n, part in enumerate(parts):
                start = pl.multiple_of((half * len(parts) + n) * width, width)
                for w, out in enumerate(results):
                    out[:, pl.ds(start, width)] = part[w]


def local(query_input, key_input, value_input, out_grad, key_blocks, key_counts, block_position):
    n_seq = lax.axis_size("seq")
    n_grp = lax.axis_size("grp")
    n_pieces = n_seq // CORES
    n_listed = key_blocks.shape[1]

    def cross(array, by):
        return lax.ppermute(array, "seq", [(m, m ^ by) for m in range(n_seq)])

    def along(array, by):
        return cross(array, CORES * by)

    def onward(array):
        return lax.ppermute(array, "grp", [(g, g + 1) for g in range(n_grp - 1)])

    def back(array):
        return lax.ppermute(array, "grp", [(g + 1, g) for g in range(n_grp - 1)])

    table = trig_table(block_position.shape[0])
    n_far = min(n_seq, n_listed - 1)
    split = 2 * CORES
    piece = (2, HALF_KV, BLK, HEAD_DIM)
    chip = (CORES, *piece)
    q_shape = jax.ShapeDtypeStruct((2, HALF_KV, RATIO, BLK, HEAD_DIM), BF16)
    kv_shape = jax.ShapeDtypeStruct(piece, BF16)
    stats_shape = jax.ShapeDtypeStruct((2, HALF_KV, 8, ROWS), F32)
    low = jax.ShapeDtypeStruct(chip, BF16)
    high = jax.ShapeDtypeStruct(chip, F32)
    lists, counts = call(
        functools.partial(make_lists, n_seq, split),
        (
            jax.ShapeDtypeStruct((2, 4, n_listed + 1), jnp.int32),
            jax.ShapeDtypeStruct((2, 4), jnp.int32),
        ),
        2, us=2, name="block_lists",
    )(key_blocks, key_counts)

    halves = pltpu.VMEM((CORES, query_input.shape[0], HEADS // CORES * HEAD_DIM), BF16)
    kv_keep, kv_send, q_keep, q_send = call(
        functools.partial(prepare, n_seq), (kv_shape, kv_shape, q_shape, q_shape), 1,
        [
            pltpu.VMEM(key_input.shape, BF16), pltpu.VMEM(value_input.shape, BF16),
            pltpu.VMEM(table.shape, F32), halves, halves, pltpu.VMEM(q_shape.shape, BF16),
            pltpu.SemaphoreType.DMA((8,)),
        ],
        us=3, name="prepare", n_hbm=5, hbm_out=2,
    )(block_position, key_input, value_input, query_input, out_grad, table)
    kv_got = cross(kv_send, 1)
    q_send, kv_got = lax.optimization_barrier((q_send, kv_got))
    q_got = cross(q_send, 1)
    near = [jnp.stack([kv_keep, kv_got])]
    near.append(along(near[0], 1))
    ready, first_far = lax.optimization_barrier((near[1], onward(near[0])))
    far = [first_far, None]
    for k in range(2, n_pieces, 2):
        piece_k, lists, counts, _ = lax.optimization_barrier(
            (along(near[0], k), lists, counts, ready)
        )
        near += [piece_k, along(piece_k, 1)]
        far += [onward(piece_k), None]
    stats = call(
        functools.partial(current_stats, 1), stats_shape, 2, [pltpu.VMEM((split, *piece), BF16)],
        us=4, name="near_statistics", hold=(2,),
    )(lists, counts, q_keep, q_got, *near[:2])
    ready, far[2], stats = lax.optimization_barrier((ready, far[2], stats))
    far[1] = onward(ready)
    for k in range(2, n_pieces, 2):
        far[k + 1] = along(far[k], 1)
    stats = call(
        functools.partial(current_stats, 2), stats_shape, 2,
        [pltpu.VMEM((n_seq - split, *piece), BF16)], us=4, name="far_statistics",
    )(lists, counts, q_keep, q_got, stats, *near[2:])

    def grads_call(kernel, n_slots, n_store, outs, us, name, kept=(), more=()):
        pair = (n_slots, HALF_KV, 2, BLK, ROWS)
        saved = jax.ShapeDtypeStruct((2, *pair), BF16)
        return call(
            kernel, (*outs, saved, *more), 2,
            [
                pltpu.VMEM((n_store, *piece), BF16), pltpu.VMEM((n_store, *piece), F32),
                pltpu.VMEM(pair, BF16), pltpu.SemaphoreType.DMA((n_slots,)), *kept,
            ],
            us=us, name=name, hbm_out=len(outs),
        )

    kept = pltpu.VMEM((n_far, HALF_KV, BLK, ROWS), F32)
    two = jax.ShapeDtypeStruct((2 * CORES, *piece), BF16)
    first_far, *far_grads, far_saved, stats = grads_call(
        functools.partial(previous_grads, n_pieces), n_far, n_seq, (two,) + (low,) * (n_pieces - 2),
        14, "previous_gradients", (kept, kept), (stats_shape,),
    )(lists, counts, q_keep, q_got, stats, *far)

    def current_call(section, outs, name, pieces, after):
        stats_late, _ = lax.optimization_barrier((stats, after))
        n_store = CORES * len(pieces)
        *grads, saved = grads_call(
            functools.partial(current_grads, section, len(pieces)), min(n_store, n_listed), n_store,
            outs, 6, name,
        )(lists, counts, q_keep, q_got, stats_late, *pieces)
        return grads, saved

    def total(*terms):
        return sum(term.astype(F32) for term in terms).astype(BF16)

    from_far = back(first_far)
    crossing = [along(grad, 1) for grad in far_grads[1::2]]
    high_grads, high_saved = current_call(
        2, [high, low] * (n_pieces // 2 - 1), "far_current_gradients", near[2:], far_grads[0]
    )
    crossing, high_grads = lax.optimization_barrier((crossing, high_grads))
    arrived = [
        back(total(grad, extra)) for grad, extra in zip(far_grads[0::2], crossing)
    ]
    swapped = [along(grad, 1) for grad in high_grads[1::2]]
    low_grads, low_saved = current_call(
        1, [high, high], "near_current_gradients", near[:2], high_grads[0]
    )
    low_grads, from_far = lax.optimization_barrier((low_grads, from_far))
    from_next = along(total(low_grads[1], from_far[CORES:]), 1)
    merged = [
        total(*terms) for terms in zip(high_grads[0::2], arrived, swapped)
    ]
    half_out = jax.ShapeDtypeStruct((2, BLK, RATIO * HEAD_DIM), BF16)
    place_late, _ = lax.optimization_barrier((block_position, merged))
    wide = pltpu.VMEM((HEAD_DIM, ROWS), F32)
    slots = (HALF_KV, 2, n_listed + 3)
    halves = call(
        functools.partial(query_results, n_seq), (half_out,) * (2 * HALF_KV), 3,
        [
            pltpu.VMEM((2 * n_seq, *piece), BF16), pltpu.VMEM((*slots, 2, BLK, ROWS), BF16),
            wide, wide, pltpu.SemaphoreType.DMA(slots),
        ],
        us=20, name="query_results", n_hbm=3,
    )(lists, counts, place_late, far_saved, low_saved, high_saved, *far, *near, table)
    own_halves, other_halves = halves[:HALF_KV], halves[HALF_KV:]
    other_halves = lax.optimization_barrier(list(other_halves))
    got_halves = [cross(half, 1) for half in other_halves]
    final = [low_grads[0], from_far[:CORES], from_next]
    final += [along(part, 2 + 2 * n) for n, part in enumerate(merged)]
    own_halves = list(own_halves)
    final[0], own_halves[1] = lax.optimization_barrier((final[0], own_halves[1]))
    kv_half = jax.ShapeDtypeStruct((2, BLK, HALF_KV * HEAD_DIM), BF16)
    own_kv, other_kv = call(
        functools.partial(finish_kv, n_seq), (kv_half, kv_half), 1, us=2, name="key_gradients"
    )(block_position, *final, table)
    got_kv = cross(other_kv, 1)
    q_out = jax.ShapeDtypeStruct(query_input.shape, BF16)
    kv_out = jax.ShapeDtypeStruct(key_input.shape, BF16)
    out_rows, query_grad, key_grad, value_grad = call(
        join_halves, (q_out, q_out, kv_out, kv_out), 0, us=2, name="join_halves"
    )(*own_halves, *got_halves, own_kv, got_kv)
    return (out_rows, query_grad, key_grad, value_grad)


def solution(mesh):
    split = P(("grp", "seq"), None)
    return jax.shard_map(
        local,
        mesh=mesh,
        in_specs=(split, split, split, split, P(), P(), P()),
        out_specs=(split, split, split, split),
        check_vma=False,
    )
```
